32 devices in a mesh: space: 16 (over z, y, x), sig: 2 (over core).
Axes of the slice: x: 2, y: 2, z: 4, core: 2. Of those that a mesh axis runs over, the one named last changes fastest.
Arguments:
- positions: float32 [3, 32768], P(None, 'space'), may hold values from 0 to 8, as said below
- density: bfloat16 [34, 32768], P('sig', 'space'), may hold values from -4.2 to 13.2
- leaf_count: int32 [128], P('space'), may hold values from 1 to 256, as said below
- sigma_weights: float32 [34], P('sig'), may hold values from 0.1 to 2
Outputs:
- potential: float32 [34, 32768], P('sig', 'space')
- ensemble_mean: float32 [32768], P('space')
The draws below stay inside these ranges and needn't reach their ends.
Inputs may be any that keep to these rules, and one draw needn't show every extreme that they name: `positions`: each point lies in the unit cell of its leaf: g_l <= x_p < g_l + 1 in each component. `leaf_count`: in every draw some box has all 8 of its leaves at 256 points.
All inputs are finite; a program needn't handle non-finite values.
Results may differ from the reference program's by a relative error of at most 0.0003.
Values may be sent and summed in bfloat16 or wider, within the bound.
No kernel may reach another device: no remote copies, remote signals or barrier semaphores. Data moves between devices by JAX's collectives and lax.ppermute only.
A program may use at most 64 MiB of HBM per device.

```python
import math
import jax
import jax.numpy as jnp
import numpy as np
from jax import lax

ORDER = 5
LEAF_PTS = 256
SIGMAS = 34
LEAVES = 128
POINTS = 32768


def draw_positions(key, part):
    key = jax.random.fold_in(key, 11)
    labels = jnp.arange(POINTS) // LEAF_PTS
    box_label = labels // 8
    octant = labels % 8
    corner_x = 2 * (box_label % 4) + octant % 2
    corner_y = octant // 2 % 2
    corner_z = 2 * (box_label // 4) + octant // 4
    fresh = jax.random.uniform(key, (3, POINTS), jnp.float32)
    corners = jnp.stack([corner_x, corner_y, corner_z]).astype(jnp.float32)
    return corners + fresh


def draw_density(key, part):
    key = jax.random.fold_in(key, 12)
    base_key, column_key, noise_key = jax.random.split(key, 3)
    base_mass = jnp.exp(jax.random.uniform(base_key, (POINTS,), jnp.float32, math.log(0.3), math.log(3.0)))
    column_scale = jnp.exp(jax.random.uniform(column_key, (SIGMAS,), jnp.float32, math.log(0.3), math.log(3.0)))
    noise_part = jnp.clip(0.7 * jax.random.normal(noise_key, (SIGMAS, POINTS), jnp.float32), -4.2, 4.2)
    return (column_scale[:, None] * base_mass[None, :] + noise_part).astype(jnp.bfloat16)


def draw_leaf_count(key, part):
    key = jax.random.fold_in(key, 13)
    level_key, trim_key, full_key = jax.random.split(key, 3)
    boxes = LEAVES // 8
    region = jax.random.randint(level_key, (boxes,), 0, 4)
    ceiling = LEAF_PTS // 8 * jnp.power(2, region)
    ceiling_leaf = jnp.repeat(ceiling, 8)
    trimmed = ceiling_leaf - jax.random.randint(trim_key, (LEAVES,), 0, ceiling_leaf // 4 + 1)
    chosen = jax.random.randint(full_key, (), 0, boxes)
    filled = jnp.arange(LEAVES) // 8 == chosen
    return jnp.where(filled, LEAF_PTS, trimmed).astype(jnp.int32)


def level_of(own_key, extent, cuts, smallest, top_value):
    level = 1.0
    for position, shards_of in cuts:
        draws = jax.random.uniform(jax.random.fold_in(jax.random.fold_in(own_key, 6), position), (shards_of,), jnp.float32, smallest / len(cuts), top_value / len(cuts))
        level = level * jnp.repeat(jnp.exp(draws), extent[position] // shards_of).reshape((-1,) + (1,) * (len(extent) - 1 - position))
    return level


def setup_inputs(seed: int = 0) -> dict:
    splits = jax.random.split(jax.random.key(seed), 5)
    return {
        "positions": draw_positions(jax.random.fold_in(splits[4], 71), 0),
        "density": draw_density(jax.random.fold_in(splits[4], 71), 0),
        "leaf_count": draw_leaf_count(jax.random.fold_in(splits[4], 71), 0),
        "sigma_weights": jnp.clip(jnp.exp(math.log(2.0) - 2.9957323 * jax.random.uniform(splits[3], (SIGMAS,), jnp.float32) ** level_of(splits[3], (SIGMAS,), ((0, 2),), -0.2, 0.2)), 0.1, 2.0),
    }


softening = 0.1
across = 4
highest = lax.Precision.HIGHEST

def exponent_table(order_max):
    entries_list = []
    for degree in range(order_max + 1):
        for first_power in range(degree, -1, -1):
            for second_power in range(degree - first_power, -1, -1):
                entries_list.append((first_power, second_power, degree - first_power - second_power))
    return np.array(entries_list, dtype=np.int32)

def node_table(count_nodes, offset_value):
    counter = np.arange(1, count_nodes + 1, dtype=np.float32)[:, None]
    stride_set = np.array([0.7548776662466927, 0.5698402909980532, 0.4142135623730951], dtype=np.float32)[None, :]
    unit_points = np.mod(counter * stride_set + np.float32(offset_value), np.float32(1.0))
    return (np.float32(2.0) * unit_points - np.float32(1.0)).astype(np.float32)

def monomials(scaled, power_table):
    highest_power = int(power_table.max())
    power_lists = []
    for axis_number in range(3):
        current = jnp.ones_like(scaled[axis_number])
        column_list = [current]
        for repeat_count in range(highest_power):
            current = current * scaled[axis_number]
            column_list.append(current)
        power_lists.append(column_list)
    return jnp.stack([power_lists[0][int(exponents[0])] * power_lists[1][int(exponents[1])] * power_lists[2][int(exponents[2])] for exponents in power_table])

def kernel_value(first_part, second_part, third_part, coupling):
    return coupling / jnp.sqrt(first_part * first_part + second_part * second_part + third_part * third_part + softening * softening)

def translation(separation, half_width, check_nodes, equiv_nodes, coupling):
    shifted = [separation[..., axis_number, None, None] + half_width * (check_nodes[:, axis_number][:, None] - equiv_nodes[:, axis_number][None, :]) for axis_number in range(3)]
    return kernel_value(shifted[0], shifted[1], shifted[2], coupling) / check_nodes.shape[0]

def directions():
    return [(step_x, step_z) for step_z in (-1, 0, 1) for step_x in (-1, 0, 1) if step_x != 0 or step_z != 0]

def leaf_at(cell_x, cell_y, cell_z):
    box_label = cell_x // 2 + across * (cell_z // 2)
    return 8 * box_label + cell_x % 2 + 2 * cell_y + 4 * (cell_z % 2)

def leaf_lists(boxes):
    depth_z = boxes // across
    pad_row = 8 * boxes
    near_rows = np.full((8 * boxes, 18), pad_row, np.int32)
    far_rows = np.full((8 * boxes, 54), pad_row, np.int32)
    far_offsets = np.zeros((8 * boxes, 54, 3), np.float32)
    for leaf_label in range(8 * boxes):
        box_label = leaf_label // 8
        octant = leaf_label % 8
        box_x = box_label % across
        box_z = box_label // across
        cell_x = 2 * box_x + octant % 2
        cell_y = octant // 2 % 2
        cell_z = 2 * box_z + octant // 4
        near_count = 0
        for step_z in (-1, 0, 1):
            for step_x in (-1, 0, 1):
                for layer_y in (0, 1):
                    other_x = cell_x + step_x
                    other_z = cell_z + step_z
                    if 0 <= other_x < 2 * across and 0 <= other_z < 2 * depth_z:
                        near_rows[leaf_label, near_count] = leaf_at(other_x, layer_y, other_z)
                    near_count += 1
        far_count = 0
        for step_x, step_z in directions():
            for source_octant in range(8):
                gap_x = 2 * step_x + source_octant % 2 - octant % 2
                gap_y = source_octant // 2 % 2 - cell_y
                gap_z = 2 * step_z + source_octant // 4 - octant // 4
                if max(abs(gap_x), abs(gap_z)) >= 2:
                    inside = 0 <= box_x + step_x < across and 0 <= box_z + step_z < depth_z
                    if inside:
                        far_rows[leaf_label, far_count] = 8 * (box_x + step_x + across * (box_z + step_z)) + source_octant
                    far_offsets[leaf_label, far_count] = (-gap_x, -gap_y, -gap_z)
                    far_count += 1
    return (near_rows, far_rows, far_offsets)

def reference(positions, density, leaf_count, sigma_weights):
    leaves = leaf_count.shape[0]
    boxes = leaves // 8
    leaf_pts = positions.shape[1] // leaves
    sigmas = density.shape[0]
    power_table = exponent_table(ORDER)
    coeffs = power_table.shape[0]
    coupling = 1.0 / (128.0 * leaf_pts)
    check_nodes = jnp.asarray(node_table(coeffs, 0.5))
    equiv_nodes = jnp.asarray(node_table(coeffs, 0.0))
    near_rows, far_rows, far_offsets = leaf_lists(boxes)
    box_index = np.arange(boxes, dtype=np.int32)
    box_coords = np.stack([box_index % across, np.zeros((boxes,), np.int32), box_index // across], 1)
    octant_index = np.arange(8, dtype=np.int32)
    octant_bits = np.stack([octant_index % 2, octant_index // 2 % 2, octant_index // 4], 1)
    leaf_coords = (2 * box_coords[:, None, :] + octant_bits[None, :, :]).reshape(-1, 3)
    leaf_centre = jnp.asarray(leaf_coords.astype(np.float32) + np.float32(0.5))
    box_centre = jnp.asarray((2 * box_coords + 1).astype(np.float32))
    slot_mask = (jnp.arange(leaf_pts)[None, :] < leaf_count[:, None]).astype(jnp.float32)
    leaf_mass = jnp.transpose(density.astype(jnp.float32).reshape(sigmas, leaves, leaf_pts), (1, 0, 2)) * slot_mask[:, None, :]
    leaf_points = jnp.transpose(positions.reshape(3, leaves, leaf_pts), (1, 0, 2))
    leaf_basis = monomials(2.0 * (jnp.transpose(leaf_points, (1, 0, 2)) - jnp.transpose(leaf_centre)[:, :, None]), power_table)
    leaf_moment = jnp.einsum('klp,lsp->lks', leaf_basis, leaf_mass, precision=highest)
    box_points = positions.reshape(3, boxes, 8 * leaf_pts)
    box_basis = monomials(box_points - jnp.transpose(box_centre)[:, :, None], power_table)
    box_mass = jnp.transpose(leaf_mass.reshape(boxes, 8, sigmas, leaf_pts), (0, 2, 1, 3)).reshape(boxes, sigmas, 8 * leaf_pts)
    box_moment = jnp.einsum('kbp,bsp->bks', box_basis, box_mass, precision=highest)
    padded_points = jnp.concatenate([leaf_points, jnp.zeros((1, 3, leaf_pts), jnp.float32)], 0)
    padded_mass = jnp.concatenate([leaf_mass, jnp.zeros((1, sigmas, leaf_pts), jnp.float32)], 0)
    padded_moment = jnp.concatenate([leaf_moment, jnp.zeros((1, coeffs, sigmas), jnp.float32)], 0)

    def leaf_potential(inputs):
        target_points, near_index, far_index, far_separation, target_basis = inputs
        source_points = jnp.transpose(padded_points[near_index], (1, 0, 2)).reshape(3, -1)
        kernel_block = kernel_value(target_points[0][:, None] - source_points[0][None, :], target_points[1][:, None] - source_points[1][None, :], target_points[2][:, None] - source_points[2][None, :], coupling)
        source_mass = jnp.transpose(padded_mass[near_index], (1, 0, 2)).reshape(sigmas, -1)
        near_part = jnp.dot(source_mass, jnp.transpose(kernel_block), precision=highest)
        operator = translation(far_separation, 0.5, check_nodes, equiv_nodes, coupling)
        local_leaf = jnp.einsum('ejk,eks->js', operator, padded_moment[far_index], precision=highest)
        far_part = jnp.einsum('kp,ks->sp', target_basis, local_leaf, precision=highest)
        return near_part + far_part
    leaf_part = lax.map(leaf_potential, (leaf_points, jnp.asarray(near_rows, jnp.int32), jnp.asarray(far_rows, jnp.int32), jnp.asarray(far_offsets), jnp.transpose(leaf_basis, (1, 0, 2))))

    def box_potential(inputs):
        target_centre, target_basis = inputs
        separation = target_centre[None, :] - box_centre
        far_flag = (jnp.maximum(jnp.abs(separation[:, 0]), jnp.abs(separation[:, 2])) >= 3.5).astype(jnp.float32)
        operator = translation(separation, 1.0, check_nodes, equiv_nodes, coupling) * far_flag[:, None, None]
        local_box = jnp.einsum('bjk,bks->js', operator, box_moment, precision=highest)
        return jnp.einsum('kp,ks->sp', target_basis, local_box, precision=highest)
    coarse_part = lax.map(box_potential, (box_centre, jnp.transpose(box_basis, (1, 0, 2))))
    coarse_leaf = jnp.transpose(coarse_part.reshape(boxes, sigmas, 8, leaf_pts), (0, 2, 1, 3)).reshape(leaves, sigmas, leaf_pts)
    total_leaf = (leaf_part + coarse_leaf) * slot_mask[:, None, :]
    potential = jnp.transpose(total_leaf, (1, 0, 2)).reshape(sigmas, leaves * leaf_pts)
    weighted = lax.optimization_barrier(jnp.sum(sigma_weights[:, None] * potential, 0))
    ensemble_mean = weighted / jnp.sum(sigma_weights)
    return (potential, ensemble_mean)
```

```python
import functools
import math

import jax
import jax.numpy as jnp
import numpy as np
from jax import lax
from jax.experimental import pallas as pl
from jax.experimental.pallas import tpu as pltpu
from jax.sharding import PartitionSpec as P

ORDER = 5
SOFTENING = 0.1
ACROSS = 4
SLOT = 64
ROWS = 32
FEATURES = 48


def exponent_table(order_max):
    entries_list = []
    for degree in range(order_max + 1):
        for first_power in range(degree, -1, -1):
            for second_power in range(degree - first_power, -1, -1):
                entries_list.append((first_power, second_power, degree - first_power - second_power))
    return entries_list


def node_table(count_nodes, offset_value):
    counter = np.arange(1, count_nodes + 1, dtype=np.float32)[:, None]
    stride_set = np.array([0.7548776662466927, 0.5698402909980532, 0.4142135623730951], dtype=np.float32)[None, :]
    unit_points = np.mod(counter * stride_set + np.float32(offset_value), np.float32(1.0))
    return (np.float32(2.0) * unit_points - np.float32(1.0)).astype(np.float32)


EXPONENTS = exponent_table(ORDER)
COEFFS = len(EXPONENTS)
CHECK = node_table(COEFFS, 0.5).astype(np.float64)
EQUIV = node_table(COEFFS, 0.0).astype(np.float64)
STEPS = [(sx, sz) for sz in (-1, 0, 1) for sx in (-1, 0, 1) if sx != 0 or sz != 0]


def bits(octant):
    return octant % 2, octant // 2 % 2, octant // 4


def facing_octants(step_x, step_z):
    chosen = []
    for octant in range(8):
        bit_x, _, bit_z = bits(octant)
        keep_x = step_x == 0 or bit_x == (0 if step_x > 0 else 1)
        keep_z = step_z == 0 or bit_z == (0 if step_z > 0 else 1)
        if keep_x and keep_z:
            chosen.append(octant)
    return chosen


def leaf_slot(octant):
    bit_x, bit_y, bit_z = bits(octant)
    return (bit_x + 2 * bit_z) * 2 + bit_y


def split_table(table):
    high = table.astype(np.float32).astype(jnp.bfloat16)
    low = (table - high.astype(np.float64)).astype(np.float32).astype(jnp.bfloat16)
    return high, low


@functools.lru_cache(None)
def far_table():
    shape = (len(STEPS), 8, SLOT, 8, SLOT)
    table = np.zeros(shape)
    gap_nodes = 0.5 * (CHECK[None, :, :] - EQUIV[:, None, :])
    for index, (step_x, step_z) in enumerate(STEPS):
        for source in range(8):
            for target in range(8):
                s, t = bits(source), bits(target)
                gap = np.array([2 * step_x + s[0] - t[0], s[1] - t[1], 2 * step_z + s[2] - t[2]], np.float64)
                if max(abs(gap[0]), abs(gap[2])) >= 2:
                    shifted = gap_nodes - gap
                    value = 1.0 / np.sqrt(np.sum(shifted * shifted, -1) + SOFTENING * SOFTENING) / COEFFS
                    table[index, source, :COEFFS, target, :COEFFS] = value
    return split_table(table.reshape(len(STEPS) * 8 * SLOT, 8 * SLOT))


@functools.lru_cache(None)
def shift_table():
    table = np.zeros((8, SLOT, SLOT))
    for leaf in range(8):
        offset = [bit - 0.5 for bit in bits(leaf)]
        for k, target in enumerate(EXPONENTS):
            for i, source in enumerate(EXPONENTS):
                if all(b <= a for a, b in zip(target, source)):
                    value = 1.0
                    for a, b, h in zip(target, source, offset):
                        value *= math.comb(a, b) * 0.5**b * h ** (a - b)
                    table[leaf, i, k] = value
    return table.reshape(8 * SLOT, SLOT)


@functools.lru_cache(None)
def box_nodes():
    gaps = np.zeros((3, SLOT, SLOT))
    gaps[:, :COEFFS, :COEFFS] = np.moveaxis(CHECK[None, :, :] - EQUIV[:, None, :], -1, 0)
    gaps[1] = gaps[1] ** 2 + SOFTENING * SOFTENING
    return gaps.astype(np.float32)


def centre_table(leaf_pts):
    table = np.zeros((3, 8, leaf_pts), np.float32)
    for octant in range(8):
        for axis, bit in enumerate(bits(octant)):
            table[axis, octant] = bit + 0.5
    return table.reshape(3, 8 * leaf_pts)


def high_low(value):
    high = value.astype(jnp.bfloat16)
    low = (value - high.astype(jnp.float32)).astype(jnp.bfloat16)
    return high, low


def dot(left, right):
    return jnp.dot(left, right, preferred_element_type=jnp.float32)


def dot_nt(left, right):
    return lax.dot_general(left, right, (((1,), (1,)), ((), ())), preferred_element_type=jnp.float32)


def by_row(values, shape):
    row = lax.broadcasted_iota(jnp.int32, shape, 0)
    result = jnp.zeros(shape, jnp.float32)
    for index, value in enumerate(values):
        result = jnp.where(row == index, value, result)
    return result


def box_place():
    label = lax.axis_index("space")
    return lax.rem(label, ACROSS), lax.div(label, ACROSS)


def pack_kernel(count, positions, density, centres, shift, own, basis, slots, *rest):
    payloads, mono = rest[:-1], rest[-1]
    fields, points = density.shape
    pts = points // 8
    box_x, box_z = box_place()
    corner = by_row([2.0 * box_x.astype(jnp.float32), 0.0, 2.0 * box_z.astype(jnp.float32)], (3, 1))
    local = positions[...] - (centres[...] + corner)
    high = local.astype(jnp.bfloat16).astype(jnp.float32)
    middle = (local - high).astype(jnp.bfloat16).astype(jnp.float32)
    low = local - high - middle
    lane = lax.broadcasted_iota(jnp.int32, (fields, pts), 1)
    raw = density[...].astype(jnp.float32)
    mass = jnp.concatenate(
        [jnp.where(lane < count[leaf], raw[:, leaf * pts : (leaf + 1) * pts], 0.0) for leaf in range(8)], axis=1
    )
    spare = jnp.zeros((ROWS - fields - 9, points), jnp.float32)
    own[...] = jnp.concatenate([mass, high, middle, low, spare], axis=0).astype(jnp.bfloat16)

    scaled = 2.0 * local
    axes = [
        jnp.concatenate([scaled[a : a + 1, leaf * pts : (leaf + 1) * pts] for leaf in range(8)], axis=0)
        for a in range(3)
    ]
    made = {(0, 0, 0): jnp.ones((8, pts), jnp.float32)}
    for k, powers in enumerate(EXPONENTS):
        if powers not in made:
            a = next(i for i in range(3) if powers[i] > 0)
            before = tuple(p - (i == a) for i, p in enumerate(powers))
            made[powers] = made[before] * axes[a]
        mono[k] = made[powers]
    mono[COEFFS:SLOT] = jnp.zeros((SLOT - COEFFS, 8, pts), jnp.float32)
    moments = []
    for leaf in range(8):
        part = pl.ds(leaf * pts, pts)
        basis_high, basis_low = high_low(mono[:, leaf, :])
        basis[0:SLOT, part] = basis_high
        basis[SLOT : 2 * SLOT, part] = basis_low
        block = own[:, part]
        moments.append(dot_nt(block, basis_high) + dot_nt(block, basis_low))
    moment_high, moment_low = high_low(jnp.concatenate(moments, axis=1))
    box_moment = dot(moment_high, shift[...]) + dot(moment_low, shift[...])
    slot = jnp.concatenate([box_moment, jnp.zeros_like(box_moment)], axis=1)
    slots[...] = jnp.broadcast_to(slot[None], slots.shape)
    for (step_x, step_z), payload in zip(STEPS, payloads):
        chosen = facing_octants(step_x, step_z)
        for place, leaf in enumerate(chosen):
            payload[:, pl.ds(place * pts, pts)] = own[:, pl.ds(leaf * pts, pts)]
        base = len(chosen) * pts
        payload[:, pl.ds(base, 8 * SLOT)] = moment_high
        payload[:, pl.ds(base + 8 * SLOT, 8 * SLOT)] = moment_low


def features(piece, centre, target):
    value = piece.astype(jnp.float32)
    x = value[1:4] + value[4:7] + value[7:10] + by_row(centre, (3, 1))
    norm = jnp.sum(x * x, axis=0, keepdims=True)
    if target:
        norm = norm + SOFTENING * SOFTENING
    parts, norms = [], []
    for source, out in ((x, parts), (norm, norms)):
        left = source
        for _ in range(3):
            high = left.astype(jnp.bfloat16).astype(jnp.float32)
            out.append(high)
            left = left - high
    one = jnp.ones_like(norm)
    zero = jnp.zeros_like(norm)
    blank = jnp.zeros((3, norm.shape[1]), jnp.float32)
    blocks = []
    order = (0, 1, 0, 2, 0, 1) if target else (0, 0, 1, 0, 2, 1)
    for index, which in enumerate(order):
        coords = -2.0 * parts[which] if target else parts[which]
        if index < 3:
            pair = [one, norms[index]] if target else [norms[index], one]
        else:
            pair = [zero, zero]
        blocks += [coords, *pair, blank]
    return jnp.concatenate(blocks, axis=0)


def cell_places(pts):
    places = [None] * 32
    for octant in range(8):
        x, y, z = bits(octant)
        places[1 + x + 4 * y + 8 * (1 + z)] = (-1, octant * pts)
    for index, (step_x, step_z) in enumerate(STEPS):
        for place, octant in enumerate(facing_octants(step_x, step_z)):
            bit_x, bit_y, bit_z = bits(octant)
            x = 1 + bit_x + 2 * step_x
            z = 1 + bit_z + 2 * step_z
            places[x + 4 * bit_y + 8 * z] = (index, place * pts)
    return [
        (array, lane, (cell % 4 - 1.5, cell // 4 % 2 - 0.5, cell // 8 - 1.5))
        for cell, (array, lane) in enumerate(places)
    ]


def field_kernel(count, weights, own, basis, slots, nodes, shift, *rest):
    payloads, rest = rest[: len(STEPS)], rest[len(STEPS) :]
    far_high, far_low, potential, sums, source, masses, target, near, table_high, table_low, sems = rest
    fields, points = potential.shape
    pts = points // 8
    boxes = slots.shape[0]
    loads = [
        pltpu.make_async_copy(far_high, table_high, sems.at[0]),
        pltpu.make_async_copy(far_low, table_low, sems.at[1]),
    ]
    for load in loads:
        load.start()

    for cell, (array, lane, centre) in enumerate(cell_places(pts)):
        held = own if array < 0 else payloads[array]
        place = pl.ds(cell * pts, pts)
        piece = held[16:32, pl.ds(lane, pts)]
        masses[:, place] = held[0:ROWS, pl.ds(lane, pts)]
        source[place, :] = jnp.transpose(features(piece, centre, False)).astype(jnp.bfloat16)
        if array < 0:
            leaf = lane // pts
            target[:, pl.ds(leaf_slot(leaf) * pts, pts)] = features(piece, centre, True).astype(jnp.bfloat16)

    wide = 2 * pts
    for group in range(4):
        first = group % 2 + 8 * (group // 2)
        points_in = target[:, group * wide : (group + 1) * wide]

        def layer(index, total, first=first, points_in=points_in):
            for step_y in range(2):
                start = pl.multiple_of((first + 4 * step_y + 8 * index) * pts, pts)
                for step_x in range(3):
                    place = pl.ds(start + step_x * pts, pts)
                    kernel = lax.rsqrt(dot(source[place, :], points_in))
                    kernel_high, kernel_low = high_low(kernel)
                    mass = masses[:, place]
                    total = total + dot(mass, kernel_high) + dot(mass, kernel_low)
            return total

        near[:, group * wide : (group + 1) * wide] = lax.fori_loop(
            0, 3, layer, jnp.zeros((ROWS, wide), jnp.float32)
        )

    box_x, box_z = box_place()
    lefts, rights = [], []
    for box in range(0, boxes, 2):
        lefts.append(jnp.concatenate([slots[box][:, :SLOT], slots[box + 1][:, :SLOT]], axis=1))
    for box in range(boxes):
        gap_x = 2 * (box_x - box % ACROSS)
        gap_z = 2 * (box_z - box // ACROSS)
        across_x = nodes[0] + gap_x.astype(jnp.float32)
        across_z = nodes[2] + gap_z.astype(jnp.float32)
        value = lax.rsqrt(across_x * across_x + across_z * across_z + nodes[1])
        far = jnp.maximum(jnp.abs(gap_x), jnp.abs(gap_z)) >= 4
        rights.append(value * jnp.where(far, 1.0 / COEFFS, 0.0))
    left_high, left_low = high_low(jnp.concatenate(lefts, axis=1))
    right_high, right_low = high_low(jnp.concatenate(rights, axis=0))
    box_local = dot(left_high, right_high) + dot(left_high, right_low) + dot(left_low, right_high)
    box_high, box_low = high_low(box_local)
    local = dot(box_high, shift[...]) + dot(box_low, shift[...])

    highs, lows = [], []
    for (step_x, step_z), payload in zip(STEPS, payloads):
        base = len(facing_octants(step_x, step_z)) * pts
        highs.append(payload[:, pl.ds(base, 8 * SLOT)])
        lows.append(payload[:, pl.ds(base + 8 * SLOT, 8 * SLOT)])
    for load in loads:
        load.wait()
    for index in range(len(STEPS)):
        rows = pl.ds(index * 8 * SLOT, 8 * SLOT)
        local = local + dot(highs[index], table_high[rows, :]) + dot(lows[index], table_high[rows, :])
        local = local + dot(highs[index], table_low[rows, :])
    local_high, local_low = high_low(local)

    weight_column = by_row([weights[field] for field in range(fields)], (fields, 1))
    lane_index = lax.broadcasted_iota(jnp.int32, (fields, pts), 1)
    coupling = 1.0 / (128.0 * pts)
    for leaf in range(8):
        part = pl.ds(leaf * pts, pts)
        here = slice(leaf * SLOT, (leaf + 1) * SLOT)
        left = jnp.concatenate([local_high[:, here], local_high[:, here]], axis=1)
        far_part = dot(left, basis[:, part]) + dot(local_low[:, here], basis[0:SLOT, part])
        total = (near[:, pl.ds(leaf_slot(leaf) * pts, pts)] + far_part)[:fields]
        total = jnp.where(lane_index < count[leaf], total * coupling, 0.0)
        potential[:, part] = total
        sums[:, part] = jnp.sum(total * weight_column, axis=0, keepdims=True)
    sums[:, points:] = jnp.broadcast_to(jnp.sum(weight_column), (1, sums.shape[1] - points))


def sent_on(block, step_x, step_z):
    boxes = lax.axis_size("space")
    route = []
    for box in range(boxes):
        x, z = box % ACROSS + step_x, box // ACROSS + step_z
        if 0 <= x < ACROSS and 0 <= z < boxes // ACROSS:
            route.append((x + ACROSS * z, box))
    return lax.ppermute(block, "space", route)


def per_device(positions, density, leaf_count, sigma_weights):
    fields, points = density.shape
    pts = points // 8
    boxes = lax.axis_size("space")
    vmem, smem = pl.BlockSpec(memory_space=pltpu.VMEM), pl.BlockSpec(memory_space=pltpu.SMEM)
    anywhere = pl.BlockSpec(memory_space=pl.ANY)
    limit = pltpu.CompilerParams(vmem_limit_bytes=48 * 1024 * 1024)
    shift = shift_table()
    payload_shapes = [
        jax.ShapeDtypeStruct((ROWS, len(facing_octants(*step)) * pts + 16 * SLOT), jnp.bfloat16) for step in STEPS
    ]
    own, basis, slots, *payloads = pl.pallas_call(
        pack_kernel,
        in_specs=[smem, vmem, vmem, vmem, vmem],
        out_specs=[vmem] * (3 + len(STEPS)),
        out_shape=[
            jax.ShapeDtypeStruct((ROWS, points), jnp.bfloat16),
            jax.ShapeDtypeStruct((2 * SLOT, points), jnp.bfloat16),
            jax.ShapeDtypeStruct((boxes, ROWS, 2 * SLOT), jnp.float32),
            *payload_shapes,
        ],
        scratch_shapes=[pltpu.VMEM((SLOT, 8, pts), jnp.float32)],
        compiler_params=limit,
        name="pack",
    )(leaf_count, positions, density, jnp.asarray(centre_table(pts)), jnp.asarray(shift, jnp.bfloat16))
    all_slots = lax.all_to_all(slots, "space", 0, 0, tiled=True)
    received = [sent_on(payload, *step) for step, payload in zip(STEPS, payloads)]
    far_high, far_low = far_table()
    potential, sums = pl.pallas_call(
        field_kernel,
        in_specs=[smem, smem] + [vmem] * (5 + len(STEPS)) + [anywhere, anywhere],
        out_specs=[vmem, vmem],
        out_shape=[
            jax.ShapeDtypeStruct((fields, points), jnp.float32),
            jax.ShapeDtypeStruct((1, points + 128), jnp.float32),
        ],
        scratch_shapes=[
            pltpu.VMEM((32 * pts, FEATURES), jnp.bfloat16),
            pltpu.VMEM((ROWS, 32 * pts), jnp.bfloat16),
            pltpu.VMEM((FEATURES, points), jnp.bfloat16),
            pltpu.VMEM((ROWS, points), jnp.float32),
            pltpu.VMEM(far_high.shape, jnp.bfloat16),
            pltpu.VMEM(far_low.shape, jnp.bfloat16),
            pltpu.SemaphoreType.DMA((2,)),
        ],
        compiler_params=limit,
        name="field",
    )(
        leaf_count,
        sigma_weights,
        own,
        basis,
        all_slots,
        jnp.asarray(box_nodes()),
        jnp.asarray(shift.T.copy(), jnp.bfloat16),
        *received,
        jnp.asarray(far_high),
        jnp.asarray(far_low),
    )
    sums = lax.psum(sums, "sig")
    return potential, sums[0, :points] / sums[0, points]


def solution(mesh):
    in_specs = (P(None, "space"), P("sig", "space"), P("space"), P("sig"))
    out_specs = (P("sig", "space"), P("space"))
    return jax.shard_map(per_device, mesh=mesh, in_specs=in_specs, out_specs=out_specs, check_vma=False)
```

```python
import functools
import math

import jax
import jax.numpy as jnp
import numpy as np
from jax import lax
from jax.experimental import pallas as pl
from jax.experimental.pallas import tpu as pltpu
from jax.sharding import PartitionSpec as P

ORDER = 5
SOFTENING = 0.1
ACROSS = 4
SLOT = 64
ROWS = 32
LEAVES = 8 * SLOT
MEGA = 1024 * 1024
FEATURES = 48


def exponent_table(order_max):
    entries_list = []
    for degree in range(order_max + 1):
        for first_power in range(degree, -1, -1):
            for second_power in range(degree - first_power, -1, -1):
                entries_list.append((first_power, second_power, degree - first_power - second_power))
    return entries_list


def node_table(count_nodes, offset_value):
    counter = np.arange(1, count_nodes + 1, dtype=np.float32)[:, None]
    stride_set = np.array([0.7548776662466927, 0.5698402909980532, 0.4142135623730951], dtype=np.float32)[None, :]
    unit_points = np.mod(counter * stride_set + np.float32(offset_value), np.float32(1.0))
    return (np.float32(2.0) * unit_points - np.float32(1.0)).astype(np.float32)


EXPONENTS = exponent_table(ORDER)
COEFFS = len(EXPONENTS)
CHECK = node_table(COEFFS, 0.5).astype(np.float64)
EQUIV = node_table(COEFFS, 0.0).astype(np.float64)
STEPS = [(sx, sz) for sz in (-1, 0, 1) for sx in (-1, 0, 1) if sx != 0 or sz != 0]


def bits(octant):
    return octant % 2, octant // 2 % 2, octant // 4


def touching(distance):
    return distance & (distance + 1) == 0


def leaf_slot(octant):
    bit_x, bit_y, bit_z = bits(octant)
    return (bit_x + 2 * bit_z) * 2 + bit_y


@functools.lru_cache(None)
def far_table():
    shape = (len(STEPS), 8, SLOT, 8, SLOT)
    table = np.zeros(shape)
    gap_nodes = 0.5 * (CHECK[None, :, :] - EQUIV[:, None, :])
    for index, (step_x, step_z) in enumerate(STEPS):
        for source in range(8):
            for target in range(8):
                s, t = bits(source), bits(target)
                gap = np.array([2 * step_x + s[0] - t[0], s[1] - t[1], 2 * step_z + s[2] - t[2]], np.float64)
                if max(abs(gap[0]), abs(gap[2])) >= 2:
                    shifted = gap_nodes - gap
                    value = 1.0 / np.sqrt(np.sum(shifted * shifted, -1) + SOFTENING * SOFTENING) / COEFFS
                    table[index, source, :COEFFS, target, :COEFFS] = value
    return table.reshape(len(STEPS) * LEAVES, LEAVES)


@functools.lru_cache(None)
def shift_table():
    table = np.zeros((8, SLOT, SLOT))
    for leaf in range(8):
        offset = [bit - 0.5 for bit in bits(leaf)]
        for k, target in enumerate(EXPONENTS):
            for i, source in enumerate(EXPONENTS):
                if all(b <= a for a, b in zip(target, source)):
                    value = 1.0
                    for a, b, h in zip(target, source, offset):
                        value *= math.comb(a, b) * 0.5**b * h ** (a - b)
                    table[leaf, i, k] = value
    return table.reshape(8 * SLOT, SLOT)


@functools.lru_cache(None)
def box_nodes():
    gaps = np.zeros((3, SLOT, SLOT))
    gaps[:, :COEFFS, :COEFFS] = np.moveaxis(CHECK[None, :, :] - EQUIV[:, None, :], -1, 0)
    gaps[1] = gaps[1] ** 2 + SOFTENING * SOFTENING
    return gaps.astype(np.float32)


def dot(left, right):
    return jnp.dot(left, right, preferred_element_type=jnp.float32)


def dot_nt(left, right):
    return lax.dot_general(left, right, (((1,), (1,)), ((), ())), preferred_element_type=jnp.float32)


def low_bits(value):
    return value.astype(jnp.bfloat16)


def high_low(value):
    high = low_bits(value)
    return high, low_bits(value - high.astype(jnp.float32))


def by_row(values, shape):
    row = lax.broadcasted_iota(jnp.int32, shape, 0)
    result = jnp.zeros(shape, jnp.float32)
    for index, value in enumerate(values):
        result = jnp.where(row == index, value, result)
    return result


def box_place():
    label = lax.axis_index("space")
    return lax.rem(label, ACROSS), lax.div(label, ACROSS)


def lanes(start, size):
    return pl.ds(start if isinstance(start, int) else pl.multiple_of(start, 128), size)


def fetch(pairs, sems):
    copies = [pltpu.make_async_copy(src, dst, sems.at[i]) for i, (src, dst) in enumerate(pairs)]
    for copy in copies:
        copy.start()
    return copies


def pack_kernel(count_in, positions_in, density_in, shift_in, own, basis, moments, totals, *rest):
    payloads, (count, positions, density, shift, mono, sems) = rest[:3], rest[3:]
    copies = fetch(
        [(count_in, count), (positions_in, positions), (density_in, density), (shift_in, shift)], sems
    )
    fields, points = density.shape
    pts = points // 8
    box_x, box_z = box_place()
    for copy in copies:
        copy.wait()
    local = []
    for leaf in range(8):
        bit_x, bit_y, bit_z = bits(leaf)
        centre = by_row(
            [2.0 * box_x.astype(jnp.float32) + (bit_x + 0.5), bit_y + 0.5, 2.0 * box_z.astype(jnp.float32) + (bit_z + 0.5)],
            (3, 1),
        )
        here = slice(leaf * pts, (leaf + 1) * pts)
        offset = positions[:, here] - centre
        local.append(offset)
        high = low_bits(offset).astype(jnp.float32)
        middle = low_bits(offset - high).astype(jnp.float32)
        low = offset - high - middle
        raw = density[:, here].astype(jnp.float32)
        mass = jnp.where(lax.broadcasted_iota(jnp.int32, raw.shape, 1) < count[leaf], raw, 0.0)
        spare = jnp.zeros((ROWS - fields - 9, pts), jnp.float32)
        own[:, here] = low_bits(jnp.concatenate([mass, high, middle, low, spare], axis=0))

    axes = [2.0 * jnp.concatenate([part[a : a + 1] for part in local], axis=0) for a in range(3)]
    made = {(0, 0, 0): jnp.ones((8, pts), jnp.float32)}
    for k, powers in enumerate(EXPONENTS):
        if powers not in made:
            a = next(i for i in range(3) if powers[i] > 0)
            before = tuple(p - (i == a) for i, p in enumerate(powers))
            made[powers] = made[before] * axes[a]
        mono[k] = made[powers]
    mono[COEFFS:SLOT] = jnp.zeros((SLOT - COEFFS, 8, pts), jnp.float32)
    parts = []
    for leaf in range(8):
        here = slice(leaf * pts, (leaf + 1) * pts)
        high, low = high_low(mono[:, leaf, :])
        basis[0:SLOT, here] = high
        basis[SLOT:, here] = low
        parts.append(dot_nt(own[:, here], high))
    moment, rest = high_low(jnp.concatenate(parts, axis=1))
    moments[...] = moment
    total = dot(moment, shift[...]) + dot(rest, shift[...])
    total = jnp.concatenate(high_low(total), axis=1)
    totals[...] = total
    payloads[1][...] = total
    for distance, payload in ((1, payloads[0]), (3, payloads[2])):
        bit = jnp.where((box_x ^ distance) > box_x, 1, 0)
        for place in range(4):
            payload[:, lanes(place * pts, pts)] = own[:, lanes((bit + 2 * place) * pts, pts)]
        payload[:, lanes(4 * pts, LEAVES)] = moment
        payload[:, lanes(4 * pts + LEAVES, 2 * SLOT)] = total


def features(held, start, size, centre, target):
    value = held[16:32, lanes(start, size)].astype(jnp.float32)
    x = value[1:4] + value[4:7] + value[7:10] + by_row(centre, (3, 1))
    norm = jnp.sum(x * x, axis=0, keepdims=True)
    if target:
        norm = norm + SOFTENING * SOFTENING
    parts, norms = [], []
    for source, out in ((x, parts), (norm, norms)):
        left = source
        for _ in range(3):
            high = low_bits(left).astype(jnp.float32)
            out.append(high)
            left = left - high
    one = jnp.ones_like(norm)
    zero = jnp.zeros_like(norm)
    blank = jnp.zeros((3, norm.shape[1]), jnp.float32)
    blocks = []
    order = (0, 1, 0, 2, 0, 1) if target else (0, 0, 1, 0, 2, 1)
    for index, which in enumerate(order):
        coords = -2.0 * parts[which] if target else parts[which]
        if index < 3:
            pair = [one, norms[index]] if target else [norms[index], one]
        else:
            pair = [zero, zero]
        blocks += [coords, *pair, blank]
    return jnp.concatenate(blocks, axis=0)


def source_features(held, start, size, centre):
    return low_bits(jnp.transpose(features(held, start, size, centre, False)))


def pulled(total, wanted, source, masses, starts, pts):
    for start in starts:
        place = lanes(start, pts)
        kernel = lax.rsqrt(dot(source[place, :], wanted))
        high = low_bits(kernel)
        low = low_bits(kernel - high.astype(jnp.float32))
        mass = masses[:, place]
        total = total + dot(mass, high) + dot(mass, low)
    return total


def own_kernel(own, far_in, nodes_in, spread_in, near, source, target, far, nodes, spread, sems):
    copies = fetch([(far_in, far), (nodes_in, nodes), (spread_in, spread)], sems)
    points = own.shape[1]
    pts = points // 8
    for leaf in range(8):
        centre = [bit - 0.5 for bit in bits(leaf)]
        source[lanes(leaf * pts, pts), :] = source_features(own, leaf * pts, pts, centre)
        target[:, lanes(leaf_slot(leaf) * pts, pts)] = low_bits(features(own, leaf * pts, pts, centre, True))

    def group(index, carry):
        here = lanes(index * (2 * pts), 2 * pts)
        zero = jnp.zeros((ROWS, 2 * pts), jnp.float32)
        near[:, here] = pulled(zero, target[:, here], source, own, [leaf * pts for leaf in range(8)], pts)
        return carry

    lax.fori_loop(0, 2, group, 0)
    for copy in copies:
        copy.wait()


def row_kernel(depth, own, moments, totals, from_1, from_2, from_3, far, nodes, spread, *rest):
    left, right, own_local, *payloads = rest
    points = own.shape[1]
    pts = points // 8
    box_x, box_z = box_place()
    wide = 4 * pts + LEAVES
    for side, step in ((left, -1), (right, 1)):
        side[...] = jnp.zeros(side.shape, side.dtype)
        for distance, held in ((1, from_1), (3, from_3)):

            @pl.when((box_x ^ distance) - box_x == step)
            def _(side=side, held=held):
                side[...] = held[:, lanes(0, wide)]

    base = 4 * pts
    row = jnp.concatenate([left[:, lanes(base, LEAVES)], moments[...], right[:, lanes(base, LEAVES)]], axis=1)
    below_rows, same_rows, above_rows = pl.ds(0, 3 * LEAVES), pl.ds(3 * LEAVES, 2 * LEAVES), pl.ds(5 * LEAVES, 3 * LEAVES)
    up = dot(row, far[below_rows, :])
    down = dot(row, far[above_rows, :])
    same = dot(jnp.concatenate([row[:, :LEAVES], row[:, 2 * LEAVES :]], axis=1), far[same_rows, :])

    boxes = [totals[...], from_1[:, lanes(wide, 2 * SLOT)], from_2[...], from_3[:, lanes(wide, 2 * SLOT)]]
    boxes_high = jnp.concatenate([held[:, :SLOT] for held in boxes], axis=1)
    boxes_low = jnp.concatenate([held[:, SLOT:] for held in boxes], axis=1)
    columns = []
    for distance_z in range(depth):
        gap_z = 2 * ((box_z ^ distance_z) - box_z)
        across_z = nodes[2] + gap_z.astype(jnp.float32)
        rest_z = across_z * across_z + nodes[1]
        blocks = []
        for distance_x in range(ACROSS):
            gap_x = 2 * (box_x - (box_x ^ distance_x))
            across_x = nodes[0] + gap_x.astype(jnp.float32)
            distant = jnp.maximum(jnp.abs(gap_x), jnp.abs(gap_z)) >= 4
            blocks.append(lax.rsqrt(across_x * across_x + rest_z) * jnp.where(distant, 1.0 / COEFFS, 0.0))
        columns.append(jnp.concatenate(blocks, axis=0))
    columns = low_bits(jnp.concatenate(columns, axis=1))
    coarse = dot(boxes_high, columns) + dot(boxes_low, columns)
    coarse = jnp.concatenate([coarse[:, d * SLOT : (d + 1) * SLOT] for d in range(depth)], axis=0)
    coarse_high, coarse_low = high_low(coarse)
    coarse = dot(coarse_high, spread[...]) + dot(coarse_low, spread[...])

    own_local[...] = same + coarse[:ROWS]
    for distance in range(1, depth):
        payload = payloads[distance - 1]
        gap = (box_z ^ distance) - box_z
        given = coarse[distance * ROWS : (distance + 1) * ROWS]
        if touching(distance):
            given = given + jnp.where(gap == 1, up, 0.0) + jnp.where(gap == -1, down, 0.0)
            bit = jnp.where(gap > 0, 1, 0)
            for y in range(2):
                for x in range(4):
                    place = lanes((4 * y + x) * pts, pts)
                    if x in (0, 3):
                        side = left if x == 0 else right
                        payload[:, place] = side[:, lanes((y + 2 * bit) * pts, pts)]
                    else:
                        payload[:, place] = own[:, lanes((x - 1 + 2 * y + 4 * bit) * pts, pts)]
        start = payload.shape[1] - 2 * LEAVES
        given_high, given_low = high_low(given)
        payload[:, lanes(start, LEAVES)] = given_high
        payload[:, lanes(start + LEAVES, LEAVES)] = given_low


def side_kernel(own, left, right, half, source, target, near, sides):
    points = own.shape[1]
    pts = points // 8

    def group(index, carry):
        here = lanes(index * (2 * pts), 2 * pts)
        zero = jnp.zeros((ROWS, 2 * pts), jnp.float32)
        near[:, here] = pulled(zero, target[:, here], source, own, [leaf * pts for leaf in range(8)], pts)
        return carry

    near[:, lanes(0, 4 * pts)] = half[...]
    lax.fori_loop(2, 4, group, 0)
    for step, side in ((0, left), (1, right)):
        for place in range(4):
            centre = (1.5 if step else -1.5, place % 2 - 0.5, place // 2 - 0.5)
            sides[lanes(place * pts, pts), :] = source_features(side, place * pts, pts, centre)

        def layer(index, carry, step=step, side=side):
            here = lanes((step + 2 * index) * (2 * pts), 2 * pts)
            near[:, here] = pulled(near[:, here], target[:, here], sides, side, [p * pts for p in range(4)], pts)
            return carry

        lax.fori_loop(0, 2, layer, 0)


def last_kernel(depth, count_in, weights_in, near, target, basis, own_local, *rest):
    received, rest = rest[: depth - 1], rest[depth - 1 :]
    potential, sums, held, sides, total, count, weights, sems = rest
    copies = fetch([(count_in, count), (weights_in, weights)], sems)
    fields, points = potential.shape
    pts = points // 8
    _, box_z = box_place()
    for step in range(2):
        held[...] = jnp.zeros(held.shape, held.dtype)
        for distance in range(1, depth):
            if touching(distance):

                @pl.when((box_z ^ distance) - box_z == 2 * step - 1)
                def _(block=received[distance - 1]):
                    held[...] = block[:, lanes(0, points)]

        for place in range(8):
            centre = (place % 4 - 1.5, place // 4 - 0.5, 1.5 if step else -1.5)
            sides[lanes(place * pts, pts), :] = source_features(held, place * pts, pts, centre)

        def pair(index, carry, step=step):
            here = lanes((index + 2 * step) * (2 * pts), 2 * pts)
            starts = [(4 * y + x + index) * pts for y in range(2) for x in range(3)]
            total[:, here] = pulled(near[:, here], target[:, here], sides, held, starts, pts)
            return carry

        lax.fori_loop(0, 2, pair, 0)

    local = own_local[...]
    for distance in range(1, depth):
        block = received[distance - 1]
        start = block.shape[1] - 2 * LEAVES
        local = local + block[:, lanes(start, LEAVES)].astype(jnp.float32)
        local = local + block[:, lanes(start + LEAVES, LEAVES)].astype(jnp.float32)
    local_high, local_low = high_low(local)
    for copy in copies:
        copy.wait()
    column = by_row([weights[field] for field in range(fields)], (fields, 1))
    lane_index = lax.broadcasted_iota(jnp.int32, (fields, pts), 1)
    coupling = 1.0 / (128.0 * pts)
    for leaf in range(8):
        here = slice(leaf * pts, (leaf + 1) * pts)
        slot = slice(leaf * SLOT, (leaf + 1) * SLOT)
        left = jnp.concatenate([local_high[:, slot], local_high[:, slot]], axis=1)
        far_part = dot(left, basis[:, here]) + dot(local_low[:, slot], basis[0:SLOT, here])
        value = (total[:, lanes(leaf_slot(leaf) * pts, pts)] + far_part)[:fields]
        value = jnp.where(lane_index < count[leaf], value * coupling, 0.0)
        potential[:, here] = value
        sums[:, here] = jnp.sum(value * column, axis=0, keepdims=True)
    sums[:, points:] = jnp.broadcast_to(jnp.sum(column), (1, sums.shape[1] - points))


def mean_kernel(mine, other, mean):
    points = mean.shape[1]
    total = mine[...] + other[...]
    mean[...] = total[:, :points] / total[:, points : points + 1]


def swapped(block, axis, partner):
    return lax.ppermute(block, axis, [(i, partner(i)) for i in range(lax.axis_size(axis))])


def per_device(positions, density, leaf_count, sigma_weights):
    fields, points = density.shape
    pts = points // 8
    depth = lax.axis_size("space") // ACROSS
    vmem, hbm = pl.BlockSpec(memory_space=pltpu.VMEM), pl.BlockSpec(memory_space=pltpu.HBM)

    def call(kernel, name, in_specs, outs, scratch, *args):
        return pl.pallas_call(
            kernel,
            in_specs=in_specs,
            out_specs=[vmem] * len(outs),
            out_shape=[jax.ShapeDtypeStruct(shape, dtype) for shape, dtype in outs],
            scratch_shapes=scratch,
            compiler_params=pltpu.CompilerParams(vmem_limit_bytes=24 * MEGA),
            name=name,
        )(*(pltpu.with_memory_space_constraint(a, pltpu.HBM) if s is hbm else a for s, a in zip(in_specs, args)))

    half, full = jnp.bfloat16, jnp.float32
    shift = shift_table()
    face = 4 * pts + LEAVES + 2 * SLOT
    own, basis, moments, totals, *given = call(
        pack_kernel,
        "pack",
        [hbm] * 4,
        [
            ((ROWS, points), half),
            ((2 * SLOT, points), half),
            ((ROWS, LEAVES), half),
            ((ROWS, 2 * SLOT), half),
            ((ROWS, face), half),
            ((ROWS, 2 * SLOT), half),
            ((ROWS, face), half),
        ],
        [
            pltpu.SMEM((8,), jnp.int32),
            pltpu.VMEM((3, points), full),
            pltpu.VMEM((fields, points), half),
            pltpu.VMEM((LEAVES, SLOT), half),
            pltpu.VMEM((SLOT, 8, pts), full),
            pltpu.SemaphoreType.DMA((4,)),
        ],
        leaf_count,
        positions,
        density,
        jnp.asarray(shift, half),
    )
    from_2 = swapped(given[1], "space", lambda i: i ^ 2)
    from_3 = swapped(given[2], "space", lambda i: i ^ 3)
    from_1 = swapped(given[0], "space", lambda i: i ^ 1)
    near, source, target, far, nodes, spread = call(
        own_kernel,
        "near_own",
        [vmem] + [hbm] * 3,
        [
            ((ROWS, points // 2), full),
            ((points, FEATURES), half),
            ((FEATURES, points), half),
            ((len(STEPS) * LEAVES, LEAVES), half),
            ((3, SLOT, SLOT), full),
            ((SLOT, LEAVES), half),
        ],
        [pltpu.SemaphoreType.DMA((3,))],
        own,
        jnp.asarray(far_table(), half),
        jnp.asarray(box_nodes()),
        jnp.asarray(shift.T.copy(), half),
    )
    widths = [(points if touching(d) else 0) + 2 * LEAVES for d in range(1, depth)]
    left, right, own_local, *given = call(
        functools.partial(row_kernel, depth),
        "row",
        [vmem] * 9,
        [((ROWS, 4 * pts + LEAVES), half)] * 2 + [((ROWS, LEAVES), full)] + [((ROWS, w), half) for w in widths],
        [],
        own,
        moments,
        totals,
        from_1,
        from_2,
        from_3,
        far,
        nodes,
        spread,
    )
    received = [None] * (depth - 1)
    for d in sorted(range(1, depth), key=lambda d: (touching(d), -d)):
        received[d - 1] = swapped(given[d - 1], "space", lambda i: i ^ (ACROSS * d))
    near, = call(
        side_kernel,
        "near_side",
        [vmem] * 6,
        [((ROWS, points), full)],
        [pltpu.VMEM((4 * pts, FEATURES), half)],
        own,
        left,
        right,
        near,
        source,
        target,
    )
    potential, sums = call(
        functools.partial(last_kernel, depth),
        "near_rows",
        [hbm] * 2 + [vmem] * (4 + len(received)),
        [((fields, points), full), ((1, points + 128), full)],
        [
            pltpu.VMEM((ROWS, points), half),
            pltpu.VMEM((8 * pts, FEATURES), half),
            pltpu.VMEM((ROWS, points), full),
            pltpu.SMEM((8,), jnp.int32),
            pltpu.SMEM((fields,), full),
            pltpu.SemaphoreType.DMA((2,)),
        ],
        leaf_count,
        sigma_weights,
        near,
        target,
        basis,
        own_local,
        *received,
    )
    if lax.axis_size("sig") == 2:
        other = swapped(sums, "sig", lambda i: i ^ 1)
    else:
        other = lax.psum(sums, "sig") - sums
    mean, = call(mean_kernel, "mean", [vmem] * 2, [((1, points), full)], [], sums, other)
    return potential, mean.reshape(points)


def solution(mesh):
    in_specs = (P(None, "space"), P("sig", "space"), P("space"), P("sig"))
    out_specs = (P("sig", "space"), P("space"))
    return jax.shard_map(per_device, mesh=mesh, in_specs=in_specs, out_specs=out_specs, check_vma=False)
```

```python
import functools
import math

import jax
import jax.numpy as jnp
import numpy as np
from jax import lax
from jax.experimental import pallas as pl
from jax.experimental.pallas import tpu as pltpu
from jax.sharding import PartitionSpec as P

ORDER = 5
SOFTENING = 0.1
ACROSS = 4
SLOT = 64
ROWS = 32
LEAVES = 8 * SLOT
MEGA = 1024 * 1024
FEATURES = 48


def exponent_table(order_max):
    entries_list = []
    for degree in range(order_max + 1):
        for first_power in range(degree, -1, -1):
            for second_power in range(degree - first_power, -1, -1):
                entries_list.append((first_power, second_power, degree - first_power - second_power))
    return entries_list


def node_table(count_nodes, offset_value):
    counter = np.arange(1, count_nodes + 1, dtype=np.float32)[:, None]
    stride_set = np.array([0.7548776662466927, 0.5698402909980532, 0.4142135623730951], dtype=np.float32)[None, :]
    unit_points = np.mod(counter * stride_set + np.float32(offset_value), np.float32(1.0))
    return (np.float32(2.0) * unit_points - np.float32(1.0)).astype(np.float32)


EXPONENTS = exponent_table(ORDER)
COEFFS = len(EXPONENTS)
CHECK = node_table(COEFFS, 0.5).astype(np.float64)
EQUIV = node_table(COEFFS, 0.0).astype(np.float64)
STEPS = [(sx, sz) for sz in (-1, 0, 1) for sx in (-1, 0, 1) if sx != 0 or sz != 0]


def bits(octant):
    return octant % 2, octant // 2 % 2, octant // 4


def touching(distance):
    return distance & (distance + 1) == 0


def leaf_slot(octant):
    bit_x, bit_y, bit_z = bits(octant)
    return (bit_x + 2 * bit_z) * 2 + bit_y


@functools.lru_cache(None)
def far_table():
    shape = (len(STEPS), 8, SLOT, 8, SLOT)
    table = np.zeros(shape)
    gap_nodes = 0.5 * (CHECK[None, :, :] - EQUIV[:, None, :])
    for index, (step_x, step_z) in enumerate(STEPS):
        for source in range(8):
            for target in range(8):
                s, t = bits(source), bits(target)
                gap = np.array([2 * step_x + s[0] - t[0], s[1] - t[1], 2 * step_z + s[2] - t[2]], np.float64)
                if max(abs(gap[0]), abs(gap[2])) >= 2:
                    shifted = gap_nodes - gap
                    value = 1.0 / np.sqrt(np.sum(shifted * shifted, -1) + SOFTENING * SOFTENING) / COEFFS
                    table[index, source, :COEFFS, target, :COEFFS] = value
    return table.reshape(len(STEPS) * LEAVES, LEAVES)


@functools.lru_cache(None)
def shift_table():
    table = np.zeros((8, SLOT, SLOT))
    for leaf in range(8):
        offset = [bit - 0.5 for bit in bits(leaf)]
        for k, target in enumerate(EXPONENTS):
            for i, source in enumerate(EXPONENTS):
                if all(b <= a for a, b in zip(target, source)):
                    value = 1.0
                    for a, b, h in zip(target, source, offset):
                        value *= math.comb(a, b) * 0.5**b * h ** (a - b)
                    table[leaf, i, k] = value
    return table.reshape(8 * SLOT, SLOT)


@functools.lru_cache(None)
def box_nodes():
    gaps = np.zeros((3, SLOT, SLOT))
    gaps[:, :COEFFS, :COEFFS] = np.moveaxis(CHECK[None, :, :] - EQUIV[:, None, :], -1, 0)
    gaps[1] = gaps[1] ** 2 + SOFTENING * SOFTENING
    return gaps.astype(np.float32)


def dot(left, right):
    return jnp.dot(left, right, preferred_element_type=jnp.float32)


def dot_nt(left, right):
    return lax.dot_general(left, right, (((1,), (1,)), ((), ())), preferred_element_type=jnp.float32)


def low_bits(value):
    return value.astype(jnp.bfloat16)


def high_low(value):
    high = low_bits(value)
    return high, low_bits(value - high.astype(jnp.float32))


def by_row(values, shape):
    row = lax.broadcasted_iota(jnp.int32, shape, 0)
    result = jnp.zeros(shape, jnp.float32)
    for index, value in enumerate(values):
        result = jnp.where(row == index, value, result)
    return result


def box_place():
    label = lax.axis_index("space")
    return lax.rem(label, ACROSS), lax.div(label, ACROSS)


def lanes(start, size):
    return pl.ds(start if isinstance(start, int) else pl.multiple_of(start, 128), size)


def fetch(pairs, sems):
    copies = [pltpu.make_async_copy(src, dst, sems.at[i]) for i, (src, dst) in enumerate(pairs)]
    for copy in copies:
        copy.start()
    return copies


def pack_kernel(count_in, positions_in, density_in, shift_in, own, basis, moments, totals, *rest):
    payloads, (count, positions, density, shift, mono, sems) = rest[:3], rest[3:]
    copies = fetch(
        [(count_in, count), (positions_in, positions), (density_in, density), (shift_in, shift)], sems
    )
    fields, points = density.shape
    pts = points // 8
    box_x, box_z = box_place()
    for copy in copies:
        copy.wait()
    local = []
    for leaf in range(8):
        bit_x, bit_y, bit_z = bits(leaf)
        centre = by_row(
            [2.0 * box_x.astype(jnp.float32) + (bit_x + 0.5), bit_y + 0.5, 2.0 * box_z.astype(jnp.float32) + (bit_z + 0.5)],
            (3, 1),
        )
        here = slice(leaf * pts, (leaf + 1) * pts)
        offset = positions[:, here] - centre
        local.append(offset)
        high = low_bits(offset).astype(jnp.float32)
        middle = low_bits(offset - high).astype(jnp.float32)
        low = offset - high - middle
        raw = density[:, here].astype(jnp.float32)
        mass = jnp.where(lax.broadcasted_iota(jnp.int32, raw.shape, 1) < count[leaf], raw, 0.0)
        spare = jnp.zeros((ROWS - fields - 9, pts), jnp.float32)
        own[:, here] = low_bits(jnp.concatenate([mass, high, middle, low, spare], axis=0))

    axes = [2.0 * jnp.concatenate([part[a : a + 1] for part in local], axis=0) for a in range(3)]
    made = {(0, 0, 0): jnp.ones((8, pts), jnp.float32)}
    for k, powers in enumerate(EXPONENTS):
        if powers not in made:
            a = next(i for i in range(3) if powers[i] > 0)
            before = tuple(p - (i == a) for i, p in enumerate(powers))
            made[powers] = made[before] * axes[a]
        mono[k] = made[powers]
    mono[COEFFS:SLOT] = jnp.zeros((SLOT - COEFFS, 8, pts), jnp.float32)
    parts = []
    for leaf in range(8):
        here = slice(leaf * pts, (leaf + 1) * pts)
        high, low = high_low(mono[:, leaf, :])
        basis[0:SLOT, here] = high
        basis[SLOT:, here] = low
        parts.append(dot_nt(own[:, here], high))
    moment, rest = high_low(jnp.concatenate(parts, axis=1))
    moments[...] = moment
    total = dot(moment, shift[...]) + dot(rest, shift[...])
    total = jnp.concatenate(high_low(total), axis=1)
    totals[...] = total
    payloads[1][...] = total
    for distance, payload in ((1, payloads[0]), (3, payloads[2])):
        bit = jnp.where((box_x ^ distance) > box_x, 1, 0)
        for place in range(4):
            payload[:, lanes(place * pts, pts)] = own[:, lanes((bit + 2 * place) * pts, pts)]
        payload[:, lanes(4 * pts, LEAVES)] = moment
        payload[:, lanes(4 * pts + LEAVES, 2 * SLOT)] = total


def features(held, start, size, centre, target):
    value = held[16:32, lanes(start, size)].astype(jnp.float32)
    x = value[1:4] + value[4:7] + value[7:10] + by_row(centre, (3, 1))
    norm = jnp.sum(x * x, axis=0, keepdims=True)
    if target:
        norm = norm + SOFTENING * SOFTENING
    parts, norms = [], []
    for source, out in ((x, parts), (norm, norms)):
        left = source
        for _ in range(3):
            high = low_bits(left).astype(jnp.float32)
            out.append(high)
            left = left - high
    one = jnp.ones_like(norm)
    zero = jnp.zeros_like(norm)
    blank = jnp.zeros((3, norm.shape[1]), jnp.float32)
    blocks = []
    order = (0, 1, 0, 2, 0, 1) if target else (0, 0, 1, 0, 2, 1)
    for index, which in enumerate(order):
        coords = -2.0 * parts[which] if target else parts[which]
        if index < 3:
            pair = [one, norms[index]] if target else [norms[index], one]
        else:
            pair = [zero, zero]
        blocks += [coords, *pair, blank]
    return jnp.concatenate(blocks, axis=0)


def columns_of(held, start, size):
    return low_bits(jnp.transpose(held[0:ROWS, lanes(start, size)].astype(jnp.float32)))


def pulled(total, wanted, source, masses, starts, pts):
    for start in starts:
        place = lanes(start, pts)
        kernel = lax.rsqrt(dot(wanted, source[:, place]))
        high = low_bits(kernel)
        low = low_bits(kernel - high.astype(jnp.float32))
        mass = masses[place, :]
        total = total + dot(high, mass) + dot(low, mass)
    return total


def own_kernel(own, far_in, nodes_in, spread_in, near, source, target, masses, far, nodes, spread, sems):
    copies = fetch([(far_in, far), (nodes_in, nodes), (spread_in, spread)], sems)
    points = own.shape[1]
    pts = points // 8
    for leaf in range(8):
        centre = [bit - 0.5 for bit in bits(leaf)]
        here = lanes(leaf * pts, pts)
        source[:, here] = low_bits(features(own, leaf * pts, pts, centre, False))
        wanted = features(own, leaf * pts, pts, centre, True)
        target[lanes(leaf_slot(leaf) * pts, pts), :] = low_bits(jnp.transpose(wanted))
        masses[here, :] = columns_of(own, leaf * pts, pts)

    def group(index, carry):
        here = lanes(index * (2 * pts), 2 * pts)
        zero = jnp.zeros((2 * pts, ROWS), jnp.float32)
        near[here, :] = pulled(zero, target[here, :], source, masses, [leaf * pts for leaf in range(8)], pts)
        return carry

    lax.fori_loop(0, 2, group, 0)
    for copy in copies:
        copy.wait()


def row_kernel(depth, own, moments, totals, from_1, from_2, from_3, far, nodes, spread, *rest):
    left, right, own_local, *payloads = rest
    points = own.shape[1]
    pts = points // 8
    box_x, box_z = box_place()
    wide = 4 * pts + LEAVES
    for side, step in ((left, -1), (right, 1)):
        side[...] = jnp.zeros(side.shape, side.dtype)
        for distance, held in ((1, from_1), (3, from_3)):

            @pl.when((box_x ^ distance) - box_x == step)
            def _(side=side, held=held):
                side[...] = held[:, lanes(0, wide)]

    base = 4 * pts
    row = jnp.concatenate([left[:, lanes(base, LEAVES)], moments[...], right[:, lanes(base, LEAVES)]], axis=1)
    below_rows, same_rows, above_rows = pl.ds(0, 3 * LEAVES), pl.ds(3 * LEAVES, 2 * LEAVES), pl.ds(5 * LEAVES, 3 * LEAVES)
    up = dot(row, far[below_rows, :])
    down = dot(row, far[above_rows, :])
    same = dot(jnp.concatenate([row[:, :LEAVES], row[:, 2 * LEAVES :]], axis=1), far[same_rows, :])

    boxes = [totals[...], from_1[:, lanes(wide, 2 * SLOT)], from_2[...], from_3[:, lanes(wide, 2 * SLOT)]]
    boxes_high = jnp.concatenate([held[:, :SLOT] for held in boxes], axis=1)
    boxes_low = jnp.concatenate([held[:, SLOT:] for held in boxes], axis=1)
    columns = []
    for distance_z in range(depth):
        gap_z = 2 * ((box_z ^ distance_z) - box_z)
        across_z = nodes[2] + gap_z.astype(jnp.float32)
        rest_z = across_z * across_z + nodes[1]
        blocks = []
        for distance_x in range(ACROSS):
            gap_x = 2 * (box_x - (box_x ^ distance_x))
            across_x = nodes[0] + gap_x.astype(jnp.float32)
            distant = jnp.maximum(jnp.abs(gap_x), jnp.abs(gap_z)) >= 4
            blocks.append(lax.rsqrt(across_x * across_x + rest_z) * jnp.where(distant, 1.0 / COEFFS, 0.0))
        columns.append(jnp.concatenate(blocks, axis=0))
    columns = low_bits(jnp.concatenate(columns, axis=1))
    coarse = dot(boxes_high, columns) + dot(boxes_low, columns)
    coarse = jnp.concatenate([coarse[:, d * SLOT : (d + 1) * SLOT] for d in range(depth)], axis=0)
    coarse_high, coarse_low = high_low(coarse)
    coarse = dot(coarse_high, spread[...]) + dot(coarse_low, spread[...])

    own_local[...] = same + coarse[:ROWS]
    for distance in range(1, depth):
        payload = payloads[distance - 1]
        gap = (box_z ^ distance) - box_z
        given = coarse[distance * ROWS : (distance + 1) * ROWS]
        if touching(distance):
            given = given + jnp.where(gap == 1, up, 0.0) + jnp.where(gap == -1, down, 0.0)
            bit = jnp.where(gap > 0, 1, 0)
            for y in range(2):
                for x in range(4):
                    place = lanes((4 * y + x) * pts, pts)
                    if x in (0, 3):
                        side = left if x == 0 else right
                        payload[:, place] = side[:, lanes((y + 2 * bit) * pts, pts)]
                    else:
                        payload[:, place] = own[:, lanes((x - 1 + 2 * y + 4 * bit) * pts, pts)]
        start = payload.shape[1] - 2 * LEAVES
        given_high, given_low = high_low(given)
        payload[:, lanes(start, LEAVES)] = given_high
        payload[:, lanes(start + LEAVES, LEAVES)] = given_low


def side_kernel(left, right, half, source, target, masses, near, sides, side_masses):
    points = source.shape[1]
    pts = points // 8

    def group(index, carry):
        here = lanes(index * (2 * pts), 2 * pts)
        zero = jnp.zeros((2 * pts, ROWS), jnp.float32)
        near[here, :] = pulled(zero, target[here, :], source, masses, [leaf * pts for leaf in range(8)], pts)
        return carry

    near[lanes(0, 4 * pts), :] = half[...]
    lax.fori_loop(2, 4, group, 0)
    for step, side in ((0, left), (1, right)):
        for place in range(4):
            centre = (1.5 if step else -1.5, place % 2 - 0.5, place // 2 - 0.5)
            here = lanes(place * pts, pts)
            sides[:, here] = low_bits(features(side, place * pts, pts, centre, False))
            side_masses[here, :] = columns_of(side, place * pts, pts)

        def layer(index, carry, step=step):
            here = lanes((step + 2 * index) * (2 * pts), 2 * pts)
            starts = [p * pts for p in range(4)]
            near[here, :] = pulled(near[here, :], target[here, :], sides, side_masses, starts, pts)
            return carry

        lax.fori_loop(0, 2, layer, 0)


def last_kernel(depth, count_in, weights_in, near, target, basis, own_local, *rest):
    received, rest = rest[: depth - 1], rest[depth - 1 :]
    potential, sums, held, sides, side_masses, total, count, weights, sems = rest
    copies = fetch([(count_in, count), (weights_in, weights)], sems)
    fields, points = potential.shape
    pts = points // 8
    _, box_z = box_place()
    for step in range(2):
        held[...] = jnp.zeros(held.shape, held.dtype)
        for distance in range(1, depth):
            if touching(distance):

                @pl.when((box_z ^ distance) - box_z == 2 * step - 1)
                def _(block=received[distance - 1]):
                    held[...] = block[:, lanes(0, points)]

        for place in range(8):
            centre = (place % 4 - 1.5, place // 4 - 0.5, 1.5 if step else -1.5)
            here = lanes(place * pts, pts)
            sides[:, here] = low_bits(features(held, place * pts, pts, centre, False))
            side_masses[here, :] = columns_of(held, place * pts, pts)

        def pair(index, carry, step=step):
            here = lanes((index + 2 * step) * (2 * pts), 2 * pts)
            starts = [(4 * y + x + index) * pts for y in range(2) for x in range(3)]
            total[here, :] = pulled(near[here, :], target[here, :], sides, side_masses, starts, pts)
            return carry

        lax.fori_loop(0, 2, pair, 0)

    local = own_local[...]
    for distance in range(1, depth):
        block = received[distance - 1]
        start = block.shape[1] - 2 * LEAVES
        local = local + block[:, lanes(start, LEAVES)].astype(jnp.float32)
        local = local + block[:, lanes(start + LEAVES, LEAVES)].astype(jnp.float32)
    local_high, local_low = high_low(local)
    for copy in copies:
        copy.wait()
    column = by_row([weights[field] for field in range(fields)], (fields, 1))
    lane_index = lax.broadcasted_iota(jnp.int32, (fields, pts), 1)
    coupling = 1.0 / (128.0 * pts)
    for leaf in range(8):
        here = slice(leaf * pts, (leaf + 1) * pts)
        slot = slice(leaf * SLOT, (leaf + 1) * SLOT)
        left = jnp.concatenate([local_high[:, slot], local_high[:, slot]], axis=1)
        far_part = dot(left, basis[:, here]) + dot(local_low[:, slot], basis[0:SLOT, here])
        near_part = jnp.transpose(total[lanes(leaf_slot(leaf) * pts, pts), :])
        value = (near_part + far_part)[:fields]
        value = jnp.where(lane_index < count[leaf], value * coupling, 0.0)
        potential[:, here] = value
        sums[:, here] = jnp.sum(value * column, axis=0, keepdims=True)
    sums[:, points:] = jnp.broadcast_to(jnp.sum(column), (1, sums.shape[1] - points))


def mean_kernel(mine, other, mean):
    points = mean.shape[1]
    total = mine[...] + other[...]
    mean[...] = total[:, :points] / total[:, points : points + 1]


def swapped(block, axis, partner):
    return lax.ppermute(block, axis, [(i, partner(i)) for i in range(lax.axis_size(axis))])


def per_device(positions, density, leaf_count, sigma_weights):
    fields, points = density.shape
    pts = points // 8
    depth = lax.axis_size("space") // ACROSS
    vmem, hbm = pl.BlockSpec(memory_space=pltpu.VMEM), pl.BlockSpec(memory_space=pltpu.HBM)

    def call(kernel, name, in_specs, outs, scratch, *args):
        return pl.pallas_call(
            kernel,
            in_specs=in_specs,
            out_specs=[vmem] * len(outs),
            out_shape=[jax.ShapeDtypeStruct(shape, dtype) for shape, dtype in outs],
            scratch_shapes=scratch,
            compiler_params=pltpu.CompilerParams(vmem_limit_bytes=24 * MEGA),
            name=name,
        )(*(pltpu.with_memory_space_constraint(a, pltpu.HBM) if s is hbm else a for s, a in zip(in_specs, args)))

    half, full = jnp.bfloat16, jnp.float32
    shift = shift_table()
    face = 4 * pts + LEAVES + 2 * SLOT
    own, basis, moments, totals, *given = call(
        pack_kernel,
        "pack",
        [hbm] * 4,
        [
            ((ROWS, points), half),
            ((2 * SLOT, points), half),
            ((ROWS, LEAVES), half),
            ((ROWS, 2 * SLOT), half),
            ((ROWS, face), half),
            ((ROWS, 2 * SLOT), half),
            ((ROWS, face), half),
        ],
        [
            pltpu.SMEM((8,), jnp.int32),
            pltpu.VMEM((3, points), full),
            pltpu.VMEM((fields, points), half),
            pltpu.VMEM((LEAVES, SLOT), half),
            pltpu.VMEM((SLOT, 8, pts), full),
            pltpu.SemaphoreType.DMA((4,)),
        ],
        leaf_count,
        positions,
        density,
        jnp.asarray(shift, half),
    )
    from_2 = swapped(given[1], "space", lambda i: i ^ 2)
    from_3 = swapped(given[2], "space", lambda i: i ^ 3)
    from_1 = swapped(given[0], "space", lambda i: i ^ 1)
    near, source, target, masses, far, nodes, spread = call(
        own_kernel,
        "near_own",
        [vmem] + [hbm] * 3,
        [
            ((points // 2, ROWS), full),
            ((FEATURES, points), half),
            ((points, FEATURES), half),
            ((points, ROWS), half),
            ((len(STEPS) * LEAVES, LEAVES), half),
            ((3, SLOT, SLOT), full),
            ((SLOT, LEAVES), half),
        ],
        [pltpu.SemaphoreType.DMA((3,))],
        own,
        jnp.asarray(far_table(), half),
        jnp.asarray(box_nodes()),
        jnp.asarray(shift.T.copy(), half),
    )
    widths = [(points if touching(d) else 0) + 2 * LEAVES for d in range(1, depth)]
    left, right, own_local, *given = call(
        functools.partial(row_kernel, depth),
        "row",
        [vmem] * 9,
        [((ROWS, 4 * pts + LEAVES), half)] * 2 + [((ROWS, LEAVES), full)] + [((ROWS, w), half) for w in widths],
        [],
        own,
        moments,
        totals,
        from_1,
        from_2,
        from_3,
        far,
        nodes,
        spread,
    )
    received = [None] * (depth - 1)
    for d in sorted(range(1, depth), key=lambda d: (touching(d), -d)):
        received[d - 1] = swapped(given[d - 1], "space", lambda i: i ^ (ACROSS * d))
    near, = call(
        side_kernel,
        "near_side",
        [vmem] * 6,
        [((points, ROWS), full)],
        [pltpu.VMEM((FEATURES, 4 * pts), half), pltpu.VMEM((4 * pts, ROWS), half)],
        left,
        right,
        near,
        source,
        target,
        masses,
    )
    potential, sums = call(
        functools.partial(last_kernel, depth),
        "near_rows",
        [hbm] * 2 + [vmem] * (4 + len(received)),
        [((fields, points), full), ((1, points + 128), full)],
        [
            pltpu.VMEM((ROWS, points), half),
            pltpu.VMEM((FEATURES, 8 * pts), half),
            pltpu.VMEM((8 * pts, ROWS), half),
            pltpu.VMEM((points, ROWS), full),
            pltpu.SMEM((8,), jnp.int32),
            pltpu.SMEM((fields,), full),
            pltpu.SemaphoreType.DMA((2,)),
        ],
        leaf_count,
        sigma_weights,
        near,
        target,
        basis,
        own_local,
        *received,
    )
    if lax.axis_size("sig") == 2:
        other = swapped(sums, "sig", lambda i: i ^ 1)
    else:
        other = lax.psum(sums, "sig") - sums
    mean, = call(mean_kernel, "mean", [vmem] * 2, [((1, points), full)], [], sums, other)
    return potential, mean.reshape(points)


def solution(mesh):
    in_specs = (P(None, "space"), P("sig", "space"), P("space"), P("sig"))
    out_specs = (P("sig", "space"), P("space"))
    return jax.shard_map(per_device, mesh=mesh, in_specs=in_specs, out_specs=out_specs, check_vma=False)
```

```python
import functools
import math

import jax
import jax.numpy as jnp
import numpy as np
from jax import lax
from jax.experimental import pallas as pl
from jax.experimental.pallas import tpu as pltpu
from jax.sharding import PartitionSpec as P

ORDER = 5
SOFTENING = 0.1
ACROSS = 4
SLOT = 64
ROWS = 32
LEAVES = 8 * SLOT
MEGA = 1024 * 1024
FEATURES = 48


def exponent_table(order_max):
    entries_list = []
    for degree in range(order_max + 1):
        for first_power in range(degree, -1, -1):
            for second_power in range(degree - first_power, -1, -1):
                entries_list.append((first_power, second_power, degree - first_power - second_power))
    return entries_list


def node_table(count_nodes, offset_value):
    counter = np.arange(1, count_nodes + 1, dtype=np.float32)[:, None]
    stride_set = np.array([0.7548776662466927, 0.5698402909980532, 0.4142135623730951], dtype=np.float32)[None, :]
    unit_points = np.mod(counter * stride_set + np.float32(offset_value), np.float32(1.0))
    return (np.float32(2.0) * unit_points - np.float32(1.0)).astype(np.float32)


EXPONENTS = exponent_table(ORDER)
COEFFS = len(EXPONENTS)
CHECK = node_table(COEFFS, 0.5).astype(np.float64)
EQUIV = node_table(COEFFS, 0.0).astype(np.float64)
STEPS = [(sx, sz) for sz in (-1, 0, 1) for sx in (-1, 0, 1) if sx != 0 or sz != 0]


def bits(octant):
    return octant % 2, octant // 2 % 2, octant // 4


def touching(distance):
    return distance & (distance + 1) == 0


def leaf_slot(octant):
    bit_x, bit_y, bit_z = bits(octant)
    return (bit_x + 2 * bit_z) * 2 + bit_y


@functools.lru_cache(None)
def far_table():
    shape = (len(STEPS), 8, SLOT, 8, SLOT)
    table = np.zeros(shape)
    gap_nodes = 0.5 * (CHECK[None, :, :] - EQUIV[:, None, :])
    for index, (step_x, step_z) in enumerate(STEPS):
        for source in range(8):
            for target in range(8):
                s, t = bits(source), bits(target)
                gap = np.array([2 * step_x + s[0] - t[0], s[1] - t[1], 2 * step_z + s[2] - t[2]], np.float64)
                if max(abs(gap[0]), abs(gap[2])) >= 2:
                    shifted = gap_nodes - gap
                    value = 1.0 / np.sqrt(np.sum(shifted * shifted, -1) + SOFTENING * SOFTENING) / COEFFS
                    table[index, source, :COEFFS, target, :COEFFS] = value
    return table.reshape(len(STEPS) * LEAVES, LEAVES)


@functools.lru_cache(None)
def shift_table():
    table = np.zeros((8, SLOT, SLOT))
    for leaf in range(8):
        offset = [bit - 0.5 for bit in bits(leaf)]
        for k, target in enumerate(EXPONENTS):
            for i, source in enumerate(EXPONENTS):
                if all(b <= a for a, b in zip(target, source)):
                    value = 1.0
                    for a, b, h in zip(target, source, offset):
                        value *= math.comb(a, b) * 0.5**b * h ** (a - b)
                    table[leaf, i, k] = value
    return table.reshape(8 * SLOT, SLOT)


@functools.lru_cache(None)
def box_nodes():
    gaps = np.zeros((3, SLOT, SLOT))
    gaps[:, :COEFFS, :COEFFS] = np.moveaxis(CHECK[None, :, :] - EQUIV[:, None, :], -1, 0)
    gaps[1] = gaps[1] ** 2 + SOFTENING * SOFTENING
    return gaps.astype(np.float32)


def dot(left, right):
    return jnp.dot(left, right, preferred_element_type=jnp.float32)


def dot_nt(left, right):
    return lax.dot_general(left, right, (((1,), (1,)), ((), ())), preferred_element_type=jnp.float32)


def low_bits(value):
    return value.astype(jnp.bfloat16)


def high_low(value):
    high = low_bits(value)
    return high, low_bits(value - high.astype(jnp.float32))


def by_row(values, shape):
    row = lax.broadcasted_iota(jnp.int32, shape, 0)
    result = jnp.zeros(shape, jnp.float32)
    for index, value in enumerate(values):
        result = jnp.where(row == index, value, result)
    return result


def box_place():
    label = lax.axis_index("space")
    return lax.rem(label, ACROSS), lax.div(label, ACROSS)


def lanes(start, size):
    return pl.ds(start if isinstance(start, int) else pl.multiple_of(start, 128), size)


def fetch(pairs, sems):
    copies = [pltpu.make_async_copy(src, dst, sems.at[i]) for i, (src, dst) in enumerate(pairs)]
    for copy in copies:
        copy.start()
    return copies


def pack_kernel(count_in, positions_in, density_in, shift_in, own, basis, moments, totals, *rest):
    payloads, (count, positions, density, shift, mono, sems) = rest[:3], rest[3:]
    copies = fetch(
        [(count_in, count), (positions_in, positions), (density_in, density), (shift_in, shift)], sems
    )
    fields, points = density.shape
    pts = points // 8
    box_x, box_z = box_place()
    for copy in copies:
        copy.wait()
    local = []
    for leaf in range(8):
        bit_x, bit_y, bit_z = bits(leaf)
        centre = by_row(
            [2.0 * box_x.astype(jnp.float32) + (bit_x + 0.5), bit_y + 0.5, 2.0 * box_z.astype(jnp.float32) + (bit_z + 0.5)],
            (3, 1),
        )
        here = slice(leaf * pts, (leaf + 1) * pts)
        offset = positions[:, here] - centre
        local.append(offset)
        high = low_bits(offset).astype(jnp.float32)
        middle = low_bits(offset - high).astype(jnp.float32)
        low = offset - high - middle
        raw = density[:, here].astype(jnp.float32)
        mass = jnp.where(lax.broadcasted_iota(jnp.int32, raw.shape, 1) < count[leaf], raw, 0.0)
        spare = jnp.zeros((ROWS - fields - 9, pts), jnp.float32)
        own[:, here] = low_bits(jnp.concatenate([mass, high, middle, low, spare], axis=0))

    axes = [2.0 * jnp.concatenate([part[a : a + 1] for part in local], axis=0) for a in range(3)]
    made = {(0, 0, 0): jnp.ones((8, pts), jnp.float32)}
    for k, powers in enumerate(EXPONENTS):
        if powers not in made:
            a = next(i for i in range(3) if powers[i] > 0)
            before = tuple(p - (i == a) for i, p in enumerate(powers))
            made[powers] = made[before] * axes[a]
        mono[k] = made[powers]
    mono[COEFFS:SLOT] = jnp.zeros((SLOT - COEFFS, 8, pts), jnp.float32)
    parts = []
    for leaf in range(8):
        here = slice(leaf * pts, (leaf + 1) * pts)
        high, low = high_low(mono[:, leaf, :])
        basis[0:SLOT, here] = high
        basis[SLOT:, here] = low
        parts.append(dot_nt(own[:, here], high))
    moment, rest = high_low(jnp.concatenate(parts, axis=1))
    moments[...] = moment
    total = dot(moment, shift[...]) + dot(rest, shift[...])
    total = jnp.concatenate(high_low(total), axis=1)
    totals[...] = total
    payloads[1][...] = total
    for distance, payload in ((1, payloads[0]), (3, payloads[2])):
        bit = jnp.where((box_x ^ distance) > box_x, 1, 0)
        for place in range(4):
            payload[:, lanes(place * pts, pts)] = own[:, lanes((bit + 2 * place) * pts, pts)]
        payload[:, lanes(4 * pts, LEAVES)] = moment
        payload[:, lanes(4 * pts + LEAVES, 2 * SLOT)] = total


def features(held, start, size, centre, target):
    value = held[16:32, lanes(start, size)].astype(jnp.float32)
    x = value[1:4] + value[4:7] + value[7:10] + by_row(centre, (3, 1))
    norm = jnp.sum(x * x, axis=0, keepdims=True)
    if target:
        norm = norm + SOFTENING * SOFTENING
    parts, norms = [], []
    for source, out in ((x, parts), (norm, norms)):
        left = source
        for _ in range(3):
            high = low_bits(left).astype(jnp.float32)
            out.append(high)
            left = left - high
    one = jnp.ones_like(norm)
    zero = jnp.zeros_like(norm)
    blank = jnp.zeros((3, norm.shape[1]), jnp.float32)
    blocks = []
    order = (0, 1, 0, 2, 0, 1) if target else (0, 0, 1, 0, 2, 1)
    for index, which in enumerate(order):
        coords = -2.0 * parts[which] if target else parts[which]
        if index < 3:
            pair = [one, norms[index]] if target else [norms[index], one]
        else:
            pair = [zero, zero]
        blocks += [coords, *pair, blank]
    return jnp.concatenate(blocks, axis=0)


def source_features(held, start, size, centre):
    return low_bits(jnp.transpose(features(held, start, size, centre, False)))


def pulled(total, wanted, source, masses, starts, pts):
    for start in starts:
        place = lanes(start, pts)
        kernel = lax.rsqrt(dot(source[place, :], wanted))
        total = total + dot(masses[:, place], low_bits(kernel))
    return total


def own_kernel(own, far_in, nodes_in, spread_in, near, source, target, far, nodes, spread, sems):
    copies = fetch([(far_in, far), (nodes_in, nodes), (spread_in, spread)], sems)
    points = own.shape[1]
    pts = points // 8
    for leaf in range(8):
        centre = [bit - 0.5 for bit in bits(leaf)]
        source[lanes(leaf * pts, pts), :] = source_features(own, leaf * pts, pts, centre)
        target[:, lanes(leaf_slot(leaf) * pts, pts)] = low_bits(features(own, leaf * pts, pts, centre, True))

    def group(index, carry):
        here = lanes(index * (2 * pts), 2 * pts)
        zero = jnp.zeros((ROWS, 2 * pts), jnp.float32)
        near[:, here] = pulled(zero, target[:, here], source, own, [leaf * pts for leaf in range(8)], pts)
        return carry

    lax.fori_loop(0, 2, group, 0)
    for copy in copies:
        copy.wait()


def row_kernel(depth, own, moments, totals, from_1, from_2, from_3, far, nodes, spread, *rest):
    left, right, own_local, *payloads = rest
    points = own.shape[1]
    pts = points // 8
    box_x, box_z = box_place()
    wide = 4 * pts + LEAVES
    for side, step in ((left, -1), (right, 1)):
        side[...] = jnp.zeros(side.shape, side.dtype)
        for distance, held in ((1, from_1), (3, from_3)):

            @pl.when((box_x ^ distance) - box_x == step)
            def _(side=side, held=held):
                side[...] = held[:, lanes(0, wide)]

    base = 4 * pts
    row = jnp.concatenate([left[:, lanes(base, LEAVES)], moments[...], right[:, lanes(base, LEAVES)]], axis=1)
    below_rows, same_rows, above_rows = pl.ds(0, 3 * LEAVES), pl.ds(3 * LEAVES, 2 * LEAVES), pl.ds(5 * LEAVES, 3 * LEAVES)
    up = dot(row, far[below_rows, :])
    down = dot(row, far[above_rows, :])
    same = dot(jnp.concatenate([row[:, :LEAVES], row[:, 2 * LEAVES :]], axis=1), far[same_rows, :])

    boxes = [totals[...], from_1[:, lanes(wide, 2 * SLOT)], from_2[...], from_3[:, lanes(wide, 2 * SLOT)]]
    boxes_high = jnp.concatenate([held[:, :SLOT] for held in boxes], axis=1)
    boxes_low = jnp.concatenate([held[:, SLOT:] for held in boxes], axis=1)
    columns = []
    for distance_z in range(depth):
        gap_z = 2 * ((box_z ^ distance_z) - box_z)
        across_z = nodes[2] + gap_z.astype(jnp.float32)
        rest_z = across_z * across_z + nodes[1]
        blocks = []
        for distance_x in range(ACROSS):
            gap_x = 2 * (box_x - (box_x ^ distance_x))
            across_x = nodes[0] + gap_x.astype(jnp.float32)
            distant = jnp.maximum(jnp.abs(gap_x), jnp.abs(gap_z)) >= 4
            blocks.append(lax.rsqrt(across_x * across_x + rest_z) * jnp.where(distant, 1.0 / COEFFS, 0.0))
        columns.append(jnp.concatenate(blocks, axis=0))
    columns = low_bits(jnp.concatenate(columns, axis=1))
    coarse = dot(boxes_high, columns) + dot(boxes_low, columns)
    coarse = jnp.concatenate([coarse[:, d * SLOT : (d + 1) * SLOT] for d in range(depth)], axis=0)
    coarse_high, coarse_low = high_low(coarse)
    coarse = dot(coarse_high, spread[...]) + dot(coarse_low, spread[...])

    own_local[...] = same + coarse[:ROWS]
    for distance in range(1, depth):
        payload = payloads[distance - 1]
        gap = (box_z ^ distance) - box_z
        given = coarse[distance * ROWS : (distance + 1) * ROWS]
        if touching(distance):
            given = given + jnp.where(gap == 1, up, 0.0) + jnp.where(gap == -1, down, 0.0)
            bit = jnp.where(gap > 0, 1, 0)
            for y in range(2):
                for x in range(4):
                    place = lanes((4 * y + x) * pts, pts)
                    if x in (0, 3):
                        side = left if x == 0 else right
                        payload[:, place] = side[:, lanes((y + 2 * bit) * pts, pts)]
                    else:
                        payload[:, place] = own[:, lanes((x - 1 + 2 * y + 4 * bit) * pts, pts)]
        start = payload.shape[1] - 2 * LEAVES
        given_high, given_low = high_low(given)
        payload[:, lanes(start, LEAVES)] = given_high
        payload[:, lanes(start + LEAVES, LEAVES)] = given_low


def side_kernel(own, left, right, half, source, target, near, sides):
    points = own.shape[1]
    pts = points // 8

    def group(index, carry):
        here = lanes(index * (2 * pts), 2 * pts)
        zero = jnp.zeros((ROWS, 2 * pts), jnp.float32)
        near[:, here] = pulled(zero, target[:, here], source, own, [leaf * pts for leaf in range(8)], pts)
        return carry

    near[:, lanes(0, 4 * pts)] = half[...]
    lax.fori_loop(2, 4, group, 0)
    for step, side in ((0, left), (1, right)):
        for place in range(4):
            centre = (1.5 if step else -1.5, place % 2 - 0.5, place // 2 - 0.5)
            sides[lanes(place * pts, pts), :] = source_features(side, place * pts, pts, centre)

        def layer(index, carry, step=step, side=side):
            here = lanes((step + 2 * index) * (2 * pts), 2 * pts)
            near[:, here] = pulled(near[:, here], target[:, here], sides, side, [p * pts for p in range(4)], pts)
            return carry

        lax.fori_loop(0, 2, layer, 0)


def last_kernel(depth, count_in, weights_in, near, target, basis, own_local, *rest):
    received, rest = rest[: depth - 1], rest[depth - 1 :]
    potential, sums, held, sides, total, count, weights, sems = rest
    copies = fetch([(count_in, count), (weights_in, weights)], sems)
    fields, points = potential.shape
    pts = points // 8
    _, box_z = box_place()
    for step in range(2):
        held[...] = jnp.zeros(held.shape, held.dtype)
        for distance in range(1, depth):
            if touching(distance):

                @pl.when((box_z ^ distance) - box_z == 2 * step - 1)
                def _(block=received[distance - 1]):
                    held[...] = block[:, lanes(0, points)]

        for place in range(8):
            centre = (place % 4 - 1.5, place // 4 - 0.5, 1.5 if step else -1.5)
            sides[lanes(place * pts, pts), :] = source_features(held, place * pts, pts, centre)

        def pair(index, carry, step=step):
            here = lanes((index + 2 * step) * (2 * pts), 2 * pts)
            starts = [(4 * y + x + index) * pts for y in range(2) for x in range(3)]
            total[:, here] = pulled(near[:, here], target[:, here], sides, held, starts, pts)
            return carry

        lax.fori_loop(0, 2, pair, 0)

    local = own_local[...]
    for distance in range(1, depth):
        block = received[distance - 1]
        start = block.shape[1] - 2 * LEAVES
        local = local + block[:, lanes(start, LEAVES)].astype(jnp.float32)
        local = local + block[:, lanes(start + LEAVES, LEAVES)].astype(jnp.float32)
    local_high, local_low = high_low(local)
    for copy in copies:
        copy.wait()
    column = by_row([weights[field] for field in range(fields)], (fields, 1))
    lane_index = lax.broadcasted_iota(jnp.int32, (fields, pts), 1)
    coupling = 1.0 / (128.0 * pts)
    for leaf in range(8):
        here = slice(leaf * pts, (leaf + 1) * pts)
        slot = slice(leaf * SLOT, (leaf + 1) * SLOT)
        left = jnp.concatenate([local_high[:, slot], local_high[:, slot]], axis=1)
        far_part = dot(left, basis[:, here]) + dot(local_low[:, slot], basis[0:SLOT, here])
        value = (total[:, lanes(leaf_slot(leaf) * pts, pts)] + far_part)[:fields]
        value = jnp.where(lane_index < count[leaf], value * coupling, 0.0)
        potential[:, here] = value
        sums[:, here] = jnp.sum(value * column, axis=0, keepdims=True)
    sums[:, points:] = jnp.broadcast_to(jnp.sum(column), (1, sums.shape[1] - points))


def mean_kernel(mine, other, mean):
    points = mean.shape[1]
    total = mine[...] + other[...]
    mean[...] = total[:, :points] / total[:, points : points + 1]


def swapped(block, axis, partner):
    return lax.ppermute(block, axis, [(i, partner(i)) for i in range(lax.axis_size(axis))])


def per_device(positions, density, leaf_count, sigma_weights):
    fields, points = density.shape
    pts = points // 8
    depth = lax.axis_size("space") // ACROSS
    vmem, hbm = pl.BlockSpec(memory_space=pltpu.VMEM), pl.BlockSpec(memory_space=pltpu.HBM)

    def call(kernel, name, in_specs, outs, scratch, *args):
        return pl.pallas_call(
            kernel,
            in_specs=in_specs,
            out_specs=[vmem] * len(outs),
            out_shape=[jax.ShapeDtypeStruct(shape, dtype) for shape, dtype in outs],
            scratch_shapes=scratch,
            compiler_params=pltpu.CompilerParams(vmem_limit_bytes=24 * MEGA),
            name=name,
        )(*(pltpu.with_memory_space_constraint(a, pltpu.HBM) if s is hbm else a for s, a in zip(in_specs, args)))

    half, full = jnp.bfloat16, jnp.float32
    shift = shift_table()
    face = 4 * pts + LEAVES + 2 * SLOT
    own, basis, moments, totals, *given = call(
        pack_kernel,
        "pack",
        [hbm] * 4,
        [
            ((ROWS, points), half),
            ((2 * SLOT, points), half),
            ((ROWS, LEAVES), half),
            ((ROWS, 2 * SLOT), half),
            ((ROWS, face), half),
            ((ROWS, 2 * SLOT), half),
            ((ROWS, face), half),
        ],
        [
            pltpu.SMEM((8,), jnp.int32),
            pltpu.VMEM((3, points), full),
            pltpu.VMEM((fields, points), half),
            pltpu.VMEM((LEAVES, SLOT), half),
            pltpu.VMEM((SLOT, 8, pts), full),
            pltpu.SemaphoreType.DMA((4,)),
        ],
        leaf_count,
        positions,
        density,
        jnp.asarray(shift, half),
    )
    from_2 = swapped(given[1], "space", lambda i: i ^ 2)
    from_3 = swapped(given[2], "space", lambda i: i ^ 3)
    from_1 = swapped(given[0], "space", lambda i: i ^ 1)
    near, source, target, far, nodes, spread = call(
        own_kernel,
        "near_own",
        [vmem] + [hbm] * 3,
        [
            ((ROWS, points // 2), full),
            ((points, FEATURES), half),
            ((FEATURES, points), half),
            ((len(STEPS) * LEAVES, LEAVES), half),
            ((3, SLOT, SLOT), full),
            ((SLOT, LEAVES), half),
        ],
        [pltpu.SemaphoreType.DMA((3,))],
        own,
        jnp.asarray(far_table(), half),
        jnp.asarray(box_nodes()),
        jnp.asarray(shift.T.copy(), half),
    )
    widths = [(points if touching(d) else 0) + 2 * LEAVES for d in range(1, depth)]
    left, right, own_local, *given = call(
        functools.partial(row_kernel, depth),
        "row",
        [vmem] * 9,
        [((ROWS, 4 * pts + LEAVES), half)] * 2 + [((ROWS, LEAVES), full)] + [((ROWS, w), half) for w in widths],
        [],
        own,
        moments,
        totals,
        from_1,
        from_2,
        from_3,
        far,
        nodes,
        spread,
    )
    received = [None] * (depth - 1)
    for d in sorted(range(1, depth), key=lambda d: (touching(d), -d)):
        received[d - 1] = swapped(given[d - 1], "space", lambda i: i ^ (ACROSS * d))
    near, = call(
        side_kernel,
        "near_side",
        [vmem] * 6,
        [((ROWS, points), full)],
        [pltpu.VMEM((4 * pts, FEATURES), half)],
        own,
        left,
        right,
        near,
        source,
        target,
    )
    potential, sums = call(
        functools.partial(last_kernel, depth),
        "near_rows",
        [hbm] * 2 + [vmem] * (4 + len(received)),
        [((fields, points), full), ((1, points + 128), full)],
        [
            pltpu.VMEM((ROWS, points), half),
            pltpu.VMEM((8 * pts, FEATURES), half),
            pltpu.VMEM((ROWS, points), full),
            pltpu.SMEM((8,), jnp.int32),
            pltpu.SMEM((fields,), full),
            pltpu.SemaphoreType.DMA((2,)),
        ],
        leaf_count,
        sigma_weights,
        near,
        target,
        basis,
        own_local,
        *received,
    )
    if lax.axis_size("sig") == 2:
        other = swapped(sums, "sig", lambda i: i ^ 1)
    else:
        other = lax.psum(sums, "sig") - sums
    mean, = call(mean_kernel, "mean", [vmem] * 2, [((1, points), full)], [], sums, other)
    return potential, mean.reshape(points)


def solution(mesh):
    in_specs = (P(None, "space"), P("sig", "space"), P("space"), P("sig"))
    out_specs = (P("sig", "space"), P("space"))
    return jax.shard_map(per_device, mesh=mesh, in_specs=in_specs, out_specs=out_specs, check_vma=False)
```

```python
import functools
import math

import jax
import jax.numpy as jnp
import numpy as np
from jax import lax
from jax.experimental import pallas as pl
from jax.experimental.pallas import tpu as pltpu
from jax.sharding import PartitionSpec as P

ORDER = 5
SOFTENING = 0.1
ACROSS = 4
SLOT = 64
ROWS = 32
LEAVES = 8 * SLOT
MEGA = 1024 * 1024
FEATURES = 48


def exponent_table(order_max):
    entries_list = []
    for degree in range(order_max + 1):
        for first_power in range(degree, -1, -1):
            for second_power in range(degree - first_power, -1, -1):
                entries_list.append((first_power, second_power, degree - first_power - second_power))
    return entries_list


def node_table(count_nodes, offset_value):
    counter = np.arange(1, count_nodes + 1, dtype=np.float32)[:, None]
    stride_set = np.array([0.7548776662466927, 0.5698402909980532, 0.4142135623730951], dtype=np.float32)[None, :]
    unit_points = np.mod(counter * stride_set + np.float32(offset_value), np.float32(1.0))
    return (np.float32(2.0) * unit_points - np.float32(1.0)).astype(np.float32)


EXPONENTS = exponent_table(ORDER)
COEFFS = len(EXPONENTS)
CHECK = node_table(COEFFS, 0.5).astype(np.float64)
EQUIV = node_table(COEFFS, 0.0).astype(np.float64)
STEPS = [(sx, sz) for sz in (-1, 0, 1) for sx in (-1, 0, 1) if sx != 0 or sz != 0]


def bits(octant):
    return octant % 2, octant // 2 % 2, octant // 4


def leaf_slot(octant):
    bit_x, bit_y, bit_z = bits(octant)
    return (bit_x + 2 * bit_z) * 2 + bit_y


@functools.lru_cache(None)
def far_table():
    shape = (len(STEPS), 8, SLOT, 8, SLOT)
    table = np.zeros(shape)
    gap_nodes = 0.5 * (CHECK[None, :, :] - EQUIV[:, None, :])
    for index, (step_x, step_z) in enumerate(STEPS):
        for source in range(8):
            for target in range(8):
                s, t = bits(source), bits(target)
                gap = np.array([2 * step_x + s[0] - t[0], s[1] - t[1], 2 * step_z + s[2] - t[2]], np.float64)
                if max(abs(gap[0]), abs(gap[2])) >= 2:
                    shifted = gap_nodes - gap
                    value = 1.0 / np.sqrt(np.sum(shifted * shifted, -1) + SOFTENING * SOFTENING) / COEFFS
                    table[index, source, :COEFFS, target, :COEFFS] = value
    return table.reshape(len(STEPS) * LEAVES, LEAVES)


@functools.lru_cache(None)
def shift_table():
    table = np.zeros((8, SLOT, SLOT))
    for leaf in range(8):
        offset = [bit - 0.5 for bit in bits(leaf)]
        for k, target in enumerate(EXPONENTS):
            for i, source in enumerate(EXPONENTS):
                if all(b <= a for a, b in zip(target, source)):
                    value = 1.0
                    for a, b, h in zip(target, source, offset):
                        value *= math.comb(a, b) * 0.5**b * h ** (a - b)
                    table[leaf, i, k] = value
    return table.reshape(8 * SLOT, SLOT)


@functools.lru_cache(None)
def box_nodes():
    gaps = np.zeros((3, SLOT, SLOT))
    gaps[:, :COEFFS, :COEFFS] = np.moveaxis(CHECK[None, :, :] - EQUIV[:, None, :], -1, 0)
    gaps[1] = gaps[1] ** 2 + SOFTENING * SOFTENING
    return gaps.astype(np.float32)


def dot(left, right):
    return jnp.dot(left, right, preferred_element_type=jnp.float32)


def dot_nt(left, right):
    return lax.dot_general(left, right, (((1,), (1,)), ((), ())), preferred_element_type=jnp.float32)


def low_bits(value):
    return value.astype(jnp.bfloat16)


def high_low(value):
    high = low_bits(value)
    return high, low_bits(value - high.astype(jnp.float32))


def by_row(values, shape):
    row = lax.broadcasted_iota(jnp.int32, shape, 0)
    result = jnp.zeros(shape, jnp.float32)
    for index, value in enumerate(values):
        result = jnp.where(row == index, value, result)
    return result


def box_place():
    label = lax.axis_index("space")
    return lax.rem(label, ACROSS), lax.div(label, ACROSS)


def lanes(start, size):
    return pl.ds(start if isinstance(start, int) else pl.multiple_of(start, 128), size)


def fetch(pairs, sems):
    copies = [pltpu.make_async_copy(src, dst, sems.at[i]) for i, (src, dst) in enumerate(pairs)]
    for copy in copies:
        copy.start()
    return copies


def pack_kernel(count_in, positions_in, density_in, shift_in, own, basis, moments, payload, *rest):
    count, positions, density, shift, mono, sems = rest
    copies = fetch(
        [(count_in, count), (positions_in, positions), (density_in, density), (shift_in, shift)], sems
    )
    fields, points = density.shape
    pts = points // 8
    box_x, box_z = box_place()
    for copy in copies:
        copy.wait()
    local = []
    for leaf in range(8):
        bit_x, bit_y, bit_z = bits(leaf)
        centre = by_row(
            [2.0 * box_x.astype(jnp.float32) + (bit_x + 0.5), bit_y + 0.5, 2.0 * box_z.astype(jnp.float32) + (bit_z + 0.5)],
            (3, 1),
        )
        here = slice(leaf * pts, (leaf + 1) * pts)
        offset = positions[:, here] - centre
        local.append(offset)
        high = low_bits(offset).astype(jnp.float32)
        middle = low_bits(offset - high).astype(jnp.float32)
        low = offset - high - middle
        raw = density[:, here].astype(jnp.float32)
        mass = jnp.where(lax.broadcasted_iota(jnp.int32, raw.shape, 1) < count[leaf], raw, 0.0)
        spare = jnp.zeros((ROWS - fields - 9, pts), jnp.float32)
        own[:, here] = low_bits(jnp.concatenate([mass, high, middle, low, spare], axis=0))

    axes = [2.0 * jnp.concatenate([part[a : a + 1] for part in local], axis=0) for a in range(3)]
    made = {(0, 0, 0): jnp.ones((8, pts), jnp.float32)}
    for k, powers in enumerate(EXPONENTS):
        if powers not in made:
            a = next(i for i in range(3) if powers[i] > 0)
            before = tuple(p - (i == a) for i, p in enumerate(powers))
            made[powers] = made[before] * axes[a]
        mono[k] = made[powers]
    mono[COEFFS:SLOT] = jnp.zeros((SLOT - COEFFS, 8, pts), jnp.float32)
    parts = []
    for leaf in range(8):
        here = slice(leaf * pts, (leaf + 1) * pts)
        high, low = high_low(mono[:, leaf, :])
        basis[0:SLOT, here] = high
        basis[SLOT:, here] = low
        parts.append(dot_nt(own[:, here], high))
    moment, rest = high_low(jnp.concatenate(parts, axis=1))
    moments[...] = moment
    total = dot(moment, shift[...]) + dot(rest, shift[...])
    total = jnp.concatenate(high_low(total), axis=1)
    for box in range(ACROSS):
        bit = jnp.where(box > box_x, 1, 0)
        for place in range(4):
            payload[box, :, lanes(place * pts, pts)] = own[:, lanes((bit + 2 * place) * pts, pts)]
        payload[box, :, lanes(4 * pts, LEAVES)] = moment
        payload[box, :, lanes(4 * pts + LEAVES, 2 * SLOT)] = total


def features(held, start, size, centre, target):
    value = held[16:32, lanes(start, size)].astype(jnp.float32)
    x = value[1:4] + value[4:7] + value[7:10] + by_row(centre, (3, 1))
    norm = jnp.sum(x * x, axis=0, keepdims=True)
    if target:
        norm = norm + SOFTENING * SOFTENING
    parts, norms = [], []
    for source, out in ((x, parts), (norm, norms)):
        left = source
        for _ in range(3):
            high = low_bits(left).astype(jnp.float32)
            out.append(high)
            left = left - high
    one = jnp.ones_like(norm)
    zero = jnp.zeros_like(norm)
    blank = jnp.zeros((3, norm.shape[1]), jnp.float32)
    blocks = []
    order = (0, 1, 0, 2, 0, 1) if target else (0, 0, 1, 0, 2, 1)
    for index, which in enumerate(order):
        coords = -2.0 * parts[which] if target else parts[which]
        if index < 3:
            pair = [one, norms[index]] if target else [norms[index], one]
        else:
            pair = [zero, zero]
        blocks += [coords, *pair, blank]
    return jnp.concatenate(blocks, axis=0)


def source_features(held, start, size, centre):
    return low_bits(jnp.transpose(features(held, start, size, centre, False)))


def pulled(total, wanted, source, masses, starts, pts):
    for start in starts:
        place = lanes(start, pts)
        kernel = lax.rsqrt(low_bits(dot(source[place, :], wanted)))
        total = total + dot(masses[:, place], kernel)
    return total


def own_kernel(own, far_in, nodes_in, spread_in, near, source, target, far, nodes, spread, sems):
    copies = fetch([(far_in, far), (nodes_in, nodes), (spread_in, spread)], sems)
    points = own.shape[1]
    pts = points // 8
    for leaf in range(8):
        centre = [bit - 0.5 for bit in bits(leaf)]
        source[lanes(leaf * pts, pts), :] = source_features(own, leaf * pts, pts, centre)
        target[:, lanes(leaf_slot(leaf) * pts, pts)] = low_bits(features(own, leaf * pts, pts, centre, True))

    def group(index, carry):
        here = lanes(index * (2 * pts), 2 * pts)
        zero = jnp.zeros((ROWS, 2 * pts), jnp.float32)
        near[:, here] = pulled(zero, target[:, here], source, own, [leaf * pts for leaf in range(8)], pts)
        return carry

    lax.fori_loop(0, 2, group, 0)
    for copy in copies:
        copy.wait()


def row_kernel(depth, own, moments, received, far, nodes, spread, left, right, given, faces_even, faces_odd):
    points = own.shape[1]
    pts = points // 8
    box_x, box_z = box_place()
    wide = 4 * pts + LEAVES
    for side, step in ((left, -1), (right, 1)):
        neighbour = box_x + step
        inside = (neighbour >= 0) & (neighbour < ACROSS)

        @pl.when(inside)
        def _(side=side, neighbour=neighbour):
            side[...] = received[neighbour, :, lanes(0, wide)]

        @pl.when(jnp.logical_not(inside))
        def _(side=side):
            side[...] = jnp.zeros(side.shape, side.dtype)

    base = 4 * pts
    row = jnp.concatenate([left[:, lanes(base, LEAVES)], moments[...], right[:, lanes(base, LEAVES)]], axis=1)
    below_rows, same_rows, above_rows = pl.ds(0, 3 * LEAVES), pl.ds(3 * LEAVES, 2 * LEAVES), pl.ds(5 * LEAVES, 3 * LEAVES)
    up = dot(row, far[below_rows, :])
    down = dot(row, far[above_rows, :])
    same = dot(jnp.concatenate([row[:, :LEAVES], row[:, 2 * LEAVES :]], axis=1), far[same_rows, :])

    boxes = [received[box, :, lanes(wide, 2 * SLOT)] for box in range(ACROSS)]
    boxes_high = jnp.concatenate([held[:, :SLOT] for held in boxes], axis=1)
    boxes_low = jnp.concatenate([held[:, SLOT:] for held in boxes], axis=1)
    columns = []
    for layer in range(depth):
        gap_z = 2 * (layer - box_z)
        across_z = nodes[2] + gap_z.astype(jnp.float32)
        rest_z = across_z * across_z + nodes[1]
        blocks = []
        for box in range(ACROSS):
            gap_x = 2 * (box_x - box)
            across_x = nodes[0] + gap_x.astype(jnp.float32)
            distant = jnp.maximum(jnp.abs(gap_x), jnp.abs(gap_z)) >= 4
            blocks.append(lax.rsqrt(across_x * across_x + rest_z) * jnp.where(distant, 1.0 / COEFFS, 0.0))
        columns.append(jnp.concatenate(blocks, axis=0))
    columns = low_bits(jnp.concatenate(columns, axis=1))
    coarse = dot(boxes_high, columns) + dot(boxes_low, columns)
    coarse = jnp.concatenate([coarse[:, d * SLOT : (d + 1) * SLOT] for d in range(depth)], axis=0)
    coarse_high, coarse_low = high_low(coarse)
    coarse = dot(coarse_high, spread[...]) + dot(coarse_low, spread[...])
    kept = given.shape[1]
    for layer in range(depth):
        gap = layer - box_z
        value = coarse[layer * ROWS : layer * ROWS + kept]
        value = value + jnp.where(gap == 0, same[:kept], jnp.where(gap == 1, up[:kept], jnp.where(gap == -1, down[:kept], 0.0)))
        given[layer] = value
    odd = lax.rem(box_z, 2)
    for faces, bit in ((faces_even, 1 - odd), (faces_odd, odd)):
        for y in range(2):
            for x in range(4):
                place = lanes((4 * y + x) * pts, pts)
                if x in (0, 3):
                    side = left if x == 0 else right
                    faces[:, place] = side[:, lanes((y + 2 * bit) * pts, pts)]
                else:
                    faces[:, place] = own[:, lanes((x - 1 + 2 * y + 4 * bit) * pts, pts)]


def side_kernel(own, left, right, half, source, target, near, sides):
    points = own.shape[1]
    pts = points // 8

    def group(index, carry):
        here = lanes(index * (2 * pts), 2 * pts)
        zero = jnp.zeros((ROWS, 2 * pts), jnp.float32)
        near[:, here] = pulled(zero, target[:, here], source, own, [leaf * pts for leaf in range(8)], pts)
        return carry

    near[:, lanes(0, 4 * pts)] = half[...]
    lax.fori_loop(2, 4, group, 0)
    for step, side in ((0, left), (1, right)):
        for place in range(4):
            centre = (1.5 if step else -1.5, place % 2 - 0.5, place // 2 - 0.5)
            sides[lanes(place * pts, pts), :] = source_features(side, place * pts, pts, centre)

        def layer(index, carry, step=step, side=side):
            here = lanes((step + 2 * index) * (2 * pts), 2 * pts)
            near[:, here] = pulled(near[:, here], target[:, here], sides, side, [p * pts for p in range(4)], pts)
            return carry

        lax.fori_loop(0, 2, layer, 0)


def last_kernel(depth, count_in, weights_in, near, target, basis, given, faces_even, faces_odd, *rest):
    potential, sums, held, sides, total, count, weights, sems = rest
    copies = fetch([(count_in, count), (weights_in, weights)], sems)
    fields, points = potential.shape
    pts = points // 8
    _, box_z = box_place()
    for step in range(2):
        odd = lax.rem(box_z, 2)
        inside = (box_z + 2 * step - 1 >= 0) & (box_z + 2 * step - 1 < depth)
        for faces, parity in ((faces_even, 1 - step), (faces_odd, step)):

            @pl.when(inside & (odd == parity))
            def _(faces=faces):
                held[...] = faces[...]

        @pl.when(jnp.logical_not(inside))
        def _():
            held[...] = jnp.zeros(held.shape, held.dtype)

        for place in range(8):
            centre = (place % 4 - 1.5, place // 4 - 0.5, 1.5 if step else -1.5)
            sides[lanes(place * pts, pts), :] = source_features(held, place * pts, pts, centre)

        def pair(index, carry, step=step):
            here = lanes((index + 2 * step) * (2 * pts), 2 * pts)
            starts = [(4 * y + x + index) * pts for y in range(2) for x in range(3)]
            total[:, here] = pulled(near[:, here], target[:, here], sides, held, starts, pts)
            return carry

        lax.fori_loop(0, 2, pair, 0)

    local = given[0]
    for layer in range(1, depth):
        local = local + given[layer]
    local_high, local_low = high_low(local)
    for copy in copies:
        copy.wait()
    column = by_row([weights[field] for field in range(fields)], (fields, 1))
    lane_index = lax.broadcasted_iota(jnp.int32, (fields, pts), 1)
    coupling = 1.0 / (128.0 * pts)
    for leaf in range(8):
        here = slice(leaf * pts, (leaf + 1) * pts)
        slot = slice(leaf * SLOT, (leaf + 1) * SLOT)
        left = jnp.concatenate([local_high[:, slot], local_high[:, slot]], axis=1)
        far_part = dot(left, basis[:, here]) + dot(local_low[:, slot], basis[0:SLOT, here])
        value = total[0:fields, lanes(leaf_slot(leaf) * pts, pts)] + far_part[:fields]
        value = jnp.where(lane_index < count[leaf], value * coupling, 0.0)
        potential[:, here] = value
        sums[:, here] = jnp.sum(value * column, axis=0, keepdims=True)
    sums[:, points:] = jnp.broadcast_to(jnp.sum(column), (1, sums.shape[1] - points))


def mean_kernel(mine, other, mean):
    points = mean.shape[1]
    total = mine[...] + other[...]
    mean[...] = total[:, :points] / total[:, points : points + 1]


def swapped(block, axis, partner):
    size = lax.axis_size(axis)
    return lax.ppermute(block, axis, [(partner(i), i) for i in range(size) if 0 <= partner(i) < size])


def traded(slots, groups):
    return lax.all_to_all(slots, "space", 0, 0, axis_index_groups=groups, tiled=True)


def per_device(positions, density, leaf_count, sigma_weights):
    fields, points = density.shape
    pts = points // 8
    depth = lax.axis_size("space") // ACROSS
    vmem, hbm = pl.BlockSpec(memory_space=pltpu.VMEM), pl.BlockSpec(memory_space=pltpu.HBM)

    def call(kernel, name, in_specs, outs, scratch, *args):
        return pl.pallas_call(
            kernel,
            in_specs=in_specs,
            out_specs=[vmem] * len(outs),
            out_shape=[jax.ShapeDtypeStruct(shape, dtype) for shape, dtype in outs],
            scratch_shapes=scratch,
            compiler_params=pltpu.CompilerParams(vmem_limit_bytes=24 * MEGA),
            name=name,
        )(*(pltpu.with_memory_space_constraint(a, pltpu.HBM) if s is hbm else a for s, a in zip(in_specs, args)))

    half, full = jnp.bfloat16, jnp.float32
    shift = shift_table()
    face = 4 * pts + LEAVES + 2 * SLOT
    own, basis, moments, payload = call(
        pack_kernel,
        "pack",
        [hbm] * 4,
        [
            ((ROWS, points), half),
            ((2 * SLOT, points), half),
            ((ROWS, LEAVES), half),
            ((ACROSS, ROWS, face), half),
        ],
        [
            pltpu.SMEM((8,), jnp.int32),
            pltpu.VMEM((3, points), full),
            pltpu.VMEM((fields, points), half),
            pltpu.VMEM((LEAVES, SLOT), half),
            pltpu.VMEM((SLOT, 8, pts), full),
            pltpu.SemaphoreType.DMA((4,)),
        ],
        leaf_count,
        positions,
        density,
        jnp.asarray(shift, half),
    )
    received = traded(payload, [[z * ACROSS + x for x in range(ACROSS)] for z in range(depth)])
    near, source, target, far, nodes, spread = call(
        own_kernel,
        "near_own",
        [vmem] + [hbm] * 3,
        [
            ((ROWS, points // 2), full),
            ((points, FEATURES), half),
            ((FEATURES, points), half),
            ((len(STEPS) * LEAVES, LEAVES), half),
            ((3, SLOT, SLOT), full),
            ((SLOT, LEAVES), half),
        ],
        [pltpu.SemaphoreType.DMA((3,))],
        own,
        jnp.asarray(far_table(), half),
        jnp.asarray(box_nodes()),
        jnp.asarray(shift.T.copy(), half),
    )
    left, right, given, faces_even, faces_odd = call(
        functools.partial(row_kernel, depth),
        "row",
        [vmem] * 6,
        [
            ((ROWS, 4 * pts + LEAVES), half),
            ((ROWS, 4 * pts + LEAVES), half),
            ((depth, 24, LEAVES), full),
            ((ROWS, points), half),
            ((ROWS, points), half),
        ],
        [],
        own,
        moments,
        received,
        far,
        nodes,
        spread,
    )
    given = traded(given, [[z * ACROSS + x for z in range(depth)] for x in range(ACROSS)])
    faces_even = swapped(faces_even, "space", lambda i: i ^ ACROSS)
    faces_odd = swapped(faces_odd, "space", lambda i: i + ACROSS if i // ACROSS % 2 else i - ACROSS)
    near, = call(
        side_kernel,
        "near_side",
        [vmem] * 6,
        [((ROWS, points), full)],
        [pltpu.VMEM((4 * pts, FEATURES), half)],
        own,
        left,
        right,
        near,
        source,
        target,
    )
    potential, sums = call(
        functools.partial(last_kernel, depth),
        "near_rows",
        [hbm] * 2 + [vmem] * 6,
        [((fields, points), full), ((1, points + 128), full)],
        [
            pltpu.VMEM((ROWS, points), half),
            pltpu.VMEM((8 * pts, FEATURES), half),
            pltpu.VMEM((ROWS, points), full),
            pltpu.SMEM((8,), jnp.int32),
            pltpu.SMEM((fields,), full),
            pltpu.SemaphoreType.DMA((2,)),
        ],
        leaf_count,
        sigma_weights,
        near,
        target,
        basis,
        given,
        faces_even,
        faces_odd,
    )
    if lax.axis_size("sig") == 2:
        other = swapped(sums, "sig", lambda i: i ^ 1)
    else:
        other = lax.psum(sums, "sig") - sums
    mean, = call(mean_kernel, "mean", [vmem] * 2, [((1, points), full)], [], sums, other)
    return potential, mean.reshape(points)


def solution(mesh):
    in_specs = (P(None, "space"), P("sig", "space"), P("space"), P("sig"))
    out_specs = (P("sig", "space"), P("space"))
    return jax.shard_map(per_device, mesh=mesh, in_specs=in_specs, out_specs=out_specs, check_vma=False)
```

```python
import functools
import math

import jax
import jax.numpy as jnp
import numpy as np
from jax import lax
from jax.experimental import pallas as pl
from jax.experimental.pallas import tpu as pltpu
from jax.sharding import PartitionSpec as P

ORDER = 5
SOFTENING = 0.1
ACROSS = 4
SLOT = 64
ROWS = 32
LEAVES = 8 * SLOT
MEGA = 1024 * 1024
FEATURES = 48


def exponent_table(order_max):
    entries_list = []
    for degree in range(order_max + 1):
        for first_power in range(degree, -1, -1):
            for second_power in range(degree - first_power, -1, -1):
                entries_list.append((first_power, second_power, degree - first_power - second_power))
    return entries_list


def node_table(count_nodes, offset_value):
    counter = np.arange(1, count_nodes + 1, dtype=np.float32)[:, None]
    stride_set = np.array([0.7548776662466927, 0.5698402909980532, 0.4142135623730951], dtype=np.float32)[None, :]
    unit_points = np.mod(counter * stride_set + np.float32(offset_value), np.float32(1.0))
    return (np.float32(2.0) * unit_points - np.float32(1.0)).astype(np.float32)


EXPONENTS = exponent_table(ORDER)
COEFFS = len(EXPONENTS)
CHECK = node_table(COEFFS, 0.5).astype(np.float64)
EQUIV = node_table(COEFFS, 0.0).astype(np.float64)
STEPS = [(sx, sz) for sz in (-1, 0, 1) for sx in (-1, 0, 1) if sx != 0 or sz != 0]


def bits(octant):
    return octant % 2, octant // 2 % 2, octant // 4


def touching(distance):
    return distance & (distance + 1) == 0


def leaf_slot(octant):
    bit_x, bit_y, bit_z = bits(octant)
    return (bit_x + 2 * bit_z) * 2 + bit_y


@functools.lru_cache(None)
def far_table():
    shape = (len(STEPS), 8, SLOT, 8, SLOT)
    table = np.zeros(shape)
    gap_nodes = 0.5 * (CHECK[None, :, :] - EQUIV[:, None, :])
    for index, (step_x, step_z) in enumerate(STEPS):
        for source in range(8):
            for target in range(8):
                s, t = bits(source), bits(target)
                gap = np.array([2 * step_x + s[0] - t[0], s[1] - t[1], 2 * step_z + s[2] - t[2]], np.float64)
                if max(abs(gap[0]), abs(gap[2])) >= 2:
                    shifted = gap_nodes - gap
                    value = 1.0 / np.sqrt(np.sum(shifted * shifted, -1) + SOFTENING * SOFTENING) / COEFFS
                    table[index, source, :COEFFS, target, :COEFFS] = value
    return table.reshape(len(STEPS) * LEAVES, LEAVES)


@functools.lru_cache(None)
def shift_table():
    table = np.zeros((8, SLOT, SLOT))
    for leaf in range(8):
        offset = [bit - 0.5 for bit in bits(leaf)]
        for k, target in enumerate(EXPONENTS):
            for i, source in enumerate(EXPONENTS):
                if all(b <= a for a, b in zip(target, source)):
                    value = 1.0
                    for a, b, h in zip(target, source, offset):
                        value *= math.comb(a, b) * 0.5**b * h ** (a - b)
                    table[leaf, i, k] = value
    return table.reshape(8 * SLOT, SLOT)


@functools.lru_cache(None)
def box_nodes():
    gaps = np.zeros((3, SLOT, SLOT))
    gaps[:, :COEFFS, :COEFFS] = np.moveaxis(CHECK[None, :, :] - EQUIV[:, None, :], -1, 0)
    gaps[1] = gaps[1] ** 2 + SOFTENING * SOFTENING
    return gaps.astype(np.float32)


def dot(left, right):
    return jnp.dot(left, right, preferred_element_type=jnp.float32)


def dot_nt(left, right):
    return lax.dot_general(left, right, (((1,), (1,)), ((), ())), preferred_element_type=jnp.float32)


def low_bits(value):
    return value.astype(jnp.bfloat16)


def high_low(value):
    high = low_bits(value)
    return high, low_bits(value - high.astype(jnp.float32))


def by_row(values, shape):
    row = lax.broadcasted_iota(jnp.int32, shape, 0)
    result = jnp.zeros(shape, jnp.float32)
    for index, value in enumerate(values):
        result = jnp.where(row == index, value, result)
    return result


def box_place():
    label = lax.axis_index("space")
    return lax.rem(label, ACROSS), lax.div(label, ACROSS)


def lanes(start, size):
    return pl.ds(start if isinstance(start, int) else pl.multiple_of(start, 128), size)


def fetch(pairs, sems):
    copies = [pltpu.make_async_copy(src, dst, sems.at[i]) for i, (src, dst) in enumerate(pairs)]
    for copy in copies:
        copy.start()
    return copies


def pack_kernel(count_in, positions_in, density_in, shift_in, own, basis, moments, totals, *rest):
    payloads, (count, positions, density, shift, mono, sems) = rest[:3], rest[3:]
    copies = fetch(
        [(count_in, count), (positions_in, positions), (density_in, density), (shift_in, shift)], sems
    )
    fields, points = density.shape
    pts = points // 8
    box_x, box_z = box_place()
    for copy in copies:
        copy.wait()
    local = []
    for leaf in range(8):
        bit_x, bit_y, bit_z = bits(leaf)
        centre = by_row(
            [2.0 * box_x.astype(jnp.float32) + (bit_x + 0.5), bit_y + 0.5, 2.0 * box_z.astype(jnp.float32) + (bit_z + 0.5)],
            (3, 1),
        )
        here = slice(leaf * pts, (leaf + 1) * pts)
        offset = positions[:, here] - centre
        local.append(offset)
        high = low_bits(offset).astype(jnp.float32)
        middle = low_bits(offset - high).astype(jnp.float32)
        low = offset - high - middle
        raw = density[:, here].astype(jnp.float32)
        mass = jnp.where(lax.broadcasted_iota(jnp.int32, raw.shape, 1) < count[leaf], raw, 0.0)
        spare = jnp.zeros((ROWS - fields - 9, pts), jnp.float32)
        own[:, here] = low_bits(jnp.concatenate([mass, high, middle, low, spare], axis=0))

    axes = [2.0 * jnp.concatenate([part[a : a + 1] for part in local], axis=0) for a in range(3)]
    made = {(0, 0, 0): jnp.ones((8, pts), jnp.float32)}
    for k, powers in enumerate(EXPONENTS):
        if powers not in made:
            a = next(i for i in range(3) if powers[i] > 0)
            before = tuple(p - (i == a) for i, p in enumerate(powers))
            made[powers] = made[before] * axes[a]
        mono[k] = made[powers]
    mono[COEFFS:SLOT] = jnp.zeros((SLOT - COEFFS, 8, pts), jnp.float32)
    parts = []
    for leaf in range(8):
        here = slice(leaf * pts, (leaf + 1) * pts)
        high, low = high_low(mono[:, leaf, :])
        basis[0:SLOT, here] = high
        basis[SLOT:, here] = low
        parts.append(dot_nt(own[:, here], high))
    moment, rest = high_low(jnp.concatenate(parts, axis=1))
    moments[...] = moment
    total = dot(moment, shift[...]) + dot(rest, shift[...])
    total = jnp.concatenate(high_low(total), axis=1)
    totals[...] = total
    payloads[1][...] = total
    for distance, payload in ((1, payloads[0]), (3, payloads[2])):
        bit = jnp.where((box_x ^ distance) > box_x, 1, 0)
        for place in range(4):
            payload[:, lanes(place * pts, pts)] = own[:, lanes((bit + 2 * place) * pts, pts)]
        payload[:, lanes(4 * pts, LEAVES)] = moment
        payload[:, lanes(4 * pts + LEAVES, 2 * SLOT)] = total


def features(held, start, size, centre, target):
    value = held[16:32, lanes(start, size)].astype(jnp.float32)
    x = value[1:4] + value[4:7] + value[7:10] + by_row(centre, (3, 1))
    norm = jnp.sum(x * x, axis=0, keepdims=True)
    if target:
        norm = norm + SOFTENING * SOFTENING
    parts, norms = [], []
    for source, out in ((x, parts), (norm, norms)):
        left = source
        for _ in range(3):
            high = low_bits(left).astype(jnp.float32)
            out.append(high)
            left = left - high
    one = jnp.ones_like(norm)
    zero = jnp.zeros_like(norm)
    blank = jnp.zeros((3, norm.shape[1]), jnp.float32)
    blocks = []
    order = (0, 1, 0, 2, 0, 1) if target else (0, 0, 1, 0, 2, 1)
    for index, which in enumerate(order):
        coords = -2.0 * parts[which] if target else parts[which]
        if index < 3:
            pair = [one, norms[index]] if target else [norms[index], one]
        else:
            pair = [zero, zero]
        blocks += [coords, *pair, blank]
    return jnp.concatenate(blocks, axis=0)


def source_features(held, start, size, centre):
    return low_bits(jnp.transpose(features(held, start, size, centre, False)))


def pulled(near, index, width, target, source, masses, starts, size, first=None):
    pair = target.shape[1] // 4
    for piece in range(0, pair, width):
        here = lanes(index * pair + piece, width)
        wanted = target[:, here]
        total = jnp.zeros((ROWS, width), jnp.float32) if first is None else first[:, here]
        ahead = dot(source[lanes(starts[0], size), :], wanted)
        for place, start in enumerate(starts):
            square = ahead
            if place + 1 < len(starts):
                ahead = dot(source[lanes(starts[place + 1], size), :], wanted)
            total = total + dot(masses[:, lanes(start, size)], low_bits(lax.rsqrt(square)))
        near[:, here] = total


def own_kernel(own, far_in, nodes_in, spread_in, near, source, target, far, nodes, spread, sems):
    copies = fetch([(far_in, far), (nodes_in, nodes), (spread_in, spread)], sems)
    points = own.shape[1]
    pts = points // 8
    for leaf in range(8):
        centre = [bit - 0.5 for bit in bits(leaf)]
        source[lanes(leaf * pts, pts), :] = source_features(own, leaf * pts, pts, centre)
        target[:, lanes(leaf_slot(leaf) * pts, pts)] = low_bits(features(own, leaf * pts, pts, centre, True))

    def group(index, carry):
        pulled(near, index, 2 * pts, target, source, own, [leaf * pts for leaf in range(8)], pts)
        return carry

    lax.fori_loop(0, 2, group, 0)
    for copy in copies:
        copy.wait()


def row_kernel(depth, own, moments, totals, from_1, from_2, from_3, far, nodes, spread, *rest):
    left, right, own_local, faces_even, faces_odd, *distant = rest
    points = own.shape[1]
    pts = points // 8
    box_x, box_z = box_place()
    wide = 4 * pts + LEAVES
    for side, step in ((left, -1), (right, 1)):
        side[...] = jnp.zeros(side.shape, side.dtype)
        for distance, held in ((1, from_1), (3, from_3)):

            @pl.when((box_x ^ distance) - box_x == step)
            def _(side=side, held=held):
                side[...] = held[:, lanes(0, wide)]

    base = 4 * pts
    row = jnp.concatenate([left[:, lanes(base, LEAVES)], moments[...], right[:, lanes(base, LEAVES)]], axis=1)
    below_rows, same_rows, above_rows = pl.ds(0, 3 * LEAVES), pl.ds(3 * LEAVES, 2 * LEAVES), pl.ds(5 * LEAVES, 3 * LEAVES)
    up = dot(row, far[below_rows, :])
    down = dot(row, far[above_rows, :])
    same = dot(jnp.concatenate([row[:, :LEAVES], row[:, 2 * LEAVES :]], axis=1), far[same_rows, :])

    boxes = [totals[...], from_1[:, lanes(wide, 2 * SLOT)], from_2[...], from_3[:, lanes(wide, 2 * SLOT)]]
    boxes_high = jnp.concatenate([held[:, :SLOT] for held in boxes], axis=1)
    boxes_low = jnp.concatenate([held[:, SLOT:] for held in boxes], axis=1)
    columns = []
    for distance_z in range(depth):
        gap_z = 2 * ((box_z ^ distance_z) - box_z)
        across_z = nodes[2] + gap_z.astype(jnp.float32)
        rest_z = across_z * across_z + nodes[1]
        blocks = []
        for distance_x in range(ACROSS):
            gap_x = 2 * (box_x - (box_x ^ distance_x))
            across_x = nodes[0] + gap_x.astype(jnp.float32)
            apart = jnp.maximum(jnp.abs(gap_x), jnp.abs(gap_z)) >= 4
            blocks.append(lax.rsqrt(across_x * across_x + rest_z) * jnp.where(apart, 1.0 / COEFFS, 0.0))
        columns.append(jnp.concatenate(blocks, axis=0))
    columns = low_bits(jnp.concatenate(columns, axis=1))
    coarse = dot(boxes_high, columns) + dot(boxes_low, columns)
    coarse = jnp.concatenate([coarse[:, d * SLOT : (d + 1) * SLOT] for d in range(depth)], axis=0)
    coarse_high, coarse_low = high_low(coarse)
    coarse = dot(coarse_high, spread[...]) + dot(coarse_low, spread[...])

    own_local[...] = same + coarse[:ROWS]
    sums = [coarse[distance * ROWS : (distance + 1) * ROWS] for distance in range(depth)]
    for distance in range(2, depth):
        distant[distance - 2][...] = sums[distance][: distant[0].shape[0]]
    odd = lax.rem(box_z, 2)
    beside = jnp.zeros_like(sums[0])
    for distance in range(3, depth):
        if touching(distance):
            beside = jnp.where(jnp.abs((box_z ^ distance) - box_z) == 1, sums[distance], beside)
    for faces, bit, base in ((faces_even, 1 - odd, sums[1]), (faces_odd, odd, beside)):
        for y in range(2):
            for x in range(4):
                place = lanes((2 * x + y) * pts, pts)
                if x in (0, 3):
                    side = left if x == 0 else right
                    faces[:, place] = side[:, lanes((y + 2 * bit) * pts, pts)]
                else:
                    faces[:, place] = own[:, lanes((x - 1 + 2 * y + 4 * bit) * pts, pts)]
        given_high, given_low = high_low(base + jnp.where(bit == 1, up, down))
        faces[:, lanes(points, LEAVES)] = given_high
        faces[:, lanes(points + LEAVES, LEAVES)] = given_low


def side_kernel(own, left, right, half, source, target, near, sides):
    points = own.shape[1]
    pts = points // 8

    def group(index, carry):
        pulled(near, index, pts, target, source, own, [leaf * pts for leaf in range(8)], pts)
        return carry

    near[:, lanes(0, 4 * pts)] = half[...]
    lax.fori_loop(2, 4, group, 0)
    for step, side in ((0, left), (1, right)):
        for place in range(4):
            centre = (1.5 if step else -1.5, place % 2 - 0.5, place // 2 - 0.5)
            sides[lanes(place * pts, pts), :] = source_features(side, place * pts, pts, centre)

        def layer(index, carry, step=step, side=side):
            pulled(near, step + 2 * index, pts, target, sides, side, [p * pts for p in range(4)], pts, near)
            return carry

        lax.fori_loop(0, 2, layer, 0)


def last_kernel(depth, count_in, weights_in, near, target, basis, own_local, faces_even, faces_odd, *rest):
    distant, rest = rest[: depth - 2], rest[depth - 2 :]
    potential, sums, held, sides, total, count, weights, sems = rest
    copies = fetch([(count_in, count), (weights_in, weights)], sems)
    fields, points = potential.shape
    pts = points // 8
    _, box_z = box_place()
    for step in range(2):
        odd = lax.rem(box_z, 2)
        inside = (box_z + 2 * step - 1 >= 0) & (box_z + 2 * step - 1 < depth)
        for faces, parity in ((faces_even, 1 - step), (faces_odd, step)):

            @pl.when(inside & (odd == parity))
            def _(faces=faces):
                held[...] = faces[:, lanes(0, points)]

        @pl.when(jnp.logical_not(inside))
        def _():
            held[...] = jnp.zeros(held.shape, held.dtype)

        for place in range(8):
            centre = (place // 2 - 1.5, place % 2 - 0.5, 1.5 if step else -1.5)
            sides[lanes(place * pts, pts), :] = source_features(held, place * pts, pts, centre)

        def pair(index, carry, step=step):
            starts = [(2 * x + 2 * index) * pts for x in range(3)]
            pulled(total, index + 2 * step, pts, target, sides, held, starts, 2 * pts, near)
            return carry

        lax.fori_loop(0, 2, pair, 0)

    local = own_local[...]
    for faces in (faces_even, faces_odd):
        local = local + faces[:, lanes(points, LEAVES)].astype(jnp.float32)
        local = local + faces[:, lanes(points + LEAVES, LEAVES)].astype(jnp.float32)
    for block in distant:
        local = local + jnp.concatenate([block[...], jnp.zeros((ROWS - block.shape[0], LEAVES), jnp.float32)], axis=0)
    local_high, local_low = high_low(local)
    for copy in copies:
        copy.wait()
    column = by_row([weights[field] for field in range(fields)], (fields, 1))
    lane_index = lax.broadcasted_iota(jnp.int32, (fields, pts), 1)
    coupling = 1.0 / (128.0 * pts)
    for leaf in range(8):
        here = slice(leaf * pts, (leaf + 1) * pts)
        slot = slice(leaf * SLOT, (leaf + 1) * SLOT)
        left = jnp.concatenate([local_high[:, slot], local_high[:, slot]], axis=1)
        far_part = dot(left, basis[:, here]) + dot(local_low[:, slot], basis[0:SLOT, here])
        value = (total[:, lanes(leaf_slot(leaf) * pts, pts)] + far_part)[:fields]
        value = jnp.where(lane_index < count[leaf], value * coupling, 0.0)
        potential[:, here] = value
        sums[:, here] = jnp.sum(value * column, axis=0, keepdims=True)
    sums[:, points:] = jnp.broadcast_to(jnp.sum(column), (1, sums.shape[1] - points))


def mean_kernel(mine, other, mean):
    points = mean.shape[1]
    total = mine[...] + other[...]
    mean[...] = total[:, :points] / total[:, points : points + 1]


def swapped(block, axis, partner):
    size = lax.axis_size(axis)
    return lax.ppermute(block, axis, [(partner(i), i) for i in range(size) if 0 <= partner(i) < size])


def across_layers(block, distance):
    pairs = [(i, i ^ (ACROSS * distance)) for i in range(lax.axis_size("space"))]
    return lax.ppermute(block, "space", [pair for pair in pairs if abs(pair[0] - pair[1]) > ACROSS])


def per_device(positions, density, leaf_count, sigma_weights):
    fields, points = density.shape
    pts = points // 8
    depth = lax.axis_size("space") // ACROSS
    vmem, hbm = pl.BlockSpec(memory_space=pltpu.VMEM), pl.BlockSpec(memory_space=pltpu.HBM)

    def call(kernel, name, in_specs, outs, scratch, *args):
        return pl.pallas_call(
            kernel,
            in_specs=in_specs,
            out_specs=[vmem] * len(outs),
            out_shape=[jax.ShapeDtypeStruct(shape, dtype) for shape, dtype in outs],
            scratch_shapes=scratch,
            compiler_params=pltpu.CompilerParams(vmem_limit_bytes=24 * MEGA),
            name=name,
        )(*(pltpu.with_memory_space_constraint(a, pltpu.HBM) if s is hbm else a for s, a in zip(in_specs, args)))

    half, full = jnp.bfloat16, jnp.float32
    shift = shift_table()
    face = 4 * pts + LEAVES + 2 * SLOT
    own, basis, moments, totals, *given = call(
        pack_kernel,
        "pack",
        [hbm] * 4,
        [
            ((ROWS, points), half),
            ((2 * SLOT, points), half),
            ((ROWS, LEAVES), half),
            ((ROWS, 2 * SLOT), half),
            ((ROWS, face), half),
            ((ROWS, 2 * SLOT), half),
            ((ROWS, face), half),
        ],
        [
            pltpu.SMEM((8,), jnp.int32),
            pltpu.VMEM((3, points), full),
            pltpu.VMEM((fields, points), half),
            pltpu.VMEM((LEAVES, SLOT), half),
            pltpu.VMEM((SLOT, 8, pts), full),
            pltpu.SemaphoreType.DMA((4,)),
        ],
        leaf_count,
        positions,
        density,
        jnp.asarray(shift, half),
    )
    from_2 = swapped(given[1], "space", lambda i: i ^ 2)
    from_3 = swapped(given[2], "space", lambda i: i ^ 3)
    from_1 = swapped(given[0], "space", lambda i: i ^ 1)
    near, source, target, far, nodes, spread = call(
        own_kernel,
        "near_own",
        [vmem] + [hbm] * 3,
        [
            ((ROWS, points // 2), full),
            ((points, FEATURES), half),
            ((FEATURES, points), half),
            ((len(STEPS) * LEAVES, LEAVES), half),
            ((3, SLOT, SLOT), full),
            ((SLOT, LEAVES), half),
        ],
        [pltpu.SemaphoreType.DMA((3,))],
        own,
        jnp.asarray(far_table(), half),
        jnp.asarray(box_nodes()),
        jnp.asarray(shift.T.copy(), half),
    )
    left, right, own_local, faces_even, faces_odd, *distant = call(
        functools.partial(row_kernel, depth),
        "row",
        [vmem] * 9,
        [((ROWS, 4 * pts + LEAVES), half)] * 2
        + [((ROWS, LEAVES), full)]
        + [((ROWS, points + 2 * LEAVES), half)] * 2
        + [((24, LEAVES), full)] * (depth - 2),
        [],
        own,
        moments,
        totals,
        from_1,
        from_2,
        from_3,
        far,
        nodes,
        spread,
    )
    distant = [across_layers(block, distance + 2) for distance, block in enumerate(distant)]
    faces_even = swapped(faces_even, "space", lambda i: i ^ ACROSS)
    faces_odd = swapped(faces_odd, "space", lambda i: i + ACROSS if i // ACROSS % 2 else i - ACROSS)
    near, = call(
        side_kernel,
        "near_side",
        [vmem] * 6,
        [((ROWS, points), full)],
        [pltpu.VMEM((4 * pts, FEATURES), half)],
        own,
        left,
        right,
        near,
        source,
        target,
    )
    potential, sums = call(
        functools.partial(last_kernel, depth),
        "near_rows",
        [hbm] * 2 + [vmem] * (6 + len(distant)),
        [((fields, points), full), ((1, points + 128), full)],
        [
            pltpu.VMEM((ROWS, points), half),
            pltpu.VMEM((8 * pts, FEATURES), half),
            pltpu.VMEM((ROWS, points), full),
            pltpu.SMEM((8,), jnp.int32),
            pltpu.SMEM((fields,), full),
            pltpu.SemaphoreType.DMA((2,)),
        ],
        leaf_count,
        sigma_weights,
        near,
        target,
        basis,
        own_local,
        faces_even,
        faces_odd,
        *distant,
    )
    if lax.axis_size("sig") == 2:
        other = swapped(sums, "sig", lambda i: i ^ 1)
    else:
        other = lax.psum(sums, "sig") - sums
    mean, = call(mean_kernel, "mean", [vmem] * 2, [((1, points), full)], [], sums, other)
    return potential, mean.reshape(points)


def solution(mesh):
    in_specs = (P(None, "space"), P("sig", "space"), P("space"), P("sig"))
    out_specs = (P("sig", "space"), P("space"))
    return jax.shard_map(per_device, mesh=mesh, in_specs=in_specs, out_specs=out_specs, check_vma=False)
```

```python
import functools
import math

import jax
import jax.numpy as jnp
import numpy as np
from jax import lax
from jax.experimental import pallas as pl
from jax.experimental.pallas import tpu as pltpu
from jax.sharding import PartitionSpec as P

ORDER = 5
SOFTENING = 0.1
ACROSS = 4
SLOT = 64
ROWS = 24
LEAVES = 8 * SLOT
MEGA = 1024 * 1024
FEATURES = 48
EARLY = 3


def exponent_table(order_max):
    entries_list = []
    for degree in range(order_max + 1):
        for first_power in range(degree, -1, -1):
            for second_power in range(degree - first_power, -1, -1):
                entries_list.append((first_power, second_power, degree - first_power - second_power))
    return entries_list


def node_table(count_nodes, offset_value):
    counter = np.arange(1, count_nodes + 1, dtype=np.float32)[:, None]
    stride_set = np.array([0.7548776662466927, 0.5698402909980532, 0.4142135623730951], dtype=np.float32)[None, :]
    unit_points = np.mod(counter * stride_set + np.float32(offset_value), np.float32(1.0))
    return (np.float32(2.0) * unit_points - np.float32(1.0)).astype(np.float32)


EXPONENTS = exponent_table(ORDER)
COEFFS = len(EXPONENTS)
CHECK = node_table(COEFFS, 0.5).astype(np.float64)
EQUIV = node_table(COEFFS, 0.0).astype(np.float64)
STEPS = [(sx, sz) for sz in (-1, 0, 1) for sx in (-1, 0, 1) if sx != 0 or sz != 0]


def bits(octant):
    return octant % 2, octant // 2 % 2, octant // 4


def touching(distance):
    return distance & (distance + 1) == 0


def leaf_slot(octant):
    bit_x, bit_y, bit_z = bits(octant)
    return (bit_x + 2 * bit_z) * 2 + bit_y


@functools.lru_cache(None)
def far_table():
    shape = (len(STEPS), 8, SLOT, 8, SLOT)
    table = np.zeros(shape)
    gap_nodes = 0.5 * (CHECK[None, :, :] - EQUIV[:, None, :])
    for index, (step_x, step_z) in enumerate(STEPS):
        for source in range(8):
            for target in range(8):
                s, t = bits(source), bits(target)
                gap = np.array([2 * step_x + s[0] - t[0], s[1] - t[1], 2 * step_z + s[2] - t[2]], np.float64)
                if max(abs(gap[0]), abs(gap[2])) >= 2:
                    shifted = gap_nodes - gap
                    value = 1.0 / np.sqrt(np.sum(shifted * shifted, -1) + SOFTENING * SOFTENING) / COEFFS
                    table[index, source, :COEFFS, target, :COEFFS] = value
    return table.reshape(len(STEPS) * LEAVES, LEAVES)


@functools.lru_cache(None)
def shift_table():
    table = np.zeros((8, SLOT, SLOT))
    for leaf in range(8):
        offset = [bit - 0.5 for bit in bits(leaf)]
        for k, target in enumerate(EXPONENTS):
            for i, source in enumerate(EXPONENTS):
                if all(b <= a for a, b in zip(target, source)):
                    value = 1.0
                    for a, b, h in zip(target, source, offset):
                        value *= math.comb(a, b) * 0.5**b * h ** (a - b)
                    table[leaf, i, k] = value
    return table.reshape(8 * SLOT, SLOT)


@functools.lru_cache(None)
def box_nodes():
    gaps = np.zeros((3, SLOT, SLOT))
    gaps[:, :COEFFS, :COEFFS] = np.moveaxis(CHECK[None, :, :] - EQUIV[:, None, :], -1, 0)
    gaps[1] = gaps[1] ** 2 + SOFTENING * SOFTENING
    return gaps.astype(np.float32)


def dot(left, right):
    return jnp.dot(left, right, preferred_element_type=jnp.float32)


def dot_nt(left, right):
    return lax.dot_general(left, right, (((1,), (1,)), ((), ())), preferred_element_type=jnp.float32)


def low_bits(value):
    return value.astype(jnp.bfloat16)


def high_low(value):
    high = low_bits(value)
    return high, low_bits(value - high.astype(jnp.float32))


def by_row(values, shape):
    row = lax.broadcasted_iota(jnp.int32, shape, 0)
    result = jnp.zeros(shape, jnp.float32)
    for index, value in enumerate(values):
        result = jnp.where(row == index, value, result)
    return result


def box_place():
    label = lax.axis_index("space")
    return lax.rem(label, ACROSS), lax.div(label, ACROSS)


def lanes(start, size):
    return pl.ds(start if isinstance(start, int) else pl.multiple_of(start, 128), size)


def fetch(pairs, sems):
    copies = [pltpu.make_async_copy(src, dst, sems.at[i]) for i, (src, dst) in enumerate(pairs)]
    for copy in copies:
        copy.start()
    return copies


def pack_kernel(count_in, positions_in, density_in, shift_in, own, basis, moments, totals, *rest):
    payloads, (count, positions, density, shift, mono, sems) = rest[:3], rest[3:]
    copies = fetch(
        [(count_in, count), (positions_in, positions), (density_in, density), (shift_in, shift)], sems
    )
    fields, points = density.shape
    pts = points // 8
    box_x, box_z = box_place()
    for copy in copies:
        copy.wait()
    local = []
    for leaf in range(8):
        bit_x, bit_y, bit_z = bits(leaf)
        centre = by_row(
            [2.0 * box_x.astype(jnp.float32) + (bit_x + 0.5), bit_y + 0.5, 2.0 * box_z.astype(jnp.float32) + (bit_z + 0.5)],
            (3, 1),
        )
        here = slice(leaf * pts, (leaf + 1) * pts)
        offset = positions[:, here] - centre
        local.append(offset)
        high = low_bits(offset).astype(jnp.float32)
        middle = low_bits(offset - high).astype(jnp.float32)
        raw = density[:, here].astype(jnp.float32)
        mass = jnp.where(lax.broadcasted_iota(jnp.int32, raw.shape, 1) < count[leaf], raw, 0.0)
        spare = jnp.zeros((ROWS - fields - 6, pts), jnp.float32)
        own[:, here] = low_bits(jnp.concatenate([mass, high, middle, spare], axis=0))

    axes = [2.0 * jnp.concatenate([part[a : a + 1] for part in local], axis=0) for a in range(3)]
    made = {(0, 0, 0): jnp.ones((8, pts), jnp.float32)}
    for k, powers in enumerate(EXPONENTS):
        if powers not in made:
            a = next(i for i in range(3) if powers[i] > 0)
            before = tuple(p - (i == a) for i, p in enumerate(powers))
            made[powers] = made[before] * axes[a]
        mono[k] = made[powers]
    mono[COEFFS:SLOT] = jnp.zeros((SLOT - COEFFS, 8, pts), jnp.float32)
    parts = []
    for leaf in range(8):
        here = slice(leaf * pts, (leaf + 1) * pts)
        high, low = high_low(mono[:, leaf, :])
        basis[0:SLOT, here] = high
        basis[SLOT:, here] = low
        parts.append(dot_nt(own[:, here], high))
    moment, rest = high_low(jnp.concatenate(parts, axis=1))
    moments[...] = moment
    total = dot(moment, shift[...]) + dot(rest, shift[...])
    total = jnp.concatenate(high_low(total), axis=1)
    totals[...] = total
    payloads[1][...] = total
    for distance, payload in ((1, payloads[0]), (3, payloads[2])):
        bit = jnp.where((box_x ^ distance) > box_x, 1, 0)
        for place in range(4):
            payload[:, lanes(place * pts, pts)] = own[:, lanes((bit + 2 * place) * pts, pts)]
        payload[:, lanes(4 * pts, LEAVES)] = moment
        payload[:, lanes(4 * pts + LEAVES, 2 * SLOT)] = total


def features(held, start, size, centre, target):
    value = held[16:ROWS, lanes(start, size)].astype(jnp.float32)
    x = value[1:4] + value[4:7] + by_row(centre, (3, 1))
    norm = jnp.sum(x * x, axis=0, keepdims=True)
    if target:
        norm = norm + SOFTENING * SOFTENING
    parts, norms = [], []
    for source, out in ((x, parts), (norm, norms)):
        left = source
        for _ in range(3):
            high = low_bits(left).astype(jnp.float32)
            out.append(high)
            left = left - high
    one = jnp.ones_like(norm)
    zero = jnp.zeros_like(norm)
    blank = jnp.zeros((3, norm.shape[1]), jnp.float32)
    blocks = []
    order = (0, 1, 0, 2, 0, 1) if target else (0, 0, 1, 0, 2, 1)
    for index, which in enumerate(order):
        coords = -2.0 * parts[which] if target else parts[which]
        if index < 3:
            pair = [one, norms[index]] if target else [norms[index], one]
        else:
            pair = [zero, zero]
        blocks += [coords, *pair, blank]
    return jnp.concatenate(blocks, axis=0)


def source_features(held, start, size, centre):
    return low_bits(jnp.transpose(features(held, start, size, centre, False)))


def pulled(near, index, target, source, masses, starts, size, first=None):
    width = target.shape[1] // 8
    tiles = [(piece, turn) for piece in range(2) for turn in range(len(starts))]
    places = [lanes((2 * index + piece) * width, width) for piece in range(2)]

    def squares(piece, turn):
        return dot(source[lanes(starts[turn], size), :], target[:, places[piece]])

    ahead = squares(*tiles[0])
    for place, (piece, turn) in enumerate(tiles):
        square = ahead
        if place + 1 < len(tiles):
            ahead = squares(*tiles[place + 1])
        if turn == 0:
            total = jnp.zeros((ROWS, width), jnp.float32) if first is None else first[:, places[piece]]
        total = total + dot(masses[:, lanes(starts[turn], size)], low_bits(lax.rsqrt(square)))
        if turn + 1 == len(starts):
            near[:, places[piece]] = total


def own_kernel(own, far_in, nodes_in, spread_in, near, source, target, far, nodes, spread, sems):
    copies = fetch([(far_in, far), (nodes_in, nodes), (spread_in, spread)], sems)
    points = own.shape[1]
    pts = points // 8
    for leaf in range(8):
        centre = [bit - 0.5 for bit in bits(leaf)]
        source[lanes(leaf * pts, pts), :] = source_features(own, leaf * pts, pts, centre)
        target[:, lanes(leaf_slot(leaf) * pts, pts)] = low_bits(features(own, leaf * pts, pts, centre, True))

    def group(index, carry):
        pulled(near, index, target, source, own, [2 * p * pts for p in range(4)], 2 * pts)
        return carry

    lax.fori_loop(0, EARLY, group, 0)
    for copy in copies:
        copy.wait()


def row_kernel(depth, own, moments, totals, from_1, from_2, from_3, far, nodes, spread, *rest):
    left, right, own_local, faces_even, faces_odd, *distant = rest
    points = own.shape[1]
    pts = points // 8
    box_x, box_z = box_place()
    wide = 4 * pts + LEAVES
    for side, step in ((left, -1), (right, 1)):
        side[...] = jnp.zeros(side.shape, side.dtype)
        for distance, held in ((1, from_1), (3, from_3)):

            @pl.when((box_x ^ distance) - box_x == step)
            def _(side=side, held=held):
                side[...] = held[:, lanes(0, wide)]

    base = 4 * pts
    row = jnp.concatenate([left[:, lanes(base, LEAVES)], moments[...], right[:, lanes(base, LEAVES)]], axis=1)
    below_rows, same_rows, above_rows = pl.ds(0, 3 * LEAVES), pl.ds(3 * LEAVES, 2 * LEAVES), pl.ds(5 * LEAVES, 3 * LEAVES)
    up = dot(row, far[below_rows, :])
    down = dot(row, far[above_rows, :])
    same = dot(jnp.concatenate([row[:, :LEAVES], row[:, 2 * LEAVES :]], axis=1), far[same_rows, :])

    boxes = [totals[...], from_1[:, lanes(wide, 2 * SLOT)], from_2[...], from_3[:, lanes(wide, 2 * SLOT)]]
    boxes_high = jnp.concatenate([held[:, :SLOT] for held in boxes], axis=1)
    boxes_low = jnp.concatenate([held[:, SLOT:] for held in boxes], axis=1)
    columns = []
    for distance_z in range(depth):
        gap_z = 2 * ((box_z ^ distance_z) - box_z)
        across_z = nodes[2] + gap_z.astype(jnp.float32)
        rest_z = across_z * across_z + nodes[1]
        blocks = []
        for distance_x in range(ACROSS):
            gap_x = 2 * (box_x - (box_x ^ distance_x))
            across_x = nodes[0] + gap_x.astype(jnp.float32)
            apart = jnp.maximum(jnp.abs(gap_x), jnp.abs(gap_z)) >= 4
            blocks.append(lax.rsqrt(across_x * across_x + rest_z) * jnp.where(apart, 1.0 / COEFFS, 0.0))
        columns.append(jnp.concatenate(blocks, axis=0))
    columns = low_bits(jnp.concatenate(columns, axis=1))
    coarse = dot(boxes_high, columns) + dot(boxes_low, columns)
    coarse = jnp.concatenate([coarse[:, d * SLOT : (d + 1) * SLOT] for d in range(depth)], axis=0)
    coarse_high, coarse_low = high_low(coarse)
    coarse = dot(coarse_high, spread[...]) + dot(coarse_low, spread[...])

    own_local[...] = same + coarse[:ROWS]
    sums = [coarse[distance * ROWS : (distance + 1) * ROWS] for distance in range(depth)]
    for distance in range(2, depth):
        distant[distance - 2][...] = sums[distance][: distant[0].shape[0]]
    odd = lax.rem(box_z, 2)
    beside = jnp.zeros_like(sums[0])
    for distance in range(3, depth):
        if touching(distance):
            beside = jnp.where(jnp.abs((box_z ^ distance) - box_z) == 1, sums[distance], beside)
    for faces, bit, base in ((faces_even, 1 - odd, sums[1]), (faces_odd, odd, beside)):
        for y in range(2):
            for x in range(4):
                place = lanes((2 * x + y) * pts, pts)
                if x in (0, 3):
                    side = left if x == 0 else right
                    faces[:, place] = side[:, lanes((y + 2 * bit) * pts, pts)]
                else:
                    faces[:, place] = own[:, lanes((x - 1 + 2 * y + 4 * bit) * pts, pts)]
        given_high, given_low = high_low(base + jnp.where(bit == 1, up, down))
        faces[:, lanes(points, LEAVES)] = given_high
        faces[:, lanes(points + LEAVES, LEAVES)] = given_low


def side_kernel(own, left, right, early, source, target, *rest):
    count = (len(rest) - 2) // 2
    near, sides = rest[count], rest[-1]
    for block, passed in zip(rest[:count], rest[count + 1 : -1]):
        passed[...] = block[...]
    points = own.shape[1]
    pts = points // 8

    def group(index, carry):
        pulled(near, index, target, source, own, [2 * p * pts for p in range(4)], 2 * pts)
        return carry

    near[:, lanes(0, 2 * EARLY * pts)] = early[...]
    lax.fori_loop(EARLY, 4, group, 0)
    for step, side in ((0, left), (1, right)):
        for place in range(4):
            centre = (1.5 if step else -1.5, place % 2 - 0.5, place // 2 - 0.5)
            sides[lanes(place * pts, pts), :] = source_features(side, place * pts, pts, centre)

        def layer(index, carry, step=step, side=side):
            pulled(near, step + 2 * index, target, sides, side, [0, 2 * pts], 2 * pts, near)
            return carry

        lax.fori_loop(0, 2, layer, 0)


def rows_kernel(depth, count_in, weights_in, near, target, own_local, faces_even, faces_odd, *rest):
    total, local, scale, column, held, sides, count, weights, sems = rest
    copies = fetch([(count_in, count), (weights_in, weights)], sems)
    points = total.shape[1]
    pts = points // 8
    _, box_z = box_place()
    for step in range(2):
        odd = lax.rem(box_z, 2)
        inside = (box_z + 2 * step - 1 >= 0) & (box_z + 2 * step - 1 < depth)
        for faces, parity in ((faces_even, 1 - step), (faces_odd, step)):

            @pl.when(inside & (odd == parity))
            def _(faces=faces):
                held[...] = faces[:, lanes(0, points)]

        @pl.when(jnp.logical_not(inside))
        def _():
            held[...] = jnp.zeros(held.shape, held.dtype)

        for place in range(8):
            centre = (place // 2 - 1.5, place % 2 - 0.5, 1.5 if step else -1.5)
            sides[lanes(place * pts, pts), :] = source_features(held, place * pts, pts, centre)

        def pair(index, carry, step=step):
            starts = [(2 * x + 2 * index) * pts for x in range(3)]
            pulled(total, index + 2 * step, target, sides, held, starts, 2 * pts, near)
            return carry

        lax.fori_loop(0, 2, pair, 0)

    value = own_local[...]
    for faces in (faces_even, faces_odd):
        value = value + faces[:, lanes(points, LEAVES)].astype(jnp.float32)
        value = value + faces[:, lanes(points + LEAVES, LEAVES)].astype(jnp.float32)
    local[...] = value
    for copy in copies:
        copy.wait()
    column[...] = by_row([weights[field] for field in range(weights.shape[0])], column.shape)
    lane_index = lax.broadcasted_iota(jnp.int32, (1, pts), 1)
    for leaf in range(8):
        scale[:, leaf * pts : (leaf + 1) * pts] = jnp.where(lane_index < count[leaf], 1.0 / (128.0 * pts), 0.0)


def last_kernel(near, basis, scale, column, local, *rest):
    distant, (potential, sums) = rest[:-2], rest[-2:]
    fields, points = potential.shape
    pts = points // 8
    value = local[...]
    for block in distant:
        value = value + block[...]
    local_high, local_low = high_low(value)
    weight = column[0:fields, 0:1]
    for leaf in range(8):
        here = slice(leaf * pts, (leaf + 1) * pts)
        slot = slice(leaf * SLOT, (leaf + 1) * SLOT)
        left = jnp.concatenate([local_high[:, slot], local_high[:, slot]], axis=1)
        far_part = dot(left, basis[:, here]) + dot(local_low[:, slot], basis[0:SLOT, here])
        total = near[0:fields, lanes(leaf_slot(leaf) * pts, pts)] + far_part[:fields]
        total = total * scale[:, here]
        potential[:, here] = total
        sums[:, here] = jnp.sum(total * weight, axis=0, keepdims=True)
    sums[:, points:] = jnp.broadcast_to(jnp.sum(weight), (1, sums.shape[1] - points))


def mean_kernel(mine, other, mean):
    points = mean.shape[1]
    total = mine[...] + other[...]
    mean[...] = total[:, :points] / total[:, points : points + 1]


def swapped(block, axis, partner):
    size = lax.axis_size(axis)
    return lax.ppermute(block, axis, [(partner(i), i) for i in range(size) if 0 <= partner(i) < size])


def across_layers(block, distance):
    pairs = [(i, i ^ (ACROSS * distance)) for i in range(lax.axis_size("space"))]
    return lax.ppermute(block, "space", [pair for pair in pairs if abs(pair[0] - pair[1]) > ACROSS])


def per_device(positions, density, leaf_count, sigma_weights):
    fields, points = density.shape
    pts = points // 8
    depth = lax.axis_size("space") // ACROSS
    vmem, hbm = pl.BlockSpec(memory_space=pltpu.VMEM), pl.BlockSpec(memory_space=pltpu.HBM)

    def call(kernel, name, in_specs, outs, scratch, *args):
        return pl.pallas_call(
            kernel,
            in_specs=in_specs,
            out_specs=[vmem] * len(outs),
            out_shape=[jax.ShapeDtypeStruct(shape, dtype) for shape, dtype in outs],
            scratch_shapes=scratch,
            compiler_params=pltpu.CompilerParams(vmem_limit_bytes=24 * MEGA),
            name=name,
        )(*(pltpu.with_memory_space_constraint(a, pltpu.HBM) if s is hbm else a for s, a in zip(in_specs, args)))

    half, full = jnp.bfloat16, jnp.float32
    shift = shift_table()
    face = 4 * pts + LEAVES + 2 * SLOT
    own, basis, moments, totals, *given = call(
        pack_kernel,
        "pack",
        [hbm] * 4,
        [
            ((ROWS, points), half),
            ((2 * SLOT, points), half),
            ((ROWS, LEAVES), half),
            ((ROWS, 2 * SLOT), half),
            ((ROWS, face), half),
            ((ROWS, 2 * SLOT), half),
            ((ROWS, face), half),
        ],
        [
            pltpu.SMEM((8,), jnp.int32),
            pltpu.VMEM((3, points), full),
            pltpu.VMEM((fields, points), half),
            pltpu.VMEM((LEAVES, SLOT), half),
            pltpu.VMEM((SLOT, 8, pts), full),
            pltpu.SemaphoreType.DMA((4,)),
        ],
        leaf_count,
        positions,
        density,
        jnp.asarray(shift, half),
    )
    from_2 = swapped(given[1], "space", lambda i: i ^ 2)
    from_3 = swapped(given[2], "space", lambda i: i ^ 3)
    from_1 = swapped(given[0], "space", lambda i: i ^ 1)
    near, source, target, far, nodes, spread = call(
        own_kernel,
        "near_own",
        [vmem] + [hbm] * 3,
        [
            ((ROWS, EARLY * points // 4), full),
            ((points, FEATURES), half),
            ((FEATURES, points), half),
            ((len(STEPS) * LEAVES, LEAVES), half),
            ((3, SLOT, SLOT), full),
            ((SLOT, LEAVES), half),
        ],
        [pltpu.SemaphoreType.DMA((3,))],
        own,
        jnp.asarray(far_table(), half),
        jnp.asarray(box_nodes()),
        jnp.asarray(shift.T.copy(), half),
    )
    left, right, own_local, faces_even, faces_odd, *distant = call(
        functools.partial(row_kernel, depth),
        "row",
        [vmem] * 9,
        [((ROWS, 4 * pts + LEAVES), half)] * 2
        + [((ROWS, LEAVES), full)]
        + [((ROWS, points + 2 * LEAVES), half)] * 2
        + [((ROWS, LEAVES), full)] * (depth - 2),
        [],
        own,
        moments,
        totals,
        from_1,
        from_2,
        from_3,
        far,
        nodes,
        spread,
    )
    faces_even = swapped(faces_even, "space", lambda i: i ^ ACROSS)
    faces_odd = swapped(faces_odd, "space", lambda i: i + ACROSS if i // ACROSS % 2 else i - ACROSS)
    near, *distant = call(
        side_kernel,
        "near_side",
        [vmem] * (6 + len(distant)),
        [((ROWS, points), full)] + [((ROWS, LEAVES), full)] * len(distant),
        [pltpu.VMEM((4 * pts, FEATURES), half)],
        own,
        left,
        right,
        near,
        source,
        target,
        *distant,
    )
    distant = [across_layers(block, distance + 2) for distance, block in enumerate(distant)]
    near, local, scale, column = call(
        functools.partial(rows_kernel, depth),
        "near_rows",
        [hbm] * 2 + [vmem] * 5,
        [((ROWS, points), full), ((ROWS, LEAVES), full), ((1, points), full), ((ROWS, 128), full)],
        [
            pltpu.VMEM((ROWS, points), half),
            pltpu.VMEM((8 * pts, FEATURES), half),
            pltpu.SMEM((8,), jnp.int32),
            pltpu.SMEM((fields,), full),
            pltpu.SemaphoreType.DMA((2,)),
        ],
        leaf_count,
        sigma_weights,
        near,
        target,
        own_local,
        faces_even,
        faces_odd,
    )
    potential, sums = call(
        last_kernel,
        "evaluate",
        [vmem] * (5 + len(distant)),
        [((fields, points), full), ((1, points + 128), full)],
        [],
        near,
        basis,
        scale,
        column,
        local,
        *distant,
    )
    if lax.axis_size("sig") == 2:
        other = swapped(sums, "sig", lambda i: i ^ 1)
    else:
        other = lax.psum(sums, "sig") - sums
    mean, = call(mean_kernel, "mean", [vmem] * 2, [((1, points), full)], [], sums, other)
    return potential, mean.reshape(points)


def solution(mesh):
    in_specs = (P(None, "space"), P("sig", "space"), P("space"), P("sig"))
    out_specs = (P("sig", "space"), P("space"))
    return jax.shard_map(per_device, mesh=mesh, in_specs=in_specs, out_specs=out_specs, check_vma=False)
```

```python
import functools
import math

import jax
import jax.numpy as jnp
import numpy as np
from jax import lax
from jax.experimental import pallas as pl
from jax.experimental.pallas import tpu as pltpu
from jax.sharding import PartitionSpec as P

ORDER = 5
SOFTENING = 0.1
ACROSS = 4
SLOT = 64
ROWS = 24
LEAVES = 8 * SLOT
MEGA = 1024 * 1024
FEATURES = 48


def exponent_table(order_max):
    entries_list = []
    for degree in range(order_max + 1):
        for first_power in range(degree, -1, -1):
            for second_power in range(degree - first_power, -1, -1):
                entries_list.append((first_power, second_power, degree - first_power - second_power))
    return entries_list


def node_table(count_nodes, offset_value):
    counter = np.arange(1, count_nodes + 1, dtype=np.float32)[:, None]
    stride_set = np.array([0.7548776662466927, 0.5698402909980532, 0.4142135623730951], dtype=np.float32)[None, :]
    unit_points = np.mod(counter * stride_set + np.float32(offset_value), np.float32(1.0))
    return (np.float32(2.0) * unit_points - np.float32(1.0)).astype(np.float32)


EXPONENTS = exponent_table(ORDER)
COEFFS = len(EXPONENTS)
CHECK = node_table(COEFFS, 0.5).astype(np.float64)
EQUIV = node_table(COEFFS, 0.0).astype(np.float64)
STEPS = [(sx, sz) for sz in (-1, 0, 1) for sx in (-1, 0, 1) if sx != 0 or sz != 0]


def bits(octant):
    return octant % 2, octant // 2 % 2, octant // 4


def leaf_slot(octant):
    bit_x, bit_y, bit_z = bits(octant)
    return (bit_x + 2 * bit_z) * 2 + bit_y


@functools.lru_cache(None)
def far_table():
    shape = (len(STEPS), 8, SLOT, 8, SLOT)
    table = np.zeros(shape)
    gap_nodes = 0.5 * (CHECK[None, :, :] - EQUIV[:, None, :])
    for index, (step_x, step_z) in enumerate(STEPS):
        for source in range(8):
            for target in range(8):
                s, t = bits(source), bits(target)
                gap = np.array([2 * step_x + s[0] - t[0], s[1] - t[1], 2 * step_z + s[2] - t[2]], np.float64)
                if max(abs(gap[0]), abs(gap[2])) >= 2:
                    shifted = gap_nodes - gap
                    value = 1.0 / np.sqrt(np.sum(shifted * shifted, -1) + SOFTENING * SOFTENING) / COEFFS
                    table[index, source, :COEFFS, target, :COEFFS] = value
    return table.reshape(len(STEPS) * LEAVES, LEAVES)


@functools.lru_cache(None)
def shift_table():
    table = np.zeros((8, SLOT, SLOT))
    for leaf in range(8):
        offset = [bit - 0.5 for bit in bits(leaf)]
        for k, target in enumerate(EXPONENTS):
            for i, source in enumerate(EXPONENTS):
                if all(b <= a for a, b in zip(target, source)):
                    value = 1.0
                    for a, b, h in zip(target, source, offset):
                        value *= math.comb(a, b) * 0.5**b * h ** (a - b)
                    table[leaf, i, k] = value
    return table.reshape(8 * SLOT, SLOT)


@functools.lru_cache(None)
def box_nodes():
    gaps = np.zeros((3, SLOT, SLOT))
    gaps[:, :COEFFS, :COEFFS] = np.moveaxis(CHECK[None, :, :] - EQUIV[:, None, :], -1, 0)
    gaps[1] = gaps[1] ** 2 + SOFTENING * SOFTENING
    return gaps.astype(np.float32)


def dot(left, right):
    return jnp.dot(left, right, preferred_element_type=jnp.float32)


def dot_nt(left, right):
    return lax.dot_general(left, right, (((1,), (1,)), ((), ())), preferred_element_type=jnp.float32)


def low_bits(value):
    return value.astype(jnp.bfloat16)


def high_low(value):
    high = low_bits(value)
    return high, low_bits(value - high.astype(jnp.float32))


def by_row(values, shape):
    row = lax.broadcasted_iota(jnp.int32, shape, 0)
    result = jnp.zeros(shape, jnp.float32)
    for index, value in enumerate(values):
        result = jnp.where(row == index, value, result)
    return result


def box_place():
    label = lax.axis_index("space")
    return lax.rem(label, ACROSS), lax.div(label, ACROSS)


def lanes(start, size):
    return pl.ds(start if isinstance(start, int) else pl.multiple_of(start, 128), size)


def fetch(pairs, sems):
    copies = [pltpu.make_async_copy(src, dst, sems.at[i]) for i, (src, dst) in enumerate(pairs)]
    for copy in copies:
        copy.start()
    return copies


def pack_kernel(count_in, positions_in, density_in, own, basis, count, positions, density, mono, sems):
    copies = fetch([(count_in, count), (positions_in, positions), (density_in, density)], sems)
    fields, points = density.shape
    pts = points // 8
    box_x, box_z = box_place()
    for copy in copies:
        copy.wait()
    local = []
    for leaf in range(8):
        bit_x, bit_y, bit_z = bits(leaf)
        centre = by_row(
            [2.0 * box_x.astype(jnp.float32) + (bit_x + 0.5), bit_y + 0.5, 2.0 * box_z.astype(jnp.float32) + (bit_z + 0.5)],
            (3, 1),
        )
        here = slice(leaf * pts, (leaf + 1) * pts)
        offset = positions[:, here] - centre
        local.append(offset)
        high = low_bits(offset).astype(jnp.float32)
        middle = low_bits(offset - high).astype(jnp.float32)
        raw = density[:, here].astype(jnp.float32)
        mass = jnp.where(lax.broadcasted_iota(jnp.int32, raw.shape, 1) < count[leaf], raw, 0.0)
        spare = jnp.zeros((ROWS - fields - 6, pts), jnp.float32)
        own[:, here] = low_bits(jnp.concatenate([mass, high, middle, spare], axis=0))

    axes = [2.0 * jnp.concatenate([part[a : a + 1] for part in local], axis=0) for a in range(3)]
    made = {(0, 0, 0): jnp.ones((8, pts), jnp.float32)}
    for k, powers in enumerate(EXPONENTS):
        if powers not in made:
            a = next(i for i in range(3) if powers[i] > 0)
            before = tuple(p - (i == a) for i, p in enumerate(powers))
            made[powers] = made[before] * axes[a]
        mono[k] = made[powers]
    mono[COEFFS:SLOT] = jnp.zeros((SLOT - COEFFS, 8, pts), jnp.float32)
    parts = []
    for leaf in range(8):
        here = slice(leaf * pts, (leaf + 1) * pts)
        high, low = high_low(mono[:, leaf, :])
        basis[0:SLOT, here] = high
        basis[SLOT:, here] = low
        parts.append(dot_nt(own[:, here], high))
    own[:, points:] = low_bits(jnp.concatenate(parts, axis=1))


def features(held, start, size, centre, target):
    value = held[16:ROWS, lanes(start, size)].astype(jnp.float32)
    x = value[1:4] + value[4:7] + by_row(centre, (3, 1))
    norm = jnp.sum(x * x, axis=0, keepdims=True)
    if target:
        norm = norm + SOFTENING * SOFTENING
    parts, norms = [], []
    for source, out in ((x, parts), (norm, norms)):
        left = source
        for _ in range(3):
            high = low_bits(left).astype(jnp.float32)
            out.append(high)
            left = left - high
    one = jnp.ones_like(norm)
    zero = jnp.zeros_like(norm)
    blank = jnp.zeros((3, norm.shape[1]), jnp.float32)
    blocks = []
    order = (0, 1, 0, 2, 0, 1) if target else (0, 0, 1, 0, 2, 1)
    for index, which in enumerate(order):
        coords = -2.0 * parts[which] if target else parts[which]
        if index < 3:
            pair = [one, norms[index]] if target else [norms[index], one]
        else:
            pair = [zero, zero]
        blocks += [coords, *pair, blank]
    return jnp.concatenate(blocks, axis=0)


def source_features(held, start, size, centre):
    return low_bits(jnp.transpose(features(held, start, size, centre, False)))


def pulled(near, index, target, source, masses, starts, size, first=None):
    width = target.shape[1] // 8
    tiles = [(piece, turn) for piece in range(2) for turn in range(len(starts))]
    places = [lanes((2 * index + piece) * width, width) for piece in range(2)]

    def squares(piece, turn):
        return dot(source[lanes(starts[turn], size), :], target[:, places[piece]])

    ahead = squares(*tiles[0])
    for place, (piece, turn) in enumerate(tiles):
        square = ahead
        if place + 1 < len(tiles):
            ahead = squares(*tiles[place + 1])
        if turn == 0:
            total = jnp.zeros((ROWS, width), jnp.float32) if first is None else first[:, places[piece]]
        total = total + dot(masses[:, lanes(starts[turn], size)], low_bits(lax.rsqrt(square)))
        if turn + 1 == len(starts):
            near[:, places[piece]] = total


def own_kernel(count_in, weights_in, own, *rest):
    tables, (near, source, target, scale, column), rest = rest[:4], rest[4:9], rest[9:]
    copies = fetch([*zip(tables, rest[:4]), (count_in, rest[4]), (weights_in, rest[5])], rest[6])
    count, weights = rest[4:6]
    points = near.shape[1]
    pts = points // 8
    for leaf in range(8):
        centre = [bit - 0.5 for bit in bits(leaf)]
        source[lanes(leaf * pts, pts), :] = source_features(own, leaf * pts, pts, centre)
        target[:, lanes(leaf_slot(leaf) * pts, pts)] = low_bits(features(own, leaf * pts, pts, centre, True))

    def group(index, carry):
        pulled(near, index, target, source, own, [2 * p * pts for p in range(4)], 2 * pts)
        return carry

    lax.fori_loop(0, 4, group, 0)
    for copy in copies:
        copy.wait()
    column[...] = by_row([weights[field] for field in range(weights.shape[0])], column.shape)
    lane_index = lax.broadcasted_iota(jnp.int32, (1, pts), 1)
    for leaf in range(8):
        scale[:, leaf * pts : (leaf + 1) * pts] = jnp.where(lane_index < count[leaf], 1.0 / (128.0 * pts), 0.0)


def box_columns(depth, box_x, box_z, nodes):
    blocks = []
    for box in range(ACROSS * depth):
        gap_x = 2 * (box_x - box % ACROSS)
        gap_z = 2 * (box_z - box // ACROSS)
        across_x = nodes[0] + gap_x.astype(jnp.float32)
        across_z = nodes[2] + gap_z.astype(jnp.float32)
        apart = jnp.maximum(jnp.abs(gap_x), jnp.abs(gap_z)) >= 4
        value = lax.rsqrt(across_x * across_x + across_z * across_z + nodes[1])
        blocks.append(low_bits(value * jnp.where(apart, 1.0 / COEFFS, 0.0)))
    return jnp.concatenate(blocks, axis=0)


def rest_kernel(depth, gathered, early, target, scale, column, basis, far, nodes, spread, shift, *rest):
    potential, sums, left, right, below, above, moments, sides, near, sems = rest
    fields, points = potential.shape
    pts = points // 8
    box_x, box_z = box_place()
    all_moments = pltpu.make_async_copy(gathered.at[:, :, pl.ds(points, LEAVES)], moments, sems.at[0])
    all_moments.start()
    valid, label, faces = {}, {}, {}
    for index, (step_x, step_z) in enumerate(STEPS):
        x, z = box_x + step_x, box_z + step_z
        inside = (x >= 0) & (x < ACROSS) & (z >= 0) & (z < depth)
        step = (step_x, step_z)
        valid[step] = inside
        label[step] = jnp.where(inside, x + ACROSS * z, box_x + ACROSS * box_z)
        pairs = []
        for octant in range(8):
            bit_x, bit_y, bit_z = bits(octant)
            if step_x and bit_x != (step_x < 0) or step_z and bit_z != (step_z < 0):
                continue
            if step_z:
                place = 2 * (1 + bit_x + 2 * step_x) + bit_y
                held = above if step_z > 0 else below
            else:
                place = bit_y + 2 * bit_z
                held = right if step_x > 0 else left
            pairs.append((octant * pts, held.at[:, pl.ds(place * pts, pts)]))
        faces[step] = pairs

    def copies(index, step):
        return [
            pltpu.make_async_copy(gathered.at[label[step], :, pl.ds(start, pts)], place, sems.at[1 + 4 * index + turn])
            for turn, (start, place) in enumerate(faces[step])
        ]

    for index, step in enumerate(STEPS):

        @pl.when(valid[step])
        def _(index=index, step=step):
            for copy in copies(index, step):
                copy.start()

        @pl.when(jnp.logical_not(valid[step]))
        def _(step=step):
            for _, place in faces[step]:
                place[...] = jnp.zeros(place.shape, jnp.bfloat16)

    columns = box_columns(depth, box_x, box_z, nodes)
    for index, step in enumerate(STEPS):

        @pl.when(valid[step])
        def _(index=index, step=step):
            for copy in copies(index, step):
                copy.wait()

    near[...] = early[...]
    for step, side in ((0, left), (1, right)):
        for place in range(4):
            centre = (1.5 if step else -1.5, place % 2 - 0.5, place // 2 - 0.5)
            sides[lanes(place * pts, pts), :] = source_features(side, place * pts, pts, centre)

        def layer(index, carry, step=step, side=side):
            pulled(near, step + 2 * index, target, sides, side, [0, 2 * pts], 2 * pts, near)
            return carry

        lax.fori_loop(0, 2, layer, 0)
    for step, held in ((0, below), (1, above)):
        for place in range(8):
            centre = (place // 2 - 1.5, place % 2 - 0.5, 1.5 if step else -1.5)
            sides[lanes(place * pts, pts), :] = source_features(held, place * pts, pts, centre)

        def pair(index, carry, step=step, held=held):
            starts = [(2 * x + 2 * index) * pts for x in range(3)]
            pulled(near, index + 2 * step, target, sides, held, starts, 2 * pts, near)
            return carry

        lax.fori_loop(0, 2, pair, 0)

    all_moments.wait()
    boxes = ACROSS * depth
    totals = dot(jnp.concatenate([moments[box] for box in range(boxes)], axis=0), shift[...])
    totals = jnp.concatenate([totals[box * ROWS : (box + 1) * ROWS] for box in range(boxes)], axis=1)
    totals_high, totals_low = high_low(totals)
    coarse_high, coarse_low = high_low(dot(totals_high, columns) + dot(totals_low, columns))
    value = dot(coarse_high, spread[...]) + dot(coarse_low, spread[...])
    around = [jnp.where(valid[step], moments[label[step]], jnp.bfloat16(0)) for step in STEPS]
    value = value + dot(jnp.concatenate(around, axis=1), far[...])
    local_high, local_low = high_low(value)
    weight = column[0:fields, 0:1]
    for leaf in range(8):
        here = slice(leaf * pts, (leaf + 1) * pts)
        slot = slice(leaf * SLOT, (leaf + 1) * SLOT)
        doubled = jnp.concatenate([local_high[:, slot], local_high[:, slot]], axis=1)
        far_part = dot(doubled, basis[:, here]) + dot(local_low[:, slot], basis[0:SLOT, here])
        total = near[0:fields, lanes(leaf_slot(leaf) * pts, pts)] + far_part[:fields]
        total = total * scale[:, here]
        potential[:, here] = total
        sums[:, here] = jnp.sum(total * weight, axis=0, keepdims=True)
    sums[:, points:] = jnp.broadcast_to(jnp.sum(weight), (1, sums.shape[1] - points))


def mean_kernel(mine, other, mean):
    points = mean.shape[1]
    total = mine[...] + other[...]
    mean[...] = total[:, :points] / total[:, points : points + 1]


def swapped(block, axis, partner):
    size = lax.axis_size(axis)
    return lax.ppermute(block, axis, [(partner(i), i) for i in range(size) if 0 <= partner(i) < size])


def per_device(positions, density, leaf_count, sigma_weights):
    fields, points = density.shape
    pts = points // 8
    depth = lax.axis_size("space") // ACROSS
    vmem, hbm = pl.BlockSpec(memory_space=pltpu.VMEM), pl.BlockSpec(memory_space=pltpu.HBM)

    def call(kernel, name, in_specs, outs, scratch, *args):
        return pl.pallas_call(
            kernel,
            in_specs=in_specs,
            out_specs=[vmem] * len(outs),
            out_shape=[jax.ShapeDtypeStruct(shape, dtype) for shape, dtype in outs],
            scratch_shapes=scratch,
            compiler_params=pltpu.CompilerParams(vmem_limit_bytes=24 * MEGA),
            name=name,
        )(*(pltpu.with_memory_space_constraint(a, pltpu.HBM) if s is hbm else a for s, a in zip(in_specs, args)))

    half, full = jnp.bfloat16, jnp.float32
    shift = shift_table()
    own, basis = call(
        pack_kernel,
        "pack",
        [hbm] * 3,
        [((ROWS, points + LEAVES), half), ((2 * SLOT, points), half)],
        [
            pltpu.SMEM((8,), jnp.int32),
            pltpu.VMEM((3, points), full),
            pltpu.VMEM((fields, points), half),
            pltpu.VMEM((SLOT, 8, pts), full),
            pltpu.SemaphoreType.DMA((3,)),
        ],
        leaf_count,
        positions,
        density,
    )
    gathered = lax.all_gather(own, "space")
    tables = [
        jnp.asarray(far_table(), half),
        jnp.asarray(box_nodes()),
        jnp.asarray(shift.T.copy(), half),
        jnp.asarray(shift, half),
    ]
    near, source, target, scale, column, *tables = call(
        own_kernel,
        "near_own",
        [hbm] * 2 + [vmem] + [hbm] * 4,
        [
            ((ROWS, points), full),
            ((points, FEATURES), half),
            ((FEATURES, points), half),
            ((1, points), full),
            ((ROWS, 128), full),
            *[(table.shape, table.dtype) for table in tables],
        ],
        [pltpu.SMEM((8,), jnp.int32), pltpu.SMEM((fields,), full), pltpu.SemaphoreType.DMA((6,))],
        leaf_count,
        sigma_weights,
        own,
        *tables,
    )
    potential, sums = call(
        functools.partial(rest_kernel, depth),
        "near_rest",
        [hbm] + [vmem] * 9,
        [((fields, points), full), ((1, points + 128), full)],
        [
            pltpu.VMEM((ROWS, 4 * pts), half),
            pltpu.VMEM((ROWS, 4 * pts), half),
            pltpu.VMEM((ROWS, points), half),
            pltpu.VMEM((ROWS, points), half),
            pltpu.VMEM((ACROSS * depth, ROWS, LEAVES), half),
            pltpu.VMEM((8 * pts, FEATURES), half),
            pltpu.VMEM((ROWS, points), full),
            pltpu.SemaphoreType.DMA((1 + 4 * len(STEPS),)),
        ],
        gathered,
        near,
        target,
        scale,
        column,
        basis,
        *tables,
    )
    if lax.axis_size("sig") == 2:
        other = swapped(sums, "sig", lambda i: i ^ 1)
    else:
        other = lax.psum(sums, "sig") - sums
    mean, = call(mean_kernel, "mean", [vmem] * 2, [((1, points), full)], [], sums, other)
    return potential, mean.reshape(points)


def solution(mesh):
    in_specs = (P(None, "space"), P("sig", "space"), P("space"), P("sig"))
    out_specs = (P("sig", "space"), P("space"))
    return jax.shard_map(per_device, mesh=mesh, in_specs=in_specs, out_specs=out_specs, check_vma=False)
```

```python
import functools
import math

import jax
import jax.numpy as jnp
import numpy as np
from jax import lax
from jax.experimental import pallas as pl
from jax.experimental.pallas import tpu as pltpu
from jax.sharding import PartitionSpec as P

ORDER = 5
SOFTENING = 0.1
ACROSS = 4
SLOT = 64
ROWS = 24
LEAVES = 8 * SLOT
MEGA = 1024 * 1024
FEATURES = 48
EARLY = 2


def exponent_table(order_max):
    entries_list = []
    for degree in range(order_max + 1):
        for first_power in range(degree, -1, -1):
            for second_power in range(degree - first_power, -1, -1):
                entries_list.append((first_power, second_power, degree - first_power - second_power))
    return entries_list


def node_table(count_nodes, offset_value):
    counter = np.arange(1, count_nodes + 1, dtype=np.float32)[:, None]
    stride_set = np.array([0.7548776662466927, 0.5698402909980532, 0.4142135623730951], dtype=np.float32)[None, :]
    unit_points = np.mod(counter * stride_set + np.float32(offset_value), np.float32(1.0))
    return (np.float32(2.0) * unit_points - np.float32(1.0)).astype(np.float32)


EXPONENTS = exponent_table(ORDER)
COEFFS = len(EXPONENTS)
CHECK = node_table(COEFFS, 0.5).astype(np.float64)
EQUIV = node_table(COEFFS, 0.0).astype(np.float64)
STEPS = [(sx, sz) for sz in (-1, 0, 1) for sx in (-1, 0, 1) if sx != 0 or sz != 0]


def bits(octant):
    return octant % 2, octant // 2 % 2, octant // 4


def leaf_slot(octant):
    bit_x, bit_y, bit_z = bits(octant)
    return (bit_x + 2 * bit_z) * 2 + bit_y


@functools.lru_cache(None)
def far_table():
    shape = (len(STEPS), 8, SLOT, 8, SLOT)
    table = np.zeros(shape)
    gap_nodes = 0.5 * (CHECK[None, :, :] - EQUIV[:, None, :])
    for index, (step_x, step_z) in enumerate(STEPS):
        for source in range(8):
            for target in range(8):
                s, t = bits(source), bits(target)
                gap = np.array([2 * step_x + s[0] - t[0], s[1] - t[1], 2 * step_z + s[2] - t[2]], np.float64)
                if max(abs(gap[0]), abs(gap[2])) >= 2:
                    shifted = gap_nodes - gap
                    value = 1.0 / np.sqrt(np.sum(shifted * shifted, -1) + SOFTENING * SOFTENING) / COEFFS
                    table[index, source, :COEFFS, target, :COEFFS] = value
    return table.reshape(len(STEPS) * LEAVES, LEAVES)


@functools.lru_cache(None)
def shift_table():
    table = np.zeros((8, SLOT, SLOT))
    for leaf in range(8):
        offset = [bit - 0.5 for bit in bits(leaf)]
        for k, target in enumerate(EXPONENTS):
            for i, source in enumerate(EXPONENTS):
                if all(b <= a for a, b in zip(target, source)):
                    value = 1.0
                    for a, b, h in zip(target, source, offset):
                        value *= math.comb(a, b) * 0.5**b * h ** (a - b)
                    table[leaf, i, k] = value
    return table.reshape(8 * SLOT, SLOT)


@functools.lru_cache(None)
def box_nodes():
    gaps = np.zeros((3, SLOT, SLOT))
    gaps[:, :COEFFS, :COEFFS] = np.moveaxis(CHECK[None, :, :] - EQUIV[:, None, :], -1, 0)
    gaps[1] = gaps[1] ** 2 + SOFTENING * SOFTENING
    return gaps.astype(np.float32)


def dot(left, right):
    return jnp.dot(left, right, preferred_element_type=jnp.float32)


def dot_nt(left, right):
    return lax.dot_general(left, right, (((1,), (1,)), ((), ())), preferred_element_type=jnp.float32)


def low_bits(value):
    return value.astype(jnp.bfloat16)


def high_low(value):
    high = low_bits(value)
    return high, low_bits(value - high.astype(jnp.float32))


def by_row(values, shape):
    row = lax.broadcasted_iota(jnp.int32, shape, 0)
    result = jnp.zeros(shape, jnp.float32)
    for index, value in enumerate(values):
        result = jnp.where(row == index, value, result)
    return result


def box_place():
    label = lax.axis_index("space")
    return lax.rem(label, ACROSS), lax.div(label, ACROSS)


def lanes(start, size):
    return pl.ds(start if isinstance(start, int) else pl.multiple_of(start, 128), size)


def fetch(pairs, sems):
    copies = [pltpu.make_async_copy(src, dst, sems.at[i]) for i, (src, dst) in enumerate(pairs)]
    for copy in copies:
        copy.start()
    return copies


def pack_kernel(count_in, positions_in, density_in, shift_in, own, basis, moments, totals, *rest):
    payloads, (count, positions, density, shift, mono, sems) = rest[:2], rest[2:]
    copies = fetch(
        [(count_in, count), (positions_in, positions), (density_in, density), (shift_in, shift)], sems
    )
    fields, points = density.shape
    pts = points // 8
    box_x, box_z = box_place()
    for copy in copies:
        copy.wait()
    local = []
    for leaf in range(8):
        bit_x, bit_y, bit_z = bits(leaf)
        centre = by_row(
            [2.0 * box_x.astype(jnp.float32) + (bit_x + 0.5), bit_y + 0.5, 2.0 * box_z.astype(jnp.float32) + (bit_z + 0.5)],
            (3, 1),
        )
        here = slice(leaf * pts, (leaf + 1) * pts)
        offset = positions[:, here] - centre
        local.append(offset)
        high = low_bits(offset).astype(jnp.float32)
        middle = low_bits(offset - high).astype(jnp.float32)
        raw = density[:, here].astype(jnp.float32)
        mass = jnp.where(lax.broadcasted_iota(jnp.int32, raw.shape, 1) < count[leaf], raw, 0.0)
        spare = jnp.zeros((ROWS - fields - 6, pts), jnp.float32)
        own[:, here] = low_bits(jnp.concatenate([mass, high, middle, spare], axis=0))

    axes = [2.0 * jnp.concatenate([part[a : a + 1] for part in local], axis=0) for a in range(3)]
    made = {(0, 0, 0): jnp.ones((8, pts), jnp.float32)}
    for k, powers in enumerate(EXPONENTS):
        if powers not in made:
            a = next(i for i in range(3) if powers[i] > 0)
            before = tuple(p - (i == a) for i, p in enumerate(powers))
            made[powers] = made[before] * axes[a]
        mono[k] = made[powers]
    mono[COEFFS:SLOT] = jnp.zeros((SLOT - COEFFS, 8, pts), jnp.float32)
    parts = []
    for leaf in range(8):
        here = slice(leaf * pts, (leaf + 1) * pts)
        high, low = high_low(mono[:, leaf, :])
        basis[0:SLOT, here] = high
        basis[SLOT:, here] = low
        parts.append(dot_nt(own[:, here], high))
    moment, rest = high_low(jnp.concatenate(parts, axis=1))
    moments[...] = moment
    total = dot(moment, shift[...]) + dot(rest, shift[...])
    totals[...] = jnp.concatenate(high_low(total), axis=1)
    for distance, payload in zip((1, 3), payloads):
        bit = jnp.where((box_x ^ distance) > box_x, 1, 0)
        for place in range(4):
            payload[:, lanes(place * pts, pts)] = own[:, lanes((bit + 2 * place) * pts, pts)]
        payload[:, lanes(4 * pts, LEAVES)] = moment


def features(held, start, size, centre, target):
    value = held[16:ROWS, lanes(start, size)].astype(jnp.float32)
    x = value[1:4] + value[4:7] + by_row(centre, (3, 1))
    norm = jnp.sum(x * x, axis=0, keepdims=True)
    if target:
        norm = norm + SOFTENING * SOFTENING
    parts, norms = [], []
    for source, out in ((x, parts), (norm, norms)):
        left = source
        for _ in range(3):
            high = low_bits(left).astype(jnp.float32)
            out.append(high)
            left = left - high
    one = jnp.ones_like(norm)
    zero = jnp.zeros_like(norm)
    blank = jnp.zeros((3, norm.shape[1]), jnp.float32)
    blocks = []
    order = (0, 1, 0, 2, 0, 1) if target else (0, 0, 1, 0, 2, 1)
    for index, which in enumerate(order):
        coords = -2.0 * parts[which] if target else parts[which]
        if index < 3:
            pair = [one, norms[index]] if target else [norms[index], one]
        else:
            pair = [zero, zero]
        blocks += [coords, *pair, blank]
    return jnp.concatenate(blocks, axis=0)


def source_features(held, start, size, centre):
    return low_bits(jnp.transpose(features(held, start, size, centre, False)))


def pulled(near, index, target, source, masses, starts, size, first=None):
    width = target.shape[1] // 8
    tiles = [(piece, turn) for piece in range(2) for turn in range(len(starts))]
    places = [lanes((2 * index + piece) * width, width) for piece in range(2)]

    def squares(piece, turn):
        return dot(source[lanes(starts[turn], size), :], target[:, places[piece]])

    ahead = squares(*tiles[0])
    for place, (piece, turn) in enumerate(tiles):
        square = ahead
        if place + 1 < len(tiles):
            ahead = squares(*tiles[place + 1])
        if turn == 0:
            total = jnp.zeros((ROWS, width), jnp.float32) if first is None else first[:, places[piece]]
        total = total + dot(masses[:, lanes(starts[turn], size)], low_bits(lax.rsqrt(square)))
        if turn + 1 == len(starts):
            near[:, places[piece]] = total


def own_groups(near, first, last, target, source, own):
    pts = source.shape[0] // 8

    def group(index, carry):
        pulled(near, index, target, source, own, [2 * p * pts for p in range(4)], 2 * pts)
        return carry

    lax.fori_loop(first, last, group, 0)


def box_columns(depth, box_x, box_z, nodes):
    blocks = []
    for box in range(ACROSS * depth):
        gap_x = 2 * (box_x - box % ACROSS)
        gap_z = 2 * (box_z - box // ACROSS)
        across_x = nodes[0] + gap_x.astype(jnp.float32)
        across_z = nodes[2] + gap_z.astype(jnp.float32)
        apart = jnp.maximum(jnp.abs(gap_x), jnp.abs(gap_z)) >= 4
        value = lax.rsqrt(across_x * across_x + across_z * across_z + nodes[1])
        blocks.append(low_bits(value * jnp.where(apart, 1.0 / COEFFS, 0.0)))
    return jnp.concatenate(blocks, axis=0)


def own_kernel(depth, count_in, weights_in, own, *rest):
    tables, outs, rest = rest[:3], rest[3:11], rest[11:]
    near, source, target, scale, column, columns, far, spread = outs
    nodes, count, weights, sems = rest
    copies = fetch([*zip(tables, (far, spread, nodes)), (count_in, count), (weights_in, weights)], sems)
    points = own.shape[1]
    pts = points // 8
    for leaf in range(8):
        centre = [bit - 0.5 for bit in bits(leaf)]
        source[lanes(leaf * pts, pts), :] = source_features(own, leaf * pts, pts, centre)
        target[:, lanes(leaf_slot(leaf) * pts, pts)] = low_bits(features(own, leaf * pts, pts, centre, True))
    own_groups(near, 0, EARLY, target, source, own)
    for copy in copies:
        copy.wait()
    columns[...] = box_columns(depth, *box_place(), nodes)
    column[...] = by_row([weights[field] for field in range(weights.shape[0])], column.shape)
    lane_index = lax.broadcasted_iota(jnp.int32, (1, pts), 1)
    for leaf in range(8):
        scale[:, leaf * pts : (leaf + 1) * pts] = jnp.where(lane_index < count[leaf], 1.0 / (128.0 * pts), 0.0)


def faces_of(faces, bit, given, own, left, right):
    points = own.shape[1]
    pts = points // 8
    for y in range(2):
        for x in range(4):
            place = lanes((2 * x + y) * pts, pts)
            if x in (0, 3):
                side = left if x == 0 else right
                faces[:, place] = side[:, lanes((y + 2 * bit) * pts, pts)]
            else:
                faces[:, place] = own[:, lanes((x - 1 + 2 * y + 4 * bit) * pts, pts)]
    given_high, given_low = high_low(given)
    faces[:, lanes(points, LEAVES)] = given_high
    faces[:, lanes(points + LEAVES, LEAVES)] = given_low


def row_kernel(own, moments, from_1, from_3, far, left, right, same, other, faces_even):
    points = own.shape[1]
    pts = points // 8
    box_x, box_z = box_place()
    for side, step in ((left, -1), (right, 1)):
        side[...] = jnp.zeros(side.shape, side.dtype)
        for distance, held in ((1, from_1), (3, from_3)):

            @pl.when((box_x ^ distance) - box_x == step)
            def _(side=side, held=held):
                side[...] = held[...]

    base = 4 * pts
    row = jnp.concatenate([left[:, lanes(base, LEAVES)], moments[...], right[:, lanes(base, LEAVES)]], axis=1)
    below_rows, same_rows, above_rows = pl.ds(0, 3 * LEAVES), pl.ds(3 * LEAVES, 2 * LEAVES), pl.ds(5 * LEAVES, 3 * LEAVES)
    up = dot(row, far[below_rows, :])
    down = dot(row, far[above_rows, :])
    same[...] = dot(jnp.concatenate([row[:, :LEAVES], row[:, 2 * LEAVES :]], axis=1), far[same_rows, :])
    odd = lax.rem(box_z, 2)
    faces_of(faces_even, 1 - odd, jnp.where(odd == 0, up, down), own, left, right)
    other[...] = jnp.where(odd == 0, down, up)


def middle_kernel(own, left, right, other, early, source, target, near, faces_odd):
    points = own.shape[1]
    _, box_z = box_place()
    faces_of(faces_odd, lax.rem(box_z, 2), other[...], own, left, right)
    near[:, lanes(0, EARLY * points // 4)] = early[...]
    own_groups(near, EARLY, 4, target, source, own)


def side_kernel(left, right, early, target, near, sides):
    pts = early.shape[1] // 8
    for step, side in ((0, left), (1, right)):
        for place in range(4):
            centre = (1.5 if step else -1.5, place % 2 - 0.5, place // 2 - 0.5)
            sides[lanes(place * pts, pts), :] = source_features(side, place * pts, pts, centre)

        def layer(index, carry, step=step, side=side):
            pulled(near, step + 2 * index, target, sides, side, [0, 2 * pts], 2 * pts, early)
            return carry

        lax.fori_loop(0, 2, layer, 0)


def layer_pulls(near, early, step, inside, target, faces, sides):
    points = early.shape[1]
    pts = points // 8

    @pl.when(inside)
    def _():
        for place in range(8):
            height = jnp.where(step == 1, 1.5, -1.5)
            centre = (place // 2 - 1.5, place % 2 - 0.5, height)
            sides[lanes(place * pts, pts), :] = source_features(faces, place * pts, pts, centre)

        def pair(index, carry):
            starts = [(2 * x + 2 * index) * pts for x in range(3)]
            pulled(near, index + 2 * step, target, sides, faces, starts, 2 * pts, early)
            return carry

        lax.fori_loop(0, 2, pair, 0)

    @pl.when(jnp.logical_not(inside))
    def _():
        here = lanes(step * (points // 2), points // 2)
        near[:, here] = early[:, here]


def even_kernel(early, target, faces, near, sides):
    _, box_z = box_place()
    points = early.shape[1]
    step = 1 - lax.rem(box_z, 2)
    other = lanes((1 - step) * (points // 2), points // 2)
    near[:, other] = early[:, other]
    layer_pulls(near, early, step, box_z >= 0, target, faces, sides)


def last_kernel(depth, early, target, faces_even, faces_odd, basis, scale, column, columns, spread, same, boxes, *rest):
    potential, sums, near, sides = rest
    fields, points = potential.shape
    pts = points // 8
    _, box_z = box_place()
    step = lax.rem(box_z, 2)
    other = lanes((1 - step) * (points // 2), points // 2)
    near[:, other] = early[:, other]
    inside = (box_z + 2 * step - 1 >= 0) & (box_z + 2 * step - 1 < depth)
    layer_pulls(near, early, step, inside, target, faces_odd, sides)

    totals_high = jnp.concatenate([boxes[box][:, :SLOT] for box in range(ACROSS * depth)], axis=1)
    totals_low = jnp.concatenate([boxes[box][:, SLOT:] for box in range(ACROSS * depth)], axis=1)
    coarse_high, coarse_low = high_low(dot(totals_high, columns[...]) + dot(totals_low, columns[...]))
    value = same[...] + dot(coarse_high, spread[...]) + dot(coarse_low, spread[...])
    for faces in (faces_even, faces_odd):
        value = value + faces[:, lanes(points, LEAVES)].astype(jnp.float32)
        value = value + faces[:, lanes(points + LEAVES, LEAVES)].astype(jnp.float32)
    local_high, local_low = high_low(value)
    weight = column[0:fields, 0:1]
    for leaf in range(8):
        here = slice(leaf * pts, (leaf + 1) * pts)
        slot = slice(leaf * SLOT, (leaf + 1) * SLOT)
        doubled = jnp.concatenate([local_high[:, slot], local_high[:, slot]], axis=1)
        far_part = dot(doubled, basis[:, here]) + dot(local_low[:, slot], basis[0:SLOT, here])
        total = near[0:fields, lanes(leaf_slot(leaf) * pts, pts)] + far_part[:fields]
        total = total * scale[:, here]
        potential[:, here] = total
        sums[:, here] = jnp.sum(total * weight, axis=0, keepdims=True)
    sums[:, points:] = jnp.broadcast_to(jnp.sum(weight), (1, sums.shape[1] - points))


def mean_kernel(mine, other, mean):
    points = mean.shape[1]
    total = mine[...] + other[...]
    mean[...] = total[:, :points] / total[:, points : points + 1]


def swapped(block, axis, partner):
    size = lax.axis_size(axis)
    return lax.ppermute(block, axis, [(partner(i), i) for i in range(size) if 0 <= partner(i) < size])


def per_device(positions, density, leaf_count, sigma_weights):
    fields, points = density.shape
    pts = points // 8
    depth = lax.axis_size("space") // ACROSS
    vmem, hbm = pl.BlockSpec(memory_space=pltpu.VMEM), pl.BlockSpec(memory_space=pltpu.HBM)

    def call(kernel, name, in_specs, outs, scratch, *args):
        return pl.pallas_call(
            kernel,
            in_specs=in_specs,
            out_specs=[vmem] * len(outs),
            out_shape=[jax.ShapeDtypeStruct(shape, dtype) for shape, dtype in outs],
            scratch_shapes=scratch,
            compiler_params=pltpu.CompilerParams(vmem_limit_bytes=24 * MEGA),
            name=name,
        )(*(pltpu.with_memory_space_constraint(a, pltpu.HBM) if s is hbm else a for s, a in zip(in_specs, args)))

    half, full = jnp.bfloat16, jnp.float32
    shift = shift_table()
    side_shape = ((ROWS, 4 * pts + LEAVES), half)
    faces_shape = ((ROWS, points + 2 * LEAVES), half)
    near_shape, sums_shape = ((ROWS, points), full), ((ROWS, LEAVES), full)
    rows_scratch = pltpu.VMEM((8 * pts, FEATURES), half)
    own, basis, moments, totals, *given = call(
        pack_kernel,
        "pack",
        [hbm] * 4,
        [
            ((ROWS, points), half),
            ((2 * SLOT, points), half),
            ((ROWS, LEAVES), half),
            ((ROWS, 2 * SLOT), half),
            side_shape,
            side_shape,
        ],
        [
            pltpu.SMEM((8,), jnp.int32),
            pltpu.VMEM((3, points), full),
            pltpu.VMEM((fields, points), half),
            pltpu.VMEM((LEAVES, SLOT), half),
            pltpu.VMEM((SLOT, 8, pts), full),
            pltpu.SemaphoreType.DMA((4,)),
        ],
        leaf_count,
        positions,
        density,
        jnp.asarray(shift, half),
    )
    boxes = lax.all_gather(totals, "space")
    from_1 = swapped(given[0], "space", lambda i: i ^ 1)
    from_3 = swapped(given[1], "space", lambda i: i ^ 3)
    near, source, target, scale, column, columns, far, spread = call(
        functools.partial(own_kernel, depth),
        "near_own",
        [hbm] * 2 + [vmem] + [hbm] * 3,
        [
            ((ROWS, EARLY * points // 4), full),
            ((points, FEATURES), half),
            ((FEATURES, points), half),
            ((1, points), full),
            ((ROWS, 128), full),
            ((ACROSS * depth * SLOT, SLOT), half),
            ((len(STEPS) * LEAVES, LEAVES), half),
            ((SLOT, LEAVES), half),
        ],
        [
            pltpu.VMEM((3, SLOT, SLOT), full),
            pltpu.SMEM((8,), jnp.int32),
            pltpu.SMEM((fields,), full),
            pltpu.SemaphoreType.DMA((5,)),
        ],
        leaf_count,
        sigma_weights,
        own,
        jnp.asarray(far_table(), half),
        jnp.asarray(shift.T.copy(), half),
        jnp.asarray(box_nodes()),
    )
    left, right, same, other, faces_even = call(
        row_kernel,
        "row",
        [vmem] * 5,
        [side_shape, side_shape, sums_shape, sums_shape, faces_shape],
        [],
        own,
        moments,
        from_1,
        from_3,
        far,
    )
    faces_even = swapped(faces_even, "space", lambda i: i ^ ACROSS)
    near, faces_odd = call(
        middle_kernel,
        "near_middle",
        [vmem] * 7,
        [near_shape, faces_shape],
        [],
        own,
        left,
        right,
        other,
        near,
        source,
        target,
    )
    faces_odd = swapped(faces_odd, "space", lambda i: i + ACROSS if i // ACROSS % 2 else i - ACROSS)
    near, = call(
        side_kernel,
        "near_side",
        [vmem] * 4,
        [near_shape],
        [pltpu.VMEM((4 * pts, FEATURES), half)],
        left,
        right,
        near,
        target,
    )
    near, = call(even_kernel, "near_even", [vmem] * 3, [near_shape], [rows_scratch], near, target, faces_even)
    potential, sums = call(
        functools.partial(last_kernel, depth),
        "near_odd",
        [vmem] * 11,
        [((fields, points), full), ((1, points + 128), full)],
        [pltpu.VMEM((ROWS, points), full), rows_scratch],
        near,
        target,
        faces_even,
        faces_odd,
        basis,
        scale,
        column,
        columns,
        spread,
        same,
        boxes,
    )
    if lax.axis_size("sig") == 2:
        other = swapped(sums, "sig", lambda i: i ^ 1)
    else:
        other = lax.psum(sums, "sig") - sums
    mean, = call(mean_kernel, "mean", [vmem] * 2, [((1, points), full)], [], sums, other)
    return potential, mean.reshape(points)


def solution(mesh):
    in_specs = (P(None, "space"), P("sig", "space"), P("space"), P("sig"))
    out_specs = (P("sig", "space"), P("space"))
    return jax.shard_map(per_device, mesh=mesh, in_specs=in_specs, out_specs=out_specs, check_vma=False)
```

```python
import functools
import math

import jax
import jax.numpy as jnp
import numpy as np
from jax import lax
from jax.experimental import pallas as pl
from jax.experimental.pallas import tpu as pltpu
from jax.sharding import PartitionSpec as P

ORDER = 5
SOFTENING = 0.1
ACROSS = 4
SLOT = 64
ROWS = 24
LEAVES = 8 * SLOT
MEGA = 1024 * 1024
FEATURES = 48
EARLY = 2


def exponent_table(order_max):
    entries_list = []
    for degree in range(order_max + 1):
        for first_power in range(degree, -1, -1):
            for second_power in range(degree - first_power, -1, -1):
                entries_list.append((first_power, second_power, degree - first_power - second_power))
    return entries_list


def node_table(count_nodes, offset_value):
    counter = np.arange(1, count_nodes + 1, dtype=np.float32)[:, None]
    stride_set = np.array([0.7548776662466927, 0.5698402909980532, 0.4142135623730951], dtype=np.float32)[None, :]
    unit_points = np.mod(counter * stride_set + np.float32(offset_value), np.float32(1.0))
    return (np.float32(2.0) * unit_points - np.float32(1.0)).astype(np.float32)


EXPONENTS = exponent_table(ORDER)
COEFFS = len(EXPONENTS)
CHECK = node_table(COEFFS, 0.5).astype(np.float64)
EQUIV = node_table(COEFFS, 0.0).astype(np.float64)
STEPS = [(sx, sz) for sz in (-1, 0, 1) for sx in (-1, 0, 1) if sx != 0 or sz != 0]


def bits(octant):
    return octant % 2, octant // 2 % 2, octant // 4


def leaf_slot(octant):
    bit_x, bit_y, bit_z = bits(octant)
    return (bit_x + 2 * bit_z) * 2 + bit_y


@functools.lru_cache(None)
def far_table():
    shape = (len(STEPS), 8, SLOT, 8, SLOT)
    table = np.zeros(shape)
    gap_nodes = 0.5 * (CHECK[None, :, :] - EQUIV[:, None, :])
    for index, (step_x, step_z) in enumerate(STEPS):
        for source in range(8):
            for target in range(8):
                s, t = bits(source), bits(target)
                gap = np.array([2 * step_x + s[0] - t[0], s[1] - t[1], 2 * step_z + s[2] - t[2]], np.float64)
                if max(abs(gap[0]), abs(gap[2])) >= 2:
                    shifted = gap_nodes - gap
                    value = 1.0 / np.sqrt(np.sum(shifted * shifted, -1) + SOFTENING * SOFTENING) / COEFFS
                    table[index, source, :COEFFS, target, :COEFFS] = value
    return table.reshape(len(STEPS) * LEAVES, LEAVES)


@functools.lru_cache(None)
def shift_table():
    table = np.zeros((8, SLOT, SLOT))
    for leaf in range(8):
        offset = [bit - 0.5 for bit in bits(leaf)]
        for k, target in enumerate(EXPONENTS):
            for i, source in enumerate(EXPONENTS):
                if all(b <= a for a, b in zip(target, source)):
                    value = 1.0
                    for a, b, h in zip(target, source, offset):
                        value *= math.comb(a, b) * 0.5**b * h ** (a - b)
                    table[leaf, i, k] = value
    return table.reshape(8 * SLOT, SLOT)


@functools.lru_cache(None)
def box_nodes():
    gaps = np.zeros((3, SLOT, SLOT))
    gaps[:, :COEFFS, :COEFFS] = np.moveaxis(CHECK[None, :, :] - EQUIV[:, None, :], -1, 0)
    gaps[1] = gaps[1] ** 2 + SOFTENING * SOFTENING
    return gaps.astype(np.float32)


def dot(left, right):
    return jnp.dot(left, right, preferred_element_type=jnp.float32)


def dot_nt(left, right):
    return lax.dot_general(left, right, (((1,), (1,)), ((), ())), preferred_element_type=jnp.float32)


def low_bits(value):
    return value.astype(jnp.bfloat16)


def high_low(value):
    high = low_bits(value)
    return high, low_bits(value - high.astype(jnp.float32))


def by_row(values, shape):
    row = lax.broadcasted_iota(jnp.int32, shape, 0)
    result = jnp.zeros(shape, jnp.float32)
    for index, value in enumerate(values):
        result = jnp.where(row == index, value, result)
    return result


def box_place():
    label = lax.axis_index("space")
    return lax.rem(label, ACROSS), lax.div(label, ACROSS)


def lanes(start, size):
    return pl.ds(start if isinstance(start, int) else pl.multiple_of(start, 128), size)


def fetch(pairs, sems):
    copies = [pltpu.make_async_copy(src, dst, sems.at[i]) for i, (src, dst) in enumerate(pairs)]
    for copy in copies:
        copy.start()
    return copies


def pack_kernel(count_in, positions_in, density_in, shift_in, own, basis, moments, totals, *rest):
    payloads, (count, positions, density, shift, mono, sems) = rest[:2], rest[2:]
    copies = fetch(
        [(count_in, count), (positions_in, positions), (density_in, density), (shift_in, shift)], sems
    )
    fields, points = density.shape
    pts = points // 8
    box_x, box_z = box_place()
    for copy in copies:
        copy.wait()
    local = []
    for leaf in range(8):
        bit_x, bit_y, bit_z = bits(leaf)
        centre = by_row(
            [2.0 * box_x.astype(jnp.float32) + (bit_x + 0.5), bit_y + 0.5, 2.0 * box_z.astype(jnp.float32) + (bit_z + 0.5)],
            (3, 1),
        )
        here = slice(leaf * pts, (leaf + 1) * pts)
        offset = positions[:, here] - centre
        local.append(offset)
        high = low_bits(offset).astype(jnp.float32)
        middle = low_bits(offset - high).astype(jnp.float32)
        raw = density[:, here].astype(jnp.float32)
        mass = jnp.where(lax.broadcasted_iota(jnp.int32, raw.shape, 1) < count[leaf], raw, 0.0)
        spare = jnp.zeros((ROWS - fields - 6, pts), jnp.float32)
        own[:, here] = low_bits(jnp.concatenate([mass, high, middle, spare], axis=0))

    axes = [2.0 * jnp.concatenate([part[a : a + 1] for part in local], axis=0) for a in range(3)]
    made = {(0, 0, 0): jnp.ones((8, pts), jnp.float32)}
    for k, powers in enumerate(EXPONENTS):
        if powers not in made:
            a = next(i for i in range(3) if powers[i] > 0)
            before = tuple(p - (i == a) for i, p in enumerate(powers))
            made[powers] = made[before] * axes[a]
        mono[k] = made[powers]
    mono[COEFFS:SLOT] = jnp.zeros((SLOT - COEFFS, 8, pts), jnp.float32)
    parts = []
    for leaf in range(8):
        here = slice(leaf * pts, (leaf + 1) * pts)
        high, low = high_low(mono[:, leaf, :])
        basis[0:SLOT, here] = high
        basis[SLOT:, here] = low
        parts.append(dot_nt(own[:, here], high))
    moment, rest = high_low(jnp.concatenate(parts, axis=1))
    moments[...] = moment
    total = dot(moment, shift[...]) + dot(rest, shift[...])
    totals[...] = jnp.broadcast_to(jnp.concatenate(high_low(total), axis=1)[None], totals.shape)
    for distance, payload in zip((1, 3), payloads):
        bit = jnp.where((box_x ^ distance) > box_x, 1, 0)
        for place in range(4):
            payload[:, lanes(place * pts, pts)] = own[:, lanes((bit + 2 * place) * pts, pts)]
        payload[:, lanes(4 * pts, LEAVES)] = moment


def features(held, start, size, centre, target):
    value = held[16:ROWS, lanes(start, size)].astype(jnp.float32)
    x = value[1:4] + value[4:7] + by_row(centre, (3, 1))
    norm = jnp.sum(x * x, axis=0, keepdims=True)
    if target:
        norm = norm + SOFTENING * SOFTENING
    parts, norms = [], []
    for source, out in ((x, parts), (norm, norms)):
        left = source
        for _ in range(3):
            high = low_bits(left).astype(jnp.float32)
            out.append(high)
            left = left - high
    one = jnp.ones_like(norm)
    zero = jnp.zeros_like(norm)
    blank = jnp.zeros((3, norm.shape[1]), jnp.float32)
    blocks = []
    order = (0, 1, 0, 2, 0, 1) if target else (0, 0, 1, 0, 2, 1)
    for index, which in enumerate(order):
        coords = -2.0 * parts[which] if target else parts[which]
        if index < 3:
            pair = [one, norms[index]] if target else [norms[index], one]
        else:
            pair = [zero, zero]
        blocks += [coords, *pair, blank]
    return jnp.concatenate(blocks, axis=0)


def source_features(held, start, size, centre):
    return low_bits(jnp.transpose(features(held, start, size, centre, False)))


def pulled(near, index, target, source, masses, starts, size, first=None):
    width = target.shape[1] // 8
    tiles = [(piece, turn) for piece in range(2) for turn in range(len(starts))]
    places = [lanes((2 * index + piece) * width, width) for piece in range(2)]

    def squares(piece, turn):
        return dot(source[lanes(starts[turn], size), :], target[:, places[piece]])

    ahead = squares(*tiles[0])
    for place, (piece, turn) in enumerate(tiles):
        square = ahead
        if place + 1 < len(tiles):
            ahead = squares(*tiles[place + 1])
        if turn == 0:
            total = jnp.zeros((ROWS, width), jnp.float32) if first is None else first[:, places[piece]]
        total = total + dot(masses[:, lanes(starts[turn], size)], low_bits(lax.rsqrt(square)))
        if turn + 1 == len(starts):
            near[:, places[piece]] = total


def own_groups(near, first, last, target, source, own):
    pts = source.shape[0] // 8

    def group(index, carry):
        pulled(near, index, target, source, own, [2 * p * pts for p in range(4)], 2 * pts)
        return carry

    lax.fori_loop(first, last, group, 0)


def box_columns(depth, box_x, box_z, nodes):
    blocks = []
    for box in range(ACROSS * depth):
        gap_x = 2 * (box_x - box % ACROSS)
        gap_z = 2 * (box_z - box // ACROSS)
        across_x = nodes[0] + gap_x.astype(jnp.float32)
        across_z = nodes[2] + gap_z.astype(jnp.float32)
        apart = jnp.maximum(jnp.abs(gap_x), jnp.abs(gap_z)) >= 4
        value = lax.rsqrt(across_x * across_x + across_z * across_z + nodes[1])
        blocks.append(low_bits(value * jnp.where(apart, 1.0 / COEFFS, 0.0)))
    return jnp.concatenate(blocks, axis=0)


def own_kernel(depth, count_in, weights_in, own, *rest):
    tables, outs, rest = rest[:3], rest[3:11], rest[11:]
    near, source, target, scale, column, columns, far, spread = outs
    nodes, count, weights, sems = rest
    copies = fetch([*zip(tables, (far, spread, nodes)), (count_in, count), (weights_in, weights)], sems)
    points = own.shape[1]
    pts = points // 8
    for leaf in range(8):
        centre = [bit - 0.5 for bit in bits(leaf)]
        source[lanes(leaf * pts, pts), :] = source_features(own, leaf * pts, pts, centre)
        target[:, lanes(leaf_slot(leaf) * pts, pts)] = low_bits(features(own, leaf * pts, pts, centre, True))
    own_groups(near, 0, EARLY, target, source, own)
    for copy in copies:
        copy.wait()
    columns[...] = box_columns(depth, *box_place(), nodes)
    column[...] = by_row([weights[field] for field in range(weights.shape[0])], column.shape)
    lane_index = lax.broadcasted_iota(jnp.int32, (1, pts), 1)
    for leaf in range(8):
        scale[:, leaf * pts : (leaf + 1) * pts] = jnp.where(lane_index < count[leaf], 1.0 / (128.0 * pts), 0.0)


def faces_of(faces, bit, given, own, left, right):
    points = own.shape[1]
    pts = points // 8
    for y in range(2):
        for x in range(4):
            place = lanes((2 * x + y) * pts, pts)
            if x in (0, 3):
                side = left if x == 0 else right
                faces[:, place] = side[:, lanes((y + 2 * bit) * pts, pts)]
            else:
                faces[:, place] = own[:, lanes((x - 1 + 2 * y + 4 * bit) * pts, pts)]
    given_high, given_low = high_low(given)
    faces[:, lanes(points, LEAVES)] = given_high
    faces[:, lanes(points + LEAVES, LEAVES)] = given_low


def row_kernel(own, moments, from_1, from_3, far, left, right, same, other, faces_even):
    points = own.shape[1]
    pts = points // 8
    box_x, box_z = box_place()
    for side, step in ((left, -1), (right, 1)):
        side[...] = jnp.zeros(side.shape, side.dtype)
        for distance, held in ((1, from_1), (3, from_3)):

            @pl.when((box_x ^ distance) - box_x == step)
            def _(side=side, held=held):
                side[...] = held[...]

    base = 4 * pts
    row = jnp.concatenate([left[:, lanes(base, LEAVES)], moments[...], right[:, lanes(base, LEAVES)]], axis=1)
    below_rows, same_rows, above_rows = pl.ds(0, 3 * LEAVES), pl.ds(3 * LEAVES, 2 * LEAVES), pl.ds(5 * LEAVES, 3 * LEAVES)
    up = dot(row, far[below_rows, :])
    down = dot(row, far[above_rows, :])
    same[...] = dot(jnp.concatenate([row[:, :LEAVES], row[:, 2 * LEAVES :]], axis=1), far[same_rows, :])
    odd = lax.rem(box_z, 2)
    faces_of(faces_even, 1 - odd, jnp.where(odd == 0, up, down), own, left, right)
    other[...] = jnp.where(odd == 0, down, up)


def middle_kernel(own, left, right, other, early, source, target, near, faces_odd):
    points = own.shape[1]
    _, box_z = box_place()
    faces_of(faces_odd, lax.rem(box_z, 2), other[...], own, left, right)
    near[:, lanes(0, EARLY * points // 4)] = early[...]
    own_groups(near, EARLY, 4, target, source, own)


def side_kernel(left, right, early, target, near, sides):
    pts = early.shape[1] // 8
    for step, side in ((0, left), (1, right)):
        for place in range(4):
            centre = (1.5 if step else -1.5, place % 2 - 0.5, place // 2 - 0.5)
            sides[lanes(place * pts, pts), :] = source_features(side, place * pts, pts, centre)

        def layer(index, carry, step=step, side=side):
            pulled(near, step + 2 * index, target, sides, side, [0, 2 * pts], 2 * pts, early)
            return carry

        lax.fori_loop(0, 2, layer, 0)


def layer_pulls(near, early, step, inside, target, faces, sides):
    points = early.shape[1]
    pts = points // 8

    @pl.when(inside)
    def _():
        for place in range(8):
            height = jnp.where(step == 1, 1.5, -1.5)
            centre = (place // 2 - 1.5, place % 2 - 0.5, height)
            sides[lanes(place * pts, pts), :] = source_features(faces, place * pts, pts, centre)

        def pair(index, carry):
            starts = [(2 * x + 2 * index) * pts for x in range(3)]
            pulled(near, index + 2 * step, target, sides, faces, starts, 2 * pts, early)
            return carry

        lax.fori_loop(0, 2, pair, 0)

    @pl.when(jnp.logical_not(inside))
    def _():
        here = lanes(step * (points // 2), points // 2)
        near[:, here] = early[:, here]


def even_kernel(early, target, faces, near, sides):
    _, box_z = box_place()
    points = early.shape[1]
    step = 1 - lax.rem(box_z, 2)
    other = lanes((1 - step) * (points // 2), points // 2)
    near[:, other] = early[:, other]
    layer_pulls(near, early, step, box_z >= 0, target, faces, sides)


def last_kernel(depth, early, target, faces_even, faces_odd, basis, scale, column, columns, spread, same, boxes, *rest):
    potential, sums, near, sides = rest
    fields, points = potential.shape
    pts = points // 8
    _, box_z = box_place()
    step = lax.rem(box_z, 2)
    other = lanes((1 - step) * (points // 2), points // 2)
    near[:, other] = early[:, other]
    inside = (box_z + 2 * step - 1 >= 0) & (box_z + 2 * step - 1 < depth)
    layer_pulls(near, early, step, inside, target, faces_odd, sides)

    totals_high = jnp.concatenate([boxes[box][:, :SLOT] for box in range(ACROSS * depth)], axis=1)
    totals_low = jnp.concatenate([boxes[box][:, SLOT:] for box in range(ACROSS * depth)], axis=1)
    coarse_high, coarse_low = high_low(dot(totals_high, columns[...]) + dot(totals_low, columns[...]))
    value = same[...] + dot(coarse_high, spread[...]) + dot(coarse_low, spread[...])
    for faces in (faces_even, faces_odd):
        value = value + faces[:, lanes(points, LEAVES)].astype(jnp.float32)
        value = value + faces[:, lanes(points + LEAVES, LEAVES)].astype(jnp.float32)
    local_high, local_low = high_low(value)
    weight = column[0:fields, 0:1]
    for leaf in range(8):
        here = slice(leaf * pts, (leaf + 1) * pts)
        slot = slice(leaf * SLOT, (leaf + 1) * SLOT)
        doubled = jnp.concatenate([local_high[:, slot], local_high[:, slot]], axis=1)
        far_part = dot(doubled, basis[:, here]) + dot(local_low[:, slot], basis[0:SLOT, here])
        total = near[0:fields, lanes(leaf_slot(leaf) * pts, pts)] + far_part[:fields]
        total = total * scale[:, here]
        potential[:, here] = total
        sums[:, here] = jnp.sum(total * weight, axis=0, keepdims=True)
    sums[:, points:] = jnp.broadcast_to(jnp.sum(weight), (1, sums.shape[1] - points))


def mean_kernel(mine, other, mean):
    points = mean.shape[1]
    total = mine[...] + other[...]
    mean[...] = total[:, :points] / total[:, points : points + 1]


def swapped(block, axis, partner):
    size = lax.axis_size(axis)
    return lax.ppermute(block, axis, [(partner(i), i) for i in range(size) if 0 <= partner(i) < size])


def per_device(positions, density, leaf_count, sigma_weights):
    fields, points = density.shape
    pts = points // 8
    depth = lax.axis_size("space") // ACROSS
    vmem, hbm = pl.BlockSpec(memory_space=pltpu.VMEM), pl.BlockSpec(memory_space=pltpu.HBM)

    def call(kernel, name, in_specs, outs, scratch, *args):
        return pl.pallas_call(
            kernel,
            in_specs=in_specs,
            out_specs=[vmem] * len(outs),
            out_shape=[jax.ShapeDtypeStruct(shape, dtype) for shape, dtype in outs],
            scratch_shapes=scratch,
            compiler_params=pltpu.CompilerParams(vmem_limit_bytes=24 * MEGA),
            name=name,
        )(*(pltpu.with_memory_space_constraint(a, pltpu.HBM) if s is hbm else a for s, a in zip(in_specs, args)))

    half, full = jnp.bfloat16, jnp.float32
    shift = shift_table()
    side_shape = ((ROWS, 4 * pts + LEAVES), half)
    faces_shape = ((ROWS, points + 2 * LEAVES), half)
    near_shape, sums_shape = ((ROWS, points), full), ((ROWS, LEAVES), full)
    rows_scratch = pltpu.VMEM((8 * pts, FEATURES), half)
    own, basis, moments, totals, *given = call(
        pack_kernel,
        "pack",
        [hbm] * 4,
        [
            ((ROWS, points), half),
            ((2 * SLOT, points), half),
            ((ROWS, LEAVES), half),
            ((ACROSS * depth, ROWS, 2 * SLOT), half),
            side_shape,
            side_shape,
        ],
        [
            pltpu.SMEM((8,), jnp.int32),
            pltpu.VMEM((3, points), full),
            pltpu.VMEM((fields, points), half),
            pltpu.VMEM((LEAVES, SLOT), half),
            pltpu.VMEM((SLOT, 8, pts), full),
            pltpu.SemaphoreType.DMA((4,)),
        ],
        leaf_count,
        positions,
        density,
        jnp.asarray(shift, half),
    )
    boxes = lax.all_to_all(totals, "space", 0, 0, tiled=True)
    from_1 = swapped(given[0], "space", lambda i: i ^ 1)
    from_3 = swapped(given[1], "space", lambda i: i ^ 3)
    near, source, target, scale, column, columns, far, spread = call(
        functools.partial(own_kernel, depth),
        "near_own",
        [hbm] * 2 + [vmem] + [hbm] * 3,
        [
            ((ROWS, EARLY * points // 4), full),
            ((points, FEATURES), half),
            ((FEATURES, points), half),
            ((1, points), full),
            ((ROWS, 128), full),
            ((ACROSS * depth * SLOT, SLOT), half),
            ((len(STEPS) * LEAVES, LEAVES), half),
            ((SLOT, LEAVES), half),
        ],
        [
            pltpu.VMEM((3, SLOT, SLOT), full),
            pltpu.SMEM((8,), jnp.int32),
            pltpu.SMEM((fields,), full),
            pltpu.SemaphoreType.DMA((5,)),
        ],
        leaf_count,
        sigma_weights,
        own,
        jnp.asarray(far_table(), half),
        jnp.asarray(shift.T.copy(), half),
        jnp.asarray(box_nodes()),
    )
    left, right, same, other, faces_even = call(
        row_kernel,
        "row",
        [vmem] * 5,
        [side_shape, side_shape, sums_shape, sums_shape, faces_shape],
        [],
        own,
        moments,
        from_1,
        from_3,
        far,
    )
    faces_even = swapped(faces_even, "space", lambda i: i ^ ACROSS)
    near, faces_odd = call(
        middle_kernel,
        "near_middle",
        [vmem] * 7,
        [near_shape, faces_shape],
        [],
        own,
        left,
        right,
        other,
        near,
        source,
        target,
    )
    faces_odd = swapped(faces_odd, "space", lambda i: i + ACROSS if i // ACROSS % 2 else i - ACROSS)
    near, = call(
        side_kernel,
        "near_side",
        [vmem] * 4,
        [near_shape],
        [pltpu.VMEM((4 * pts, FEATURES), half)],
        left,
        right,
        near,
        target,
    )
    near, = call(even_kernel, "near_even", [vmem] * 3, [near_shape], [rows_scratch], near, target, faces_even)
    potential, sums = call(
        functools.partial(last_kernel, depth),
        "near_odd",
        [vmem] * 11,
        [((fields, points), full), ((1, points + 128), full)],
        [pltpu.VMEM((ROWS, points), full), rows_scratch],
        near,
        target,
        faces_even,
        faces_odd,
        basis,
        scale,
        column,
        columns,
        spread,
        same,
        boxes,
    )
    if lax.axis_size("sig") == 2:
        other = swapped(sums, "sig", lambda i: i ^ 1)
    else:
        other = lax.psum(sums, "sig") - sums
    mean, = call(mean_kernel, "mean", [vmem] * 2, [((1, points), full)], [], sums, other)
    return potential, mean.reshape(points)


def solution(mesh):
    in_specs = (P(None, "space"), P("sig", "space"), P("space"), P("sig"))
    out_specs = (P("sig", "space"), P("space"))
    return jax.shard_map(per_device, mesh=mesh, in_specs=in_specs, out_specs=out_specs, check_vma=False)
```

```python
import functools
import math

import jax
import jax.numpy as jnp
import numpy as np
from jax import lax
from jax.experimental import pallas as pl
from jax.experimental.pallas import tpu as pltpu
from jax.sharding import PartitionSpec as P

ORDER = 5
SOFTENING = 0.1
ACROSS = 4
SLOT = 64
ROWS = 24
LEAVES = 8 * SLOT
MEGA = 1024 * 1024
FEATURES = 48
EARLY = 2


def exponent_table(order_max):
    entries_list = []
    for degree in range(order_max + 1):
        for first_power in range(degree, -1, -1):
            for second_power in range(degree - first_power, -1, -1):
                entries_list.append((first_power, second_power, degree - first_power - second_power))
    return entries_list


def node_table(count_nodes, offset_value):
    counter = np.arange(1, count_nodes + 1, dtype=np.float32)[:, None]
    stride_set = np.array([0.7548776662466927, 0.5698402909980532, 0.4142135623730951], dtype=np.float32)[None, :]
    unit_points = np.mod(counter * stride_set + np.float32(offset_value), np.float32(1.0))
    return (np.float32(2.0) * unit_points - np.float32(1.0)).astype(np.float32)


EXPONENTS = exponent_table(ORDER)
COEFFS = len(EXPONENTS)
CHECK = node_table(COEFFS, 0.5).astype(np.float64)
EQUIV = node_table(COEFFS, 0.0).astype(np.float64)
STEPS = [(sx, sz) for sz in (-1, 0, 1) for sx in (-1, 0, 1) if sx != 0 or sz != 0]


def bits(octant):
    return octant % 2, octant // 2 % 2, octant // 4


def leaf_slot(octant):
    bit_x, bit_y, bit_z = bits(octant)
    return (bit_x + 2 * bit_z) * 2 + bit_y


@functools.lru_cache(None)
def far_table():
    shape = (len(STEPS), 8, SLOT, 8, SLOT)
    table = np.zeros(shape)
    gap_nodes = 0.5 * (CHECK[None, :, :] - EQUIV[:, None, :])
    for index, (step_x, step_z) in enumerate(STEPS):
        for source in range(8):
            for target in range(8):
                s, t = bits(source), bits(target)
                gap = np.array([2 * step_x + s[0] - t[0], s[1] - t[1], 2 * step_z + s[2] - t[2]], np.float64)
                if max(abs(gap[0]), abs(gap[2])) >= 2:
                    shifted = gap_nodes - gap
                    value = 1.0 / np.sqrt(np.sum(shifted * shifted, -1) + SOFTENING * SOFTENING) / COEFFS
                    table[index, source, :COEFFS, target, :COEFFS] = value
    return table.reshape(len(STEPS) * LEAVES, LEAVES)


@functools.lru_cache(None)
def shift_table():
    table = np.zeros((8, SLOT, SLOT))
    for leaf in range(8):
        offset = [bit - 0.5 for bit in bits(leaf)]
        for k, target in enumerate(EXPONENTS):
            for i, source in enumerate(EXPONENTS):
                if all(b <= a for a, b in zip(target, source)):
                    value = 1.0
                    for a, b, h in zip(target, source, offset):
                        value *= math.comb(a, b) * 0.5**b * h ** (a - b)
                    table[leaf, i, k] = value
    return table.reshape(8 * SLOT, SLOT)


@functools.lru_cache(None)
def box_nodes():
    gaps = np.zeros((3, SLOT, SLOT))
    gaps[:, :COEFFS, :COEFFS] = np.moveaxis(CHECK[None, :, :] - EQUIV[:, None, :], -1, 0)
    gaps[1] = gaps[1] ** 2 + SOFTENING * SOFTENING
    return gaps.astype(np.float32)


def dot(left, right):
    return jnp.dot(left, right, preferred_element_type=jnp.float32)


def dot_nt(left, right):
    return lax.dot_general(left, right, (((1,), (1,)), ((), ())), preferred_element_type=jnp.float32)


def low_bits(value):
    return value.astype(jnp.bfloat16)


def high_low(value):
    high = low_bits(value)
    return high, low_bits(value - high.astype(jnp.float32))


def by_row(values, shape):
    row = lax.broadcasted_iota(jnp.int32, shape, 0)
    result = jnp.zeros(shape, jnp.float32)
    for index, value in enumerate(values):
        result = jnp.where(row == index, value, result)
    return result


def box_place():
    label = lax.axis_index("space")
    return lax.rem(label, ACROSS), lax.div(label, ACROSS)


def lanes(start, size):
    return pl.ds(start if isinstance(start, int) else pl.multiple_of(start, 128), size)


def fetch(pairs, sems):
    copies = [pltpu.make_async_copy(src, dst, sems.at[i]) for i, (src, dst) in enumerate(pairs)]
    for copy in copies:
        copy.start()
    return copies


def pack_kernel(count_in, positions_in, density_in, shift_in, own, basis, moments, totals, *rest):
    payloads, (count, positions, density, shift, mono, sems) = rest[:2], rest[2:]
    copies = fetch(
        [(count_in, count), (positions_in, positions), (density_in, density), (shift_in, shift)], sems
    )
    fields, points = density.shape
    pts = points // 8
    box_x, box_z = box_place()
    for copy in copies:
        copy.wait()
    local = []
    for leaf in range(8):
        bit_x, bit_y, bit_z = bits(leaf)
        centre = by_row(
            [2.0 * box_x.astype(jnp.float32) + (bit_x + 0.5), bit_y + 0.5, 2.0 * box_z.astype(jnp.float32) + (bit_z + 0.5)],
            (3, 1),
        )
        here = slice(leaf * pts, (leaf + 1) * pts)
        offset = positions[:, here] - centre
        local.append(offset)
        high = low_bits(offset).astype(jnp.float32)
        middle = low_bits(offset - high).astype(jnp.float32)
        raw = density[:, here].astype(jnp.float32)
        mass = jnp.where(lax.broadcasted_iota(jnp.int32, raw.shape, 1) < count[leaf], raw, 0.0)
        spare = jnp.zeros((ROWS - fields - 6, pts), jnp.float32)
        own[:, here] = low_bits(jnp.concatenate([mass, high, middle, spare], axis=0))

    axes = [2.0 * jnp.concatenate([part[a : a + 1] for part in local], axis=0) for a in range(3)]
    made = {(0, 0, 0): jnp.ones((8, pts), jnp.float32)}
    for k, powers in enumerate(EXPONENTS):
        if powers not in made:
            a = next(i for i in range(3) if powers[i] > 0)
            before = tuple(p - (i == a) for i, p in enumerate(powers))
            made[powers] = made[before] * axes[a]
        mono[k] = made[powers]
    mono[COEFFS:SLOT] = jnp.zeros((SLOT - COEFFS, 8, pts), jnp.float32)
    parts = []
    for leaf in range(8):
        here = slice(leaf * pts, (leaf + 1) * pts)
        high, low = high_low(mono[:, leaf, :])
        basis[0:SLOT, here] = high
        basis[SLOT:, here] = low
        parts.append(dot_nt(own[:, here], high))
    moment, rest = high_low(jnp.concatenate(parts, axis=1))
    moments[...] = moment
    total = dot(moment, shift[...]) + dot(rest, shift[...])
    total = jnp.concatenate(high_low(total), axis=1)
    totals[...] = total
    for distance, payload in zip((1, 3), payloads):
        bit = jnp.where((box_x ^ distance) > box_x, 1, 0)
        for place in range(4):
            payload[:, lanes(place * pts, pts)] = own[:, lanes((bit + 2 * place) * pts, pts)]
        payload[:, lanes(4 * pts, LEAVES)] = moment
        payload[:, lanes(4 * pts + LEAVES, 2 * SLOT)] = total


def features(held, start, size, centre, target):
    value = held[16:ROWS, lanes(start, size)].astype(jnp.float32)
    x = value[1:4] + value[4:7] + by_row(centre, (3, 1))
    norm = jnp.sum(x * x, axis=0, keepdims=True)
    if target:
        norm = norm + SOFTENING * SOFTENING
    parts, norms = [], []
    for source, out in ((x, parts), (norm, norms)):
        left = source
        for _ in range(3):
            high = low_bits(left).astype(jnp.float32)
            out.append(high)
            left = left - high
    one = jnp.ones_like(norm)
    zero = jnp.zeros_like(norm)
    blank = jnp.zeros((3, norm.shape[1]), jnp.float32)
    blocks = []
    order = (0, 1, 0, 2, 0, 1) if target else (0, 0, 1, 0, 2, 1)
    for index, which in enumerate(order):
        coords = -2.0 * parts[which] if target else parts[which]
        if index < 3:
            pair = [one, norms[index]] if target else [norms[index], one]
        else:
            pair = [zero, zero]
        blocks += [coords, *pair, blank]
    return jnp.concatenate(blocks, axis=0)


def source_features(held, start, size, centre):
    return low_bits(jnp.transpose(features(held, start, size, centre, False)))


def pulled(near, index, target, source, masses, starts, size, first=None):
    width = target.shape[1] // 8
    tiles = [(piece, turn) for piece in range(2) for turn in range(len(starts))]
    places = [lanes((2 * index + piece) * width, width) for piece in range(2)]

    def squares(piece, turn):
        return dot(source[lanes(starts[turn], size), :], target[:, places[piece]])

    ahead = squares(*tiles[0])
    for place, (piece, turn) in enumerate(tiles):
        square = ahead
        if place + 1 < len(tiles):
            ahead = squares(*tiles[place + 1])
        if turn == 0:
            total = jnp.zeros((ROWS, width), jnp.float32) if first is None else first[:, places[piece]]
        total = total + dot(masses[:, lanes(starts[turn], size)], low_bits(lax.rsqrt(square)))
        if turn + 1 == len(starts):
            near[:, places[piece]] = total


def own_groups(near, first, last, target, source, own):
    pts = source.shape[0] // 8

    def group(index, carry):
        pulled(near, index, target, source, own, [2 * p * pts for p in range(4)], 2 * pts)
        return carry

    lax.fori_loop(first, last, group, 0)


def box_columns(depth, box_x, box_z, nodes):
    blocks = []
    for layer, distance in [(layer, distance) for layer in range(depth) for distance in range(ACROSS)]:
        gap_x = 2 * (box_x - (box_x ^ distance))
        gap_z = 2 * (box_z - layer)
        across_x = nodes[0] + gap_x.astype(jnp.float32)
        across_z = nodes[2] + gap_z.astype(jnp.float32)
        apart = jnp.maximum(jnp.abs(gap_x), jnp.abs(gap_z)) >= 4
        value = lax.rsqrt(across_x * across_x + across_z * across_z + nodes[1])
        blocks.append(low_bits(value * jnp.where(apart, 1.0 / COEFFS, 0.0)))
    return jnp.concatenate(blocks, axis=0)


def own_kernel(depth, count_in, weights_in, own, *rest):
    tables, outs, rest = rest[:3], rest[3:11], rest[11:]
    near, source, target, scale, column, columns, far, spread = outs
    nodes, count, weights, sems = rest
    copies = fetch([*zip(tables, (far, spread, nodes)), (count_in, count), (weights_in, weights)], sems)
    points = own.shape[1]
    pts = points // 8
    for leaf in range(8):
        centre = [bit - 0.5 for bit in bits(leaf)]
        source[lanes(leaf * pts, pts), :] = source_features(own, leaf * pts, pts, centre)
        target[:, lanes(leaf_slot(leaf) * pts, pts)] = low_bits(features(own, leaf * pts, pts, centre, True))
    own_groups(near, 0, EARLY, target, source, own)
    for copy in copies:
        copy.wait()
    columns[...] = box_columns(depth, *box_place(), nodes)
    column[...] = by_row([weights[field] for field in range(weights.shape[0])], column.shape)
    lane_index = lax.broadcasted_iota(jnp.int32, (1, pts), 1)
    for leaf in range(8):
        scale[:, leaf * pts : (leaf + 1) * pts] = jnp.where(lane_index < count[leaf], 1.0 / (128.0 * pts), 0.0)


def spread_first(value, node):
    starts = [leaf * SLOT + node for leaf in range(8)]
    return jnp.concatenate([jnp.broadcast_to(value[:, s : s + 1], (ROWS, SLOT)) for s in starts], axis=1)


def decoded(coded):
    value = coded.astype(jnp.float32)
    node = lax.broadcasted_iota(jnp.int32, value.shape, 1) % SLOT
    return jnp.where(node == 0, 0.0, value) + spread_first(value, 0) + spread_first(value, COEFFS)


def faces_of(faces, bit, given, own, left, right):
    points = own.shape[1]
    pts = points // 8
    for y in range(2):
        for x in range(4):
            place = lanes((2 * x + y) * pts, pts)
            if x in (0, 3):
                side = left if x == 0 else right
                faces[:, place] = side[:, lanes((y + 2 * bit) * pts, pts)]
            else:
                faces[:, place] = own[:, lanes((x - 1 + 2 * y + 4 * bit) * pts, pts)]
    node = lax.broadcasted_iota(jnp.int32, given.shape, 1) % SLOT
    base = spread_first(given, 0)
    base_high = low_bits(base).astype(jnp.float32)
    coded = jnp.where(node == 0, base_high, jnp.where(node == COEFFS, base - base_high, given - base))
    faces[:, lanes(points, LEAVES)] = low_bits(coded)


def row_kernel(own, moments, totals, from_1, from_2, from_3, far, left, right, same, other, faces_even, rows):
    points = own.shape[1]
    pts = points // 8
    box_x, box_z = box_place()
    for side, step in ((left, -1), (right, 1)):
        side[...] = jnp.zeros(side.shape, side.dtype)
        for distance, held in ((1, from_1), (3, from_3)):

            @pl.when((box_x ^ distance) - box_x == step)
            def _(side=side, held=held):
                side[...] = held[:, lanes(0, side.shape[1])]

    base = 4 * pts
    ends = lanes(base + LEAVES, 2 * SLOT)
    row = jnp.concatenate([totals[...], from_1[:, ends], from_2[...], from_3[:, ends]], axis=1)
    rows[...] = jnp.broadcast_to(row[None], rows.shape)
    row = jnp.concatenate([left[:, lanes(base, LEAVES)], moments[...], right[:, lanes(base, LEAVES)]], axis=1)
    below_rows, same_rows, above_rows = pl.ds(0, 3 * LEAVES), pl.ds(3 * LEAVES, 2 * LEAVES), pl.ds(5 * LEAVES, 3 * LEAVES)
    up = dot(row, far[below_rows, :])
    down = dot(row, far[above_rows, :])
    same[...] = dot(jnp.concatenate([row[:, :LEAVES], row[:, 2 * LEAVES :]], axis=1), far[same_rows, :])
    odd = lax.rem(box_z, 2)
    faces_of(faces_even, 1 - odd, jnp.where(odd == 0, up, down), own, left, right)
    other[...] = jnp.where(odd == 0, down, up)


def middle_kernel(own, left, right, other, early, source, target, near, faces_odd):
    points = own.shape[1]
    _, box_z = box_place()
    faces_of(faces_odd, lax.rem(box_z, 2), other[...], own, left, right)
    near[:, lanes(0, EARLY * points // 4)] = early[...]
    own_groups(near, EARLY, 4, target, source, own)


def side_kernel(left, right, early, target, rows, near, passed, sides):
    passed[...] = rows[...]
    pts = early.shape[1] // 8
    for step, side in ((0, left), (1, right)):
        for place in range(4):
            centre = (1.5 if step else -1.5, place % 2 - 0.5, place // 2 - 0.5)
            sides[lanes(place * pts, pts), :] = source_features(side, place * pts, pts, centre)

        def layer(index, carry, step=step, side=side):
            pulled(near, step + 2 * index, target, sides, side, [0, 2 * pts], 2 * pts, early)
            return carry

        lax.fori_loop(0, 2, layer, 0)


def layer_pulls(near, early, step, inside, target, faces, sides):
    points = early.shape[1]
    pts = points // 8

    @pl.when(inside)
    def _():
        for place in range(8):
            height = jnp.where(step == 1, 1.5, -1.5)
            centre = (place // 2 - 1.5, place % 2 - 0.5, height)
            sides[lanes(place * pts, pts), :] = source_features(faces, place * pts, pts, centre)

        def pair(index, carry):
            starts = [(2 * x + 2 * index) * pts for x in range(3)]
            pulled(near, index + 2 * step, target, sides, faces, starts, 2 * pts, early)
            return carry

        lax.fori_loop(0, 2, pair, 0)

    @pl.when(jnp.logical_not(inside))
    def _():
        here = lanes(step * (points // 2), points // 2)
        near[:, here] = early[:, here]


def even_kernel(early, target, faces, near, sides):
    _, box_z = box_place()
    points = early.shape[1]
    step = 1 - lax.rem(box_z, 2)
    other = lanes((1 - step) * (points // 2), points // 2)
    near[:, other] = early[:, other]
    layer_pulls(near, early, step, box_z >= 0, target, faces, sides)


def last_kernel(depth, early, target, faces_even, faces_odd, basis, scale, column, columns, spread, same, boxes, *rest):
    potential, sums, near, sides = rest
    fields, points = potential.shape
    pts = points // 8
    _, box_z = box_place()
    step = lax.rem(box_z, 2)
    other = lanes((1 - step) * (points // 2), points // 2)
    near[:, other] = early[:, other]
    inside = (box_z + 2 * step - 1 >= 0) & (box_z + 2 * step - 1 < depth)
    layer_pulls(near, early, step, inside, target, faces_odd, sides)

    pieces = [boxes[layer][:, 2 * SLOT * turn : 2 * SLOT * (turn + 1)] for layer in range(depth) for turn in range(ACROSS)]
    totals_high = jnp.concatenate([piece[:, :SLOT] for piece in pieces], axis=1)
    totals_low = jnp.concatenate([piece[:, SLOT:] for piece in pieces], axis=1)
    coarse_high, coarse_low = high_low(dot(totals_high, columns[...]) + dot(totals_low, columns[...]))
    value = same[...] + dot(coarse_high, spread[...]) + dot(coarse_low, spread[...])
    for faces in (faces_even, faces_odd):
        value = value + decoded(faces[:, lanes(points, LEAVES)])
    local_high, local_low = high_low(value)
    weight = column[0:fields, 0:1]
    for leaf in range(8):
        here = slice(leaf * pts, (leaf + 1) * pts)
        slot = slice(leaf * SLOT, (leaf + 1) * SLOT)
        doubled = jnp.concatenate([local_high[:, slot], local_high[:, slot]], axis=1)
        far_part = dot(doubled, basis[:, here]) + dot(local_low[:, slot], basis[0:SLOT, here])
        total = near[0:fields, lanes(leaf_slot(leaf) * pts, pts)] + far_part[:fields]
        total = total * scale[:, here]
        potential[:, here] = total
        sums[:, here] = jnp.sum(total * weight, axis=0, keepdims=True)
    sums[:, points:] = jnp.broadcast_to(jnp.sum(weight), (1, sums.shape[1] - points))


def mean_kernel(mine, other, mean):
    points = mean.shape[1]
    total = mine[...] + other[...]
    mean[...] = total[:, :points] / total[:, points : points + 1]


def swapped(block, axis, partner):
    size = lax.axis_size(axis)
    return lax.ppermute(block, axis, [(partner(i), i) for i in range(size) if 0 <= partner(i) < size])


def per_device(positions, density, leaf_count, sigma_weights):
    fields, points = density.shape
    pts = points // 8
    depth = lax.axis_size("space") // ACROSS
    vmem, hbm = pl.BlockSpec(memory_space=pltpu.VMEM), pl.BlockSpec(memory_space=pltpu.HBM)

    def call(kernel, name, in_specs, outs, scratch, *args):
        return pl.pallas_call(
            kernel,
            in_specs=in_specs,
            out_specs=[vmem] * len(outs),
            out_shape=[jax.ShapeDtypeStruct(shape, dtype) for shape, dtype in outs],
            scratch_shapes=scratch,
            compiler_params=pltpu.CompilerParams(vmem_limit_bytes=24 * MEGA),
            name=name,
        )(*(pltpu.with_memory_space_constraint(a, pltpu.HBM) if s is hbm else a for s, a in zip(in_specs, args)))

    half, full = jnp.bfloat16, jnp.float32
    shift = shift_table()
    side_shape = ((ROWS, 4 * pts + LEAVES), half)
    given_shape = ((ROWS, 4 * pts + LEAVES + 2 * SLOT), half)
    faces_shape = ((ROWS, points + LEAVES), half)
    rows_shape = ((depth, ROWS, 2 * SLOT * ACROSS), half)
    near_shape, sums_shape = ((ROWS, points), full), ((ROWS, LEAVES), full)
    rows_scratch = pltpu.VMEM((8 * pts, FEATURES), half)
    own, basis, moments, totals, *given = call(
        pack_kernel,
        "pack",
        [hbm] * 4,
        [
            ((ROWS, points), half),
            ((2 * SLOT, points), half),
            ((ROWS, LEAVES), half),
            ((ROWS, 2 * SLOT), half),
            given_shape,
            given_shape,
        ],
        [
            pltpu.SMEM((8,), jnp.int32),
            pltpu.VMEM((3, points), full),
            pltpu.VMEM((fields, points), half),
            pltpu.VMEM((LEAVES, SLOT), half),
            pltpu.VMEM((SLOT, 8, pts), full),
            pltpu.SemaphoreType.DMA((4,)),
        ],
        leaf_count,
        positions,
        density,
        jnp.asarray(shift, half),
    )
    from_2 = swapped(totals, "space", lambda i: i ^ 2)
    from_1 = swapped(given[0], "space", lambda i: i ^ 1)
    from_3 = swapped(given[1], "space", lambda i: i ^ 3)
    near, source, target, scale, column, columns, far, spread = call(
        functools.partial(own_kernel, depth),
        "near_own",
        [hbm] * 2 + [vmem] + [hbm] * 3,
        [
            ((ROWS, EARLY * points // 4), full),
            ((points, FEATURES), half),
            ((FEATURES, points), half),
            ((1, points), full),
            ((ROWS, 128), full),
            ((ACROSS * depth * SLOT, SLOT), half),
            ((len(STEPS) * LEAVES, LEAVES), half),
            ((SLOT, LEAVES), half),
        ],
        [
            pltpu.VMEM((3, SLOT, SLOT), full),
            pltpu.SMEM((8,), jnp.int32),
            pltpu.SMEM((fields,), full),
            pltpu.SemaphoreType.DMA((5,)),
        ],
        leaf_count,
        sigma_weights,
        own,
        jnp.asarray(far_table(), half),
        jnp.asarray(shift.T.copy(), half),
        jnp.asarray(box_nodes()),
    )
    left, right, same, other, faces_even, rows = call(
        row_kernel,
        "row",
        [vmem] * 7,
        [side_shape, side_shape, sums_shape, sums_shape, faces_shape, rows_shape],
        [],
        own,
        moments,
        totals,
        from_1,
        from_2,
        from_3,
        far,
    )
    faces_even = swapped(faces_even, "space", lambda i: i ^ ACROSS)
    near, faces_odd = call(
        middle_kernel,
        "near_middle",
        [vmem] * 7,
        [near_shape, faces_shape],
        [],
        own,
        left,
        right,
        other,
        near,
        source,
        target,
    )
    faces_odd = swapped(faces_odd, "space", lambda i: i + ACROSS if i // ACROSS % 2 else i - ACROSS)
    near, rows = call(
        side_kernel,
        "near_side",
        [vmem] * 5,
        [near_shape, rows_shape],
        [pltpu.VMEM((4 * pts, FEATURES), half)],
        left,
        right,
        near,
        target,
        rows,
    )
    columns_of_boxes = [[z * ACROSS + x for z in range(depth)] for x in range(ACROSS)]
    boxes = lax.all_to_all(rows, "space", 0, 0, axis_index_groups=columns_of_boxes, tiled=True)
    near, = call(even_kernel, "near_even", [vmem] * 3, [near_shape], [rows_scratch], near, target, faces_even)
    potential, sums = call(
        functools.partial(last_kernel, depth),
        "near_odd",
        [vmem] * 11,
        [((fields, points), full), ((1, points + 128), full)],
        [pltpu.VMEM((ROWS, points), full), rows_scratch],
        near,
        target,
        faces_even,
        faces_odd,
        basis,
        scale,
        column,
        columns,
        spread,
        same,
        boxes,
    )
    if lax.axis_size("sig") == 2:
        other = swapped(sums, "sig", lambda i: i ^ 1)
    else:
        other = lax.psum(sums, "sig") - sums
    mean, = call(mean_kernel, "mean", [vmem] * 2, [((1, points), full)], [], sums, other)
    return potential, mean.reshape(points)


def solution(mesh):
    in_specs = (P(None, "space"), P("sig", "space"), P("space"), P("sig"))
    out_specs = (P("sig", "space"), P("space"))
    return jax.shard_map(per_device, mesh=mesh, in_specs=in_specs, out_specs=out_specs, check_vma=False)
```

```python
import functools
import math

import jax
import jax.numpy as jnp
import numpy as np
from jax import lax
from jax.experimental import pallas as pl
from jax.experimental.pallas import tpu as pltpu
from jax.sharding import PartitionSpec as P

ORDER = 5
SOFTENING = 0.1
ACROSS = 4
SLOT = 64
ROWS = 24
LEAVES = 8 * SLOT
MEGA = 1024 * 1024
FEATURES = 48
EARLY = 2


def exponent_table(order_max):
    entries_list = []
    for degree in range(order_max + 1):
        for first_power in range(degree, -1, -1):
            for second_power in range(degree - first_power, -1, -1):
                entries_list.append((first_power, second_power, degree - first_power - second_power))
    return entries_list


def node_table(count_nodes, offset_value):
    counter = np.arange(1, count_nodes + 1, dtype=np.float32)[:, None]
    stride_set = np.array([0.7548776662466927, 0.5698402909980532, 0.4142135623730951], dtype=np.float32)[None, :]
    unit_points = np.mod(counter * stride_set + np.float32(offset_value), np.float32(1.0))
    return (np.float32(2.0) * unit_points - np.float32(1.0)).astype(np.float32)


EXPONENTS = exponent_table(ORDER)
COEFFS = len(EXPONENTS)
CHECK = node_table(COEFFS, 0.5).astype(np.float64)
EQUIV = node_table(COEFFS, 0.0).astype(np.float64)
STEPS = [(sx, sz) for sz in (-1, 0, 1) for sx in (-1, 0, 1) if sx != 0 or sz != 0]


def bits(octant):
    return octant % 2, octant // 2 % 2, octant // 4


def leaf_slot(octant):
    bit_x, bit_y, bit_z = bits(octant)
    return (bit_x + 2 * bit_z) * 2 + bit_y


@functools.lru_cache(None)
def far_table():
    shape = (len(STEPS), 8, SLOT, 8, SLOT)
    table = np.zeros(shape)
    gap_nodes = 0.5 * (CHECK[None, :, :] - EQUIV[:, None, :])
    for index, (step_x, step_z) in enumerate(STEPS):
        for source in range(8):
            for target in range(8):
                s, t = bits(source), bits(target)
                gap = np.array([2 * step_x + s[0] - t[0], s[1] - t[1], 2 * step_z + s[2] - t[2]], np.float64)
                if max(abs(gap[0]), abs(gap[2])) >= 2:
                    shifted = gap_nodes - gap
                    value = 1.0 / np.sqrt(np.sum(shifted * shifted, -1) + SOFTENING * SOFTENING) / COEFFS
                    table[index, source, :COEFFS, target, :COEFFS] = value
    return table.reshape(len(STEPS) * LEAVES, LEAVES)


@functools.lru_cache(None)
def shift_table():
    table = np.zeros((8, SLOT, SLOT))
    for leaf in range(8):
        offset = [bit - 0.5 for bit in bits(leaf)]
        for k, target in enumerate(EXPONENTS):
            for i, source in enumerate(EXPONENTS):
                if all(b <= a for a, b in zip(target, source)):
                    value = 1.0
                    for a, b, h in zip(target, source, offset):
                        value *= math.comb(a, b) * 0.5**b * h ** (a - b)
                    table[leaf, i, k] = value
    return table.reshape(8 * SLOT, SLOT)


@functools.lru_cache(None)
def box_nodes():
    gaps = np.zeros((3, SLOT, SLOT))
    gaps[:, :COEFFS, :COEFFS] = np.moveaxis(CHECK[None, :, :] - EQUIV[:, None, :], -1, 0)
    gaps[1] = gaps[1] ** 2 + SOFTENING * SOFTENING
    return gaps.astype(np.float32)


def dot(left, right):
    return jnp.dot(left, right, preferred_element_type=jnp.float32)


def dot_nt(left, right):
    return lax.dot_general(left, right, (((1,), (1,)), ((), ())), preferred_element_type=jnp.float32)


def low_bits(value):
    return value.astype(jnp.bfloat16)


def high_low(value):
    high = low_bits(value)
    return high, low_bits(value - high.astype(jnp.float32))


def by_row(values, shape):
    row = lax.broadcasted_iota(jnp.int32, shape, 0)
    result = jnp.zeros(shape, jnp.float32)
    for index, value in enumerate(values):
        result = jnp.where(row == index, value, result)
    return result


def turn_of():
    return lax.rem(lax.axis_index("sig"), 2)


def box_place():
    label = lax.axis_index("space")
    return lax.rem(label, ACROSS), lax.div(label, ACROSS)


def lanes(start, size):
    return pl.ds(start if isinstance(start, int) else pl.multiple_of(start, 128), size)


def fetch(pairs, sems):
    copies = [pltpu.make_async_copy(src, dst, sems.at[i]) for i, (src, dst) in enumerate(pairs)]
    for copy in copies:
        copy.start()
    return copies


def pack_kernel(count_in, positions_in, density_in, shift_in, own, basis, moments, totals, *rest):
    payloads, (count, positions, density, shift, mono, sems) = rest[:2], rest[2:]
    copies = fetch(
        [(count_in, count), (positions_in, positions), (density_in, density), (shift_in, shift)], sems
    )
    fields, points = density.shape
    pts = points // 8
    box_x, box_z = box_place()
    for copy in copies:
        copy.wait()
    local = []
    for leaf in range(8):
        bit_x, bit_y, bit_z = bits(leaf)
        centre = by_row(
            [2.0 * box_x.astype(jnp.float32) + (bit_x + 0.5), bit_y + 0.5, 2.0 * box_z.astype(jnp.float32) + (bit_z + 0.5)],
            (3, 1),
        )
        here = slice(leaf * pts, (leaf + 1) * pts)
        offset = positions[:, here] - centre
        local.append(offset)
        high = low_bits(offset).astype(jnp.float32)
        middle = low_bits(offset - high).astype(jnp.float32)
        raw = density[:, here].astype(jnp.float32)
        mass = jnp.where(lax.broadcasted_iota(jnp.int32, raw.shape, 1) < count[leaf], raw, 0.0)
        spare = jnp.zeros((ROWS - fields - 6, pts), jnp.float32)
        own[:, here] = low_bits(jnp.concatenate([mass, high, middle, spare], axis=0))

    axes = [2.0 * jnp.concatenate([part[a : a + 1] for part in local], axis=0) for a in range(3)]
    made = {(0, 0, 0): jnp.ones((8, pts), jnp.float32)}
    for k, powers in enumerate(EXPONENTS):
        if powers not in made:
            a = next(i for i in range(3) if powers[i] > 0)
            before = tuple(p - (i == a) for i, p in enumerate(powers))
            made[powers] = made[before] * axes[a]
        mono[k] = made[powers]
    mono[COEFFS:SLOT] = jnp.zeros((SLOT - COEFFS, 8, pts), jnp.float32)
    parts = []
    for leaf in range(8):
        here = slice(leaf * pts, (leaf + 1) * pts)
        high, low = high_low(mono[:, leaf, :])
        basis[0:SLOT, here] = high
        basis[SLOT:, here] = low
        parts.append(dot_nt(own[:, here], high))
    moment, rest = high_low(jnp.concatenate(parts, axis=1))
    moments[...] = moment
    total = dot(moment, shift[...]) + dot(rest, shift[...])
    totals[...] = jnp.broadcast_to(jnp.concatenate(high_low(total), axis=1)[None], totals.shape)
    for turn, payload in enumerate(payloads):
        distance = jnp.where(turn_of() == turn, 1, 3)
        bit = jnp.where((box_x ^ distance) > box_x, 1, 0)
        for place in range(4):
            payload[:, lanes(place * pts, pts)] = own[:, lanes((bit + 2 * place) * pts, pts)]
        payload[:, lanes(4 * pts, LEAVES)] = moment


def features(held, start, size, centre, target):
    value = held[16:ROWS, lanes(start, size)].astype(jnp.float32)
    x = value[1:4] + value[4:7] + by_row(centre, (3, 1))
    norm = jnp.sum(x * x, axis=0, keepdims=True)
    if target:
        norm = norm + SOFTENING * SOFTENING
    parts, norms = [], []
    for source, out in ((x, parts), (norm, norms)):
        left = source
        for _ in range(3):
            high = low_bits(left).astype(jnp.float32)
            out.append(high)
            left = left - high
    one = jnp.ones_like(norm)
    zero = jnp.zeros_like(norm)
    blank = jnp.zeros((3, norm.shape[1]), jnp.float32)
    blocks = []
    order = (0, 1, 0, 2, 0, 1) if target else (0, 0, 1, 0, 2, 1)
    for index, which in enumerate(order):
        coords = -2.0 * parts[which] if target else parts[which]
        if index < 3:
            pair = [one, norms[index]] if target else [norms[index], one]
        else:
            pair = [zero, zero]
        blocks += [coords, *pair, blank]
    return jnp.concatenate(blocks, axis=0)


def source_features(held, start, size, centre):
    return low_bits(jnp.transpose(features(held, start, size, centre, False)))


def pulled(near, index, target, source, masses, starts, size, first=None):
    width = target.shape[1] // 8
    tiles = [(piece, turn) for piece in range(2) for turn in range(len(starts))]
    places = [lanes((2 * index + piece) * width, width) for piece in range(2)]

    def squares(piece, turn):
        return dot(source[lanes(starts[turn], size), :], target[:, places[piece]])

    ahead = squares(*tiles[0])
    for place, (piece, turn) in enumerate(tiles):
        square = ahead
        if place + 1 < len(tiles):
            ahead = squares(*tiles[place + 1])
        if turn == 0:
            total = jnp.zeros((ROWS, width), jnp.float32) if first is None else first[:, places[piece]]
        total = total + dot(masses[:, lanes(starts[turn], size)], low_bits(lax.rsqrt(square)))
        if turn + 1 == len(starts):
            near[:, places[piece]] = total


def own_groups(near, first, last, target, source, own):
    pts = source.shape[0] // 8

    def group(index, carry):
        pulled(near, index, target, source, own, [2 * p * pts for p in range(4)], 2 * pts)
        return carry

    lax.fori_loop(first, last, group, 0)


def box_columns(depth, box_x, box_z, nodes):
    blocks = []
    for box in range(ACROSS * depth):
        gap_x = 2 * (box_x - box % ACROSS)
        gap_z = 2 * (box_z - box // ACROSS)
        across_x = nodes[0] + gap_x.astype(jnp.float32)
        across_z = nodes[2] + gap_z.astype(jnp.float32)
        apart = jnp.maximum(jnp.abs(gap_x), jnp.abs(gap_z)) >= 4
        value = lax.rsqrt(across_x * across_x + across_z * across_z + nodes[1])
        blocks.append(low_bits(value * jnp.where(apart, 1.0 / COEFFS, 0.0)))
    return jnp.concatenate(blocks, axis=0)


def own_kernel(depth, count_in, weights_in, own, *rest):
    tables, outs, rest = rest[:3], rest[3:11], rest[11:]
    near, source, target, scale, column, columns, far, spread = outs
    nodes, count, weights, sems = rest
    copies = fetch([*zip(tables, (far, spread, nodes)), (count_in, count), (weights_in, weights)], sems)
    points = own.shape[1]
    pts = points // 8
    for leaf in range(8):
        centre = [bit - 0.5 for bit in bits(leaf)]
        source[lanes(leaf * pts, pts), :] = source_features(own, leaf * pts, pts, centre)
        target[:, lanes(leaf_slot(leaf) * pts, pts)] = low_bits(features(own, leaf * pts, pts, centre, True))
    own_groups(near, 0, EARLY, target, source, own)
    for copy in copies:
        copy.wait()
    columns[...] = box_columns(depth, *box_place(), nodes)
    column[...] = by_row([weights[field] for field in range(weights.shape[0])], column.shape)
    lane_index = lax.broadcasted_iota(jnp.int32, (1, pts), 1)
    for leaf in range(8):
        scale[:, leaf * pts : (leaf + 1) * pts] = jnp.where(lane_index < count[leaf], 1.0 / (128.0 * pts), 0.0)


def spread_first(value, node):
    starts = [leaf * SLOT + node for leaf in range(8)]
    return jnp.concatenate([jnp.broadcast_to(value[:, s : s + 1], (ROWS, SLOT)) for s in starts], axis=1)


def decoded(coded):
    value = coded.astype(jnp.float32)
    node = lax.broadcasted_iota(jnp.int32, value.shape, 1) % SLOT
    return jnp.where(node == 0, 0.0, value) + spread_first(value, 0) + spread_first(value, COEFFS)


def faces_of(faces, bit, given, own, left, right):
    points = own.shape[1]
    pts = points // 8
    for y in range(2):
        for x in range(4):
            place = lanes((2 * x + y) * pts, pts)
            if x in (0, 3):
                side = left if x == 0 else right
                faces[:, place] = side[:, lanes((y + 2 * bit) * pts, pts)]
            else:
                faces[:, place] = own[:, lanes((x - 1 + 2 * y + 4 * bit) * pts, pts)]
    node = lax.broadcasted_iota(jnp.int32, given.shape, 1) % SLOT
    base = spread_first(given, 0)
    base_high = low_bits(base).astype(jnp.float32)
    coded = jnp.where(node == 0, base_high, jnp.where(node == COEFFS, base - base_high, given - base))
    faces[:, lanes(points, LEAVES)] = low_bits(coded)


def row_kernel(own, moments, first, second, far, left, right, same, other, faces):
    points = own.shape[1]
    pts = points // 8
    box_x, box_z = box_place()
    for side, step in ((left, -1), (right, 1)):
        side[...] = jnp.zeros(side.shape, side.dtype)
        for turn, held in ((0, first), (1, second)):
            distance = jnp.where(turn_of() == turn, 1, 3)

            @pl.when((box_x ^ distance) - box_x == step)
            def _(side=side, held=held):
                side[...] = held[...]

    base = 4 * pts
    row = jnp.concatenate([left[:, lanes(base, LEAVES)], moments[...], right[:, lanes(base, LEAVES)]], axis=1)
    below_rows, same_rows, above_rows = pl.ds(0, 3 * LEAVES), pl.ds(3 * LEAVES, 2 * LEAVES), pl.ds(5 * LEAVES, 3 * LEAVES)
    up = dot(row, far[below_rows, :])
    down = dot(row, far[above_rows, :])
    same[...] = dot(jnp.concatenate([row[:, :LEAVES], row[:, 2 * LEAVES :]], axis=1), far[same_rows, :])
    above = 1 - lax.rem(box_z + turn_of(), 2)
    faces_of(faces, above, jnp.where(above == 1, up, down), own, left, right)
    other[...] = jnp.where(above == 1, down, up)


def middle_kernel(own, left, right, other, early, source, target, near, faces):
    points = own.shape[1]
    _, box_z = box_place()
    faces_of(faces, lax.rem(box_z + turn_of(), 2), other[...], own, left, right)
    near[:, lanes(0, EARLY * points // 4)] = early[...]
    own_groups(near, EARLY, 4, target, source, own)


def side_kernel(left, right, early, target, near, sides):
    pts = early.shape[1] // 8
    for step, side in ((0, left), (1, right)):
        for place in range(4):
            centre = (1.5 if step else -1.5, place % 2 - 0.5, place // 2 - 0.5)
            sides[lanes(place * pts, pts), :] = source_features(side, place * pts, pts, centre)

        def layer(index, carry, step=step, side=side):
            pulled(near, step + 2 * index, target, sides, side, [0, 2 * pts], 2 * pts, early)
            return carry

        lax.fori_loop(0, 2, layer, 0)


def layer_pulls(near, early, step, inside, target, faces, sides):
    points = early.shape[1]
    pts = points // 8

    @pl.when(inside)
    def _():
        for place in range(8):
            height = jnp.where(step == 1, 1.5, -1.5)
            centre = (place // 2 - 1.5, place % 2 - 0.5, height)
            sides[lanes(place * pts, pts), :] = source_features(faces, place * pts, pts, centre)

        def pair(index, carry):
            starts = [(2 * x + 2 * index) * pts for x in range(3)]
            pulled(near, index + 2 * step, target, sides, faces, starts, 2 * pts, early)
            return carry

        lax.fori_loop(0, 2, pair, 0)

    @pl.when(jnp.logical_not(inside))
    def _():
        here = lanes(step * (points // 2), points // 2)
        near[:, here] = early[:, here]


def one_layer(depth, turn, early, target, faces, near, sides):
    points = early.shape[1]
    _, box_z = box_place()
    step = 1 - lax.rem(box_z + turn_of() + turn, 2)
    other = lanes((1 - step) * (points // 2), points // 2)
    near[:, other] = early[:, other]
    layer = box_z + 2 * step - 1
    layer_pulls(near, early, step, (layer >= 0) & (layer < depth), target, faces, sides)


def last_kernel(depth, early, target, faces_first, faces_second, basis, scale, column, columns, spread, same, boxes, *rest):
    potential, sums, near, sides = rest
    fields, points = potential.shape
    pts = points // 8
    one_layer(depth, 1, early, target, faces_second, near, sides)

    totals_high = jnp.concatenate([boxes[box][:, :SLOT] for box in range(ACROSS * depth)], axis=1)
    totals_low = jnp.concatenate([boxes[box][:, SLOT:] for box in range(ACROSS * depth)], axis=1)
    coarse_high, coarse_low = high_low(dot(totals_high, columns[...]) + dot(totals_low, columns[...]))
    value = same[...] + dot(coarse_high, spread[...]) + dot(coarse_low, spread[...])
    for faces in (faces_first, faces_second):
        value = value + decoded(faces[:, lanes(points, LEAVES)])
    local_high, local_low = high_low(value)
    weight = column[0:fields, 0:1]
    for leaf in range(8):
        here = slice(leaf * pts, (leaf + 1) * pts)
        slot = slice(leaf * SLOT, (leaf + 1) * SLOT)
        doubled = jnp.concatenate([local_high[:, slot], local_high[:, slot]], axis=1)
        far_part = dot(doubled, basis[:, here]) + dot(local_low[:, slot], basis[0:SLOT, here])
        total = near[0:fields, lanes(leaf_slot(leaf) * pts, pts)] + far_part[:fields]
        total = total * scale[:, here]
        potential[:, here] = total
        sums[:, here] = jnp.sum(total * weight, axis=0, keepdims=True)
    sums[:, points:] = jnp.broadcast_to(jnp.sum(weight), (1, sums.shape[1] - points))


def mean_kernel(mine, other, mean):
    points = mean.shape[1]
    total = mine[...] + other[...]
    mean[...] = total[:, :points] / total[:, points : points + 1]


def swapped(block, axis, partner):
    size = lax.axis_size(axis)
    return lax.ppermute(block, axis, [(partner(i), i) for i in range(size) if 0 <= partner(i) < size])


def taken_in_turns(block, turn, partners):
    boxes, cores = lax.axis_size("space"), lax.axis_size("sig")
    pairs = []
    for box in range(boxes):
        for core in range(cores):
            other = partners[(turn + core) % 2](box)
            if 0 <= other < boxes:
                pairs.append((other * cores + core, box * cores + core))
    return lax.ppermute(block, ("space", "sig"), pairs)


def beside(i):
    return i + ACROSS if i // ACROSS % 2 else i - ACROSS


def per_device(positions, density, leaf_count, sigma_weights):
    fields, points = density.shape
    pts = points // 8
    depth = lax.axis_size("space") // ACROSS
    vmem, hbm = pl.BlockSpec(memory_space=pltpu.VMEM), pl.BlockSpec(memory_space=pltpu.HBM)

    def call(kernel, name, in_specs, outs, scratch, *args):
        work = {"near_own": 3, "near_middle": 3, "near_side": 3, "near_first": 2, "near_second": 3}.get(name, 1)
        return pl.pallas_call(
            kernel,
            in_specs=in_specs,
            out_specs=[vmem] * len(outs),
            out_shape=[jax.ShapeDtypeStruct(shape, dtype) for shape, dtype in outs],
            scratch_shapes=scratch,
            compiler_params=pltpu.CompilerParams(vmem_limit_bytes=24 * MEGA),
            cost_estimate=pl.CostEstimate(flops=work * 10**9, transcendentals=0, bytes_accessed=work * 10**6),
            name=name,
        )(*(pltpu.with_memory_space_constraint(a, pltpu.HBM) if s is hbm else a for s, a in zip(in_specs, args)))

    half, full = jnp.bfloat16, jnp.float32
    shift = shift_table()
    side_shape = ((ROWS, 4 * pts + LEAVES), half)
    faces_shape = ((ROWS, points + LEAVES), half)
    near_shape, sums_shape = ((ROWS, points), full), ((ROWS, LEAVES), full)
    rows_scratch = pltpu.VMEM((8 * pts, FEATURES), half)
    own, basis, moments, totals, *given = call(
        pack_kernel,
        "pack",
        [hbm] * 4,
        [
            ((ROWS, points), half),
            ((2 * SLOT, points), half),
            ((ROWS, LEAVES), half),
            ((ACROSS * depth, ROWS, 2 * SLOT), half),
            side_shape,
            side_shape,
        ],
        [
            pltpu.SMEM((8,), jnp.int32),
            pltpu.VMEM((3, points), full),
            pltpu.VMEM((fields, points), half),
            pltpu.VMEM((LEAVES, SLOT), half),
            pltpu.VMEM((SLOT, 8, pts), full),
            pltpu.SemaphoreType.DMA((4,)),
        ],
        leaf_count,
        positions,
        density,
        jnp.asarray(shift, half),
    )
    boxes = lax.all_to_all(totals, "space", 0, 0, tiled=True)
    along_row = (lambda i: i ^ 1, lambda i: i ^ 3)
    first, second = [taken_in_turns(block, turn, along_row) for turn, block in enumerate(given)]
    near, source, target, scale, column, columns, far, spread = call(
        functools.partial(own_kernel, depth),
        "near_own",
        [hbm] * 2 + [vmem] + [hbm] * 3,
        [
            ((ROWS, EARLY * points // 4), full),
            ((points, FEATURES), half),
            ((FEATURES, points), half),
            ((1, points), full),
            ((ROWS, 128), full),
            ((ACROSS * depth * SLOT, SLOT), half),
            ((len(STEPS) * LEAVES, LEAVES), half),
            ((SLOT, LEAVES), half),
        ],
        [
            pltpu.VMEM((3, SLOT, SLOT), full),
            pltpu.SMEM((8,), jnp.int32),
            pltpu.SMEM((fields,), full),
            pltpu.SemaphoreType.DMA((5,)),
        ],
        leaf_count,
        sigma_weights,
        own,
        jnp.asarray(far_table(), half),
        jnp.asarray(shift.T.copy(), half),
        jnp.asarray(box_nodes()),
    )
    left, right, same, other, faces_first = call(
        row_kernel,
        "row",
        [vmem] * 5,
        [side_shape, side_shape, sums_shape, sums_shape, faces_shape],
        [],
        own,
        moments,
        first,
        second,
        far,
    )
    layers = (lambda i: i ^ ACROSS, beside)
    faces_first = taken_in_turns(faces_first, 0, layers)
    near, faces_second = call(
        middle_kernel,
        "near_middle",
        [vmem] * 7,
        [near_shape, faces_shape],
        [],
        own,
        left,
        right,
        other,
        near,
        source,
        target,
    )
    faces_second = taken_in_turns(faces_second, 1, layers)
    near, = call(
        side_kernel,
        "near_side",
        [vmem] * 4,
        [near_shape],
        [pltpu.VMEM((4 * pts, FEATURES), half)],
        left,
        right,
        near,
        target,
    )
    near, = call(
        functools.partial(one_layer, depth, 0),
        "near_first",
        [vmem] * 3,
        [near_shape],
        [rows_scratch],
        near,
        target,
        faces_first,
    )
    potential, sums = call(
        functools.partial(last_kernel, depth),
        "near_second",
        [vmem] * 11,
        [((fields, points), full), ((1, points + 128), full)],
        [pltpu.VMEM((ROWS, points), full), rows_scratch],
        near,
        target,
        faces_first,
        faces_second,
        basis,
        scale,
        column,
        columns,
        spread,
        same,
        boxes,
    )
    if lax.axis_size("sig") == 2:
        other = swapped(sums, "sig", lambda i: i ^ 1)
    else:
        other = lax.psum(sums, "sig") - sums
    mean, = call(mean_kernel, "mean", [vmem] * 2, [((1, points), full)], [], sums, other)
    return potential, mean.reshape(points)


def solution(mesh):
    in_specs = (P(None, "space"), P("sig", "space"), P("space"), P("sig"))
    out_specs = (P("sig", "space"), P("space"))
    return jax.shard_map(per_device, mesh=mesh, in_specs=in_specs, out_specs=out_specs, check_vma=False)
```

```python
import functools
import math

import jax
import jax.numpy as jnp
import numpy as np
from jax import lax
from jax.experimental import pallas as pl
from jax.experimental.pallas import tpu as pltpu
from jax.sharding import PartitionSpec as P

ORDER = 5
SOFTENING = 0.1
ACROSS = 4
SLOT = 64
ROWS = 24
LEAVES = 8 * SLOT
MEGA = 1024 * 1024
FEATURES = 48
EARLY = 2


def exponent_table(order_max):
    entries_list = []
    for degree in range(order_max + 1):
        for first_power in range(degree, -1, -1):
            for second_power in range(degree - first_power, -1, -1):
                entries_list.append((first_power, second_power, degree - first_power - second_power))
    return entries_list


def node_table(count_nodes, offset_value):
    counter = np.arange(1, count_nodes + 1, dtype=np.float32)[:, None]
    stride_set = np.array([0.7548776662466927, 0.5698402909980532, 0.4142135623730951], dtype=np.float32)[None, :]
    unit_points = np.mod(counter * stride_set + np.float32(offset_value), np.float32(1.0))
    return (np.float32(2.0) * unit_points - np.float32(1.0)).astype(np.float32)


EXPONENTS = exponent_table(ORDER)
COEFFS = len(EXPONENTS)
CHECK = node_table(COEFFS, 0.5).astype(np.float64)
EQUIV = node_table(COEFFS, 0.0).astype(np.float64)
STEPS = [(sx, sz) for sz in (-1, 0, 1) for sx in (-1, 0, 1) if sx != 0 or sz != 0]


def bits(octant):
    return octant % 2, octant // 2 % 2, octant // 4


def leaf_slot(octant):
    bit_x, bit_y, bit_z = bits(octant)
    return (bit_x + 2 * bit_z) * 2 + bit_y


@functools.lru_cache(None)
def far_table():
    shape = (len(STEPS), 8, SLOT, 8, SLOT)
    table = np.zeros(shape)
    gap_nodes = 0.5 * (CHECK[None, :, :] - EQUIV[:, None, :])
    for index, (step_x, step_z) in enumerate(STEPS):
        for source in range(8):
            for target in range(8):
                s, t = bits(source), bits(target)
                gap = np.array([2 * step_x + s[0] - t[0], s[1] - t[1], 2 * step_z + s[2] - t[2]], np.float64)
                if max(abs(gap[0]), abs(gap[2])) >= 2:
                    shifted = gap_nodes - gap
                    value = 1.0 / np.sqrt(np.sum(shifted * shifted, -1) + SOFTENING * SOFTENING) / COEFFS
                    table[index, source, :COEFFS, target, :COEFFS] = value
    return table.reshape(len(STEPS) * LEAVES, LEAVES)


@functools.lru_cache(None)
def shift_table():
    table = np.zeros((8, SLOT, SLOT))
    for leaf in range(8):
        offset = [bit - 0.5 for bit in bits(leaf)]
        for k, target in enumerate(EXPONENTS):
            for i, source in enumerate(EXPONENTS):
                if all(b <= a for a, b in zip(target, source)):
                    value = 1.0
                    for a, b, h in zip(target, source, offset):
                        value *= math.comb(a, b) * 0.5**b * h ** (a - b)
                    table[leaf, i, k] = value
    return table.reshape(8 * SLOT, SLOT)


@functools.lru_cache(None)
def box_nodes():
    gaps = np.zeros((3, SLOT, SLOT))
    gaps[:, :COEFFS, :COEFFS] = np.moveaxis(CHECK[None, :, :] - EQUIV[:, None, :], -1, 0)
    gaps[1] = gaps[1] ** 2 + SOFTENING * SOFTENING
    return gaps.astype(np.float32)


def dot(left, right):
    return jnp.dot(left, right, preferred_element_type=jnp.float32)


def dot_nt(left, right):
    return lax.dot_general(left, right, (((1,), (1,)), ((), ())), preferred_element_type=jnp.float32)


def low_bits(value):
    return value.astype(jnp.bfloat16)


def high_low(value):
    high = low_bits(value)
    return high, low_bits(value - high.astype(jnp.float32))


def by_row(values, shape):
    row = lax.broadcasted_iota(jnp.int32, shape, 0)
    result = jnp.zeros(shape, jnp.float32)
    for index, value in enumerate(values):
        result = jnp.where(row == index, value, result)
    return result


def box_place():
    label = lax.axis_index("space")
    return lax.rem(label, ACROSS), lax.div(label, ACROSS)


def lanes(start, size):
    return pl.ds(start if isinstance(start, int) else pl.multiple_of(start, 128), size)


def fetch(pairs, sems):
    copies = [pltpu.make_async_copy(src, dst, sems.at[i]) for i, (src, dst) in enumerate(pairs)]
    for copy in copies:
        copy.start()
    return copies


def pack_kernel(count_in, positions_in, density_in, shift_in, own, basis, moments, totals, *rest):
    payloads, (count, positions, density, shift, mono, sems) = rest[:2], rest[2:]
    copies = fetch(
        [(count_in, count), (positions_in, positions), (density_in, density), (shift_in, shift)], sems
    )
    fields, points = density.shape
    pts = points // 8
    box_x, box_z = box_place()
    for copy in copies:
        copy.wait()
    local = []
    for leaf in range(8):
        bit_x, bit_y, bit_z = bits(leaf)
        centre = by_row(
            [2.0 * box_x.astype(jnp.float32) + (bit_x + 0.5), bit_y + 0.5, 2.0 * box_z.astype(jnp.float32) + (bit_z + 0.5)],
            (3, 1),
        )
        here = slice(leaf * pts, (leaf + 1) * pts)
        offset = positions[:, here] - centre
        local.append(offset)
        high = low_bits(offset).astype(jnp.float32)
        middle = low_bits(offset - high).astype(jnp.float32)
        raw = density[:, here].astype(jnp.float32)
        mass = jnp.where(lax.broadcasted_iota(jnp.int32, raw.shape, 1) < count[leaf], raw, 0.0)
        spare = jnp.zeros((ROWS - fields - 6, pts), jnp.float32)
        own[:, here] = low_bits(jnp.concatenate([mass, high, middle, spare], axis=0))

    axes = [2.0 * jnp.concatenate([part[a : a + 1] for part in local], axis=0) for a in range(3)]
    made = {(0, 0, 0): jnp.ones((8, pts), jnp.float32)}
    for k, powers in enumerate(EXPONENTS):
        if powers not in made:
            a = next(i for i in range(3) if powers[i] > 0)
            before = tuple(p - (i == a) for i, p in enumerate(powers))
            made[powers] = made[before] * axes[a]
        mono[k] = made[powers]
    mono[COEFFS:SLOT] = jnp.zeros((SLOT - COEFFS, 8, pts), jnp.float32)
    parts = []
    for leaf in range(8):
        here = slice(leaf * pts, (leaf + 1) * pts)
        high, low = high_low(mono[:, leaf, :])
        basis[0:SLOT, here] = high
        basis[SLOT:, here] = low
        parts.append(dot_nt(own[:, here], high))
    moment, rest = high_low(jnp.concatenate(parts, axis=1))
    moments[...] = moment
    total = dot(moment, shift[...]) + dot(rest, shift[...])
    total = jnp.concatenate(high_low(total), axis=1)
    totals[...] = total
    for distance, payload in zip((1, 3), payloads):
        bit = jnp.where((box_x ^ distance) > box_x, 1, 0)
        for place in range(4):
            payload[:, lanes(place * pts, pts)] = own[:, lanes((bit + 2 * place) * pts, pts)]
        payload[:, lanes(4 * pts, LEAVES)] = moment
        payload[:, lanes(4 * pts + LEAVES, 2 * SLOT)] = total


def features(held, start, size, centre, target):
    value = held[16:ROWS, lanes(start, size)].astype(jnp.float32)
    x = value[1:4] + value[4:7] + by_row(centre, (3, 1))
    norm = jnp.sum(x * x, axis=0, keepdims=True)
    if target:
        norm = norm + SOFTENING * SOFTENING
    parts, norms = [], []
    for source, out in ((x, parts), (norm, norms)):
        left = source
        for _ in range(3):
            high = low_bits(left).astype(jnp.float32)
            out.append(high)
            left = left - high
    one = jnp.ones_like(norm)
    zero = jnp.zeros_like(norm)
    blank = jnp.zeros((3, norm.shape[1]), jnp.float32)
    blocks = []
    order = (0, 1, 0, 2, 0, 1) if target else (0, 0, 1, 0, 2, 1)
    for index, which in enumerate(order):
        coords = -2.0 * parts[which] if target else parts[which]
        if index < 3:
            pair = [one, norms[index]] if target else [norms[index], one]
        else:
            pair = [zero, zero]
        blocks += [coords, *pair, blank]
    return jnp.concatenate(blocks, axis=0)


def source_features(held, start, size, centre):
    return low_bits(jnp.transpose(features(held, start, size, centre, False)))


def pulled(near, jobs, target, size, first=None):
    width = target.shape[1] // 8
    tiles = []
    for group, source, masses, starts in jobs:
        for piece in range(2):
            here = lanes((2 * group + piece) * width, width)
            for turn, start in enumerate(starts):
                tiles.append((here, source, masses, lanes(start, size), turn == 0, turn + 1 == len(starts)))

    def squares(tile):
        return dot(tile[1][tile[3], :], target[:, tile[0]])

    ahead, kernel, total = squares(tiles[0]), None, None
    for turn in range(len(tiles) + 1):
        square = ahead
        if turn + 1 < len(tiles):
            ahead = squares(tiles[turn + 1])
        if turn > 0:
            here, _, masses, place, opens, closes = tiles[turn - 1]
            if opens:
                total = jnp.zeros((ROWS, width), jnp.float32) if first is None else first[:, here]
            total = total + dot(masses[:, place], kernel)
            if closes:
                near[:, here] = total
        if turn < len(tiles):
            kernel = low_bits(lax.rsqrt(square))


def own_groups(near, first, last, target, source, own):
    pts = source.shape[0] // 8
    starts = [2 * p * pts for p in range(4)]
    pulled(near, [(group, source, own, starts) for group in range(first, last)], target, 2 * pts)


def box_columns(depth, box_x, box_z, nodes):
    blocks = []
    for turn, distance in [(turn, distance) for turn in range(depth) for distance in range(ACROSS)]:
        gap_x = 2 * (box_x - (box_x ^ distance))
        gap_z = 2 * (box_z - ((box_z ^ turn) if depth == 4 else turn))
        across_x = nodes[0] + gap_x.astype(jnp.float32)
        across_z = nodes[2] + gap_z.astype(jnp.float32)
        apart = jnp.maximum(jnp.abs(gap_x), jnp.abs(gap_z)) >= 4
        value = lax.rsqrt(across_x * across_x + across_z * across_z + nodes[1])
        blocks.append(low_bits(value * jnp.where(apart, 1.0 / COEFFS, 0.0)))
    return jnp.concatenate(blocks, axis=0)


def own_kernel(depth, count_in, weights_in, own, *rest):
    tables, outs, rest = rest[:3], rest[3:11], rest[11:]
    near, source, target, scale, column, columns, far, spread = outs
    nodes, count, weights, sems = rest
    copies = fetch([*zip(tables, (far, spread, nodes)), (count_in, count), (weights_in, weights)], sems)
    points = own.shape[1]
    pts = points // 8
    for leaf in range(8):
        centre = [bit - 0.5 for bit in bits(leaf)]
        source[lanes(leaf * pts, pts), :] = source_features(own, leaf * pts, pts, centre)
        target[:, lanes(leaf_slot(leaf) * pts, pts)] = low_bits(features(own, leaf * pts, pts, centre, True))
    own_groups(near, 0, EARLY, target, source, own)
    for copy in copies:
        copy.wait()
    columns[...] = box_columns(depth, *box_place(), nodes)
    column[...] = by_row([weights[field] for field in range(weights.shape[0])], column.shape)
    lane_index = lax.broadcasted_iota(jnp.int32, (1, pts), 1)
    for leaf in range(8):
        scale[:, leaf * pts : (leaf + 1) * pts] = jnp.where(lane_index < count[leaf], 1.0 / (128.0 * pts), 0.0)


def spread_first(value, node):
    starts = [leaf * SLOT + node for leaf in range(8)]
    return jnp.concatenate([jnp.broadcast_to(value[:, s : s + 1], (ROWS, SLOT)) for s in starts], axis=1)


def decoded(coded):
    value = coded.astype(jnp.float32)
    node = lax.broadcasted_iota(jnp.int32, value.shape, 1) % SLOT
    return jnp.where(node == 0, 0.0, value) + spread_first(value, 0) + spread_first(value, COEFFS)


def faces_of(faces, bit, given, own, left, right, rows=None):
    points = own.shape[1]
    pts = points // 8
    for y in range(2):
        for x in range(4):
            place = lanes((2 * x + y) * pts, pts)
            if x in (0, 3):
                side = left if x == 0 else right
                faces[:, place] = side[:, lanes((y + 2 * bit) * pts, pts)]
            else:
                faces[:, place] = own[:, lanes((x - 1 + 2 * y + 4 * bit) * pts, pts)]
    node = lax.broadcasted_iota(jnp.int32, given.shape, 1) % SLOT
    base = spread_first(given, 0)
    base_high = low_bits(base).astype(jnp.float32)
    coded = jnp.where(node == 0, base_high, jnp.where(node == COEFFS, base - base_high, given - base))
    faces[:, lanes(points, LEAVES)] = low_bits(coded)
    if rows is not None:
        faces[:, lanes(points + LEAVES, rows.shape[1])] = rows


def row_kernel(own, moments, totals, from_1, from_2, from_3, far, left, right, same, other, faces_even, rows):
    points = own.shape[1]
    pts = points // 8
    box_x, box_z = box_place()
    for side, step in ((left, -1), (right, 1)):
        side[...] = jnp.zeros(side.shape, side.dtype)
        for distance, held in ((1, from_1), (3, from_3)):

            @pl.when((box_x ^ distance) - box_x == step)
            def _(side=side, held=held):
                side[...] = held[:, lanes(0, side.shape[1])]

    base = 4 * pts
    ends = lanes(base + LEAVES, 2 * SLOT)
    row = jnp.concatenate([totals[...], from_1[:, ends], from_2[...], from_3[:, ends]], axis=1)
    rows[...] = row
    around = jnp.concatenate([left[:, lanes(base, LEAVES)], moments[...], right[:, lanes(base, LEAVES)]], axis=1)
    below_rows, same_rows, above_rows = pl.ds(0, 3 * LEAVES), pl.ds(3 * LEAVES, 2 * LEAVES), pl.ds(5 * LEAVES, 3 * LEAVES)
    up = dot(around, far[below_rows, :])
    down = dot(around, far[above_rows, :])
    same[...] = dot(jnp.concatenate([around[:, :LEAVES], around[:, 2 * LEAVES :]], axis=1), far[same_rows, :])
    odd = lax.rem(box_z, 2)
    faces_of(faces_even, 1 - odd, jnp.where(odd == 0, up, down), own, left, right, row)
    other[...] = jnp.where(odd == 0, down, up)


def middle_kernel(own, left, right, other, early, source, target, near, faces_odd):
    points = own.shape[1]
    _, box_z = box_place()
    faces_of(faces_odd, lax.rem(box_z, 2), other[...], own, left, right)
    near[:, lanes(0, EARLY * points // 4)] = early[...]
    own_groups(near, EARLY, 4, target, source, own)


def side_kernel(left, right, early, target, rows, faces_even, near, both, sides_left, sides_right):
    pts = early.shape[1] // 8
    width = rows.shape[1]
    both[:, lanes(0, width)] = rows[...]
    both[:, lanes(width, width)] = faces_even[:, lanes(faces_even.shape[1] - width, width)]
    jobs = []
    for step, side, held in ((0, left, sides_left), (1, right, sides_right)):
        for place in range(4):
            centre = (1.5 if step else -1.5, place % 2 - 0.5, place // 2 - 0.5)
            held[lanes(place * pts, pts), :] = source_features(side, place * pts, pts, centre)
        jobs += [(step, held, side, [0, 2 * pts]), (step + 2, held, side, [0, 2 * pts])]
    pulled(near, jobs, target, 2 * pts, early)


def layer_pulls(near, early, step, inside, target, faces, sides):
    points = early.shape[1]
    pts = points // 8

    @pl.when(inside)
    def _():
        for place in range(8):
            height = jnp.where(step == 1, 1.5, -1.5)
            centre = (place // 2 - 1.5, place % 2 - 0.5, height)
            sides[lanes(place * pts, pts), :] = source_features(faces, place * pts, pts, centre)

        jobs = [(i + 2 * step, sides, faces, [2 * (x + i) * pts for x in range(3)]) for i in range(2)]
        pulled(near, jobs, target, 2 * pts, early)

    @pl.when(jnp.logical_not(inside))
    def _():
        here = lanes(step * (points // 2), points // 2)
        near[:, here] = early[:, here]


def even_kernel(early, target, faces, near, sides):
    _, box_z = box_place()
    points = early.shape[1]
    step = 1 - lax.rem(box_z, 2)
    other = lanes((1 - step) * (points // 2), points // 2)
    near[:, other] = early[:, other]
    layer_pulls(near, early, step, box_z >= 0, target, faces, sides)


def last_kernel(depth, early, target, faces_even, faces_odd, basis, scale, column, columns, spread, same, *rest):
    held, (potential, sums, near, sides) = rest[:-4], rest[-4:]
    fields, points = potential.shape
    pts = points // 8
    _, box_z = box_place()
    step = lax.rem(box_z, 2)
    other = lanes((1 - step) * (points // 2), points // 2)
    near[:, other] = early[:, other]
    inside = (box_z + 2 * step - 1 >= 0) & (box_z + 2 * step - 1 < depth)
    layer_pulls(near, early, step, inside, target, faces_odd, sides)

    if depth == 4:
        rows, distant = held
        width = rows.shape[1]
        near_rows = faces_even[:, lanes(faces_even.shape[1] - width, width)]
        layers = [rows[...], near_rows, distant[:, lanes(0, width)], distant[:, lanes(width, width)]]
    else:
        layers = [held[0][layer] for layer in range(depth)]
    pieces = [layer[:, 2 * SLOT * turn : 2 * SLOT * (turn + 1)] for layer in layers for turn in range(ACROSS)]
    totals_high = jnp.concatenate([piece[:, :SLOT] for piece in pieces], axis=1)
    totals_low = jnp.concatenate([piece[:, SLOT:] for piece in pieces], axis=1)
    coarse_high, coarse_low = high_low(dot(totals_high, columns[...]) + dot(totals_low, columns[...]))
    value = same[...] + dot(coarse_high, spread[...]) + dot(coarse_low, spread[...])
    for faces in (faces_even, faces_odd):
        value = value + decoded(faces[:, lanes(points, LEAVES)])
    local_high, local_low = high_low(value)
    weight = column[0:fields, 0:1]
    for leaf in range(8):
        here = slice(leaf * pts, (leaf + 1) * pts)
        slot = slice(leaf * SLOT, (leaf + 1) * SLOT)
        doubled = jnp.concatenate([local_high[:, slot], local_high[:, slot]], axis=1)
        far_part = dot(doubled, basis[:, here]) + dot(local_low[:, slot], basis[0:SLOT, here])
        total = near[0:fields, lanes(leaf_slot(leaf) * pts, pts)] + far_part[:fields]
        total = total * scale[:, here]
        potential[:, here] = total
        sums[:, here] = jnp.sum(total * weight, axis=0, keepdims=True)
    sums[:, points:] = jnp.broadcast_to(jnp.sum(weight), (1, sums.shape[1] - points))


def mean_kernel(mine, other, mean):
    points = mean.shape[1]
    total = mine[...] + other[...]
    mean[...] = total[:, :points] / total[:, points : points + 1]


def swapped(block, axis, partner):
    size = lax.axis_size(axis)
    return lax.ppermute(block, axis, [(partner(i), i) for i in range(size) if 0 <= partner(i) < size])


def per_device(positions, density, leaf_count, sigma_weights):
    fields, points = density.shape
    pts = points // 8
    depth = lax.axis_size("space") // ACROSS
    vmem, hbm = pl.BlockSpec(memory_space=pltpu.VMEM), pl.BlockSpec(memory_space=pltpu.HBM)

    def call(kernel, name, in_specs, outs, scratch, *args):
        return pl.pallas_call(
            kernel,
            in_specs=in_specs,
            out_specs=[vmem] * len(outs),
            out_shape=[jax.ShapeDtypeStruct(shape, dtype) for shape, dtype in outs],
            scratch_shapes=scratch,
            compiler_params=pltpu.CompilerParams(vmem_limit_bytes=24 * MEGA),
            name=name,
        )(*(pltpu.with_memory_space_constraint(a, pltpu.HBM) if s is hbm else a for s, a in zip(in_specs, args)))

    half, full = jnp.bfloat16, jnp.float32
    shift = shift_table()
    side_shape = ((ROWS, 4 * pts + LEAVES), half)
    given_shape = ((ROWS, 4 * pts + LEAVES + 2 * SLOT), half)
    faces_shape = ((ROWS, points + LEAVES), half)
    even_shape = ((ROWS, points + LEAVES + 2 * SLOT * ACROSS), half)
    rows_shape = ((ROWS, 2 * SLOT * ACROSS), half)
    both_shape = ((ROWS, 4 * SLOT * ACROSS), half)
    near_shape, sums_shape = ((ROWS, points), full), ((ROWS, LEAVES), full)
    rows_scratch = pltpu.VMEM((8 * pts, FEATURES), half)
    own, basis, moments, totals, *given = call(
        pack_kernel,
        "pack",
        [hbm] * 4,
        [
            ((ROWS, points), half),
            ((2 * SLOT, points), half),
            ((ROWS, LEAVES), half),
            ((ROWS, 2 * SLOT), half),
            given_shape,
            given_shape,
        ],
        [
            pltpu.SMEM((8,), jnp.int32),
            pltpu.VMEM((3, points), full),
            pltpu.VMEM((fields, points), half),
            pltpu.VMEM((LEAVES, SLOT), half),
            pltpu.VMEM((SLOT, 8, pts), full),
            pltpu.SemaphoreType.DMA((4,)),
        ],
        leaf_count,
        positions,
        density,
        jnp.asarray(shift, half),
    )
    from_2 = swapped(totals, "space", lambda i: i ^ 2)
    from_1 = swapped(given[0], "space", lambda i: i ^ 1)
    from_3 = swapped(given[1], "space", lambda i: i ^ 3)
    near, source, target, scale, column, columns, far, spread = call(
        functools.partial(own_kernel, depth),
        "near_own",
        [hbm] * 2 + [vmem] + [hbm] * 3,
        [
            ((ROWS, EARLY * points // 4), full),
            ((points, FEATURES), half),
            ((FEATURES, points), half),
            ((1, points), full),
            ((ROWS, 128), full),
            ((ACROSS * depth * SLOT, SLOT), half),
            ((len(STEPS) * LEAVES, LEAVES), half),
            ((SLOT, LEAVES), half),
        ],
        [
            pltpu.VMEM((3, SLOT, SLOT), full),
            pltpu.SMEM((8,), jnp.int32),
            pltpu.SMEM((fields,), full),
            pltpu.SemaphoreType.DMA((5,)),
        ],
        leaf_count,
        sigma_weights,
        own,
        jnp.asarray(far_table(), half),
        jnp.asarray(shift.T.copy(), half),
        jnp.asarray(box_nodes()),
    )
    left, right, same, other, faces_even, rows = call(
        row_kernel,
        "row",
        [vmem] * 7,
        [side_shape, side_shape, sums_shape, sums_shape, even_shape, rows_shape],
        [],
        own,
        moments,
        totals,
        from_1,
        from_2,
        from_3,
        far,
    )
    faces_even = swapped(faces_even, "space", lambda i: i ^ ACROSS)
    near, faces_odd = call(
        middle_kernel,
        "near_middle",
        [vmem] * 7,
        [near_shape, faces_shape],
        [],
        own,
        left,
        right,
        other,
        near,
        source,
        target,
    )
    faces_odd = swapped(faces_odd, "space", lambda i: i + ACROSS if i // ACROSS % 2 else i - ACROSS)
    near, both = call(
        side_kernel,
        "near_side",
        [vmem] * 6,
        [near_shape, both_shape],
        [pltpu.VMEM((4 * pts, FEATURES), half)] * 2,
        left,
        right,
        near,
        target,
        rows,
        faces_even,
    )
    if depth == 4:
        held = [rows, swapped(both, "space", lambda i: i ^ (2 * ACROSS))]
    else:
        groups = [[z * ACROSS + x for z in range(depth)] for x in range(ACROSS)]
        held = [lax.all_gather(rows, "space", axis_index_groups=groups)]
    near, = call(even_kernel, "near_even", [vmem] * 3, [near_shape], [rows_scratch], near, target, faces_even)
    potential, sums = call(
        functools.partial(last_kernel, depth),
        "near_odd",
        [vmem] * (10 + len(held)),
        [((fields, points), full), ((1, points + 128), full)],
        [pltpu.VMEM((ROWS, points), full), rows_scratch],
        near,
        target,
        faces_even,
        faces_odd,
        basis,
        scale,
        column,
        columns,
        spread,
        same,
        *held,
    )
    if lax.axis_size("sig") == 2:
        other = swapped(sums, "sig", lambda i: i ^ 1)
    else:
        other = lax.psum(sums, "sig") - sums
    mean, = call(mean_kernel, "mean", [vmem] * 2, [((1, points), full)], [], sums, other)
    return potential, mean.reshape(points)


def solution(mesh):
    in_specs = (P(None, "space"), P("sig", "space"), P("space"), P("sig"))
    out_specs = (P("sig", "space"), P("space"))
    return jax.shard_map(per_device, mesh=mesh, in_specs=in_specs, out_specs=out_specs, check_vma=False)
```

```python
import functools
import math

import jax
import jax.numpy as jnp
import numpy as np
from jax import lax
from jax.experimental import pallas as pl
from jax.experimental.pallas import tpu as pltpu
from jax.sharding import PartitionSpec as P

ORDER = 5
SOFTENING = 0.1
ACROSS = 4
SLOT = 64
ROWS = 24
LEAVES = 8 * SLOT
MEGA = 1024 * 1024
FEATURES = 48
EARLY = 2


def exponent_table(order_max):
    entries_list = []
    for degree in range(order_max + 1):
        for first_power in range(degree, -1, -1):
            for second_power in range(degree - first_power, -1, -1):
                entries_list.append((first_power, second_power, degree - first_power - second_power))
    return entries_list


def node_table(count_nodes, offset_value):
    counter = np.arange(1, count_nodes + 1, dtype=np.float32)[:, None]
    stride_set = np.array([0.7548776662466927, 0.5698402909980532, 0.4142135623730951], dtype=np.float32)[None, :]
    unit_points = np.mod(counter * stride_set + np.float32(offset_value), np.float32(1.0))
    return (np.float32(2.0) * unit_points - np.float32(1.0)).astype(np.float32)


EXPONENTS = exponent_table(ORDER)
COEFFS = len(EXPONENTS)
CHECK = node_table(COEFFS, 0.5).astype(np.float64)
EQUIV = node_table(COEFFS, 0.0).astype(np.float64)
STEPS = [(sx, sz) for sz in (-1, 0, 1) for sx in (-1, 0, 1) if sx != 0 or sz != 0]


def bits(octant):
    return octant % 2, octant // 2 % 2, octant // 4


def leaf_slot(octant):
    bit_x, bit_y, bit_z = bits(octant)
    return (bit_x + 2 * bit_z) * 2 + bit_y


@functools.lru_cache(None)
def far_table():
    shape = (len(STEPS), 8, SLOT, 8, SLOT)
    table = np.zeros(shape)
    gap_nodes = 0.5 * (CHECK[None, :, :] - EQUIV[:, None, :])
    for index, (step_x, step_z) in enumerate(STEPS):
        for source in range(8):
            for target in range(8):
                s, t = bits(source), bits(target)
                gap = np.array([2 * step_x + s[0] - t[0], s[1] - t[1], 2 * step_z + s[2] - t[2]], np.float64)
                if max(abs(gap[0]), abs(gap[2])) >= 2:
                    shifted = gap_nodes - gap
                    value = 1.0 / np.sqrt(np.sum(shifted * shifted, -1) + SOFTENING * SOFTENING) / COEFFS
                    table[index, source, :COEFFS, target, :COEFFS] = value
    return table.reshape(len(STEPS) * LEAVES, LEAVES)


@functools.lru_cache(None)
def shift_table():
    table = np.zeros((8, SLOT, SLOT))
    for leaf in range(8):
        offset = [bit - 0.5 for bit in bits(leaf)]
        for k, target in enumerate(EXPONENTS):
            for i, source in enumerate(EXPONENTS):
                if all(b <= a for a, b in zip(target, source)):
                    value = 1.0
                    for a, b, h in zip(target, source, offset):
                        value *= math.comb(a, b) * 0.5**b * h ** (a - b)
                    table[leaf, i, k] = value
    return table.reshape(8 * SLOT, SLOT)


@functools.lru_cache(None)
def box_nodes():
    gaps = np.zeros((3, SLOT, SLOT))
    gaps[:, :COEFFS, :COEFFS] = np.moveaxis(CHECK[None, :, :] - EQUIV[:, None, :], -1, 0)
    gaps[1] = gaps[1] ** 2 + SOFTENING * SOFTENING
    return gaps.astype(np.float32)


def dot(left, right):
    return jnp.dot(left, right, preferred_element_type=jnp.float32)


def dot_nt(left, right):
    return lax.dot_general(left, right, (((1,), (1,)), ((), ())), preferred_element_type=jnp.float32)


def low_bits(value):
    return value.astype(jnp.bfloat16)


def high_low(value):
    high = low_bits(value)
    return high, low_bits(value - high.astype(jnp.float32))


def by_row(values, shape):
    row = lax.broadcasted_iota(jnp.int32, shape, 0)
    result = jnp.zeros(shape, jnp.float32)
    for index, value in enumerate(values):
        result = jnp.where(row == index, value, result)
    return result


def box_place():
    label = lax.axis_index("space")
    return lax.rem(label, ACROSS), lax.div(label, ACROSS)


def lanes(start, size):
    return pl.ds(start if isinstance(start, int) else pl.multiple_of(start, 128), size)


def fetch(pairs, sems):
    copies = [pltpu.make_async_copy(src, dst, sems.at[i]) for i, (src, dst) in enumerate(pairs)]
    for copy in copies:
        copy.start()
    return copies


def pack_kernel(count_in, positions_in, density_in, shift_in, own, basis, moments, totals, *rest):
    payloads, (count, positions, density, shift, mono, sems) = rest[:2], rest[2:]
    copies = fetch(
        [(count_in, count), (positions_in, positions), (density_in, density), (shift_in, shift)], sems
    )
    fields, points = density.shape
    pts = points // 8
    box_x, box_z = box_place()
    for copy in copies:
        copy.wait()
    local = []
    for leaf in range(8):
        bit_x, bit_y, bit_z = bits(leaf)
        centre = by_row(
            [2.0 * box_x.astype(jnp.float32) + (bit_x + 0.5), bit_y + 0.5, 2.0 * box_z.astype(jnp.float32) + (bit_z + 0.5)],
            (3, 1),
        )
        here = slice(leaf * pts, (leaf + 1) * pts)
        offset = positions[:, here] - centre
        local.append(offset)
        high = low_bits(offset).astype(jnp.float32)
        middle = low_bits(offset - high).astype(jnp.float32)
        raw = density[:, here].astype(jnp.float32)
        mass = jnp.where(lax.broadcasted_iota(jnp.int32, raw.shape, 1) < count[leaf], raw, 0.0)
        spare = jnp.zeros((ROWS - fields - 6, pts), jnp.float32)
        own[:, here] = low_bits(jnp.concatenate([mass, high, middle, spare], axis=0))

    axes = [2.0 * jnp.concatenate([part[a : a + 1] for part in local], axis=0) for a in range(3)]
    made = {(0, 0, 0): jnp.ones((8, pts), jnp.float32)}
    for k, powers in enumerate(EXPONENTS):
        if powers not in made:
            a = next(i for i in range(3) if powers[i] > 0)
            before = tuple(p - (i == a) for i, p in enumerate(powers))
            made[powers] = made[before] * axes[a]
        mono[k] = made[powers]
    mono[COEFFS:SLOT] = jnp.zeros((SLOT - COEFFS, 8, pts), jnp.float32)
    parts = []
    for leaf in range(8):
        here = slice(leaf * pts, (leaf + 1) * pts)
        high, low = high_low(mono[:, leaf, :])
        basis[0:SLOT, here] = high
        basis[SLOT:, here] = low
        parts.append(dot_nt(own[:, here], high))
    moment, rest = high_low(jnp.concatenate(parts, axis=1))
    moments[...] = moment
    total = dot(moment, shift[...]) + dot(rest, shift[...])
    total = jnp.concatenate(high_low(total), axis=1)
    totals[...] = total
    for distance, payload in zip((1, 3), payloads):
        bit = jnp.where((box_x ^ distance) > box_x, 1, 0)
        for place in range(4):
            payload[:, lanes(place * pts, pts)] = own[:, lanes((bit + 2 * place) * pts, pts)]
        payload[:, lanes(4 * pts, LEAVES)] = moment
        payload[:, lanes(4 * pts + LEAVES, 2 * SLOT)] = total


def features(held, start, size, centre, target):
    value = held[16:ROWS, lanes(start, size)].astype(jnp.float32)
    x = value[1:4] + value[4:7] + by_row(centre, (3, 1))
    norm = jnp.sum(x * x, axis=0, keepdims=True)
    if target:
        norm = norm + SOFTENING * SOFTENING
    parts, norms = [], []
    for source, out in ((x, parts), (norm, norms)):
        left = source
        for _ in range(3):
            high = low_bits(left).astype(jnp.float32)
            out.append(high)
            left = left - high
    one = jnp.ones_like(norm)
    zero = jnp.zeros_like(norm)
    blank = jnp.zeros((3, norm.shape[1]), jnp.float32)
    blocks = []
    order = (0, 1, 0, 2, 0, 1) if target else (0, 0, 1, 0, 2, 1)
    for index, which in enumerate(order):
        coords = -2.0 * parts[which] if target else parts[which]
        if index < 3:
            pair = [one, norms[index]] if target else [norms[index], one]
        else:
            pair = [zero, zero]
        blocks += [coords, *pair, blank]
    return jnp.concatenate(blocks, axis=0)


def source_features(held, start, size, centre):
    return low_bits(jnp.transpose(features(held, start, size, centre, False)))


def pulled(near, jobs, target, size, first=None):
    width = target.shape[1] // 8
    tiles = []
    for group, source, masses, starts in jobs:
        for piece in range(2):
            here = lanes((2 * group + piece) * width, width)
            for turn, start in enumerate(starts):
                tiles.append((here, source, masses, lanes(start, size), turn == 0, turn + 1 == len(starts)))

    def squares(tile):
        return dot(tile[1][tile[3], :], target[:, tile[0]])

    ahead, kernel, total = squares(tiles[0]), None, None
    for turn in range(len(tiles) + 1):
        square = ahead
        if turn + 1 < len(tiles):
            ahead = squares(tiles[turn + 1])
        if turn > 0:
            here, _, masses, place, opens, closes = tiles[turn - 1]
            if opens:
                total = jnp.zeros((ROWS, width), jnp.float32) if first is None else first[:, here]
            total = total + dot(masses[:, place], kernel)
            if closes:
                near[:, here] = total
        if turn < len(tiles):
            kernel = low_bits(lax.rsqrt(square))


def own_groups(near, first, last, target, source, own):
    pts = source.shape[0] // 8
    starts = [2 * p * pts for p in range(4)]
    pulled(near, [(group, source, own, starts) for group in range(first, last)], target, 2 * pts)


def box_columns(depth, box_x, box_z, nodes):
    blocks = []
    for turn, distance in [(turn, distance) for turn in range(depth) for distance in range(ACROSS)]:
        gap_x = 2 * (box_x - (box_x ^ distance))
        gap_z = 2 * (box_z - ((box_z ^ turn) if depth == 4 else turn))
        across_x = nodes[0] + gap_x.astype(jnp.float32)
        across_z = nodes[2] + gap_z.astype(jnp.float32)
        apart = jnp.maximum(jnp.abs(gap_x), jnp.abs(gap_z)) >= 4
        value = lax.rsqrt(across_x * across_x + across_z * across_z + nodes[1])
        blocks.append(low_bits(value * jnp.where(apart, 1.0 / COEFFS, 0.0)))
    return jnp.concatenate(blocks, axis=0)


def own_kernel(depth, count_in, weights_in, own, *rest):
    tables, outs, rest = rest[:3], rest[3:11], rest[11:]
    near, source, target, scale, column, columns, far, spread = outs
    nodes, count, weights, sems = rest
    copies = fetch([*zip(tables, (far, spread, nodes)), (count_in, count), (weights_in, weights)], sems)
    points = own.shape[1]
    pts = points // 8
    for leaf in range(8):
        centre = [bit - 0.5 for bit in bits(leaf)]
        source[lanes(leaf * pts, pts), :] = source_features(own, leaf * pts, pts, centre)
        target[:, lanes(leaf_slot(leaf) * pts, pts)] = low_bits(features(own, leaf * pts, pts, centre, True))
    own_groups(near, 0, EARLY, target, source, own)
    for copy in copies:
        copy.wait()
    columns[...] = box_columns(depth, *box_place(), nodes)
    column[...] = by_row([weights[field] for field in range(weights.shape[0])], column.shape)
    lane_index = lax.broadcasted_iota(jnp.int32, (1, pts), 1)
    for leaf in range(8):
        scale[:, leaf * pts : (leaf + 1) * pts] = jnp.where(lane_index < count[leaf], 1.0 / (128.0 * pts), 0.0)


def spread_first(value, node):
    starts = [leaf * SLOT + node for leaf in range(8)]
    return jnp.concatenate([jnp.broadcast_to(value[:, s : s + 1], (ROWS, SLOT)) for s in starts], axis=1)


def decoded(coded):
    value = coded.astype(jnp.float32)
    node = lax.broadcasted_iota(jnp.int32, value.shape, 1) % SLOT
    return jnp.where(node == 0, 0.0, value) + spread_first(value, 0) + spread_first(value, COEFFS)


def faces_of(faces, bit, given, own, left, right, rows=None):
    points = own.shape[1]
    pts = points // 8
    for y in range(2):
        for x in range(4):
            place = lanes((2 * x + y) * pts, pts)
            if x in (0, 3):
                side = left if x == 0 else right
                faces[:, place] = side[:, lanes((y + 2 * bit) * pts, pts)]
            else:
                faces[:, place] = own[:, lanes((x - 1 + 2 * y + 4 * bit) * pts, pts)]
    node = lax.broadcasted_iota(jnp.int32, given.shape, 1) % SLOT
    base = spread_first(given, 0)
    base_high = low_bits(base).astype(jnp.float32)
    coded = jnp.where(node == 0, base_high, jnp.where(node == COEFFS, base - base_high, given - base))
    faces[:, lanes(points, LEAVES)] = low_bits(coded)
    if rows is not None:
        faces[:, lanes(points + LEAVES, rows.shape[1])] = rows


def row_kernel(own, moments, totals, from_1, from_2, from_3, far, left, right, same, other, faces_even, rows):
    points = own.shape[1]
    pts = points // 8
    box_x, box_z = box_place()
    for side, step in ((left, -1), (right, 1)):
        side[...] = jnp.zeros(side.shape, side.dtype)
        for distance, held in ((1, from_1), (3, from_3)):

            @pl.when((box_x ^ distance) - box_x == step)
            def _(side=side, held=held):
                side[...] = held[:, lanes(0, side.shape[1])]

    base = 4 * pts
    ends = lanes(base + LEAVES, 2 * SLOT)
    row = jnp.concatenate([totals[...], from_1[:, ends], from_2[...], from_3[:, ends]], axis=1)
    rows[...] = row
    around = jnp.concatenate([left[:, lanes(base, LEAVES)], moments[...], right[:, lanes(base, LEAVES)]], axis=1)
    below_rows, same_rows, above_rows = pl.ds(0, 3 * LEAVES), pl.ds(3 * LEAVES, 2 * LEAVES), pl.ds(5 * LEAVES, 3 * LEAVES)
    up = dot(around, far[below_rows, :])
    down = dot(around, far[above_rows, :])
    same[...] = dot(jnp.concatenate([around[:, :LEAVES], around[:, 2 * LEAVES :]], axis=1), far[same_rows, :])
    odd = lax.rem(box_z, 2)
    faces_of(faces_even, 1 - odd, jnp.where(odd == 0, up, down), own, left, right, row)
    other[...] = jnp.where(odd == 0, down, up)


def middle_kernel(own, left, right, other, early, source, target, near, faces_odd):
    points = own.shape[1]
    _, box_z = box_place()
    faces_of(faces_odd, lax.rem(box_z, 2), other[...], own, left, right)
    near[:, lanes(0, EARLY * points // 4)] = early[...]
    own_groups(near, EARLY, 4, target, source, own)


def side_kernel(left, right, early, target, rows, faces_even, near, both, sides_left, sides_right):
    pts = early.shape[1] // 8
    width = rows.shape[1]
    both[:, lanes(0, width)] = rows[...]
    both[:, lanes(width, width)] = faces_even[:, lanes(faces_even.shape[1] - width, width)]
    jobs = []
    for step, side, held in ((0, left, sides_left), (1, right, sides_right)):
        for place in range(4):
            centre = (1.5 if step else -1.5, place % 2 - 0.5, place // 2 - 0.5)
            held[lanes(place * pts, pts), :] = source_features(side, place * pts, pts, centre)
        jobs += [(step, held, side, [0, 2 * pts]), (step + 2, held, side, [0, 2 * pts])]
    pulled(near, jobs, target, 2 * pts, early)


def layer_pulls(near, early, step, inside, target, faces, sides):
    points = early.shape[1]
    pts = points // 8

    @pl.when(inside)
    def _():
        for place in range(8):
            height = jnp.where(step == 1, 1.5, -1.5)
            centre = (place // 2 - 1.5, place % 2 - 0.5, height)
            sides[lanes(place * pts, pts), :] = source_features(faces, place * pts, pts, centre)

        jobs = [(i + 2 * step, sides, faces, [2 * (x + i) * pts for x in range(3)]) for i in range(2)]
        pulled(near, jobs, target, 2 * pts, early)

    @pl.when(jnp.logical_not(inside))
    def _():
        here = lanes(step * (points // 2), points // 2)
        near[:, here] = early[:, here]


def even_kernel(early, target, faces, near, sides):
    _, box_z = box_place()
    points = early.shape[1]
    step = 1 - lax.rem(box_z, 2)
    other = lanes((1 - step) * (points // 2), points // 2)
    near[:, other] = early[:, other]
    layer_pulls(near, early, step, box_z >= 0, target, faces, sides)


def last_kernel(depth, early, target, faces_even, faces_odd, basis, scale, column, columns, spread, same, *rest):
    held, (potential, sums, near, sides) = rest[:-4], rest[-4:]
    fields, points = potential.shape
    pts = points // 8
    _, box_z = box_place()
    step = lax.rem(box_z, 2)
    other = lanes((1 - step) * (points // 2), points // 2)
    near[:, other] = early[:, other]
    inside = (box_z + 2 * step - 1 >= 0) & (box_z + 2 * step - 1 < depth)
    layer_pulls(near, early, step, inside, target, faces_odd, sides)

    if depth == 4:
        rows, distant = held
        width = rows.shape[1]
        near_rows = faces_even[:, lanes(faces_even.shape[1] - width, width)]
        layers = [rows[...], near_rows, distant[:, lanes(0, width)], distant[:, lanes(width, width)]]
    else:
        layers = [held[0][layer] for layer in range(depth)]
    pieces = [layer[:, 2 * SLOT * turn : 2 * SLOT * (turn + 1)] for layer in layers for turn in range(ACROSS)]
    totals_high = jnp.concatenate([piece[:, :SLOT] for piece in pieces], axis=1)
    totals_low = jnp.concatenate([piece[:, SLOT:] for piece in pieces], axis=1)
    coarse_high, coarse_low = high_low(dot(totals_high, columns[...]) + dot(totals_low, columns[...]))
    value = same[...] + dot(coarse_high, spread[...]) + dot(coarse_low, spread[...])
    value = value + decoded(faces_even[:, lanes(points, LEAVES)])
    value = value + jnp.where(inside, decoded(faces_odd[:, lanes(points, LEAVES)]), 0.0)
    local_high, local_low = high_low(value)
    weight = column[0:fields, 0:1]
    for leaf in range(8):
        here = slice(leaf * pts, (leaf + 1) * pts)
        slot = slice(leaf * SLOT, (leaf + 1) * SLOT)
        doubled = jnp.concatenate([local_high[:, slot], local_high[:, slot]], axis=1)
        far_part = dot(doubled, basis[:, here]) + dot(local_low[:, slot], basis[0:SLOT, here])
        total = near[0:fields, lanes(leaf_slot(leaf) * pts, pts)] + far_part[:fields]
        total = total * scale[:, here]
        potential[:, here] = total
        sums[:, here] = jnp.sum(total * weight, axis=0, keepdims=True)
    sums[:, points:] = jnp.broadcast_to(jnp.sum(weight), (1, sums.shape[1] - points))


def mean_kernel(mine, other, mean):
    points = mean.shape[1]
    total = mine[...] + other[...]
    mean[...] = total[:, :points] / total[:, points : points + 1]


def swapped(block, axis, partner):
    size = lax.axis_size(axis)
    return lax.ppermute(block, axis, [(partner(i) if 0 <= partner(i) < size else i, i) for i in range(size)])


def per_device(positions, density, leaf_count, sigma_weights):
    fields, points = density.shape
    pts = points // 8
    depth = lax.axis_size("space") // ACROSS
    vmem, hbm = pl.BlockSpec(memory_space=pltpu.VMEM), pl.BlockSpec(memory_space=pltpu.HBM)

    def call(kernel, name, in_specs, outs, scratch, *args):
        return pl.pallas_call(
            kernel,
            in_specs=in_specs,
            out_specs=[vmem] * len(outs),
            out_shape=[jax.ShapeDtypeStruct(shape, dtype) for shape, dtype in outs],
            scratch_shapes=scratch,
            compiler_params=pltpu.CompilerParams(vmem_limit_bytes=24 * MEGA),
            name=name,
        )(*(pltpu.with_memory_space_constraint(a, pltpu.HBM) if s is hbm else a for s, a in zip(in_specs, args)))

    half, full = jnp.bfloat16, jnp.float32
    shift = shift_table()
    side_shape = ((ROWS, 4 * pts + LEAVES), half)
    given_shape = ((ROWS, 4 * pts + LEAVES + 2 * SLOT), half)
    faces_shape = ((ROWS, points + LEAVES), half)
    even_shape = ((ROWS, points + LEAVES + 2 * SLOT * ACROSS), half)
    rows_shape = ((ROWS, 2 * SLOT * ACROSS), half)
    both_shape = ((ROWS, 4 * SLOT * ACROSS), half)
    near_shape, sums_shape = ((ROWS, points), full), ((ROWS, LEAVES), full)
    rows_scratch = pltpu.VMEM((8 * pts, FEATURES), half)
    own, basis, moments, totals, *given = call(
        pack_kernel,
        "pack",
        [hbm] * 4,
        [
            ((ROWS, points), half),
            ((2 * SLOT, points), half),
            ((ROWS, LEAVES), half),
            ((ROWS, 2 * SLOT), half),
            given_shape,
            given_shape,
        ],
        [
            pltpu.SMEM((8,), jnp.int32),
            pltpu.VMEM((3, points), full),
            pltpu.VMEM((fields, points), half),
            pltpu.VMEM((LEAVES, SLOT), half),
            pltpu.VMEM((SLOT, 8, pts), full),
            pltpu.SemaphoreType.DMA((4,)),
        ],
        leaf_count,
        positions,
        density,
        jnp.asarray(shift, half),
    )
    from_2 = swapped(totals, "space", lambda i: i ^ 2)
    from_1 = swapped(given[0], "space", lambda i: i ^ 1)
    from_3 = swapped(given[1], "space", lambda i: i ^ 3)
    near, source, target, scale, column, columns, far, spread = call(
        functools.partial(own_kernel, depth),
        "near_own",
        [hbm] * 2 + [vmem] + [hbm] * 3,
        [
            ((ROWS, EARLY * points // 4), full),
            ((points, FEATURES), half),
            ((FEATURES, points), half),
            ((1, points), full),
            ((ROWS, 128), full),
            ((ACROSS * depth * SLOT, SLOT), half),
            ((len(STEPS) * LEAVES, LEAVES), half),
            ((SLOT, LEAVES), half),
        ],
        [
            pltpu.VMEM((3, SLOT, SLOT), full),
            pltpu.SMEM((8,), jnp.int32),
            pltpu.SMEM((fields,), full),
            pltpu.SemaphoreType.DMA((5,)),
        ],
        leaf_count,
        sigma_weights,
        own,
        jnp.asarray(far_table(), half),
        jnp.asarray(shift.T.copy(), half),
        jnp.asarray(box_nodes()),
    )
    left, right, same, other, faces_even, rows = call(
        row_kernel,
        "row",
        [vmem] * 7,
        [side_shape, side_shape, sums_shape, sums_shape, even_shape, rows_shape],
        [],
        own,
        moments,
        totals,
        from_1,
        from_2,
        from_3,
        far,
    )
    faces_even = swapped(faces_even, "space", lambda i: i ^ ACROSS)
    near, faces_odd = call(
        middle_kernel,
        "near_middle",
        [vmem] * 7,
        [near_shape, faces_shape],
        [],
        own,
        left,
        right,
        other,
        near,
        source,
        target,
    )
    faces_odd = swapped(faces_odd, "space", lambda i: i + ACROSS if i // ACROSS % 2 else i - ACROSS)
    near, both = call(
        side_kernel,
        "near_side",
        [vmem] * 6,
        [near_shape, both_shape],
        [pltpu.VMEM((4 * pts, FEATURES), half)] * 2,
        left,
        right,
        near,
        target,
        rows,
        faces_even,
    )
    if depth == 4:
        held = [rows, swapped(both, "space", lambda i: i ^ (2 * ACROSS))]
    else:
        groups = [[z * ACROSS + x for z in range(depth)] for x in range(ACROSS)]
        held = [lax.all_gather(rows, "space", axis_index_groups=groups)]
    near, = call(even_kernel, "near_even", [vmem] * 3, [near_shape], [rows_scratch], near, target, faces_even)
    potential, sums = call(
        functools.partial(last_kernel, depth),
        "near_odd",
        [vmem] * (10 + len(held)),
        [((fields, points), full), ((1, points + 128), full)],
        [pltpu.VMEM((ROWS, points), full), rows_scratch],
        near,
        target,
        faces_even,
        faces_odd,
        basis,
        scale,
        column,
        columns,
        spread,
        same,
        *held,
    )
    if lax.axis_size("sig") == 2:
        other = swapped(sums, "sig", lambda i: i ^ 1)
    else:
        other = lax.psum(sums, "sig") - sums
    mean, = call(mean_kernel, "mean", [vmem] * 2, [((1, points), full)], [], sums, other)
    return potential, mean.reshape(points)


def solution(mesh):
    in_specs = (P(None, "space"), P("sig", "space"), P("space"), P("sig"))
    out_specs = (P("sig", "space"), P("space"))
    return jax.shard_map(per_device, mesh=mesh, in_specs=in_specs, out_specs=out_specs, check_vma=False)
```

```python
import functools
import math

import jax
import jax.numpy as jnp
import numpy as np
from jax import lax
from jax.experimental import pallas as pl
from jax.experimental.pallas import tpu as pltpu
from jax.sharding import PartitionSpec as P

ORDER = 5
SOFTENING = 0.1
ACROSS = 4
SLOT = 64
ROWS = 24
LEAVES = 8 * SLOT
MEGA = 1024 * 1024
FEATURES = 48
EARLY = 2


def exponent_table(order_max):
    entries_list = []
    for degree in range(order_max + 1):
        for first_power in range(degree, -1, -1):
            for second_power in range(degree - first_power, -1, -1):
                entries_list.append((first_power, second_power, degree - first_power - second_power))
    return entries_list


def node_table(count_nodes, offset_value):
    counter = np.arange(1, count_nodes + 1, dtype=np.float32)[:, None]
    stride_set = np.array([0.7548776662466927, 0.5698402909980532, 0.4142135623730951], dtype=np.float32)[None, :]
    unit_points = np.mod(counter * stride_set + np.float32(offset_value), np.float32(1.0))
    return (np.float32(2.0) * unit_points - np.float32(1.0)).astype(np.float32)


EXPONENTS = exponent_table(ORDER)
COEFFS = len(EXPONENTS)
CHECK = node_table(COEFFS, 0.5).astype(np.float64)
EQUIV = node_table(COEFFS, 0.0).astype(np.float64)
STEPS = [(sx, sz) for sz in (-1, 0, 1) for sx in (-1, 0, 1) if sx != 0 or sz != 0]


def bits(octant):
    return octant % 2, octant // 2 % 2, octant // 4


def leaf_slot(octant):
    bit_x, bit_y, bit_z = bits(octant)
    return (bit_x + 2 * bit_z) * 2 + bit_y


@functools.lru_cache(None)
def far_table():
    shape = (len(STEPS), 8, SLOT, 8, SLOT)
    table = np.zeros(shape)
    gap_nodes = 0.5 * (CHECK[None, :, :] - EQUIV[:, None, :])
    for index, (step_x, step_z) in enumerate(STEPS):
        for source in range(8):
            for target in range(8):
                s, t = bits(source), bits(target)
                gap = np.array([2 * step_x + s[0] - t[0], s[1] - t[1], 2 * step_z + s[2] - t[2]], np.float64)
                if max(abs(gap[0]), abs(gap[2])) >= 2:
                    shifted = gap_nodes - gap
                    value = 1.0 / np.sqrt(np.sum(shifted * shifted, -1) + SOFTENING * SOFTENING) / COEFFS
                    table[index, source, :COEFFS, target, :COEFFS] = value
    return table.reshape(len(STEPS) * LEAVES, LEAVES)


@functools.lru_cache(None)
def shift_table():
    table = np.zeros((8, SLOT, SLOT))
    for leaf in range(8):
        offset = [bit - 0.5 for bit in bits(leaf)]
        for k, target in enumerate(EXPONENTS):
            for i, source in enumerate(EXPONENTS):
                if all(b <= a for a, b in zip(target, source)):
                    value = 1.0
                    for a, b, h in zip(target, source, offset):
                        value *= math.comb(a, b) * 0.5**b * h ** (a - b)
                    table[leaf, i, k] = value
    return table.reshape(8 * SLOT, SLOT)


@functools.lru_cache(None)
def box_nodes():
    gaps = np.zeros((3, SLOT, SLOT))
    gaps[:, :COEFFS, :COEFFS] = np.moveaxis(CHECK[None, :, :] - EQUIV[:, None, :], -1, 0)
    gaps[1] = gaps[1] ** 2 + SOFTENING * SOFTENING
    return gaps.astype(np.float32)


def dot(left, right):
    return jnp.dot(left, right, preferred_element_type=jnp.float32)


def dot_nt(left, right):
    return lax.dot_general(left, right, (((1,), (1,)), ((), ())), preferred_element_type=jnp.float32)


def low_bits(value):
    return value.astype(jnp.bfloat16)


def high_low(value):
    high = low_bits(value)
    return high, low_bits(value - high.astype(jnp.float32))


def by_row(values, shape):
    row = lax.broadcasted_iota(jnp.int32, shape, 0)
    result = jnp.zeros(shape, jnp.float32)
    for index, value in enumerate(values):
        result = jnp.where(row == index, value, result)
    return result


def box_place():
    label = lax.axis_index("space")
    return lax.rem(label, ACROSS), lax.div(label, ACROSS)


def lanes(start, size):
    return pl.ds(start if isinstance(start, int) else pl.multiple_of(start, 128), size)


def fetch(pairs, sems):
    copies = [pltpu.make_async_copy(src, dst, sems.at[i]) for i, (src, dst) in enumerate(pairs)]
    for copy in copies:
        copy.start()
    return copies


def pack_kernel(count_in, positions_in, density_in, shift_in, own, basis, moments, totals, *rest):
    payloads, (count, positions, density, shift, mono, sems) = rest[:2], rest[2:]
    copies = fetch(
        [(count_in, count), (positions_in, positions), (density_in, density), (shift_in, shift)], sems
    )
    fields, points = density.shape
    pts = points // 8
    box_x, box_z = box_place()
    for copy in copies:
        copy.wait()
    local = []
    for leaf in range(8):
        bit_x, bit_y, bit_z = bits(leaf)
        centre = by_row(
            [2.0 * box_x.astype(jnp.float32) + (bit_x + 0.5), bit_y + 0.5, 2.0 * box_z.astype(jnp.float32) + (bit_z + 0.5)],
            (3, 1),
        )
        here = slice(leaf * pts, (leaf + 1) * pts)
        offset = positions[:, here] - centre
        local.append(offset)
        high = low_bits(offset).astype(jnp.float32)
        middle = low_bits(offset - high).astype(jnp.float32)
        raw = density[:, here].astype(jnp.float32)
        mass = jnp.where(lax.broadcasted_iota(jnp.int32, raw.shape, 1) < count[leaf], raw, 0.0)
        spare = jnp.zeros((ROWS - fields - 6, pts), jnp.float32)
        own[:, here] = low_bits(jnp.concatenate([mass, high, middle, spare], axis=0))

    axes = [2.0 * jnp.concatenate([part[a : a + 1] for part in local], axis=0) for a in range(3)]
    made = {(0, 0, 0): jnp.ones((8, pts), jnp.float32)}
    for k, powers in enumerate(EXPONENTS):
        if powers not in made:
            a = next(i for i in range(3) if powers[i] > 0)
            before = tuple(p - (i == a) for i, p in enumerate(powers))
            made[powers] = made[before] * axes[a]
        mono[k] = made[powers]
    mono[COEFFS:SLOT] = jnp.zeros((SLOT - COEFFS, 8, pts), jnp.float32)
    parts = []
    for leaf in range(8):
        here = slice(leaf * pts, (leaf + 1) * pts)
        high, low = high_low(mono[:, leaf, :])
        basis[0:SLOT, here] = high
        basis[SLOT:, here] = low
        parts.append(dot_nt(own[:, here], high))
    moment, rest = high_low(jnp.concatenate(parts, axis=1))
    moments[...] = moment
    total = dot(moment, shift[...]) + dot(rest, shift[...])
    total = jnp.concatenate(high_low(total), axis=1)
    totals[...] = total
    for distance, payload in zip((1, 3), payloads):
        bit = jnp.where((box_x ^ distance) > box_x, 1, 0)
        for place in range(4):
            payload[:, lanes(place * pts, pts)] = own[:, lanes((bit + 2 * place) * pts, pts)]
        payload[:, lanes(4 * pts, LEAVES)] = moment
        payload[:, lanes(4 * pts + LEAVES, 2 * SLOT)] = total


def features(held, start, size, centre, target):
    value = held[16:ROWS, lanes(start, size)].astype(jnp.float32)
    x = value[1:4] + value[4:7] + by_row(centre, (3, 1))
    norm = jnp.sum(x * x, axis=0, keepdims=True)
    if target:
        norm = norm + SOFTENING * SOFTENING
    parts, norms = [], []
    for source, out in ((x, parts), (norm, norms)):
        left = source
        for _ in range(3):
            high = low_bits(left).astype(jnp.float32)
            out.append(high)
            left = left - high
    one = jnp.ones_like(norm)
    zero = jnp.zeros_like(norm)
    blank = jnp.zeros((3, norm.shape[1]), jnp.float32)
    blocks = []
    order = (0, 1, 0, 2, 0, 1) if target else (0, 0, 1, 0, 2, 1)
    for index, which in enumerate(order):
        coords = -2.0 * parts[which] if target else parts[which]
        if index < 3:
            pair = [one, norms[index]] if target else [norms[index], one]
        else:
            pair = [zero, zero]
        blocks += [coords, *pair, blank]
    return jnp.concatenate(blocks, axis=0)


def source_features(held, start, size, centre):
    return low_bits(jnp.transpose(features(held, start, size, centre, False)))


def pulled(near, jobs, target, size, first=None):
    width = target.shape[1] // 8
    tiles = []
    for group, source, masses, starts in jobs:
        for piece in range(2):
            here = lanes((2 * group + piece) * width, width)
            for turn, start in enumerate(starts):
                tiles.append((here, source, masses, lanes(start, size), turn == 0, turn + 1 == len(starts)))

    def squares(tile):
        return dot(tile[1][tile[3], :], target[:, tile[0]])

    ahead, kernel, total = squares(tiles[0]), None, None
    for turn in range(len(tiles) + 1):
        square = ahead
        if turn + 1 < len(tiles):
            ahead = squares(tiles[turn + 1])
        if turn > 0:
            here, _, masses, place, opens, closes = tiles[turn - 1]
            if opens:
                total = jnp.zeros((ROWS, width), jnp.float32) if first is None else first[:, here]
            total = total + dot(masses[:, place], kernel)
            if closes:
                near[:, here] = total
        if turn < len(tiles):
            kernel = low_bits(lax.rsqrt(square))


def own_groups(near, first, last, target, source, own):
    pts = source.shape[0] // 8
    starts = [2 * p * pts for p in range(4)]
    pulled(near, [(group, source, own, starts) for group in range(first, last)], target, 2 * pts)


def box_columns(depth, box_x, box_z, nodes):
    blocks = []
    for turn, distance in [(turn, distance) for turn in range(depth) for distance in range(ACROSS)]:
        gap_x = 2 * (box_x - (box_x ^ distance))
        gap_z = 2 * (box_z - ((box_z ^ turn) if depth == 4 else turn))
        across_x = nodes[0] + gap_x.astype(jnp.float32)
        across_z = nodes[2] + gap_z.astype(jnp.float32)
        apart = jnp.maximum(jnp.abs(gap_x), jnp.abs(gap_z)) >= 4
        value = lax.rsqrt(across_x * across_x + across_z * across_z + nodes[1])
        blocks.append(low_bits(value * jnp.where(apart, 1.0 / COEFFS, 0.0)))
    return jnp.concatenate(blocks, axis=0)


def own_kernel(depth, count_in, weights_in, own, *rest):
    tables, outs, rest = rest[:3], rest[3:11], rest[11:]
    near, source, target, scale, column, columns, far, spread = outs
    nodes, count, weights, sems = rest
    copies = fetch([*zip(tables, (far, spread, nodes)), (count_in, count), (weights_in, weights)], sems)
    points = own.shape[1]
    pts = points // 8
    for leaf in range(8):
        centre = [bit - 0.5 for bit in bits(leaf)]
        source[lanes(leaf * pts, pts), :] = source_features(own, leaf * pts, pts, centre)
        target[:, lanes(leaf_slot(leaf) * pts, pts)] = low_bits(features(own, leaf * pts, pts, centre, True))
    own_groups(near, 0, EARLY, target, source, own)
    for copy in copies:
        copy.wait()
    columns[...] = box_columns(depth, *box_place(), nodes)
    column[...] = by_row([weights[field] for field in range(weights.shape[0])], column.shape)
    lane_index = lax.broadcasted_iota(jnp.int32, (1, pts), 1)
    for leaf in range(8):
        scale[:, leaf * pts : (leaf + 1) * pts] = jnp.where(lane_index < count[leaf], 1.0 / (128.0 * pts), 0.0)


def spread_first(value, node):
    starts = [leaf * SLOT + node for leaf in range(8)]
    return jnp.concatenate([jnp.broadcast_to(value[:, s : s + 1], (ROWS, SLOT)) for s in starts], axis=1)


def decoded(coded):
    value = coded.astype(jnp.float32)
    node = lax.broadcasted_iota(jnp.int32, value.shape, 1) % SLOT
    return jnp.where(node == 0, 0.0, value) + spread_first(value, 0) + spread_first(value, COEFFS)


def faces_of(faces, bit, given, own, left, right, rows=None):
    points = own.shape[1]
    pts = points // 8
    for y in range(2):
        for x in range(4):
            place = lanes((2 * x + y) * pts, pts)
            if x in (0, 3):
                side = left if x == 0 else right
                faces[:, place] = side[:, lanes((y + 2 * bit) * pts, pts)]
            else:
                faces[:, place] = own[:, lanes((x - 1 + 2 * y + 4 * bit) * pts, pts)]
    node = lax.broadcasted_iota(jnp.int32, given.shape, 1) % SLOT
    base = spread_first(given, 0)
    base_high = low_bits(base).astype(jnp.float32)
    coded = jnp.where(node == 0, base_high, jnp.where(node == COEFFS, base - base_high, given - base))
    faces[:, lanes(points, LEAVES)] = low_bits(coded)
    if rows is not None:
        faces[:, lanes(points + LEAVES, rows.shape[1])] = rows


def row_kernel(own, moments, totals, from_1, from_2, from_3, far, left, right, same, other, faces_even, rows):
    points = own.shape[1]
    pts = points // 8
    box_x, box_z = box_place()
    for side, step in ((left, -1), (right, 1)):
        side[...] = jnp.zeros(side.shape, side.dtype)
        for distance, held in ((1, from_1), (3, from_3)):

            @pl.when((box_x ^ distance) - box_x == step)
            def _(side=side, held=held):
                side[...] = held[:, lanes(0, side.shape[1])]

    base = 4 * pts
    ends = lanes(base + LEAVES, 2 * SLOT)
    row = jnp.concatenate([totals[...], from_1[:, ends], from_2[...], from_3[:, ends]], axis=1)
    rows[...] = row
    around = jnp.concatenate([left[:, lanes(base, LEAVES)], moments[...], right[:, lanes(base, LEAVES)]], axis=1)
    below_rows, same_rows, above_rows = pl.ds(0, 3 * LEAVES), pl.ds(3 * LEAVES, 2 * LEAVES), pl.ds(5 * LEAVES, 3 * LEAVES)
    up = dot(around, far[below_rows, :])
    down = dot(around, far[above_rows, :])
    same[...] = dot(jnp.concatenate([around[:, :LEAVES], around[:, 2 * LEAVES :]], axis=1), far[same_rows, :])
    odd = lax.rem(box_z, 2)
    faces_of(faces_even, 1 - odd, jnp.where(odd == 0, up, down), own, left, right, row)
    other[...] = jnp.where(odd == 0, down, up)


def middle_kernel(own, left, right, other, early, source, target, near, faces_odd):
    points = own.shape[1]
    _, box_z = box_place()
    faces_of(faces_odd, lax.rem(box_z, 2), other[...], own, left, right)
    near[:, lanes(0, EARLY * points // 4)] = early[...]
    own_groups(near, EARLY, 4, target, source, own)


def side_kernel(left, right, early, target, rows, faces_even, near, both, sides_left, sides_right):
    pts = early.shape[1] // 8
    width = rows.shape[1]
    both[:, lanes(0, width)] = rows[...]
    both[:, lanes(width, width)] = faces_even[:, lanes(faces_even.shape[1] - width, width)]
    jobs = []
    for step, side, held in ((0, left, sides_left), (1, right, sides_right)):
        for place in range(4):
            centre = (1.5 if step else -1.5, place % 2 - 0.5, place // 2 - 0.5)
            held[lanes(place * pts, pts), :] = source_features(side, place * pts, pts, centre)
        jobs += [(step, held, side, [0, 2 * pts]), (step + 2, held, side, [0, 2 * pts])]
    pulled(near, jobs, target, 2 * pts, early)


def layer_pulls(near, early, step, inside, target, faces, sides):
    points = early.shape[1]
    pts = points // 8

    @pl.when(inside)
    def _():
        for place in range(8):
            height = jnp.where(step == 1, 1.5, -1.5)
            centre = (place // 2 - 1.5, place % 2 - 0.5, height)
            sides[lanes(place * pts, pts), :] = source_features(faces, place * pts, pts, centre)

        jobs = [(i + 2 * step, sides, faces, [2 * (x + i) * pts for x in range(3)]) for i in range(2)]
        pulled(near, jobs, target, 2 * pts, early)

    @pl.when(jnp.logical_not(inside))
    def _():
        here = lanes(step * (points // 2), points // 2)
        near[:, here] = early[:, here]


def even_kernel(early, target, faces, near, sides):
    _, box_z = box_place()
    points = early.shape[1]
    step = 1 - lax.rem(box_z, 2)
    other = lanes((1 - step) * (points // 2), points // 2)
    near[:, other] = early[:, other]
    layer_pulls(near, early, step, box_z >= 0, target, faces, sides)


def last_kernel(depth, early, target, faces_even, faces_odd, basis, scale, column, columns, spread, same, *rest):
    held, (potential, sums, near, sides) = rest[:-4], rest[-4:]
    fields, points = potential.shape
    pts = points // 8
    _, box_z = box_place()
    step = lax.rem(box_z, 2)
    other = lanes((1 - step) * (points // 2), points // 2)
    near[:, other] = early[:, other]
    inside = (box_z + 2 * step - 1 >= 0) & (box_z + 2 * step - 1 < depth)
    layer_pulls(near, early, step, inside, target, faces_odd, sides)

    if depth == 4:
        rows, distant = held
        width = rows.shape[1]
        near_rows = faces_even[:, lanes(faces_even.shape[1] - width, width)]
        layers = [rows[...], near_rows, distant[:, lanes(0, width)], distant[:, lanes(width, width)]]
    else:
        layers = [held[0][layer] for layer in range(depth)]
    pieces = [layer[:, 2 * SLOT * turn : 2 * SLOT * (turn + 1)] for layer in layers for turn in range(ACROSS)]
    totals_high = jnp.concatenate([piece[:, :SLOT] for piece in pieces], axis=1)
    totals_low = jnp.concatenate([piece[:, SLOT:] for piece in pieces], axis=1)
    coarse_high, coarse_low = high_low(dot(totals_high, columns[...]) + dot(totals_low, columns[...]))
    value = same[...] + dot(coarse_high, spread[...]) + dot(coarse_low, spread[...])
    value = value + decoded(faces_even[:, lanes(points, LEAVES)])
    value = value + jnp.where(inside, decoded(faces_odd[:, lanes(points, LEAVES)]), 0.0)
    local_high, local_low = high_low(value)
    weight = column[0:fields, 0:1]
    for leaf in range(8):
        here = slice(leaf * pts, (leaf + 1) * pts)
        slot = slice(leaf * SLOT, (leaf + 1) * SLOT)
        doubled = jnp.concatenate([local_high[:, slot], local_high[:, slot]], axis=1)
        far_part = dot(doubled, basis[:, here]) + dot(local_low[:, slot], basis[0:SLOT, here])
        total = near[0:fields, lanes(leaf_slot(leaf) * pts, pts)] + far_part[:fields]
        total = total * scale[:, here]
        potential[:, here] = total
        sums[:, here] = jnp.sum(total * weight, axis=0, keepdims=True)
    sums[:, points:] = jnp.broadcast_to(jnp.sum(weight), (1, sums.shape[1] - points))


def mean_kernel(mine, other, mean):
    points = mean.shape[1]
    total = mine[...] + other[...]
    mean[...] = total[:, :points] / total[:, points : points + 1]


def swapped(block, axis, partner):
    size = lax.axis_size(axis)
    return lax.ppermute(block, axis, [(partner(i), i) for i in range(size)])


def swapped_odd(block):
    boxes, cores = lax.axis_size("space"), lax.axis_size("sig")
    pairs = []
    for box in range(boxes):
        other = box + ACROSS if box // ACROSS % 2 else box - ACROSS
        for core in range(cores):
            source = other * cores + core if 0 <= other < boxes else box * cores + (core ^ 1)
            pairs.append((source, box * cores + core))
    return lax.ppermute(block, ("space", "sig"), pairs)


def per_device(positions, density, leaf_count, sigma_weights):
    fields, points = density.shape
    pts = points // 8
    depth = lax.axis_size("space") // ACROSS
    vmem, hbm = pl.BlockSpec(memory_space=pltpu.VMEM), pl.BlockSpec(memory_space=pltpu.HBM)

    def call(kernel, name, in_specs, outs, scratch, *args):
        return pl.pallas_call(
            kernel,
            in_specs=in_specs,
            out_specs=[vmem] * len(outs),
            out_shape=[jax.ShapeDtypeStruct(shape, dtype) for shape, dtype in outs],
            scratch_shapes=scratch,
            compiler_params=pltpu.CompilerParams(vmem_limit_bytes=24 * MEGA),
            name=name,
        )(*(pltpu.with_memory_space_constraint(a, pltpu.HBM) if s is hbm else a for s, a in zip(in_specs, args)))

    half, full = jnp.bfloat16, jnp.float32
    shift = shift_table()
    side_shape = ((ROWS, 4 * pts + LEAVES), half)
    given_shape = ((ROWS, 4 * pts + LEAVES + 2 * SLOT), half)
    faces_shape = ((ROWS, points + LEAVES), half)
    even_shape = ((ROWS, points + LEAVES + 2 * SLOT * ACROSS), half)
    rows_shape = ((ROWS, 2 * SLOT * ACROSS), half)
    both_shape = ((ROWS, 4 * SLOT * ACROSS), half)
    near_shape, sums_shape = ((ROWS, points), full), ((ROWS, LEAVES), full)
    rows_scratch = pltpu.VMEM((8 * pts, FEATURES), half)
    own, basis, moments, totals, *given = call(
        pack_kernel,
        "pack",
        [hbm] * 4,
        [
            ((ROWS, points), half),
            ((2 * SLOT, points), half),
            ((ROWS, LEAVES), half),
            ((ROWS, 2 * SLOT), half),
            given_shape,
            given_shape,
        ],
        [
            pltpu.SMEM((8,), jnp.int32),
            pltpu.VMEM((3, points), full),
            pltpu.VMEM((fields, points), half),
            pltpu.VMEM((LEAVES, SLOT), half),
            pltpu.VMEM((SLOT, 8, pts), full),
            pltpu.SemaphoreType.DMA((4,)),
        ],
        leaf_count,
        positions,
        density,
        jnp.asarray(shift, half),
    )
    from_2 = swapped(totals, "space", lambda i: i ^ 2)
    from_1 = swapped(given[0], "space", lambda i: i ^ 1)
    from_3 = swapped(given[1], "space", lambda i: i ^ 3)
    near, source, target, scale, column, columns, far, spread = call(
        functools.partial(own_kernel, depth),
        "near_own",
        [hbm] * 2 + [vmem] + [hbm] * 3,
        [
            ((ROWS, EARLY * points // 4), full),
            ((points, FEATURES), half),
            ((FEATURES, points), half),
            ((1, points), full),
            ((ROWS, 128), full),
            ((ACROSS * depth * SLOT, SLOT), half),
            ((len(STEPS) * LEAVES, LEAVES), half),
            ((SLOT, LEAVES), half),
        ],
        [
            pltpu.VMEM((3, SLOT, SLOT), full),
            pltpu.SMEM((8,), jnp.int32),
            pltpu.SMEM((fields,), full),
            pltpu.SemaphoreType.DMA((5,)),
        ],
        leaf_count,
        sigma_weights,
        own,
        jnp.asarray(far_table(), half),
        jnp.asarray(shift.T.copy(), half),
        jnp.asarray(box_nodes()),
    )
    left, right, same, other, faces_even, rows = call(
        row_kernel,
        "row",
        [vmem] * 7,
        [side_shape, side_shape, sums_shape, sums_shape, even_shape, rows_shape],
        [],
        own,
        moments,
        totals,
        from_1,
        from_2,
        from_3,
        far,
    )
    faces_even = swapped(faces_even, "space", lambda i: i ^ ACROSS)
    near, faces_odd = call(
        middle_kernel,
        "near_middle",
        [vmem] * 7,
        [near_shape, faces_shape],
        [],
        own,
        left,
        right,
        other,
        near,
        source,
        target,
    )
    faces_odd = swapped_odd(faces_odd)
    near, both = call(
        side_kernel,
        "near_side",
        [vmem] * 6,
        [near_shape, both_shape],
        [pltpu.VMEM((4 * pts, FEATURES), half)] * 2,
        left,
        right,
        near,
        target,
        rows,
        faces_even,
    )
    if depth == 4:
        held = [rows, swapped(both, "space", lambda i: i ^ (2 * ACROSS))]
    else:
        groups = [[z * ACROSS + x for z in range(depth)] for x in range(ACROSS)]
        held = [lax.all_gather(rows, "space", axis_index_groups=groups)]
    near, = call(even_kernel, "near_even", [vmem] * 3, [near_shape], [rows_scratch], near, target, faces_even)
    potential, sums = call(
        functools.partial(last_kernel, depth),
        "near_odd",
        [vmem] * (10 + len(held)),
        [((fields, points), full), ((1, points + 128), full)],
        [pltpu.VMEM((ROWS, points), full), rows_scratch],
        near,
        target,
        faces_even,
        faces_odd,
        basis,
        scale,
        column,
        columns,
        spread,
        same,
        *held,
    )
    if lax.axis_size("sig") == 2:
        other = swapped(sums, "sig", lambda i: i ^ 1)
    else:
        other = lax.psum(sums, "sig") - sums
    mean, = call(mean_kernel, "mean", [vmem] * 2, [((1, points), full)], [], sums, other)
    return potential, mean.reshape(points)


def solution(mesh):
    in_specs = (P(None, "space"), P("sig", "space"), P("space"), P("sig"))
    out_specs = (P("sig", "space"), P("space"))
    return jax.shard_map(per_device, mesh=mesh, in_specs=in_specs, out_specs=out_specs, check_vma=False)
```

```python
import functools
import math

import jax
import jax.numpy as jnp
import numpy as np
from jax import lax
from jax.experimental import pallas as pl
from jax.experimental.pallas import tpu as pltpu
from jax.sharding import PartitionSpec as P

ORDER = 5
SOFTENING = 0.1
ACROSS = 4
SLOT = 64
ROWS = 24
LEAVES = 8 * SLOT
MEGA = 1024 * 1024
FEATURES = 48
EARLY = 3


def exponent_table(order_max):
    entries_list = []
    for degree in range(order_max + 1):
        for first_power in range(degree, -1, -1):
            for second_power in range(degree - first_power, -1, -1):
                entries_list.append((first_power, second_power, degree - first_power - second_power))
    return entries_list


def node_table(count_nodes, offset_value):
    counter = np.arange(1, count_nodes + 1, dtype=np.float32)[:, None]
    stride_set = np.array([0.7548776662466927, 0.5698402909980532, 0.4142135623730951], dtype=np.float32)[None, :]
    unit_points = np.mod(counter * stride_set + np.float32(offset_value), np.float32(1.0))
    return (np.float32(2.0) * unit_points - np.float32(1.0)).astype(np.float32)


EXPONENTS = exponent_table(ORDER)
COEFFS = len(EXPONENTS)
CHECK = node_table(COEFFS, 0.5).astype(np.float64)
EQUIV = node_table(COEFFS, 0.0).astype(np.float64)
HEAVY = [EXPONENTS.index(e) for e in ((0, 0, 0), (2, 0, 0), (0, 2, 0), (0, 0, 2), (4, 0, 0), (0, 4, 0), (0, 0, 4), (2, 0, 2))]
STEPS = [(sx, sz) for sz in (-1, 0, 1) for sx in (-1, 0, 1) if sx != 0 or sz != 0]


def bits(octant):
    return octant % 2, octant // 2 % 2, octant // 4


def leaf_slot(octant):
    bit_x, bit_y, bit_z = bits(octant)
    return (bit_x + 2 * bit_z) * 2 + bit_y


@functools.lru_cache(None)
def far_table():
    shape = (len(STEPS), 8, SLOT, 8, SLOT)
    table = np.zeros(shape)
    gap_nodes = 0.5 * (CHECK[None, :, :] - EQUIV[:, None, :])
    for index, (step_x, step_z) in enumerate(STEPS):
        for source in range(8):
            for target in range(8):
                s, t = bits(source), bits(target)
                gap = np.array([2 * step_x + s[0] - t[0], s[1] - t[1], 2 * step_z + s[2] - t[2]], np.float64)
                if max(abs(gap[0]), abs(gap[2])) >= 2:
                    shifted = gap_nodes - gap
                    value = 1.0 / np.sqrt(np.sum(shifted * shifted, -1) + SOFTENING * SOFTENING) / COEFFS
                    table[index, source, :COEFFS, target, :COEFFS] = value
    return table.reshape(len(STEPS) * LEAVES, LEAVES)


@functools.lru_cache(None)
def shift_table():
    table = np.zeros((8, SLOT, SLOT))
    for leaf in range(8):
        offset = [bit - 0.5 for bit in bits(leaf)]
        for k, target in enumerate(EXPONENTS):
            for i, source in enumerate(EXPONENTS):
                if all(b <= a for a, b in zip(target, source)):
                    value = 1.0
                    for a, b, h in zip(target, source, offset):
                        value *= math.comb(a, b) * 0.5**b * h ** (a - b)
                    table[leaf, i, k] = value
    return table.reshape(8 * SLOT, SLOT)


@functools.lru_cache(None)
def box_nodes():
    gaps = np.zeros((3, SLOT, SLOT))
    gaps[:, :COEFFS, :COEFFS] = np.moveaxis(CHECK[None, :, :] - EQUIV[:, None, :], -1, 0)
    gaps[:, COEFFS:] = gaps[:, HEAVY]
    gaps[1] = gaps[1] ** 2 + SOFTENING * SOFTENING
    return gaps.astype(np.float32)


def dot(left, right):
    return jnp.dot(left, right, preferred_element_type=jnp.float32)


def dot_nt(left, right):
    return lax.dot_general(left, right, (((1,), (1,)), ((), ())), preferred_element_type=jnp.float32)


def low_bits(value):
    return value.astype(jnp.bfloat16)


def heavy_table():
    table = np.zeros((SLOT, SLOT), np.float32)
    table[HEAVY, np.arange(COEFFS, SLOT)] = 1.0
    return table


def high_low(value):
    high = low_bits(value)
    return high, low_bits(value - high.astype(jnp.float32))


def by_row(values, shape):
    row = lax.broadcasted_iota(jnp.int32, shape, 0)
    result = jnp.zeros(shape, jnp.float32)
    for index, value in enumerate(values):
        result = jnp.where(row == index, value, result)
    return result


def box_place():
    label = lax.axis_index("space")
    return lax.rem(label, ACROSS), lax.div(label, ACROSS)


def lanes(start, size):
    return pl.ds(start if isinstance(start, int) else pl.multiple_of(start, 128), size)


def fetch(pairs, sems):
    copies = [pltpu.make_async_copy(src, dst, sems.at[i]) for i, (src, dst) in enumerate(pairs)]
    for copy in copies:
        copy.start()
    return copies


def pack_kernel(count_in, positions_in, density_in, shift_in, heavy_in, own, basis, moments, totals, *rest):
    payloads, (count, positions, density, shift, heavy, mono, sems) = rest[:2], rest[2:]
    copies = fetch(
        [(count_in, count), (positions_in, positions), (density_in, density), (shift_in, shift), (heavy_in, heavy)], sems
    )
    fields, points = density.shape
    pts = points // 8
    box_x, box_z = box_place()
    for copy in copies:
        copy.wait()
    local = []
    for leaf in range(8):
        bit_x, bit_y, bit_z = bits(leaf)
        centre = by_row(
            [2.0 * box_x.astype(jnp.float32) + (bit_x + 0.5), bit_y + 0.5, 2.0 * box_z.astype(jnp.float32) + (bit_z + 0.5)],
            (3, 1),
        )
        here = slice(leaf * pts, (leaf + 1) * pts)
        offset = positions[:, here] - centre
        local.append(offset)
        high = low_bits(offset).astype(jnp.float32)
        middle = low_bits(offset - high).astype(jnp.float32)
        raw = density[:, here].astype(jnp.float32)
        mass = jnp.where(lax.broadcasted_iota(jnp.int32, raw.shape, 1) < count[leaf], raw, 0.0)
        spare = jnp.zeros((ROWS - fields - 6, pts), jnp.float32)
        own[:, here] = low_bits(jnp.concatenate([mass, high, middle, spare], axis=0))

    axes = [2.0 * jnp.concatenate([part[a : a + 1] for part in local], axis=0) for a in range(3)]
    made = {(0, 0, 0): jnp.ones((8, pts), jnp.float32)}
    for k, powers in enumerate(EXPONENTS):
        if powers not in made:
            a = next(i for i in range(3) if powers[i] > 0)
            before = tuple(p - (i == a) for i, p in enumerate(powers))
            made[powers] = made[before] * axes[a]
        mono[k] = made[powers]
    mono[COEFFS:SLOT] = jnp.zeros((SLOT - COEFFS, 8, pts), jnp.float32)
    parts = []
    for leaf in range(8):
        here = slice(leaf * pts, (leaf + 1) * pts)
        high, low = high_low(mono[:, leaf, :])
        basis[0:SLOT, here] = high
        basis[SLOT:, here] = low
        parts.append(dot_nt(own[:, here], high))
    moment, rest = high_low(jnp.concatenate(parts, axis=1))
    moments[...] = moment
    total = dot(moment, shift[...]) + dot(rest, shift[...])
    total_high, total_low = high_low(total)
    total = low_bits(total_high.astype(jnp.float32) + dot(total_low, heavy[...]))
    total = jnp.concatenate([total, jnp.zeros_like(total)], axis=1)
    totals[...] = total
    for distance, payload in zip((1, 3), payloads):
        bit = jnp.where((box_x ^ distance) > box_x, 1, 0)
        for place in range(4):
            payload[:, lanes(place * pts, pts)] = own[:, lanes((bit + 2 * place) * pts, pts)]
        payload[:, lanes(4 * pts, LEAVES)] = moment
        payload[:, lanes(4 * pts + LEAVES, 2 * SLOT)] = total


def features(held, start, size, centre, target):
    value = held[16:ROWS, lanes(start, size)].astype(jnp.float32)
    x = value[1:4] + value[4:7] + by_row(centre, (3, 1))
    norm = jnp.sum(x * x, axis=0, keepdims=True)
    if target:
        norm = norm + SOFTENING * SOFTENING
    parts, norms = [], []
    for source, out in ((x, parts), (norm, norms)):
        left = source
        for _ in range(3):
            high = low_bits(left).astype(jnp.float32)
            out.append(high)
            left = left - high
    one = jnp.ones_like(norm)
    zero = jnp.zeros_like(norm)
    blank = jnp.zeros((3, norm.shape[1]), jnp.float32)
    blocks = []
    order = (0, 1, 0, 2, 0, 1) if target else (0, 0, 1, 0, 2, 1)
    for index, which in enumerate(order):
        coords = -2.0 * parts[which] if target else parts[which]
        if index < 3:
            pair = [one, norms[index]] if target else [norms[index], one]
        else:
            pair = [zero, zero]
        blocks += [coords, *pair, blank]
    return jnp.concatenate(blocks, axis=0)


def source_features(held, start, size, centre):
    return low_bits(jnp.transpose(features(held, start, size, centre, False)))


def pulled(near, jobs, target, size, first=None):
    width = target.shape[1] // 8
    tiles = []
    for group, source, masses, starts in jobs:
        for piece in range(2):
            here = lanes((2 * group + piece) * width, width)
            for turn, start in enumerate(starts):
                tiles.append((here, source, masses, lanes(start, size), turn == 0, turn + 1 == len(starts)))

    def squares(tile):
        return dot(tile[1][tile[3], :], target[:, tile[0]])

    ahead, kernel, total = squares(tiles[0]), None, None
    for turn in range(len(tiles) + 1):
        square = ahead
        if turn + 1 < len(tiles):
            ahead = squares(tiles[turn + 1])
        if turn > 0:
            here, _, masses, place, opens, closes = tiles[turn - 1]
            if opens:
                total = jnp.zeros((ROWS, width), jnp.float32) if first is None else first[:, here]
            total = total + dot(masses[:, place], kernel)
            if closes:
                near[:, here] = total
        if turn < len(tiles):
            kernel = low_bits(lax.rsqrt(square))


def own_groups(near, first, last, target, source, own):
    pts = source.shape[0] // 8
    starts = [2 * p * pts for p in range(4)]
    pulled(near, [(group, source, own, starts) for group in range(first, last)], target, 2 * pts)


def box_columns(depth, box_x, box_z, nodes):
    blocks = []
    for turn, distance in [(turn, distance) for turn in range(depth) for distance in range(ACROSS)]:
        gap_x = 2 * (box_x - (box_x ^ distance))
        gap_z = 2 * (box_z - ((box_z ^ turn) if depth == 4 else turn))
        across_x = nodes[0] + gap_x.astype(jnp.float32)
        across_z = nodes[2] + gap_z.astype(jnp.float32)
        apart = jnp.maximum(jnp.abs(gap_x), jnp.abs(gap_z)) >= 4
        value = lax.rsqrt(across_x * across_x + across_z * across_z + nodes[1])
        blocks.append(low_bits(value * jnp.where(apart, 1.0 / COEFFS, 0.0)))
    return jnp.concatenate(blocks, axis=0)


def own_kernel(depth, count_in, weights_in, own, *rest):
    tables, outs, rest = rest[:3], rest[3:11], rest[11:]
    near, source, target, scale, column, columns, far, spread = outs
    nodes, count, weights, sems = rest
    copies = fetch([*zip(tables, (far, spread, nodes)), (count_in, count), (weights_in, weights)], sems)
    points = own.shape[1]
    pts = points // 8
    for leaf in range(8):
        centre = [bit - 0.5 for bit in bits(leaf)]
        source[lanes(leaf * pts, pts), :] = source_features(own, leaf * pts, pts, centre)
        target[:, lanes(leaf_slot(leaf) * pts, pts)] = low_bits(features(own, leaf * pts, pts, centre, True))
    own_groups(near, 0, EARLY, target, source, own)
    for copy in copies:
        copy.wait()
    columns[...] = box_columns(depth, *box_place(), nodes)
    column[...] = by_row([weights[field] for field in range(weights.shape[0])], column.shape)
    lane_index = lax.broadcasted_iota(jnp.int32, (1, pts), 1)
    for leaf in range(8):
        scale[:, leaf * pts : (leaf + 1) * pts] = jnp.where(lane_index < count[leaf], 1.0 / (128.0 * pts), 0.0)


def spread_first(value, node):
    starts = [leaf * SLOT + node for leaf in range(8)]
    return jnp.concatenate([jnp.broadcast_to(value[:, s : s + 1], (ROWS, SLOT)) for s in starts], axis=1)


def decoded(coded):
    value = coded.astype(jnp.float32)
    node = lax.broadcasted_iota(jnp.int32, value.shape, 1) % SLOT
    return jnp.where(node == 0, 0.0, value) + spread_first(value, 0) + spread_first(value, COEFFS)


def faces_of(faces, bit, given, own, left, right, rows=None):
    points = own.shape[1]
    pts = points // 8
    for y in range(2):
        for x in range(4):
            place = lanes((2 * x + y) * pts, pts)
            if x in (0, 3):
                side = left if x == 0 else right
                faces[:, place] = side[:, lanes((y + 2 * bit) * pts, pts)]
            else:
                faces[:, place] = own[:, lanes((x - 1 + 2 * y + 4 * bit) * pts, pts)]
    node = lax.broadcasted_iota(jnp.int32, given.shape, 1) % SLOT
    base = spread_first(given, 0)
    base_high = low_bits(base).astype(jnp.float32)
    coded = jnp.where(node == 0, base_high, jnp.where(node == COEFFS, base - base_high, given - base))
    faces[:, lanes(points, LEAVES)] = low_bits(coded)
    if rows is not None:
        faces[:, lanes(points + LEAVES, rows.shape[1])] = rows


def sums_for(above, left, moments, right, far):
    base = left.shape[1] - LEAVES
    around = jnp.concatenate([left[:, lanes(base, LEAVES)], moments[...], right[:, lanes(base, LEAVES)]], axis=1)
    return dot(around, far[lanes(jnp.where(above == 1, 0, 5 * LEAVES), 3 * LEAVES), :])


def row_kernel(own, moments, totals, from_1, from_2, from_3, far, left, right, faces_even, rows):
    box_x, box_z = box_place()
    for side, step in ((left, -1), (right, 1)):
        side[...] = jnp.zeros(side.shape, side.dtype)
        for distance, held in ((1, from_1), (3, from_3)):

            @pl.when((box_x ^ distance) - box_x == step)
            def _(side=side, held=held):
                side[...] = held[:, lanes(0, side.shape[1])]

    ends = lanes(left.shape[1], 2 * SLOT)
    row = [totals[...], from_1[:, ends], from_2[...], from_3[:, ends]]
    row = jnp.concatenate([box[:, :SLOT] for box in row], axis=1)
    rows[...] = row
    above = 1 - lax.rem(box_z, 2)
    faces_of(faces_even, above, sums_for(above, left, moments, right, far), own, left, right, row)


def middle_kernel(own, left, right, moments, far, early, source, target, near, faces_odd, same):
    points = own.shape[1]
    _, box_z = box_place()
    above = lax.rem(box_z, 2)
    faces_of(faces_odd, above, sums_for(above, left, moments, right, far), own, left, right)
    base = left.shape[1] - LEAVES
    beside = jnp.concatenate([left[:, lanes(base, LEAVES)], right[:, lanes(base, LEAVES)]], axis=1)
    same[...] = dot(beside, far[lanes(3 * LEAVES, 2 * LEAVES), :])
    near[:, lanes(0, EARLY * points // 4)] = early[...]
    own_groups(near, EARLY, 4, target, source, own)


def side_kernel(left, right, early, target, rows, faces_even, near, both, sides_left, sides_right):
    pts = early.shape[1] // 8
    width = rows.shape[1]
    both[:, lanes(0, width)] = rows[...]
    both[:, lanes(width, width)] = faces_even[:, lanes(faces_even.shape[1] - width, width)]
    jobs = []
    for step, side, held in ((0, left, sides_left), (1, right, sides_right)):
        for place in range(4):
            centre = (1.5 if step else -1.5, place % 2 - 0.5, place // 2 - 0.5)
            held[lanes(place * pts, pts), :] = source_features(side, place * pts, pts, centre)
        jobs += [(step, held, side, [0, 2 * pts]), (step + 2, held, side, [0, 2 * pts])]
    pulled(near, jobs, target, 2 * pts, early)


def layer_pulls(near, early, step, inside, target, faces, sides):
    points = early.shape[1]
    pts = points // 8

    @pl.when(inside)
    def _():
        for place in range(8):
            height = jnp.where(step == 1, 1.5, -1.5)
            centre = (place // 2 - 1.5, place % 2 - 0.5, height)
            sides[lanes(place * pts, pts), :] = source_features(faces, place * pts, pts, centre)

        jobs = [(i + 2 * step, sides, faces, [2 * (x + i) * pts for x in range(3)]) for i in range(2)]
        pulled(near, jobs, target, 2 * pts, early)

    @pl.when(jnp.logical_not(inside))
    def _():
        here = lanes(step * (points // 2), points // 2)
        near[:, here] = early[:, here]


def even_kernel(early, target, faces, near, sides):
    _, box_z = box_place()
    points = early.shape[1]
    step = 1 - lax.rem(box_z, 2)
    other = lanes((1 - step) * (points // 2), points // 2)
    near[:, other] = early[:, other]
    layer_pulls(near, early, step, box_z >= 0, target, faces, sides)


def last_kernel(depth, early, target, faces_even, faces_odd, basis, scale, column, columns, spread, same, *rest):
    held, (potential, sums, near, sides) = rest[:-4], rest[-4:]
    fields, points = potential.shape
    pts = points // 8
    _, box_z = box_place()
    step = lax.rem(box_z, 2)
    other = lanes((1 - step) * (points // 2), points // 2)
    near[:, other] = early[:, other]
    inside = (box_z + 2 * step - 1 >= 0) & (box_z + 2 * step - 1 < depth)
    layer_pulls(near, early, step, inside, target, faces_odd, sides)

    if depth == 4:
        rows, distant = held
        width = rows.shape[1]
        near_rows = faces_even[:, lanes(faces_even.shape[1] - width, width)]
        layers = [rows[...], near_rows, distant[:, lanes(0, width)], distant[:, lanes(width, width)]]
    else:
        layers = [held[0][layer] for layer in range(depth)]
    coarse_high, coarse_low = high_low(dot(jnp.concatenate(layers, axis=1), columns[...]))
    value = same[...] + dot(coarse_high, spread[...]) + dot(coarse_low, spread[...])
    value = value + decoded(faces_even[:, lanes(points, LEAVES)])
    value = value + jnp.where(inside, decoded(faces_odd[:, lanes(points, LEAVES)]), 0.0)
    local_high, local_low = high_low(value)
    weight = column[0:fields, 0:1]
    for leaf in range(8):
        here = slice(leaf * pts, (leaf + 1) * pts)
        slot = slice(leaf * SLOT, (leaf + 1) * SLOT)
        doubled = jnp.concatenate([local_high[:, slot], local_high[:, slot]], axis=1)
        far_part = dot(doubled, basis[:, here]) + dot(local_low[:, slot], basis[0:SLOT, here])
        total = near[0:fields, lanes(leaf_slot(leaf) * pts, pts)] + far_part[:fields]
        total = total * scale[:, here]
        potential[:, here] = total
        sums[:, here] = jnp.sum(total * weight, axis=0, keepdims=True)
    sums[:, points:] = jnp.broadcast_to(jnp.sum(weight), (1, sums.shape[1] - points))


def mean_kernel(mine, other, mean):
    points = mean.shape[1]
    total = mine[...] + other[...]
    mean[...] = total[:, :points] / total[:, points : points + 1]


def swapped(block, axis, partner):
    size = lax.axis_size(axis)
    return lax.ppermute(block, axis, [(partner(i), i) for i in range(size)])


def swapped_odd(block):
    boxes, cores = lax.axis_size("space"), lax.axis_size("sig")
    pairs = []
    for box in range(boxes):
        other = box + ACROSS if box // ACROSS % 2 else box - ACROSS
        for core in range(cores):
            source = other * cores + core if 0 <= other < boxes else box * cores + (core ^ 1)
            pairs.append((source, box * cores + core))
    return lax.ppermute(block, ("space", "sig"), pairs)


def per_device(positions, density, leaf_count, sigma_weights):
    fields, points = density.shape
    pts = points // 8
    depth = lax.axis_size("space") // ACROSS
    vmem, hbm = pl.BlockSpec(memory_space=pltpu.VMEM), pl.BlockSpec(memory_space=pltpu.HBM)

    def call(kernel, name, in_specs, outs, scratch, *args):
        return pl.pallas_call(
            kernel,
            in_specs=in_specs,
            out_specs=[vmem] * len(outs),
            out_shape=[jax.ShapeDtypeStruct(shape, dtype) for shape, dtype in outs],
            scratch_shapes=scratch,
            compiler_params=pltpu.CompilerParams(vmem_limit_bytes=24 * MEGA),
            name=name,
        )(*(pltpu.with_memory_space_constraint(a, pltpu.HBM) if s is hbm else a for s, a in zip(in_specs, args)))

    half, full = jnp.bfloat16, jnp.float32
    shift = shift_table()
    side_shape = ((ROWS, 4 * pts + LEAVES), half)
    given_shape = ((ROWS, 4 * pts + LEAVES + 2 * SLOT), half)
    faces_shape = ((ROWS, points + LEAVES), half)
    even_shape = ((ROWS, points + LEAVES + SLOT * ACROSS), half)
    rows_shape = ((ROWS, SLOT * ACROSS), half)
    both_shape = ((ROWS, 2 * SLOT * ACROSS), half)
    near_shape, sums_shape = ((ROWS, points), full), ((ROWS, LEAVES), full)
    rows_scratch = pltpu.VMEM((8 * pts, FEATURES), half)
    own, basis, moments, totals, *given = call(
        pack_kernel,
        "pack",
        [hbm] * 5,
        [
            ((ROWS, points), half),
            ((2 * SLOT, points), half),
            ((ROWS, LEAVES), half),
            ((ROWS, 2 * SLOT), half),
            given_shape,
            given_shape,
        ],
        [
            pltpu.SMEM((8,), jnp.int32),
            pltpu.VMEM((3, points), full),
            pltpu.VMEM((fields, points), half),
            pltpu.VMEM((LEAVES, SLOT), half),
            pltpu.VMEM((SLOT, SLOT), half),
            pltpu.VMEM((SLOT, 8, pts), full),
            pltpu.SemaphoreType.DMA((5,)),
        ],
        leaf_count,
        positions,
        density,
        jnp.asarray(shift, half),
        jnp.asarray(heavy_table(), half),
    )
    from_2 = swapped(totals, "space", lambda i: i ^ 2)
    from_1 = swapped(given[0], "space", lambda i: i ^ 1)
    from_3 = swapped(given[1], "space", lambda i: i ^ 3)
    near, source, target, scale, column, columns, far, spread = call(
        functools.partial(own_kernel, depth),
        "near_own",
        [hbm] * 2 + [vmem] + [hbm] * 3,
        [
            ((ROWS, EARLY * points // 4), full),
            ((points, FEATURES), half),
            ((FEATURES, points), half),
            ((1, points), full),
            ((ROWS, 128), full),
            ((ACROSS * depth * SLOT, SLOT), half),
            ((len(STEPS) * LEAVES, LEAVES), half),
            ((SLOT, LEAVES), half),
        ],
        [
            pltpu.VMEM((3, SLOT, SLOT), full),
            pltpu.SMEM((8,), jnp.int32),
            pltpu.SMEM((fields,), full),
            pltpu.SemaphoreType.DMA((5,)),
        ],
        leaf_count,
        sigma_weights,
        own,
        jnp.asarray(far_table(), half),
        jnp.asarray(shift.T.copy(), half),
        jnp.asarray(box_nodes()),
    )
    left, right, faces_even, rows = call(
        row_kernel,
        "row",
        [vmem] * 7,
        [side_shape, side_shape, even_shape, rows_shape],
        [],
        own,
        moments,
        totals,
        from_1,
        from_2,
        from_3,
        far,
    )
    faces_even = swapped(faces_even, "space", lambda i: i ^ ACROSS)
    near, faces_odd, same = call(
        middle_kernel,
        "near_middle",
        [vmem] * 8,
        [near_shape, faces_shape, sums_shape],
        [],
        own,
        left,
        right,
        moments,
        far,
        near,
        source,
        target,
    )
    faces_odd = swapped_odd(faces_odd)
    near, both = call(
        side_kernel,
        "near_side",
        [vmem] * 6,
        [near_shape, both_shape],
        [pltpu.VMEM((4 * pts, FEATURES), half)] * 2,
        left,
        right,
        near,
        target,
        rows,
        faces_even,
    )
    if depth == 4:
        held = [rows, swapped(both, "space", lambda i: i ^ (2 * ACROSS))]
    else:
        groups = [[z * ACROSS + x for z in range(depth)] for x in range(ACROSS)]
        held = [lax.all_gather(rows, "space", axis_index_groups=groups)]
    near, = call(even_kernel, "near_even", [vmem] * 3, [near_shape], [rows_scratch], near, target, faces_even)
    potential, sums = call(
        functools.partial(last_kernel, depth),
        "near_odd",
        [vmem] * (10 + len(held)),
        [((fields, points), full), ((1, points + 128), full)],
        [pltpu.VMEM((ROWS, points), full), rows_scratch],
        near,
        target,
        faces_even,
        faces_odd,
        basis,
        scale,
        column,
        columns,
        spread,
        same,
        *held,
    )
    if lax.axis_size("sig") == 2:
        other = swapped(sums, "sig", lambda i: i ^ 1)
    else:
        other = lax.psum(sums, "sig") - sums
    mean, = call(mean_kernel, "mean", [vmem] * 2, [((1, points), full)], [], sums, other)
    return potential, mean.reshape(points)


def solution(mesh):
    in_specs = (P(None, "space"), P("sig", "space"), P("space"), P("sig"))
    out_specs = (P("sig", "space"), P("space"))
    return jax.shard_map(per_device, mesh=mesh, in_specs=in_specs, out_specs=out_specs, check_vma=False)
```

```python
import functools
import math

import jax
import jax.numpy as jnp
import numpy as np
from jax import lax
from jax.experimental import pallas as pl
from jax.experimental.pallas import tpu as pltpu
from jax.sharding import PartitionSpec as P

ORDER = 5
SOFTENING = 0.1
ACROSS = 4
SLOT = 64
ROWS = 24
LEAVES = 8 * SLOT
MEGA = 1024 * 1024
FEATURES = 48
EARLY = 3


def exponent_table(order_max):
    entries_list = []
    for degree in range(order_max + 1):
        for first_power in range(degree, -1, -1):
            for second_power in range(degree - first_power, -1, -1):
                entries_list.append((first_power, second_power, degree - first_power - second_power))
    return entries_list


def node_table(count_nodes, offset_value):
    counter = np.arange(1, count_nodes + 1, dtype=np.float32)[:, None]
    stride_set = np.array([0.7548776662466927, 0.5698402909980532, 0.4142135623730951], dtype=np.float32)[None, :]
    unit_points = np.mod(counter * stride_set + np.float32(offset_value), np.float32(1.0))
    return (np.float32(2.0) * unit_points - np.float32(1.0)).astype(np.float32)


EXPONENTS = exponent_table(ORDER)
COEFFS = len(EXPONENTS)
CHECK = node_table(COEFFS, 0.5).astype(np.float64)
EQUIV = node_table(COEFFS, 0.0).astype(np.float64)
HEAVY = [EXPONENTS.index(e) for e in ((0, 0, 0), (2, 0, 0), (0, 2, 0), (0, 0, 2), (4, 0, 0), (0, 4, 0), (0, 0, 4), (2, 0, 2))]
STEPS = [(sx, sz) for sz in (-1, 0, 1) for sx in (-1, 0, 1) if sx != 0 or sz != 0]


def bits(octant):
    return octant % 2, octant // 2 % 2, octant // 4


def leaf_slot(octant):
    bit_x, bit_y, bit_z = bits(octant)
    return (bit_x + 2 * bit_z) * 2 + bit_y


@functools.lru_cache(None)
def far_table():
    shape = (len(STEPS), 8, SLOT, 8, SLOT)
    table = np.zeros(shape)
    gap_nodes = 0.5 * (CHECK[None, :, :] - EQUIV[:, None, :])
    for index, (step_x, step_z) in enumerate(STEPS):
        for source in range(8):
            for target in range(8):
                s, t = bits(source), bits(target)
                gap = np.array([2 * step_x + s[0] - t[0], s[1] - t[1], 2 * step_z + s[2] - t[2]], np.float64)
                if max(abs(gap[0]), abs(gap[2])) >= 2:
                    shifted = gap_nodes - gap
                    value = 1.0 / np.sqrt(np.sum(shifted * shifted, -1) + SOFTENING * SOFTENING) / COEFFS
                    table[index, source, :COEFFS, target, :COEFFS] = value
    return table.reshape(len(STEPS) * LEAVES, LEAVES)


@functools.lru_cache(None)
def shift_table():
    table = np.zeros((8, SLOT, SLOT))
    for leaf in range(8):
        offset = [bit - 0.5 for bit in bits(leaf)]
        for k, target in enumerate(EXPONENTS):
            for i, source in enumerate(EXPONENTS):
                if all(b <= a for a, b in zip(target, source)):
                    value = 1.0
                    for a, b, h in zip(target, source, offset):
                        value *= math.comb(a, b) * 0.5**b * h ** (a - b)
                    table[leaf, i, k] = value
    return table.reshape(8 * SLOT, SLOT)


@functools.lru_cache(None)
def box_nodes():
    gaps = np.zeros((3, SLOT, SLOT))
    gaps[:, :COEFFS, :COEFFS] = np.moveaxis(CHECK[None, :, :] - EQUIV[:, None, :], -1, 0)
    gaps[:, COEFFS:] = gaps[:, HEAVY]
    gaps[1] = gaps[1] ** 2 + SOFTENING * SOFTENING
    return gaps.astype(np.float32)


def dot(left, right):
    return jnp.dot(left, right, preferred_element_type=jnp.float32)


def dot_nt(left, right):
    return lax.dot_general(left, right, (((1,), (1,)), ((), ())), preferred_element_type=jnp.float32)


def low_bits(value):
    return value.astype(jnp.bfloat16)


def heavy_table():
    table = np.zeros((SLOT, SLOT), np.float32)
    table[HEAVY, np.arange(COEFFS, SLOT)] = 1.0
    return table


def high_low(value):
    high = low_bits(value)
    return high, low_bits(value - high.astype(jnp.float32))


def by_row(values, shape):
    row = lax.broadcasted_iota(jnp.int32, shape, 0)
    result = jnp.zeros(shape, jnp.float32)
    for index, value in enumerate(values):
        result = jnp.where(row == index, value, result)
    return result


def box_place():
    label = lax.axis_index("space")
    return lax.rem(label, ACROSS), lax.div(label, ACROSS)


def lanes(start, size):
    return pl.ds(start if isinstance(start, int) else pl.multiple_of(start, 128), size)


def fetch(pairs, sems):
    copies = [pltpu.make_async_copy(src, dst, sems.at[i]) for i, (src, dst) in enumerate(pairs)]
    for copy in copies:
        copy.start()
    return copies


def pack_kernel(count_in, positions_in, density_in, shift_in, heavy_in, own, basis, moments, totals, *rest):
    payloads, (count, positions, density, shift, heavy, mono, sems) = rest[:2], rest[2:]
    copies = fetch(
        [(count_in, count), (positions_in, positions), (density_in, density), (shift_in, shift), (heavy_in, heavy)], sems
    )
    fields, points = density.shape
    pts = points // 8
    box_x, box_z = box_place()
    for copy in copies:
        copy.wait()
    local = []
    for leaf in range(8):
        bit_x, bit_y, bit_z = bits(leaf)
        centre = by_row(
            [2.0 * box_x.astype(jnp.float32) + (bit_x + 0.5), bit_y + 0.5, 2.0 * box_z.astype(jnp.float32) + (bit_z + 0.5)],
            (3, 1),
        )
        here = slice(leaf * pts, (leaf + 1) * pts)
        offset = positions[:, here] - centre
        local.append(offset)
        high = low_bits(offset).astype(jnp.float32)
        middle = low_bits(offset - high).astype(jnp.float32)
        raw = density[:, here].astype(jnp.float32)
        mass = jnp.where(lax.broadcasted_iota(jnp.int32, raw.shape, 1) < count[leaf], raw, 0.0)
        spare = jnp.zeros((ROWS - fields - 6, pts), jnp.float32)
        own[:, here] = low_bits(jnp.concatenate([mass, high, middle, spare], axis=0))

    axes = [2.0 * jnp.concatenate([part[a : a + 1] for part in local], axis=0) for a in range(3)]
    made = {(0, 0, 0): jnp.ones((8, pts), jnp.float32)}
    for k, powers in enumerate(EXPONENTS):
        if powers not in made:
            a = next(i for i in range(3) if powers[i] > 0)
            before = tuple(p - (i == a) for i, p in enumerate(powers))
            made[powers] = made[before] * axes[a]
        mono[k] = made[powers]
    mono[COEFFS:SLOT] = jnp.zeros((SLOT - COEFFS, 8, pts), jnp.float32)
    parts = []
    for leaf in range(8):
        here = slice(leaf * pts, (leaf + 1) * pts)
        high, low = high_low(mono[:, leaf, :])
        basis[0:SLOT, here] = high
        basis[SLOT:, here] = low
        parts.append(dot_nt(own[:, here], high))
    moment, rest = high_low(jnp.concatenate(parts, axis=1))
    moments[...] = moment
    total = dot(moment, shift[...]) + dot(rest, shift[...])
    total_high, total_low = high_low(total)
    total = low_bits(total_high.astype(jnp.float32) + dot(total_low, heavy[...]))
    total = jnp.concatenate([total, jnp.zeros_like(total)], axis=1)
    totals[...] = total
    for distance, payload in zip((1, 3), payloads):
        bit = jnp.where((box_x ^ distance) > box_x, 1, 0)
        for place in range(4):
            payload[:, lanes(place * pts, pts)] = own[:, lanes((bit + 2 * place) * pts, pts)]
        payload[:, lanes(4 * pts, LEAVES)] = moment
        payload[:, lanes(4 * pts + LEAVES, 2 * SLOT)] = total


def features(held, start, size, centre, target):
    value = held[16:ROWS, lanes(start, size)].astype(jnp.float32)
    x = value[1:4] + value[4:7] + by_row(centre, (3, 1))
    norm = jnp.sum(x * x, axis=0, keepdims=True)
    if target:
        norm = norm + SOFTENING * SOFTENING
    parts, norms = [], []
    for source, out in ((x, parts), (norm, norms)):
        left = source
        for _ in range(3):
            high = low_bits(left).astype(jnp.float32)
            out.append(high)
            left = left - high
    one = jnp.ones_like(norm)
    zero = jnp.zeros_like(norm)
    blank = jnp.zeros((3, norm.shape[1]), jnp.float32)
    blocks = []
    order = (0, 1, 0, 2, 0, 1) if target else (0, 0, 1, 0, 2, 1)
    for index, which in enumerate(order):
        coords = -2.0 * parts[which] if target else parts[which]
        if index < 3:
            pair = [one, norms[index]] if target else [norms[index], one]
        else:
            pair = [zero, zero]
        blocks += [coords, *pair, blank]
    return jnp.concatenate(blocks, axis=0)


def source_features(held, start, size, centre):
    return low_bits(jnp.transpose(features(held, start, size, centre, False)))


def pulled(near, jobs, target, size, first=None):
    width = target.shape[1] // 8
    tiles = []
    for group, source, masses, starts in jobs:
        for piece in range(2):
            here = lanes((2 * group + piece) * width, width)
            for turn, start in enumerate(starts):
                tiles.append((here, source, masses, lanes(start, size), turn == 0, turn + 1 == len(starts)))

    def squares(tile):
        return dot(tile[1][tile[3], :], target[:, tile[0]])

    ahead, kernel, total = squares(tiles[0]), None, None
    for turn in range(len(tiles) + 1):
        square = ahead
        if turn + 1 < len(tiles):
            ahead = squares(tiles[turn + 1])
        if turn > 0:
            here, _, masses, place, opens, closes = tiles[turn - 1]
            if opens:
                total = jnp.zeros((ROWS, width), jnp.float32) if first is None else first[:, here]
            total = total + dot(masses[:, place], kernel)
            if closes:
                near[:, here] = total
        if turn < len(tiles):
            kernel = low_bits(lax.rsqrt(square))


def own_groups(near, first, last, target, source, own):
    pts = source.shape[0] // 8
    starts = [2 * p * pts for p in range(4)]
    pulled(near, [(group, source, own, starts) for group in range(first, last)], target, 2 * pts)


def box_columns(depth, box_x, box_z, nodes):
    blocks = []
    for turn, distance in [(turn, distance) for turn in range(depth) for distance in range(ACROSS)]:
        gap_x = 2 * (box_x - (box_x ^ distance))
        gap_z = 2 * (box_z - ((box_z ^ turn) if depth == 4 else turn))
        across_x = nodes[0] + gap_x.astype(jnp.float32)
        across_z = nodes[2] + gap_z.astype(jnp.float32)
        apart = jnp.maximum(jnp.abs(gap_x), jnp.abs(gap_z)) >= 4
        value = lax.rsqrt(across_x * across_x + across_z * across_z + nodes[1])
        blocks.append(low_bits(value * jnp.where(apart, 1.0 / COEFFS, 0.0)))
    return jnp.concatenate(blocks, axis=0)


def own_kernel(depth, count_in, weights_in, own, *rest):
    tables, outs, rest = rest[:3], rest[3:11], rest[11:]
    near, source, target, scale, column, columns, far, spread = outs
    nodes, count, weights, sems = rest
    copies = fetch([*zip(tables, (far, spread, nodes)), (count_in, count), (weights_in, weights)], sems)
    points = own.shape[1]
    pts = points // 8
    for leaf in range(8):
        centre = [bit - 0.5 for bit in bits(leaf)]
        source[lanes(leaf * pts, pts), :] = source_features(own, leaf * pts, pts, centre)
        target[:, lanes(leaf_slot(leaf) * pts, pts)] = low_bits(features(own, leaf * pts, pts, centre, True))
    own_groups(near, 0, EARLY, target, source, own)
    for copy in copies:
        copy.wait()
    columns[...] = box_columns(depth, *box_place(), nodes)
    column[...] = by_row([weights[field] for field in range(weights.shape[0])], column.shape)
    lane_index = lax.broadcasted_iota(jnp.int32, (1, pts), 1)
    for leaf in range(8):
        scale[:, leaf * pts : (leaf + 1) * pts] = jnp.where(lane_index < count[leaf], 1.0 / (128.0 * pts), 0.0)


def spread_first(value, node):
    starts = [leaf * SLOT + node for leaf in range(8)]
    return jnp.concatenate([jnp.broadcast_to(value[:, s : s + 1], (ROWS, SLOT)) for s in starts], axis=1)


def decoded(coded):
    value = coded.astype(jnp.float32)
    node = lax.broadcasted_iota(jnp.int32, value.shape, 1) % SLOT
    return jnp.where(node == 0, 0.0, value) + spread_first(value, 0) + spread_first(value, COEFFS)


def faces_of(faces, bit, given, own, left, right, rows=None):
    points = own.shape[1]
    pts = points // 8
    for y in range(2):
        for x in range(4):
            place = lanes((2 * x + y) * pts, pts)
            if x in (0, 3):
                side = left if x == 0 else right
                faces[:, place] = side[:, lanes((y + 2 * bit) * pts, pts)]
            else:
                faces[:, place] = own[:, lanes((x - 1 + 2 * y + 4 * bit) * pts, pts)]
    node = lax.broadcasted_iota(jnp.int32, given.shape, 1) % SLOT
    base = spread_first(given, 0)
    base_high = low_bits(base).astype(jnp.float32)
    coded = jnp.where(node == 0, base_high, jnp.where(node == COEFFS, base - base_high, given - base))
    faces[:, lanes(points, LEAVES)] = low_bits(coded)
    if rows is not None:
        faces[:, lanes(points + LEAVES, rows.shape[1])] = rows


def sums_for(above, left, moments, right, far):
    base = left.shape[1] - LEAVES
    around = jnp.concatenate([left[:, lanes(base, LEAVES)], moments[...], right[:, lanes(base, LEAVES)]], axis=1)
    return dot(around, far[lanes(jnp.where(above == 1, 0, 5 * LEAVES), 3 * LEAVES), :])


def row_kernel(own, moments, totals, from_1, from_2, from_3, far, left, right, faces_even, rows):
    box_x, box_z = box_place()
    for side, step in ((left, -1), (right, 1)):
        side[...] = jnp.zeros(side.shape, side.dtype)
        for distance, held in ((1, from_1), (3, from_3)):

            @pl.when((box_x ^ distance) - box_x == step)
            def _(side=side, held=held):
                side[...] = held[:, lanes(0, side.shape[1])]

    ends = lanes(left.shape[1], 2 * SLOT)
    row = [totals[...], from_1[:, ends], from_2[...], from_3[:, ends]]
    row = jnp.concatenate([box[:, :SLOT] for box in row], axis=1)
    rows[...] = row
    above = 1 - lax.rem(box_z, 2)
    faces_of(faces_even, above, sums_for(above, left, moments, right, far), own, left, right, row)


def middle_kernel(own, left, right, moments, far, early, source, target, near, faces_odd, same):
    points = own.shape[1]
    _, box_z = box_place()
    above = lax.rem(box_z, 2)
    faces_of(faces_odd, above, sums_for(above, left, moments, right, far), own, left, right)
    base = left.shape[1] - LEAVES
    beside = jnp.concatenate([left[:, lanes(base, LEAVES)], right[:, lanes(base, LEAVES)]], axis=1)
    same[...] = dot(beside, far[lanes(3 * LEAVES, 2 * LEAVES), :])
    near[:, lanes(0, EARLY * points // 4)] = early[...]
    own_groups(near, EARLY, 4, target, source, own)


def side_kernel(left, right, early, target, near, sides_left, sides_right):
    pts = early.shape[1] // 8
    jobs = []
    for step, side, held in ((0, left, sides_left), (1, right, sides_right)):
        for place in range(4):
            centre = (1.5 if step else -1.5, place % 2 - 0.5, place // 2 - 0.5)
            held[lanes(place * pts, pts), :] = source_features(side, place * pts, pts, centre)
        jobs += [(step, held, side, [0, 2 * pts]), (step + 2, held, side, [0, 2 * pts])]
    pulled(near, jobs, target, 2 * pts, early)


def layer_pulls(near, early, step, inside, target, faces, sides):
    points = early.shape[1]
    pts = points // 8

    @pl.when(inside)
    def _():
        for place in range(8):
            height = jnp.where(step == 1, 1.5, -1.5)
            centre = (place // 2 - 1.5, place % 2 - 0.5, height)
            sides[lanes(place * pts, pts), :] = source_features(faces, place * pts, pts, centre)

        jobs = [(i + 2 * step, sides, faces, [2 * (x + i) * pts for x in range(3)]) for i in range(2)]
        pulled(near, jobs, target, 2 * pts, early)

    @pl.when(jnp.logical_not(inside))
    def _():
        here = lanes(step * (points // 2), points // 2)
        near[:, here] = early[:, here]


def even_kernel(early, target, faces, rows, near, both, sides):
    _, box_z = box_place()
    points = early.shape[1]
    width = rows.shape[1]
    both[:, lanes(0, width)] = rows[...]
    both[:, lanes(width, width)] = faces[:, lanes(faces.shape[1] - width, width)]
    step = 1 - lax.rem(box_z, 2)
    other = lanes((1 - step) * (points // 2), points // 2)
    near[:, other] = early[:, other]
    layer_pulls(near, early, step, box_z >= 0, target, faces, sides)


def odd_inside(depth):
    _, box_z = box_place()
    step = lax.rem(box_z, 2)
    return step, (box_z + 2 * step - 1 >= 0) & (box_z + 2 * step - 1 < depth)


def odd_kernel(depth, early, target, faces, near, sides):
    points = early.shape[1]
    step, inside = odd_inside(depth)
    other = lanes((1 - step) * (points // 2), points // 2)
    near[:, other] = early[:, other]
    layer_pulls(near, early, step, inside, target, faces, sides)


def last_kernel(depth, near, faces_even, faces_odd, basis, scale, column, columns, spread, same, *rest):
    held, (potential, sums) = rest[:-2], rest[-2:]
    fields, points = potential.shape
    pts = points // 8
    _, inside = odd_inside(depth)
    if depth == 4:
        rows, distant = held
        width = rows.shape[1]
        near_rows = faces_even[:, lanes(faces_even.shape[1] - width, width)]
        layers = [rows[...], near_rows, distant[:, lanes(0, width)], distant[:, lanes(width, width)]]
    else:
        layers = [held[0][layer] for layer in range(depth)]
    coarse_high, coarse_low = high_low(dot(jnp.concatenate(layers, axis=1), columns[...]))
    value = same[...] + dot(coarse_high, spread[...]) + dot(coarse_low, spread[...])
    value = value + decoded(faces_even[:, lanes(points, LEAVES)])
    value = value + jnp.where(inside, decoded(faces_odd[:, lanes(points, LEAVES)]), 0.0)
    local_high, local_low = high_low(value)
    weight = column[0:fields, 0:1]
    for leaf in range(8):
        here = slice(leaf * pts, (leaf + 1) * pts)
        slot = slice(leaf * SLOT, (leaf + 1) * SLOT)
        doubled = jnp.concatenate([local_high[:, slot], local_high[:, slot]], axis=1)
        far_part = dot(doubled, basis[:, here]) + dot(local_low[:, slot], basis[0:SLOT, here])
        total = near[0:fields, lanes(leaf_slot(leaf) * pts, pts)] + far_part[:fields]
        total = total * scale[:, here]
        potential[:, here] = total
        sums[:, here] = jnp.sum(total * weight, axis=0, keepdims=True)
    sums[:, points:] = jnp.broadcast_to(jnp.sum(weight), (1, sums.shape[1] - points))


def mean_kernel(mine, other, mean):
    points = mean.shape[1]
    total = mine[...] + other[...]
    mean[...] = total[:, :points] / total[:, points : points + 1]


def swapped(block, axis, partner):
    size = lax.axis_size(axis)
    return lax.ppermute(block, axis, [(partner(i), i) for i in range(size)])


def swapped_odd(block):
    boxes, cores = lax.axis_size("space"), lax.axis_size("sig")
    pairs = []
    for box in range(boxes):
        other = box + ACROSS if box // ACROSS % 2 else box - ACROSS
        for core in range(cores):
            source = other * cores + core if 0 <= other < boxes else box * cores + (core ^ 1)
            pairs.append((source, box * cores + core))
    return lax.ppermute(block, ("space", "sig"), pairs)


def per_device(positions, density, leaf_count, sigma_weights):
    fields, points = density.shape
    pts = points // 8
    depth = lax.axis_size("space") // ACROSS
    vmem, hbm = pl.BlockSpec(memory_space=pltpu.VMEM), pl.BlockSpec(memory_space=pltpu.HBM)

    def call(kernel, name, in_specs, outs, scratch, *args):
        return pl.pallas_call(
            kernel,
            in_specs=in_specs,
            out_specs=[vmem] * len(outs),
            out_shape=[jax.ShapeDtypeStruct(shape, dtype) for shape, dtype in outs],
            scratch_shapes=scratch,
            compiler_params=pltpu.CompilerParams(vmem_limit_bytes=24 * MEGA),
            name=name,
        )(*(pltpu.with_memory_space_constraint(a, pltpu.HBM) if s is hbm else a for s, a in zip(in_specs, args)))

    half, full = jnp.bfloat16, jnp.float32
    shift = shift_table()
    side_shape = ((ROWS, 4 * pts + LEAVES), half)
    given_shape = ((ROWS, 4 * pts + LEAVES + 2 * SLOT), half)
    faces_shape = ((ROWS, points + LEAVES), half)
    even_shape = ((ROWS, points + LEAVES + SLOT * ACROSS), half)
    rows_shape = ((ROWS, SLOT * ACROSS), half)
    both_shape = ((ROWS, 2 * SLOT * ACROSS), half)
    near_shape, sums_shape = ((ROWS, points), full), ((ROWS, LEAVES), full)
    rows_scratch = pltpu.VMEM((8 * pts, FEATURES), half)
    own, basis, moments, totals, *given = call(
        pack_kernel,
        "pack",
        [hbm] * 5,
        [
            ((ROWS, points), half),
            ((2 * SLOT, points), half),
            ((ROWS, LEAVES), half),
            ((ROWS, 2 * SLOT), half),
            given_shape,
            given_shape,
        ],
        [
            pltpu.SMEM((8,), jnp.int32),
            pltpu.VMEM((3, points), full),
            pltpu.VMEM((fields, points), half),
            pltpu.VMEM((LEAVES, SLOT), half),
            pltpu.VMEM((SLOT, SLOT), half),
            pltpu.VMEM((SLOT, 8, pts), full),
            pltpu.SemaphoreType.DMA((5,)),
        ],
        leaf_count,
        positions,
        density,
        jnp.asarray(shift, half),
        jnp.asarray(heavy_table(), half),
    )
    from_2 = swapped(totals, "space", lambda i: i ^ 2)
    from_1 = swapped(given[0], "space", lambda i: i ^ 1)
    from_3 = swapped(given[1], "space", lambda i: i ^ 3)
    near, source, target, scale, column, columns, far, spread = call(
        functools.partial(own_kernel, depth),
        "near_own",
        [hbm] * 2 + [vmem] + [hbm] * 3,
        [
            ((ROWS, EARLY * points // 4), full),
            ((points, FEATURES), half),
            ((FEATURES, points), half),
            ((1, points), full),
            ((ROWS, 128), full),
            ((ACROSS * depth * SLOT, SLOT), half),
            ((len(STEPS) * LEAVES, LEAVES), half),
            ((SLOT, LEAVES), half),
        ],
        [
            pltpu.VMEM((3, SLOT, SLOT), full),
            pltpu.SMEM((8,), jnp.int32),
            pltpu.SMEM((fields,), full),
            pltpu.SemaphoreType.DMA((5,)),
        ],
        leaf_count,
        sigma_weights,
        own,
        jnp.asarray(far_table(), half),
        jnp.asarray(shift.T.copy(), half),
        jnp.asarray(box_nodes()),
    )
    left, right, faces_even, rows = call(
        row_kernel,
        "row",
        [vmem] * 7,
        [side_shape, side_shape, even_shape, rows_shape],
        [],
        own,
        moments,
        totals,
        from_1,
        from_2,
        from_3,
        far,
    )
    faces_even = swapped(faces_even, "space", lambda i: i ^ ACROSS)
    near, faces_odd, same = call(
        middle_kernel,
        "near_middle",
        [vmem] * 8,
        [near_shape, faces_shape, sums_shape],
        [],
        own,
        left,
        right,
        moments,
        far,
        near,
        source,
        target,
    )
    faces_odd = swapped_odd(faces_odd)
    near, = call(
        side_kernel,
        "near_side",
        [vmem] * 4,
        [near_shape],
        [pltpu.VMEM((4 * pts, FEATURES), half)] * 2,
        left,
        right,
        near,
        target,
    )
    near, both = call(
        even_kernel,
        "near_even",
        [vmem] * 4,
        [near_shape, both_shape],
        [rows_scratch],
        near,
        target,
        faces_even,
        rows,
    )
    if depth == 4:
        held = [rows, swapped(both, "space", lambda i: i ^ (2 * ACROSS))]
    else:
        groups = [[z * ACROSS + x for z in range(depth)] for x in range(ACROSS)]
        held = [lax.all_gather(rows, "space", axis_index_groups=groups)]
    near, = call(
        functools.partial(odd_kernel, depth),
        "near_odd",
        [vmem] * 3,
        [near_shape],
        [rows_scratch],
        near,
        target,
        faces_odd,
    )
    potential, sums = call(
        functools.partial(last_kernel, depth),
        "evaluate",
        [vmem] * (9 + len(held)),
        [((fields, points), full), ((1, points + 128), full)],
        [],
        near,
        faces_even,
        faces_odd,
        basis,
        scale,
        column,
        columns,
        spread,
        same,
        *held,
    )
    if lax.axis_size("sig") == 2:
        other = swapped(sums, "sig", lambda i: i ^ 1)
    else:
        other = lax.psum(sums, "sig") - sums
    mean, = call(mean_kernel, "mean", [vmem] * 2, [((1, points), full)], [], sums, other)
    return potential, mean.reshape(points)


def solution(mesh):
    in_specs = (P(None, "space"), P("sig", "space"), P("space"), P("sig"))
    out_specs = (P("sig", "space"), P("space"))
    return jax.shard_map(per_device, mesh=mesh, in_specs=in_specs, out_specs=out_specs, check_vma=False)
```

```python
import functools
import math

import jax
import jax.numpy as jnp
import numpy as np
from jax import lax
from jax.experimental import pallas as pl
from jax.experimental.pallas import tpu as pltpu
from jax.sharding import PartitionSpec as P

ORDER = 5
SOFTENING = 0.1
ACROSS = 4
SLOT = 64
ROWS = 24
LEAVES = 8 * SLOT
MEGA = 1024 * 1024
FEATURES = 48
EARLY = 3


def exponent_table(order_max):
    entries_list = []
    for degree in range(order_max + 1):
        for first_power in range(degree, -1, -1):
            for second_power in range(degree - first_power, -1, -1):
                entries_list.append((first_power, second_power, degree - first_power - second_power))
    return entries_list


def node_table(count_nodes, offset_value):
    counter = np.arange(1, count_nodes + 1, dtype=np.float32)[:, None]
    stride_set = np.array([0.7548776662466927, 0.5698402909980532, 0.4142135623730951], dtype=np.float32)[None, :]
    unit_points = np.mod(counter * stride_set + np.float32(offset_value), np.float32(1.0))
    return (np.float32(2.0) * unit_points - np.float32(1.0)).astype(np.float32)


EXPONENTS = exponent_table(ORDER)
COEFFS = len(EXPONENTS)
CHECK = node_table(COEFFS, 0.5).astype(np.float64)
EQUIV = node_table(COEFFS, 0.0).astype(np.float64)
HEAVY = [EXPONENTS.index(e) for e in ((0, 0, 0), (2, 0, 0), (0, 2, 0), (0, 0, 2), (4, 0, 0), (0, 4, 0), (0, 0, 4), (2, 0, 2))]
STEPS = [(sx, sz) for sz in (-1, 0, 1) for sx in (-1, 0, 1) if sx != 0 or sz != 0]


def bits(octant):
    return octant % 2, octant // 2 % 2, octant // 4


def leaf_slot(octant):
    bit_x, bit_y, bit_z = bits(octant)
    return (bit_x + 2 * bit_z) * 2 + bit_y


@functools.lru_cache(None)
def far_table():
    shape = (len(STEPS), 8, SLOT, 8, SLOT)
    table = np.zeros(shape)
    gap_nodes = 0.5 * (CHECK[None, :, :] - EQUIV[:, None, :])
    for index, (step_x, step_z) in enumerate(STEPS):
        for source in range(8):
            for target in range(8):
                s, t = bits(source), bits(target)
                gap = np.array([2 * step_x + s[0] - t[0], s[1] - t[1], 2 * step_z + s[2] - t[2]], np.float64)
                if max(abs(gap[0]), abs(gap[2])) >= 2:
                    shifted = gap_nodes - gap
                    value = 1.0 / np.sqrt(np.sum(shifted * shifted, -1) + SOFTENING * SOFTENING) / COEFFS
                    table[index, source, :COEFFS, target, :COEFFS] = value
    return table.reshape(len(STEPS) * LEAVES, LEAVES)


@functools.lru_cache(None)
def shift_table():
    table = np.zeros((8, SLOT, SLOT))
    for leaf in range(8):
        offset = [bit - 0.5 for bit in bits(leaf)]
        for k, target in enumerate(EXPONENTS):
            for i, source in enumerate(EXPONENTS):
                if all(b <= a for a, b in zip(target, source)):
                    value = 1.0
                    for a, b, h in zip(target, source, offset):
                        value *= math.comb(a, b) * 0.5**b * h ** (a - b)
                    table[leaf, i, k] = value
    return table.reshape(8 * SLOT, SLOT)


@functools.lru_cache(None)
def box_nodes():
    gaps = np.zeros((3, SLOT, SLOT))
    gaps[:, :COEFFS, :COEFFS] = np.moveaxis(CHECK[None, :, :] - EQUIV[:, None, :], -1, 0)
    gaps[:, COEFFS:] = gaps[:, HEAVY]
    gaps[1] = gaps[1] ** 2 + SOFTENING * SOFTENING
    return gaps.astype(np.float32)


def dot(left, right):
    return jnp.dot(left, right, preferred_element_type=jnp.float32)


def dot_nt(left, right):
    return lax.dot_general(left, right, (((1,), (1,)), ((), ())), preferred_element_type=jnp.float32)


def low_bits(value):
    return value.astype(jnp.bfloat16)


def heavy_table():
    table = np.zeros((SLOT, SLOT), np.float32)
    table[HEAVY, np.arange(COEFFS, SLOT)] = 1.0
    return table


def high_low(value):
    high = low_bits(value)
    return high, low_bits(value - high.astype(jnp.float32))


def by_row(values, shape):
    row = lax.broadcasted_iota(jnp.int32, shape, 0)
    result = jnp.zeros(shape, jnp.float32)
    for index, value in enumerate(values):
        result = jnp.where(row == index, value, result)
    return result


def box_place():
    label = lax.axis_index("space")
    return lax.rem(label, ACROSS), lax.div(label, ACROSS)


def lanes(start, size):
    return pl.ds(start if isinstance(start, int) else pl.multiple_of(start, 128), size)


def fetch(pairs, sems):
    copies = [pltpu.make_async_copy(src, dst, sems.at[i]) for i, (src, dst) in enumerate(pairs)]
    for copy in copies:
        copy.start()
    return copies


def pack_kernel(count_in, positions_in, density_in, shift_in, heavy_in, own, basis, moments, totals, *rest):
    payloads, (count, positions, density, shift, heavy, mono, sems) = rest[:2], rest[2:]
    copies = fetch(
        [(count_in, count), (positions_in, positions), (density_in, density), (shift_in, shift), (heavy_in, heavy)], sems
    )
    fields, points = density.shape
    pts = points // 8
    box_x, box_z = box_place()
    for copy in copies:
        copy.wait()
    local = []
    for leaf in range(8):
        bit_x, bit_y, bit_z = bits(leaf)
        centre = by_row(
            [2.0 * box_x.astype(jnp.float32) + (bit_x + 0.5), bit_y + 0.5, 2.0 * box_z.astype(jnp.float32) + (bit_z + 0.5)],
            (3, 1),
        )
        here = slice(leaf * pts, (leaf + 1) * pts)
        offset = positions[:, here] - centre
        local.append(offset)
        high = low_bits(offset).astype(jnp.float32)
        middle = low_bits(offset - high).astype(jnp.float32)
        raw = density[:, here].astype(jnp.float32)
        mass = jnp.where(lax.broadcasted_iota(jnp.int32, raw.shape, 1) < count[leaf], raw, 0.0)
        spare = jnp.zeros((ROWS - fields - 6, pts), jnp.float32)
        own[:, here] = low_bits(jnp.concatenate([mass, high, middle, spare], axis=0))

    axes = [2.0 * jnp.concatenate([part[a : a + 1] for part in local], axis=0) for a in range(3)]
    made = {(0, 0, 0): jnp.ones((8, pts), jnp.float32)}
    for k, powers in enumerate(EXPONENTS):
        if powers not in made:
            a = next(i for i in range(3) if powers[i] > 0)
            before = tuple(p - (i == a) for i, p in enumerate(powers))
            made[powers] = made[before] * axes[a]
        mono[k] = made[powers]
    mono[COEFFS:SLOT] = jnp.zeros((SLOT - COEFFS, 8, pts), jnp.float32)
    parts = []
    for leaf in range(8):
        here = slice(leaf * pts, (leaf + 1) * pts)
        high, low = high_low(mono[:, leaf, :])
        basis[0:SLOT, here] = high
        basis[SLOT:, here] = low
        parts.append(dot_nt(own[:, here], high))
    moment, rest = high_low(jnp.concatenate(parts, axis=1))
    moments[...] = moment
    total = dot(moment, shift[...]) + dot(rest, shift[...])
    total_high, total_low = high_low(total)
    total = low_bits(total_high.astype(jnp.float32) + dot(total_low, heavy[...]))
    total = jnp.concatenate([total, jnp.zeros_like(total)], axis=1)
    totals[...] = total
    for distance, payload in zip((1, 3), payloads):
        bit = jnp.where((box_x ^ distance) > box_x, 1, 0)
        for place in range(4):
            payload[:, lanes(place * pts, pts)] = own[:, lanes((bit + 2 * place) * pts, pts)]
        payload[:, lanes(4 * pts, LEAVES)] = moment
        payload[:, lanes(4 * pts + LEAVES, 2 * SLOT)] = total


def features(held, start, size, centre, target):
    value = held[16:ROWS, lanes(start, size)].astype(jnp.float32)
    x = value[1:4] + value[4:7] + by_row(centre, (3, 1))
    norm = jnp.sum(x * x, axis=0, keepdims=True)
    if target:
        norm = norm + SOFTENING * SOFTENING
    parts, norms = [], []
    for source, out in ((x, parts), (norm, norms)):
        left = source
        for _ in range(3):
            high = low_bits(left).astype(jnp.float32)
            out.append(high)
            left = left - high
    one = jnp.ones_like(norm)
    zero = jnp.zeros_like(norm)
    blank = jnp.zeros((3, norm.shape[1]), jnp.float32)
    blocks = []
    order = (0, 1, 0, 2, 0, 1) if target else (0, 0, 1, 0, 2, 1)
    for index, which in enumerate(order):
        coords = -2.0 * parts[which] if target else parts[which]
        if index < 3:
            pair = [one, norms[index]] if target else [norms[index], one]
        else:
            pair = [zero, zero]
        blocks += [coords, *pair, blank]
    return jnp.concatenate(blocks, axis=0)


def source_features(held, start, size, centre):
    return low_bits(jnp.transpose(features(held, start, size, centre, False)))


def pulled(near, jobs, target, size, first=None):
    width = target.shape[1] // 8
    tiles = []
    for group, source, masses, starts in jobs:
        for piece in range(2):
            here = lanes((2 * group + piece) * width, width)
            for turn, start in enumerate(starts):
                tiles.append((here, source, masses, lanes(start, size), turn == 0, turn + 1 == len(starts)))

    def squares(tile):
        return dot(tile[1][tile[3], :], target[:, tile[0]])

    ahead, kernel, total = squares(tiles[0]), None, None
    for turn in range(len(tiles) + 1):
        square = ahead
        if turn + 1 < len(tiles):
            ahead = squares(tiles[turn + 1])
        if turn > 0:
            here, _, masses, place, opens, closes = tiles[turn - 1]
            if opens:
                total = jnp.zeros((ROWS, width), jnp.float32) if first is None else first[:, here]
            total = total + dot(masses[:, place], kernel)
            if closes:
                near[:, here] = total
        if turn < len(tiles):
            kernel = low_bits(lax.rsqrt(square))


def own_groups(near, first, last, target, source, own):
    pts = source.shape[0] // 8
    starts = [2 * p * pts for p in range(4)]
    pulled(near, [(group, source, own, starts) for group in range(first, last)], target, 2 * pts)


def box_columns(depth, box_x, box_z, nodes):
    blocks = []
    for turn, distance in [(turn, distance) for turn in range(depth) for distance in range(ACROSS)]:
        gap_x = 2 * (box_x - (box_x ^ distance))
        gap_z = 2 * (box_z - ((box_z ^ turn) if depth == 4 else turn))
        across_x = nodes[0] + gap_x.astype(jnp.float32)
        across_z = nodes[2] + gap_z.astype(jnp.float32)
        apart = jnp.maximum(jnp.abs(gap_x), jnp.abs(gap_z)) >= 4
        value = lax.rsqrt(across_x * across_x + across_z * across_z + nodes[1])
        blocks.append(low_bits(value * jnp.where(apart, 1.0 / COEFFS, 0.0)))
    return jnp.concatenate(blocks, axis=0)


def own_kernel(depth, count_in, weights_in, own, *rest):
    tables, outs, rest = rest[:3], rest[3:11], rest[11:]
    near, source, target, scale, column, columns, far, spread = outs
    nodes, count, weights, sems = rest
    copies = fetch([*zip(tables, (far, spread, nodes)), (count_in, count), (weights_in, weights)], sems)
    points = own.shape[1]
    pts = points // 8
    for leaf in range(8):
        centre = [bit - 0.5 for bit in bits(leaf)]
        source[lanes(leaf * pts, pts), :] = source_features(own, leaf * pts, pts, centre)
        target[:, lanes(leaf_slot(leaf) * pts, pts)] = low_bits(features(own, leaf * pts, pts, centre, True))
    own_groups(near, 0, EARLY, target, source, own)
    for copy in copies:
        copy.wait()
    columns[...] = box_columns(depth, *box_place(), nodes)
    column[...] = by_row([weights[field] for field in range(weights.shape[0])], column.shape)
    lane_index = lax.broadcasted_iota(jnp.int32, (1, pts), 1)
    for leaf in range(8):
        scale[:, leaf * pts : (leaf + 1) * pts] = jnp.where(lane_index < count[leaf], 1.0 / (128.0 * pts), 0.0)


def spread_first(value, node):
    starts = [leaf * SLOT + node for leaf in range(8)]
    return jnp.concatenate([jnp.broadcast_to(value[:, s : s + 1], (ROWS, SLOT)) for s in starts], axis=1)


def decoded(coded):
    value = coded.astype(jnp.float32)
    node = lax.broadcasted_iota(jnp.int32, value.shape, 1) % SLOT
    return jnp.where(node == 0, 0.0, value) + spread_first(value, 0) + spread_first(value, COEFFS)


def faces_of(faces, bit, given, own, left, right, rows=None):
    points = own.shape[1]
    pts = points // 8
    for y in range(2):
        for x in range(4):
            place = lanes((2 * x + y) * pts, pts)
            if x in (0, 3):
                side = left if x == 0 else right
                faces[:, place] = side[:, lanes((y + 2 * bit) * pts, pts)]
            else:
                faces[:, place] = own[:, lanes((x - 1 + 2 * y + 4 * bit) * pts, pts)]
    node = lax.broadcasted_iota(jnp.int32, given.shape, 1) % SLOT
    base = spread_first(given, 0)
    base_high = low_bits(base).astype(jnp.float32)
    coded = jnp.where(node == 0, base_high, jnp.where(node == COEFFS, base - base_high, given - base))
    faces[:, lanes(points, LEAVES)] = low_bits(coded)
    if rows is not None:
        faces[:, lanes(points + LEAVES, rows.shape[1])] = rows


def sums_for(above, left, moments, right, far):
    base = left.shape[1] - LEAVES
    around = jnp.concatenate([left[:, lanes(base, LEAVES)], moments[...], right[:, lanes(base, LEAVES)]], axis=1)
    return dot(around, far[lanes(jnp.where(above == 1, 0, 5 * LEAVES), 3 * LEAVES), :])


def row_kernel(own, moments, totals, from_1, from_2, from_3, far, left, right, faces_even, rows):
    box_x, box_z = box_place()
    for side, step in ((left, -1), (right, 1)):
        side[...] = jnp.zeros(side.shape, side.dtype)
        for distance, held in ((1, from_1), (3, from_3)):

            @pl.when((box_x ^ distance) - box_x == step)
            def _(side=side, held=held):
                side[...] = held[:, lanes(0, side.shape[1])]

    ends = lanes(left.shape[1], 2 * SLOT)
    row = [totals[...], from_1[:, ends], from_2[...], from_3[:, ends]]
    row = jnp.concatenate([box[:, :SLOT] for box in row], axis=1)
    rows[...] = row
    above = 1 - lax.rem(box_z, 2)
    faces_of(faces_even, above, sums_for(above, left, moments, right, far), own, left, right, row)


def middle_kernel(own, left, right, moments, far, early, source, target, near, faces_odd, same):
    points = own.shape[1]
    _, box_z = box_place()
    above = lax.rem(box_z, 2)
    faces_of(faces_odd, above, sums_for(above, left, moments, right, far), own, left, right)
    base = left.shape[1] - LEAVES
    beside = jnp.concatenate([left[:, lanes(base, LEAVES)], right[:, lanes(base, LEAVES)]], axis=1)
    same[...] = dot(beside, far[lanes(3 * LEAVES, 2 * LEAVES), :])
    near[:, lanes(0, EARLY * points // 4)] = early[...]
    own_groups(near, EARLY, 4, target, source, own)


def side_kernel(left, right, early, target, near, sides_left, sides_right):
    pts = early.shape[1] // 8
    jobs = []
    for step, side, held in ((0, left, sides_left), (1, right, sides_right)):
        for place in range(4):
            centre = (1.5 if step else -1.5, place % 2 - 0.5, place // 2 - 0.5)
            held[lanes(place * pts, pts), :] = source_features(side, place * pts, pts, centre)
        jobs += [(step, held, side, [0, 2 * pts]), (step + 2, held, side, [0, 2 * pts])]
    pulled(near, jobs, target, 2 * pts, early)


def layer_pulls(near, early, step, inside, target, faces, sides):
    points = early.shape[1]
    pts = points // 8

    @pl.when(inside)
    def _():
        for place in range(8):
            height = jnp.where(step == 1, 1.5, -1.5)
            centre = (place // 2 - 1.5, place % 2 - 0.5, height)
            sides[lanes(place * pts, pts), :] = source_features(faces, place * pts, pts, centre)

        jobs = [(i + 2 * step, sides, faces, [2 * (x + i) * pts for x in range(3)]) for i in range(2)]
        pulled(near, jobs, target, 2 * pts, early)

    @pl.when(jnp.logical_not(inside))
    def _():
        here = lanes(step * (points // 2), points // 2)
        near[:, here] = early[:, here]


def even_kernel(early, target, faces, rows, near, both, sides):
    _, box_z = box_place()
    points = early.shape[1]
    width = rows.shape[1]
    both[:, lanes(0, width)] = rows[...]
    both[:, lanes(width, width)] = faces[:, lanes(faces.shape[1] - width, width)]
    step = 1 - lax.rem(box_z, 2)
    other = lanes((1 - step) * (points // 2), points // 2)
    near[:, other] = early[:, other]
    layer_pulls(near, early, step, box_z >= 0, target, faces, sides)


def odd_inside(depth):
    _, box_z = box_place()
    step = lax.rem(box_z, 2)
    return step, (box_z + 2 * step - 1 >= 0) & (box_z + 2 * step - 1 < depth)


def odd_kernel(depth, early, target, faces, near, sides):
    points = early.shape[1]
    step, inside = odd_inside(depth)
    other = lanes((1 - step) * (points // 2), points // 2)
    near[:, other] = early[:, other]
    layer_pulls(near, early, step, inside, target, faces, sides)


def last_kernel(depth, near, faces_even, faces_odd, basis, scale, column, columns, spread, same, *rest):
    held, (potential, sums) = rest[:-2], rest[-2:]
    fields, points = potential.shape
    pts = points // 8
    _, inside = odd_inside(depth)
    if depth == 4:
        rows, distant = held
        width = rows.shape[1]
        near_rows = faces_even[:, lanes(faces_even.shape[1] - width, width)]
        layers = [rows[...], near_rows, distant[:, lanes(0, width)], distant[:, lanes(width, width)]]
    else:
        layers = [held[0][layer] for layer in range(depth)]
    coarse_high, coarse_low = high_low(dot(jnp.concatenate(layers, axis=1), columns[...]))
    value = same[...] + dot(coarse_high, spread[...]) + dot(coarse_low, spread[...])
    value = value + decoded(faces_even[:, lanes(points, LEAVES)])
    value = value + jnp.where(inside, decoded(faces_odd[:, lanes(points, LEAVES)]), 0.0)
    local_high, local_low = high_low(value)
    weight = column[0:fields, 0:1]
    for leaf in range(8):
        here = slice(leaf * pts, (leaf + 1) * pts)
        slot = slice(leaf * SLOT, (leaf + 1) * SLOT)
        doubled = jnp.concatenate([local_high[:, slot], local_high[:, slot]], axis=1)
        far_part = dot(doubled, basis[:, here]) + dot(local_low[:, slot], basis[0:SLOT, here])
        total = near[0:fields, lanes(leaf_slot(leaf) * pts, pts)] + far_part[:fields]
        total = total * scale[:, here]
        potential[:, here] = total
        sums[:, here] = jnp.sum(total * weight, axis=0, keepdims=True)
    sums[:, points:] = jnp.broadcast_to(jnp.sum(weight), (1, sums.shape[1] - points))


def mean_kernel(mine, other, mean):
    points = mean.shape[1]
    total = mine[...] + other[...]
    mean[...] = total[:, :points] / total[:, points : points + 1]


def swapped(block, axis, partner):
    size = lax.axis_size(axis)
    return lax.ppermute(block, axis, [(partner(i), i) for i in range(size)])


def swapped_odd(block):
    boxes, cores = lax.axis_size("space"), lax.axis_size("sig")
    pairs = []
    for box in range(boxes):
        other = box + ACROSS if box // ACROSS % 2 else box - ACROSS
        for core in range(cores):
            source = other * cores + core if 0 <= other < boxes else box * cores + (core ^ 1)
            pairs.append((source, box * cores + core))
    return lax.ppermute(block, ("space", "sig"), pairs)


def per_device(positions, density, leaf_count, sigma_weights):
    fields, points = density.shape
    pts = points // 8
    depth = lax.axis_size("space") // ACROSS
    vmem, hbm = pl.BlockSpec(memory_space=pltpu.VMEM), pl.BlockSpec(memory_space=pltpu.HBM)

    def call(kernel, name, in_specs, outs, scratch, *args):
        return pl.pallas_call(
            kernel,
            in_specs=in_specs,
            out_specs=[vmem] * len(outs),
            out_shape=[jax.ShapeDtypeStruct(shape, dtype) for shape, dtype in outs],
            scratch_shapes=scratch,
            compiler_params=pltpu.CompilerParams(vmem_limit_bytes=24 * MEGA),
            name=name,
        )(*(pltpu.with_memory_space_constraint(a, pltpu.HBM) if s is hbm else a for s, a in zip(in_specs, args)))

    half, full = jnp.bfloat16, jnp.float32
    shift = shift_table()
    side_shape = ((ROWS, 4 * pts + LEAVES), half)
    given_shape = ((ROWS, 4 * pts + LEAVES + 2 * SLOT), half)
    faces_shape = ((ROWS, points + LEAVES), half)
    even_shape = ((ROWS, points + LEAVES + SLOT * ACROSS), half)
    rows_shape = ((ROWS, SLOT * ACROSS), half)
    both_shape = ((ROWS, 2 * SLOT * ACROSS), half)
    near_shape, sums_shape = ((ROWS, points), full), ((ROWS, LEAVES), full)
    rows_scratch = pltpu.VMEM((8 * pts, FEATURES), half)
    own, basis, moments, totals, *given = call(
        pack_kernel,
        "pack",
        [hbm] * 5,
        [
            ((ROWS, points), half),
            ((2 * SLOT, points), half),
            ((ROWS, LEAVES), half),
            ((ROWS, 2 * SLOT), half),
            given_shape,
            given_shape,
        ],
        [
            pltpu.SMEM((8,), jnp.int32),
            pltpu.VMEM((3, points), full),
            pltpu.VMEM((fields, points), half),
            pltpu.VMEM((LEAVES, SLOT), half),
            pltpu.VMEM((SLOT, SLOT), half),
            pltpu.VMEM((SLOT, 8, pts), full),
            pltpu.SemaphoreType.DMA((5,)),
        ],
        leaf_count,
        positions,
        density,
        jnp.asarray(shift, half),
        jnp.asarray(heavy_table(), half),
    )
    from_2 = swapped(totals, "space", lambda i: i ^ 2)
    from_1 = swapped(given[0], "space", lambda i: i ^ 1)
    from_3 = swapped(given[1], "space", lambda i: i ^ 3)
    near, source, target, scale, column, columns, far, spread = call(
        functools.partial(own_kernel, depth),
        "near_own",
        [hbm] * 2 + [vmem] + [hbm] * 3,
        [
            ((ROWS, EARLY * points // 4), full),
            ((points, FEATURES), half),
            ((FEATURES, points), half),
            ((1, points), full),
            ((ROWS, 128), full),
            ((ACROSS * depth * SLOT, SLOT), half),
            ((len(STEPS) * LEAVES, LEAVES), half),
            ((SLOT, LEAVES), half),
        ],
        [
            pltpu.VMEM((3, SLOT, SLOT), full),
            pltpu.SMEM((8,), jnp.int32),
            pltpu.SMEM((fields,), full),
            pltpu.SemaphoreType.DMA((5,)),
        ],
        leaf_count,
        sigma_weights,
        own,
        jnp.asarray(far_table(), half),
        jnp.asarray(shift.T.copy(), half),
        jnp.asarray(box_nodes()),
    )
    left, right, faces_even, rows = call(
        row_kernel,
        "row",
        [vmem] * 7,
        [side_shape, side_shape, even_shape, rows_shape],
        [],
        own,
        moments,
        totals,
        from_1,
        from_2,
        from_3,
        far,
    )
    faces_even = swapped(faces_even, "space", lambda i: i ^ ACROSS)
    near, faces_odd, same = call(
        middle_kernel,
        "near_middle",
        [vmem] * 8,
        [near_shape, faces_shape, sums_shape],
        [],
        own,
        left,
        right,
        moments,
        far,
        near,
        source,
        target,
    )
    faces_odd = swapped_odd(faces_odd)
    near, both = call(
        even_kernel,
        "near_even",
        [vmem] * 4,
        [near_shape, both_shape],
        [rows_scratch],
        near,
        target,
        faces_even,
        rows,
    )
    if depth == 4:
        held = [rows, swapped(both, "space", lambda i: i ^ (2 * ACROSS))]
    else:
        groups = [[z * ACROSS + x for z in range(depth)] for x in range(ACROSS)]
        held = [lax.all_gather(rows, "space", axis_index_groups=groups)]
    near, = call(
        side_kernel,
        "near_side",
        [vmem] * 4,
        [near_shape],
        [pltpu.VMEM((4 * pts, FEATURES), half)] * 2,
        left,
        right,
        near,
        target,
    )
    near, = call(
        functools.partial(odd_kernel, depth),
        "near_odd",
        [vmem] * 3,
        [near_shape],
        [rows_scratch],
        near,
        target,
        faces_odd,
    )
    potential, sums = call(
        functools.partial(last_kernel, depth),
        "evaluate",
        [vmem] * (9 + len(held)),
        [((fields, points), full), ((1, points + 128), full)],
        [],
        near,
        faces_even,
        faces_odd,
        basis,
        scale,
        column,
        columns,
        spread,
        same,
        *held,
    )
    if lax.axis_size("sig") == 2:
        other = swapped(sums, "sig", lambda i: i ^ 1)
    else:
        other = lax.psum(sums, "sig") - sums
    mean, = call(mean_kernel, "mean", [vmem] * 2, [((1, points), full)], [], sums, other)
    return potential, mean.reshape(points)


def solution(mesh):
    in_specs = (P(None, "space"), P("sig", "space"), P("space"), P("sig"))
    out_specs = (P("sig", "space"), P("space"))
    return jax.shard_map(per_device, mesh=mesh, in_specs=in_specs, out_specs=out_specs, check_vma=False)
```

```python
import functools
import math

import jax
import jax.numpy as jnp
import numpy as np
from jax import lax
from jax.experimental import pallas as pl
from jax.experimental.pallas import tpu as pltpu
from jax.sharding import PartitionSpec as P

ORDER = 5
SOFTENING = 0.1
ACROSS = 4
SLOT = 64
ROWS = 24
LEAVES = 8 * SLOT
MEGA = 1024 * 1024
FEATURES = 48
EARLY = 3


def exponent_table(order_max):
    entries_list = []
    for degree in range(order_max + 1):
        for first_power in range(degree, -1, -1):
            for second_power in range(degree - first_power, -1, -1):
                entries_list.append((first_power, second_power, degree - first_power - second_power))
    return entries_list


def node_table(count_nodes, offset_value):
    counter = np.arange(1, count_nodes + 1, dtype=np.float32)[:, None]
    stride_set = np.array([0.7548776662466927, 0.5698402909980532, 0.4142135623730951], dtype=np.float32)[None, :]
    unit_points = np.mod(counter * stride_set + np.float32(offset_value), np.float32(1.0))
    return (np.float32(2.0) * unit_points - np.float32(1.0)).astype(np.float32)


EXPONENTS = exponent_table(ORDER)
COEFFS = len(EXPONENTS)
CHECK = node_table(COEFFS, 0.5).astype(np.float64)
EQUIV = node_table(COEFFS, 0.0).astype(np.float64)
HEAVY = [EXPONENTS.index(e) for e in ((0, 0, 0), (2, 0, 0), (0, 2, 0), (0, 0, 2), (4, 0, 0), (0, 4, 0), (0, 0, 4), (2, 0, 2))]
STEPS = [(sx, sz) for sz in (-1, 0, 1) for sx in (-1, 0, 1) if sx != 0 or sz != 0]


def bits(octant):
    return octant % 2, octant // 2 % 2, octant // 4


def leaf_slot(octant):
    bit_x, bit_y, bit_z = bits(octant)
    return (bit_x + 2 * bit_z) * 2 + bit_y


@functools.lru_cache(None)
def far_table():
    shape = (len(STEPS), 8, SLOT, 8, SLOT)
    table = np.zeros(shape)
    gap_nodes = 0.5 * (CHECK[None, :, :] - EQUIV[:, None, :])
    for index, (step_x, step_z) in enumerate(STEPS):
        for source in range(8):
            for target in range(8):
                s, t = bits(source), bits(target)
                gap = np.array([2 * step_x + s[0] - t[0], s[1] - t[1], 2 * step_z + s[2] - t[2]], np.float64)
                if max(abs(gap[0]), abs(gap[2])) >= 2:
                    shifted = gap_nodes - gap
                    value = 1.0 / np.sqrt(np.sum(shifted * shifted, -1) + SOFTENING * SOFTENING) / COEFFS
                    table[index, source, :COEFFS, target, :COEFFS] = value
    return table.reshape(len(STEPS) * LEAVES, LEAVES)


@functools.lru_cache(None)
def shift_table():
    table = np.zeros((8, SLOT, SLOT))
    for leaf in range(8):
        offset = [bit - 0.5 for bit in bits(leaf)]
        for k, target in enumerate(EXPONENTS):
            for i, source in enumerate(EXPONENTS):
                if all(b <= a for a, b in zip(target, source)):
                    value = 1.0
                    for a, b, h in zip(target, source, offset):
                        value *= math.comb(a, b) * 0.5**b * h ** (a - b)
                    table[leaf, i, k] = value
    return table.reshape(8 * SLOT, SLOT)


@functools.lru_cache(None)
def box_nodes():
    gaps = np.zeros((3, SLOT, SLOT))
    gaps[:, :COEFFS, :COEFFS] = np.moveaxis(CHECK[None, :, :] - EQUIV[:, None, :], -1, 0)
    gaps[:, COEFFS:] = gaps[:, HEAVY]
    gaps[1] = gaps[1] ** 2 + SOFTENING * SOFTENING
    return gaps.astype(np.float32)


def dot(left, right):
    return jnp.dot(left, right, preferred_element_type=jnp.float32)


def dot_nt(left, right):
    return lax.dot_general(left, right, (((1,), (1,)), ((), ())), preferred_element_type=jnp.float32)


def low_bits(value):
    return value.astype(jnp.bfloat16)


def heavy_table():
    table = np.zeros((SLOT, SLOT), np.float32)
    table[HEAVY, np.arange(COEFFS, SLOT)] = 1.0
    return table


def high_low(value):
    high = low_bits(value)
    return high, low_bits(value - high.astype(jnp.float32))


def by_row(values, shape):
    row = lax.broadcasted_iota(jnp.int32, shape, 0)
    result = jnp.zeros(shape, jnp.float32)
    for index, value in enumerate(values):
        result = jnp.where(row == index, value, result)
    return result


def box_place():
    label = lax.axis_index("space")
    return lax.rem(label, ACROSS), lax.div(label, ACROSS)


def lanes(start, size):
    return pl.ds(start if isinstance(start, int) else pl.multiple_of(start, 128), size)


def fetch(pairs, sems):
    copies = [pltpu.make_async_copy(src, dst, sems.at[i]) for i, (src, dst) in enumerate(pairs)]
    for copy in copies:
        copy.start()
    return copies


def pack_kernel(count_in, positions_in, density_in, shift_in, heavy_in, own, basis, moments, totals, *rest):
    payloads, (count, positions, density, shift, heavy, mono, sems) = rest[:2], rest[2:]
    copies = fetch(
        [(count_in, count), (positions_in, positions), (density_in, density), (shift_in, shift), (heavy_in, heavy)], sems
    )
    fields, points = density.shape
    pts = points // 8
    box_x, box_z = box_place()
    for copy in copies:
        copy.wait()
    local = []
    for leaf in range(8):
        bit_x, bit_y, bit_z = bits(leaf)
        centre = by_row(
            [2.0 * box_x.astype(jnp.float32) + (bit_x + 0.5), bit_y + 0.5, 2.0 * box_z.astype(jnp.float32) + (bit_z + 0.5)],
            (3, 1),
        )
        here = slice(leaf * pts, (leaf + 1) * pts)
        offset = positions[:, here] - centre
        local.append(offset)
        high = low_bits(offset).astype(jnp.float32)
        middle = low_bits(offset - high).astype(jnp.float32)
        raw = density[:, here].astype(jnp.float32)
        mass = jnp.where(lax.broadcasted_iota(jnp.int32, raw.shape, 1) < count[leaf], raw, 0.0)
        spare = jnp.zeros((ROWS - fields - 6, pts), jnp.float32)
        own[:, here] = low_bits(jnp.concatenate([mass, high, middle, spare], axis=0))

    axes = [2.0 * jnp.concatenate([part[a : a + 1] for part in local], axis=0) for a in range(3)]
    made = {(0, 0, 0): jnp.ones((8, pts), jnp.float32)}
    for k, powers in enumerate(EXPONENTS):
        if powers not in made:
            a = next(i for i in range(3) if powers[i] > 0)
            before = tuple(p - (i == a) for i, p in enumerate(powers))
            made[powers] = made[before] * axes[a]
        mono[k] = made[powers]
    mono[COEFFS:SLOT] = jnp.zeros((SLOT - COEFFS, 8, pts), jnp.float32)
    parts = []
    for leaf in range(8):
        here = slice(leaf * pts, (leaf + 1) * pts)
        high, low = high_low(mono[:, leaf, :])
        basis[0:SLOT, here] = high
        basis[SLOT:, here] = low
        parts.append(dot_nt(own[:, here], high))
    moment, rest = high_low(jnp.concatenate(parts, axis=1))
    moments[...] = moment
    total = dot(moment, shift[...]) + dot(rest, shift[...])
    total_high, total_low = high_low(total)
    total = low_bits(total_high.astype(jnp.float32) + dot(total_low, heavy[...]))
    total = jnp.concatenate([total, jnp.zeros_like(total)], axis=1)
    totals[...] = total
    for distance, payload in zip((1, 3), payloads):
        bit = jnp.where((box_x ^ distance) > box_x, 1, 0)
        for place in range(4):
            payload[:, lanes(place * pts, pts)] = own[:, lanes((bit + 2 * place) * pts, pts)]
        payload[:, lanes(4 * pts, LEAVES)] = moment
        payload[:, lanes(4 * pts + LEAVES, 2 * SLOT)] = total


def features(held, start, size, centre, target):
    value = held[16:ROWS, lanes(start, size)].astype(jnp.float32)
    x = value[1:4] + value[4:7] + by_row(centre, (3, 1))
    norm = jnp.sum(x * x, axis=0, keepdims=True)
    if target:
        norm = norm + SOFTENING * SOFTENING
    parts, norms = [], []
    for source, out in ((x, parts), (norm, norms)):
        left = source
        for _ in range(3):
            high = low_bits(left).astype(jnp.float32)
            out.append(high)
            left = left - high
    one = jnp.ones_like(norm)
    zero = jnp.zeros_like(norm)
    blank = jnp.zeros((3, norm.shape[1]), jnp.float32)
    blocks = []
    order = (0, 1, 0, 2, 0, 1) if target else (0, 0, 1, 0, 2, 1)
    for index, which in enumerate(order):
        coords = -2.0 * parts[which] if target else parts[which]
        if index < 3:
            pair = [one, norms[index]] if target else [norms[index], one]
        else:
            pair = [zero, zero]
        blocks += [coords, *pair, blank]
    return jnp.concatenate(blocks, axis=0)


def source_features(held, start, size, centre):
    return low_bits(jnp.transpose(features(held, start, size, centre, False)))


def pulled(near, jobs, target, size, first=None):
    width = target.shape[1] // 8
    tiles = []
    for group, source, masses, starts in jobs:
        for piece in range(2):
            here = lanes((2 * group + piece) * width, width)
            for turn, start in enumerate(starts):
                tiles.append((here, source, masses, lanes(start, size), turn == 0, turn + 1 == len(starts)))

    def squares(tile):
        return dot(tile[1][tile[3], :], target[:, tile[0]])

    ahead, kernel, total = squares(tiles[0]), None, None
    for turn in range(len(tiles) + 1):
        square = ahead
        if turn + 1 < len(tiles):
            ahead = squares(tiles[turn + 1])
        if turn > 0:
            here, _, masses, place, opens, closes = tiles[turn - 1]
            if opens:
                total = jnp.zeros((ROWS, width), jnp.float32) if first is None else first[:, here]
            total = total + dot(masses[:, place], kernel)
            if closes:
                near[:, here] = total
        if turn < len(tiles):
            kernel = low_bits(lax.rsqrt(square))


def own_groups(near, first, last, target, source, own):
    pts = source.shape[0] // 8
    starts = [2 * p * pts for p in range(4)]
    pulled(near, [(group, source, own, starts) for group in range(first, last)], target, 2 * pts)


def box_columns(depth, box_x, box_z, nodes):
    blocks = []
    for turn, distance in [(turn, distance) for turn in range(depth) for distance in range(ACROSS)]:
        gap_x = 2 * (box_x - (box_x ^ distance))
        gap_z = 2 * (box_z - ((box_z ^ turn) if depth == 4 else turn))
        across_x = nodes[0] + gap_x.astype(jnp.float32)
        across_z = nodes[2] + gap_z.astype(jnp.float32)
        apart = jnp.maximum(jnp.abs(gap_x), jnp.abs(gap_z)) >= 4
        value = lax.rsqrt(across_x * across_x + across_z * across_z + nodes[1])
        blocks.append(low_bits(value * jnp.where(apart, 1.0 / COEFFS, 0.0)))
    return jnp.concatenate(blocks, axis=0)


def own_kernel(depth, count_in, weights_in, own, *rest):
    tables, outs, rest = rest[:3], rest[3:11], rest[11:]
    near, source, target, scale, column, columns, far, spread = outs
    nodes, count, weights, sems = rest
    copies = fetch([*zip(tables, (far, spread, nodes)), (count_in, count), (weights_in, weights)], sems)
    points = own.shape[1]
    pts = points // 8
    for leaf in range(8):
        centre = [bit - 0.5 for bit in bits(leaf)]
        source[lanes(leaf * pts, pts), :] = source_features(own, leaf * pts, pts, centre)
        target[:, lanes(leaf_slot(leaf) * pts, pts)] = low_bits(features(own, leaf * pts, pts, centre, True))
    own_groups(near, 0, EARLY, target, source, own)
    for copy in copies:
        copy.wait()
    columns[...] = box_columns(depth, *box_place(), nodes)
    column[...] = by_row([weights[field] for field in range(weights.shape[0])], column.shape)
    lane_index = lax.broadcasted_iota(jnp.int32, (1, pts), 1)
    for leaf in range(8):
        scale[:, leaf * pts : (leaf + 1) * pts] = jnp.where(lane_index < count[leaf], 1.0 / (128.0 * pts), 0.0)


def spread_first(value, node):
    starts = [leaf * SLOT + node for leaf in range(8)]
    return jnp.concatenate([jnp.broadcast_to(value[:, s : s + 1], (ROWS, SLOT)) for s in starts], axis=1)


def decoded(coded):
    value = coded.astype(jnp.float32)
    node = lax.broadcasted_iota(jnp.int32, value.shape, 1) % SLOT
    return jnp.where(node == 0, 0.0, value) + spread_first(value, 0) + spread_first(value, COEFFS)


def faces_of(faces, bit, given, own, left, right, rows=None):
    points = own.shape[1]
    pts = points // 8
    for y in range(2):
        for x in range(4):
            place = lanes((2 * x + y) * pts, pts)
            if x in (0, 3):
                side = left if x == 0 else right
                faces[:, place] = side[:, lanes((y + 2 * bit) * pts, pts)]
            else:
                faces[:, place] = own[:, lanes((x - 1 + 2 * y + 4 * bit) * pts, pts)]
    node = lax.broadcasted_iota(jnp.int32, given.shape, 1) % SLOT
    base = spread_first(given, 0)
    base_high = low_bits(base).astype(jnp.float32)
    coded = jnp.where(node == 0, base_high, jnp.where(node == COEFFS, base - base_high, given - base))
    faces[:, lanes(points, LEAVES)] = low_bits(coded)
    if rows is not None:
        faces[:, lanes(points + LEAVES, rows.shape[1])] = rows


def sums_for(above, left, moments, right, far):
    base = left.shape[1] - LEAVES
    around = jnp.concatenate([left[:, lanes(base, LEAVES)], moments[...], right[:, lanes(base, LEAVES)]], axis=1)
    return dot(around, far[lanes(jnp.where(above == 1, 0, 5 * LEAVES), 3 * LEAVES), :])


def row_kernel(own, moments, totals, from_1, from_2, from_3, far, left, right, faces_even, rows):
    box_x, box_z = box_place()
    for side, step in ((left, -1), (right, 1)):
        side[...] = jnp.zeros(side.shape, side.dtype)
        for distance, held in ((1, from_1), (3, from_3)):

            @pl.when((box_x ^ distance) - box_x == step)
            def _(side=side, held=held):
                side[...] = held[:, lanes(0, side.shape[1])]

    ends = lanes(left.shape[1], 2 * SLOT)
    row = [totals[...], from_1[:, ends], from_2[...], from_3[:, ends]]
    row = jnp.concatenate([box[:, :SLOT] for box in row], axis=1)
    rows[...] = row
    above = 1 - lax.rem(box_z, 2)
    faces_of(faces_even, above, sums_for(above, left, moments, right, far), own, left, right, row)


def side_pulls(near, left, right, early, target, sides_left, sides_right):
    pts = early.shape[1] // 8
    jobs = []
    for step, side, held in ((0, left, sides_left), (1, right, sides_right)):
        for place in range(4):
            centre = (1.5 if step else -1.5, place % 2 - 0.5, place // 2 - 0.5)
            held[lanes(place * pts, pts), :] = source_features(side, place * pts, pts, centre)
        jobs += [(step, held, side, [0, 2 * pts]), (step + 2, held, side, [0, 2 * pts])]
    pulled(near, jobs, target, 2 * pts, early)


def middle_kernel(own, left, right, moments, far, early, source, target, near, faces_odd, same, *sides):
    points = own.shape[1]
    _, box_z = box_place()
    above = lax.rem(box_z, 2)
    faces_of(faces_odd, above, sums_for(above, left, moments, right, far), own, left, right)
    base = left.shape[1] - LEAVES
    beside = jnp.concatenate([left[:, lanes(base, LEAVES)], right[:, lanes(base, LEAVES)]], axis=1)
    same[...] = dot(beside, far[lanes(3 * LEAVES, 2 * LEAVES), :])
    near[:, lanes(0, EARLY * points // 4)] = early[...]
    own_groups(near, EARLY, 4, target, source, own)

    @pl.when(above == 1)
    def _():
        side_pulls(near, left, right, near, target, *sides)


def side_kernel(left, right, early, target, near, *sides):
    _, box_z = box_place()
    odd = lax.rem(box_z, 2) == 1

    @pl.when(odd)
    def _():
        near[...] = early[...]

    @pl.when(jnp.logical_not(odd))
    def _():
        side_pulls(near, left, right, early, target, *sides)


def both_kernel(rows, faces, both):
    width = rows.shape[1]
    both[:, lanes(0, width)] = rows[...]
    both[:, lanes(width, width)] = faces[:, lanes(faces.shape[1] - width, width)]


def layer_pulls(near, early, step, inside, target, faces, sides):
    points = early.shape[1]
    pts = points // 8

    @pl.when(inside)
    def _():
        for place in range(8):
            height = jnp.where(step == 1, 1.5, -1.5)
            centre = (place // 2 - 1.5, place % 2 - 0.5, height)
            sides[lanes(place * pts, pts), :] = source_features(faces, place * pts, pts, centre)

        jobs = [(i + 2 * step, sides, faces, [2 * (x + i) * pts for x in range(3)]) for i in range(2)]
        pulled(near, jobs, target, 2 * pts, early)

    @pl.when(jnp.logical_not(inside))
    def _():
        here = lanes(step * (points // 2), points // 2)
        near[:, here] = early[:, here]


def even_kernel(early, target, faces, near, sides):
    _, box_z = box_place()
    points = early.shape[1]
    step = 1 - lax.rem(box_z, 2)
    other = lanes((1 - step) * (points // 2), points // 2)
    near[:, other] = early[:, other]
    layer_pulls(near, early, step, box_z >= 0, target, faces, sides)


def odd_inside(depth):
    _, box_z = box_place()
    step = lax.rem(box_z, 2)
    return step, (box_z + 2 * step - 1 >= 0) & (box_z + 2 * step - 1 < depth)


def odd_kernel(depth, early, target, faces, near, sides):
    points = early.shape[1]
    step, inside = odd_inside(depth)
    other = lanes((1 - step) * (points // 2), points // 2)
    near[:, other] = early[:, other]
    layer_pulls(near, early, step, inside, target, faces, sides)


def last_kernel(depth, near, faces_even, faces_odd, basis, scale, column, columns, spread, same, *rest):
    held, (potential, sums) = rest[:-2], rest[-2:]
    fields, points = potential.shape
    pts = points // 8
    _, inside = odd_inside(depth)
    if depth == 4:
        rows, distant = held
        width = rows.shape[1]
        near_rows = faces_even[:, lanes(faces_even.shape[1] - width, width)]
        layers = [rows[...], near_rows, distant[:, lanes(0, width)], distant[:, lanes(width, width)]]
    else:
        layers = [held[0][layer] for layer in range(depth)]
    coarse_high, coarse_low = high_low(dot(jnp.concatenate(layers, axis=1), columns[...]))
    value = same[...] + dot(coarse_high, spread[...]) + dot(coarse_low, spread[...])
    value = value + decoded(faces_even[:, lanes(points, LEAVES)])
    value = value + jnp.where(inside, decoded(faces_odd[:, lanes(points, LEAVES)]), 0.0)
    local_high, local_low = high_low(value)
    weight = column[0:fields, 0:1]
    for leaf in range(8):
        here = slice(leaf * pts, (leaf + 1) * pts)
        slot = slice(leaf * SLOT, (leaf + 1) * SLOT)
        doubled = jnp.concatenate([local_high[:, slot], local_high[:, slot]], axis=1)
        far_part = dot(doubled, basis[:, here]) + dot(local_low[:, slot], basis[0:SLOT, here])
        total = near[0:fields, lanes(leaf_slot(leaf) * pts, pts)] + far_part[:fields]
        total = total * scale[:, here]
        potential[:, here] = total
        sums[:, here] = jnp.sum(total * weight, axis=0, keepdims=True)
    sums[:, points:] = jnp.broadcast_to(jnp.sum(weight), (1, sums.shape[1] - points))


def mean_kernel(mine, other, mean):
    points = mean.shape[1]
    total = mine[...] + other[...]
    mean[...] = total[:, :points] / total[:, points : points + 1]


def swapped(block, axis, partner):
    size = lax.axis_size(axis)
    return lax.ppermute(block, axis, [(partner(i), i) for i in range(size)])


def swapped_odd(block):
    boxes, cores = lax.axis_size("space"), lax.axis_size("sig")
    pairs = []
    for box in range(boxes):
        other = box + ACROSS if box // ACROSS % 2 else box - ACROSS
        for core in range(cores):
            source = other * cores + core if 0 <= other < boxes else box * cores + (core ^ 1)
            pairs.append((source, box * cores + core))
    return lax.ppermute(block, ("space", "sig"), pairs)


def per_device(positions, density, leaf_count, sigma_weights):
    fields, points = density.shape
    pts = points // 8
    depth = lax.axis_size("space") // ACROSS
    vmem, hbm = pl.BlockSpec(memory_space=pltpu.VMEM), pl.BlockSpec(memory_space=pltpu.HBM)

    def call(kernel, name, in_specs, outs, scratch, *args):
        return pl.pallas_call(
            kernel,
            in_specs=in_specs,
            out_specs=[vmem] * len(outs),
            out_shape=[jax.ShapeDtypeStruct(shape, dtype) for shape, dtype in outs],
            scratch_shapes=scratch,
            compiler_params=pltpu.CompilerParams(vmem_limit_bytes=24 * MEGA),
            name=name,
        )(*(pltpu.with_memory_space_constraint(a, pltpu.HBM) if s is hbm else a for s, a in zip(in_specs, args)))

    half, full = jnp.bfloat16, jnp.float32
    shift = shift_table()
    side_shape = ((ROWS, 4 * pts + LEAVES), half)
    given_shape = ((ROWS, 4 * pts + LEAVES + 2 * SLOT), half)
    faces_shape = ((ROWS, points + LEAVES), half)
    even_shape = ((ROWS, points + LEAVES + SLOT * ACROSS), half)
    rows_shape = ((ROWS, SLOT * ACROSS), half)
    both_shape = ((ROWS, 2 * SLOT * ACROSS), half)
    near_shape, sums_shape = ((ROWS, points), full), ((ROWS, LEAVES), full)
    side_scratch = [pltpu.VMEM((4 * pts, FEATURES), half)] * 2
    rows_scratch = pltpu.VMEM((8 * pts, FEATURES), half)
    own, basis, moments, totals, *given = call(
        pack_kernel,
        "pack",
        [hbm] * 5,
        [
            ((ROWS, points), half),
            ((2 * SLOT, points), half),
            ((ROWS, LEAVES), half),
            ((ROWS, 2 * SLOT), half),
            given_shape,
            given_shape,
        ],
        [
            pltpu.SMEM((8,), jnp.int32),
            pltpu.VMEM((3, points), full),
            pltpu.VMEM((fields, points), half),
            pltpu.VMEM((LEAVES, SLOT), half),
            pltpu.VMEM((SLOT, SLOT), half),
            pltpu.VMEM((SLOT, 8, pts), full),
            pltpu.SemaphoreType.DMA((5,)),
        ],
        leaf_count,
        positions,
        density,
        jnp.asarray(shift, half),
        jnp.asarray(heavy_table(), half),
    )
    from_2 = swapped(totals, "space", lambda i: i ^ 2)
    from_1 = swapped(given[0], "space", lambda i: i ^ 1)
    from_3 = swapped(given[1], "space", lambda i: i ^ 3)
    near, source, target, scale, column, columns, far, spread = call(
        functools.partial(own_kernel, depth),
        "near_own",
        [hbm] * 2 + [vmem] + [hbm] * 3,
        [
            ((ROWS, EARLY * points // 4), full),
            ((points, FEATURES), half),
            ((FEATURES, points), half),
            ((1, points), full),
            ((ROWS, 128), full),
            ((ACROSS * depth * SLOT, SLOT), half),
            ((len(STEPS) * LEAVES, LEAVES), half),
            ((SLOT, LEAVES), half),
        ],
        [
            pltpu.VMEM((3, SLOT, SLOT), full),
            pltpu.SMEM((8,), jnp.int32),
            pltpu.SMEM((fields,), full),
            pltpu.SemaphoreType.DMA((5,)),
        ],
        leaf_count,
        sigma_weights,
        own,
        jnp.asarray(far_table(), half),
        jnp.asarray(shift.T.copy(), half),
        jnp.asarray(box_nodes()),
    )
    left, right, faces_even, rows = call(
        row_kernel,
        "row",
        [vmem] * 7,
        [side_shape, side_shape, even_shape, rows_shape],
        [],
        own,
        moments,
        totals,
        from_1,
        from_2,
        from_3,
        far,
    )
    faces_even = swapped(faces_even, "space", lambda i: i ^ ACROSS)
    near, faces_odd, same = call(
        middle_kernel,
        "near_middle",
        [vmem] * 8,
        [near_shape, faces_shape, sums_shape],
        side_scratch,
        own,
        left,
        right,
        moments,
        far,
        near,
        source,
        target,
    )
    faces_odd = swapped_odd(faces_odd)
    near, = call(
        side_kernel,
        "near_side",
        [vmem] * 4,
        [near_shape],
        side_scratch,
        left,
        right,
        near,
        target,
    )
    if depth == 4:
        both, = call(both_kernel, "row_pairs", [vmem] * 2, [both_shape], [], rows, faces_even)
        held = [rows, swapped(both, "space", lambda i: i ^ (2 * ACROSS))]
    else:
        groups = [[z * ACROSS + x for z in range(depth)] for x in range(ACROSS)]
        held = [lax.all_gather(rows, "space", axis_index_groups=groups)]
    near, = call(even_kernel, "near_even", [vmem] * 3, [near_shape], [rows_scratch], near, target, faces_even)
    near, = call(
        functools.partial(odd_kernel, depth),
        "near_odd",
        [vmem] * 3,
        [near_shape],
        [rows_scratch],
        near,
        target,
        faces_odd,
    )
    potential, sums = call(
        functools.partial(last_kernel, depth),
        "evaluate",
        [vmem] * (9 + len(held)),
        [((fields, points), full), ((1, points + 128), full)],
        [],
        near,
        faces_even,
        faces_odd,
        basis,
        scale,
        column,
        columns,
        spread,
        same,
        *held,
    )
    if lax.axis_size("sig") == 2:
        other = swapped(sums, "sig", lambda i: i ^ 1)
    else:
        other = lax.psum(sums, "sig") - sums
    mean, = call(mean_kernel, "mean", [vmem] * 2, [((1, points), full)], [], sums, other)
    return potential, mean.reshape(points)


def solution(mesh):
    in_specs = (P(None, "space"), P("sig", "space"), P("space"), P("sig"))
    out_specs = (P("sig", "space"), P("space"))
    return jax.shard_map(per_device, mesh=mesh, in_specs=in_specs, out_specs=out_specs, check_vma=False)
```

```python
import functools
import math

import jax
import jax.numpy as jnp
import numpy as np
from jax import lax
from jax.experimental import pallas as pl
from jax.experimental.pallas import tpu as pltpu
from jax.sharding import PartitionSpec as P

ORDER = 5
SOFTENING = 0.1
ACROSS = 4
SLOT = 64
ROWS = 24
LEAVES = 8 * SLOT
MEGA = 1024 * 1024
FEATURES = 48
EARLY = 3


def exponent_table(order_max):
    entries_list = []
    for degree in range(order_max + 1):
        for first_power in range(degree, -1, -1):
            for second_power in range(degree - first_power, -1, -1):
                entries_list.append((first_power, second_power, degree - first_power - second_power))
    return entries_list


def node_table(count_nodes, offset_value):
    counter = np.arange(1, count_nodes + 1, dtype=np.float32)[:, None]
    stride_set = np.array([0.7548776662466927, 0.5698402909980532, 0.4142135623730951], dtype=np.float32)[None, :]
    unit_points = np.mod(counter * stride_set + np.float32(offset_value), np.float32(1.0))
    return (np.float32(2.0) * unit_points - np.float32(1.0)).astype(np.float32)


EXPONENTS = exponent_table(ORDER)
COEFFS = len(EXPONENTS)
CHECK = node_table(COEFFS, 0.5).astype(np.float64)
EQUIV = node_table(COEFFS, 0.0).astype(np.float64)
HEAVY = [EXPONENTS.index(e) for e in ((0, 0, 0), (2, 0, 0), (0, 2, 0), (0, 0, 2), (4, 0, 0), (0, 4, 0), (0, 0, 4), (2, 0, 2))]
STEPS = [(sx, sz) for sz in (-1, 0, 1) for sx in (-1, 0, 1) if sx != 0 or sz != 0]


def bits(octant):
    return octant % 2, octant // 2 % 2, octant // 4


def leaf_slot(octant):
    bit_x, bit_y, bit_z = bits(octant)
    return (bit_x + 2 * bit_z) * 2 + bit_y


@functools.lru_cache(None)
def far_table():
    shape = (len(STEPS), 8, SLOT, 8, SLOT)
    table = np.zeros(shape)
    gap_nodes = 0.5 * (CHECK[None, :, :] - EQUIV[:, None, :])
    for index, (step_x, step_z) in enumerate(STEPS):
        for source in range(8):
            for target in range(8):
                s, t = bits(source), bits(target)
                gap = np.array([2 * step_x + s[0] - t[0], s[1] - t[1], 2 * step_z + s[2] - t[2]], np.float64)
                if max(abs(gap[0]), abs(gap[2])) >= 2:
                    shifted = gap_nodes - gap
                    value = 1.0 / np.sqrt(np.sum(shifted * shifted, -1) + SOFTENING * SOFTENING) / COEFFS
                    table[index, source, :COEFFS, target, :COEFFS] = value
    return table.reshape(len(STEPS) * LEAVES, LEAVES)


@functools.lru_cache(None)
def shift_table():
    table = np.zeros((8, SLOT, SLOT))
    for leaf in range(8):
        offset = [bit - 0.5 for bit in bits(leaf)]
        for k, target in enumerate(EXPONENTS):
            for i, source in enumerate(EXPONENTS):
                if all(b <= a for a, b in zip(target, source)):
                    value = 1.0
                    for a, b, h in zip(target, source, offset):
                        value *= math.comb(a, b) * 0.5**b * h ** (a - b)
                    table[leaf, i, k] = value
    return table.reshape(8 * SLOT, SLOT)


@functools.lru_cache(None)
def box_nodes():
    gaps = np.zeros((3, SLOT, SLOT))
    gaps[:, :COEFFS, :COEFFS] = np.moveaxis(CHECK[None, :, :] - EQUIV[:, None, :], -1, 0)
    gaps[:, COEFFS:] = gaps[:, HEAVY]
    gaps[1] = gaps[1] ** 2 + SOFTENING * SOFTENING
    return gaps.astype(np.float32)


def dot(left, right):
    return jnp.dot(left, right, preferred_element_type=jnp.float32)


def dot_nt(left, right):
    return lax.dot_general(left, right, (((1,), (1,)), ((), ())), preferred_element_type=jnp.float32)


def low_bits(value):
    return value.astype(jnp.bfloat16)


def heavy_table():
    table = np.zeros((SLOT, SLOT), np.float32)
    table[HEAVY, np.arange(COEFFS, SLOT)] = 1.0
    return table


def high_low(value):
    high = low_bits(value)
    return high, low_bits(value - high.astype(jnp.float32))


def by_row(values, shape):
    row = lax.broadcasted_iota(jnp.int32, shape, 0)
    result = jnp.zeros(shape, jnp.float32)
    for index, value in enumerate(values):
        result = jnp.where(row == index, value, result)
    return result


def box_place():
    label = lax.axis_index("space")
    return lax.rem(label, ACROSS), lax.div(label, ACROSS)


def lanes(start, size):
    return pl.ds(start if isinstance(start, int) else pl.multiple_of(start, 128), size)


def fetch(pairs, sems):
    copies = [pltpu.make_async_copy(src, dst, sems.at[i]) for i, (src, dst) in enumerate(pairs)]
    for copy in copies:
        copy.start()
    return copies


def pack_kernel(count_in, positions_in, density_in, shift_in, heavy_in, own, mono, moments, totals, *rest):
    payloads, (count, positions, density, shift, heavy, sems) = rest[:2], rest[2:]
    copies = fetch(
        [(count_in, count), (positions_in, positions), (density_in, density), (shift_in, shift), (heavy_in, heavy)], sems
    )
    fields, points = density.shape
    pts = points // 8
    box_x, box_z = box_place()
    for copy in copies:
        copy.wait()
    local = []
    for leaf in range(8):
        bit_x, bit_y, bit_z = bits(leaf)
        centre = by_row(
            [2.0 * box_x.astype(jnp.float32) + (bit_x + 0.5), bit_y + 0.5, 2.0 * box_z.astype(jnp.float32) + (bit_z + 0.5)],
            (3, 1),
        )
        here = slice(leaf * pts, (leaf + 1) * pts)
        offset = positions[:, here] - centre
        local.append(offset)
        high = low_bits(offset).astype(jnp.float32)
        middle = low_bits(offset - high).astype(jnp.float32)
        raw = density[:, here].astype(jnp.float32)
        mass = jnp.where(lax.broadcasted_iota(jnp.int32, raw.shape, 1) < count[leaf], raw, 0.0)
        spare = jnp.zeros((ROWS - fields - 6, pts), jnp.float32)
        own[:, here] = low_bits(jnp.concatenate([mass, high, middle, spare], axis=0))

    axes = [2.0 * jnp.concatenate([part[a : a + 1] for part in local], axis=0) for a in range(3)]
    made = {(0, 0, 0): jnp.ones((8, pts), jnp.float32)}
    for k, powers in enumerate(EXPONENTS):
        if powers not in made:
            a = next(i for i in range(3) if powers[i] > 0)
            before = tuple(p - (i == a) for i, p in enumerate(powers))
            made[powers] = made[before] * axes[a]
        mono[k] = made[powers]
    mono[COEFFS:SLOT] = jnp.zeros((SLOT - COEFFS, 8, pts), jnp.float32)
    parts = []
    for leaf in range(8):
        here = slice(leaf * pts, (leaf + 1) * pts)
        parts.append(dot_nt(own[:, here], low_bits(mono[:, leaf, :])))
    moment, rest = high_low(jnp.concatenate(parts, axis=1))
    moments[...] = moment
    total = dot(moment, shift[...]) + dot(rest, shift[...])
    total_high, total_low = high_low(total)
    total = low_bits(total_high.astype(jnp.float32) + dot(total_low, heavy[...]))
    total = jnp.concatenate([total, jnp.zeros_like(total)], axis=1)
    totals[...] = total
    for distance, payload in zip((1, 3), payloads):
        bit = jnp.where((box_x ^ distance) > box_x, 1, 0)
        for place in range(4):
            payload[:, lanes(place * pts, pts)] = own[:, lanes((bit + 2 * place) * pts, pts)]
        payload[:, lanes(4 * pts, LEAVES)] = moment
        payload[:, lanes(4 * pts + LEAVES, 2 * SLOT)] = total


def features(held, start, size, centre, target):
    value = held[16:ROWS, lanes(start, size)].astype(jnp.float32)
    x = value[1:4] + value[4:7] + by_row(centre, (3, 1))
    norm = jnp.sum(x * x, axis=0, keepdims=True)
    if target:
        norm = norm + SOFTENING * SOFTENING
    parts, norms = [], []
    for source, out in ((x, parts), (norm, norms)):
        left = source
        for _ in range(3):
            high = low_bits(left).astype(jnp.float32)
            out.append(high)
            left = left - high
    one = jnp.ones_like(norm)
    zero = jnp.zeros_like(norm)
    blank = jnp.zeros((3, norm.shape[1]), jnp.float32)
    blocks = []
    order = (0, 1, 0, 2, 0, 1) if target else (0, 0, 1, 0, 2, 1)
    for index, which in enumerate(order):
        coords = -2.0 * parts[which] if target else parts[which]
        if index < 3:
            pair = [one, norms[index]] if target else [norms[index], one]
        else:
            pair = [zero, zero]
        blocks += [coords, *pair, blank]
    return jnp.concatenate(blocks, axis=0)


def source_features(held, start, size, centre):
    return low_bits(jnp.transpose(features(held, start, size, centre, False)))


def pulled(near, jobs, target, size, first=None):
    width = target.shape[1] // 8
    tiles = []
    for group, source, masses, starts in jobs:
        for piece in range(2):
            here = lanes((2 * group + piece) * width, width)
            for turn, start in enumerate(starts):
                tiles.append((here, source, masses, lanes(start, size), turn == 0, turn + 1 == len(starts)))

    def squares(tile):
        return dot(tile[1][tile[3], :], target[:, tile[0]])

    ahead, kernel, total = squares(tiles[0]), None, None
    for turn in range(len(tiles) + 1):
        square = ahead
        if turn + 1 < len(tiles):
            ahead = squares(tiles[turn + 1])
        if turn > 0:
            here, _, masses, place, opens, closes = tiles[turn - 1]
            if opens:
                total = jnp.zeros((ROWS, width), jnp.float32) if first is None else first[:, here]
            total = total + dot(masses[:, place], kernel)
            if closes:
                near[:, here] = total
        if turn < len(tiles):
            kernel = low_bits(lax.rsqrt(square))


def own_groups(near, first, last, target, source, own):
    pts = source.shape[0] // 8
    starts = [2 * p * pts for p in range(4)]
    pulled(near, [(group, source, own, starts) for group in range(first, last)], target, 2 * pts)


def box_columns(depth, box_x, box_z, nodes):
    blocks = []
    for turn, distance in [(turn, distance) for turn in range(depth) for distance in range(ACROSS)]:
        gap_x = 2 * (box_x - (box_x ^ distance))
        gap_z = 2 * (box_z - ((box_z ^ turn) if depth == 4 else turn))
        across_x = nodes[0] + gap_x.astype(jnp.float32)
        across_z = nodes[2] + gap_z.astype(jnp.float32)
        apart = jnp.maximum(jnp.abs(gap_x), jnp.abs(gap_z)) >= 4
        value = lax.rsqrt(across_x * across_x + across_z * across_z + nodes[1])
        blocks.append(low_bits(value * jnp.where(apart, 1.0 / COEFFS, 0.0)))
    return jnp.concatenate(blocks, axis=0)


def own_kernel(count_in, weights_in, own, *rest):
    tables, outs, (count, weights, sems) = rest[:3], rest[3:11], rest[11:]
    near, source, target, scale, column, far, spread, nodes = outs
    copies = fetch([*zip(tables, (far, spread, nodes)), (count_in, count), (weights_in, weights)], sems)
    points = own.shape[1]
    pts = points // 8
    for leaf in range(8):
        centre = [bit - 0.5 for bit in bits(leaf)]
        source[lanes(leaf * pts, pts), :] = source_features(own, leaf * pts, pts, centre)
        target[:, lanes(leaf_slot(leaf) * pts, pts)] = low_bits(features(own, leaf * pts, pts, centre, True))
    own_groups(near, 0, EARLY, target, source, own)
    for copy in copies:
        copy.wait()
    column[...] = by_row([weights[field] for field in range(weights.shape[0])], column.shape)
    lane_index = lax.broadcasted_iota(jnp.int32, (1, pts), 1)
    for leaf in range(8):
        scale[:, leaf * pts : (leaf + 1) * pts] = jnp.where(lane_index < count[leaf], 1.0 / (128.0 * pts), 0.0)


def spread_first(value, node):
    starts = [leaf * SLOT + node for leaf in range(8)]
    return jnp.concatenate([jnp.broadcast_to(value[:, s : s + 1], (ROWS, SLOT)) for s in starts], axis=1)


def decoded(coded):
    value = coded.astype(jnp.float32)
    node = lax.broadcasted_iota(jnp.int32, value.shape, 1) % SLOT
    return jnp.where(node == 0, 0.0, value) + spread_first(value, 0) + spread_first(value, COEFFS)


def faces_of(faces, bit, given, own, left, right, rows=None):
    points = own.shape[1]
    pts = points // 8
    for y in range(2):
        for x in range(4):
            place = lanes((2 * x + y) * pts, pts)
            if x in (0, 3):
                side = left if x == 0 else right
                faces[:, place] = side[:, lanes((y + 2 * bit) * pts, pts)]
            else:
                faces[:, place] = own[:, lanes((x - 1 + 2 * y + 4 * bit) * pts, pts)]
    node = lax.broadcasted_iota(jnp.int32, given.shape, 1) % SLOT
    base = spread_first(given, 0)
    base_high = low_bits(base).astype(jnp.float32)
    coded = jnp.where(node == 0, base_high, jnp.where(node == COEFFS, base - base_high, given - base))
    faces[:, lanes(points, LEAVES)] = low_bits(coded)
    if rows is not None:
        faces[:, lanes(points + LEAVES, rows.shape[1])] = rows


def sums_for(above, left, moments, right, far):
    base = left.shape[1] - LEAVES
    around = jnp.concatenate([left[:, lanes(base, LEAVES)], moments[...], right[:, lanes(base, LEAVES)]], axis=1)
    return dot(around, far[lanes(jnp.where(above == 1, 0, 5 * LEAVES), 3 * LEAVES), :])


def row_kernel(own, moments, totals, from_1, from_2, from_3, far, left, right, faces_even, rows):
    box_x, box_z = box_place()
    for side, step in ((left, -1), (right, 1)):
        side[...] = jnp.zeros(side.shape, side.dtype)
        for distance, held in ((1, from_1), (3, from_3)):

            @pl.when((box_x ^ distance) - box_x == step)
            def _(side=side, held=held):
                side[...] = held[:, lanes(0, side.shape[1])]

    ends = lanes(left.shape[1], 2 * SLOT)
    row = [totals[...], from_1[:, ends], from_2[...], from_3[:, ends]]
    row = jnp.concatenate([box[:, :SLOT] for box in row], axis=1)
    rows[...] = row
    above = 1 - lax.rem(box_z, 2)
    faces_of(faces_even, above, sums_for(above, left, moments, right, far), own, left, right, row)


def side_pulls(near, faces, early, target, scratch):
    pts = early.shape[1] // 8
    jobs = []
    for (step, side), held in zip(faces, scratch):
        for place in range(4):
            centre = (1.5 if step else -1.5, place % 2 - 0.5, place // 2 - 0.5)
            held[lanes(place * pts, pts), :] = source_features(side, place * pts, pts, centre)
        jobs += [(step, held, side, [0, 2 * pts]), (step + 2, held, side, [0, 2 * pts])]
    pulled(near, jobs, target, 2 * pts, early)


def middle_kernel(depth, own, left, right, moments, far, early, source, target, nodes, mono, *rest):
    (near, faces_odd, same, columns, basis), sides = rest[:5], rest[5:]
    points = own.shape[1]
    pts = points // 8
    box_x, box_z = box_place()
    columns[...] = box_columns(depth, box_x, box_z, nodes)
    for leaf in range(8):
        high, low = high_low(mono[:, leaf, :])
        basis[0:SLOT, lanes(leaf * pts, pts)] = high
        basis[SLOT:, lanes(leaf * pts, pts)] = low
    above = lax.rem(box_z, 2)
    faces_of(faces_odd, above, sums_for(above, left, moments, right, far), own, left, right)
    base = left.shape[1] - LEAVES
    beside = jnp.concatenate([left[:, lanes(base, LEAVES)], right[:, lanes(base, LEAVES)]], axis=1)
    same[...] = dot(beside, far[lanes(3 * LEAVES, 2 * LEAVES), :])
    near[:, lanes(0, EARLY * points // 4)] = early[...]
    own_groups(near, EARLY, 4, target, source, own)

    @pl.when(above == 1)
    def _():
        side_pulls(near, [(0, left), (1, right)], near, target, sides)

    @pl.when(above == 0)
    def _():
        side_pulls(near, [(0, left)], near, target, sides)


def side_kernel(right, early, target, near, held):
    _, box_z = box_place()
    odd = lax.rem(box_z, 2) == 1

    @pl.when(odd)
    def _():
        near[...] = early[...]

    @pl.when(jnp.logical_not(odd))
    def _():
        pts = early.shape[1] // 8
        for group in (0, 2):
            here = lanes(2 * group * pts, 2 * pts)
            near[:, here] = early[:, here]
        side_pulls(near, [(1, right)], early, target, [held])


def both_kernel(rows, faces, both):
    width = rows.shape[1]
    both[:, lanes(0, width)] = rows[...]
    both[:, lanes(width, width)] = faces[:, lanes(faces.shape[1] - width, width)]


def layer_pulls(near, early, step, inside, target, faces, sides):
    points = early.shape[1]
    pts = points // 8

    @pl.when(inside)
    def _():
        for place in range(8):
            height = jnp.where(step == 1, 1.5, -1.5)
            centre = (place // 2 - 1.5, place % 2 - 0.5, height)
            sides[lanes(place * pts, pts), :] = source_features(faces, place * pts, pts, centre)

        jobs = [(i + 2 * step, sides, faces, [2 * (x + i) * pts for x in range(3)]) for i in range(2)]
        pulled(near, jobs, target, 2 * pts, early)

    @pl.when(jnp.logical_not(inside))
    def _():
        here = lanes(step * (points // 2), points // 2)
        near[:, here] = early[:, here]


def even_kernel(early, target, faces, near, sides):
    _, box_z = box_place()
    points = early.shape[1]
    step = 1 - lax.rem(box_z, 2)
    other = lanes((1 - step) * (points // 2), points // 2)
    near[:, other] = early[:, other]
    layer_pulls(near, early, step, box_z >= 0, target, faces, sides)


def odd_inside(depth):
    _, box_z = box_place()
    step = lax.rem(box_z, 2)
    return step, (box_z + 2 * step - 1 >= 0) & (box_z + 2 * step - 1 < depth)


def odd_kernel(depth, early, target, faces, near, sides):
    points = early.shape[1]
    step, inside = odd_inside(depth)
    other = lanes((1 - step) * (points // 2), points // 2)
    near[:, other] = early[:, other]
    layer_pulls(near, early, step, inside, target, faces, sides)


def last_kernel(depth, near, faces_even, faces_odd, basis, scale, column, columns, spread, same, *rest):
    held, (potential, sums) = rest[:-2], rest[-2:]
    fields, points = potential.shape
    pts = points // 8
    _, inside = odd_inside(depth)
    if depth == 4:
        rows, distant = held
        width = rows.shape[1]
        near_rows = faces_even[:, lanes(faces_even.shape[1] - width, width)]
        layers = [rows[...], near_rows, distant[:, lanes(0, width)], distant[:, lanes(width, width)]]
    else:
        layers = [held[0][layer] for layer in range(depth)]
    coarse_high, coarse_low = high_low(dot(jnp.concatenate(layers, axis=1), columns[...]))
    value = same[...] + dot(coarse_high, spread[...]) + dot(coarse_low, spread[...])
    value = value + decoded(faces_even[:, lanes(points, LEAVES)])
    value = value + jnp.where(inside, decoded(faces_odd[:, lanes(points, LEAVES)]), 0.0)
    local_high, local_low = high_low(value)
    weight = column[0:fields, 0:1]
    for leaf in range(8):
        here = slice(leaf * pts, (leaf + 1) * pts)
        slot = slice(leaf * SLOT, (leaf + 1) * SLOT)
        doubled = jnp.concatenate([local_high[:, slot], local_high[:, slot]], axis=1)
        far_part = dot(doubled, basis[:, here]) + dot(local_low[:, slot], basis[0:SLOT, here])
        total = near[0:fields, lanes(leaf_slot(leaf) * pts, pts)] + far_part[:fields]
        total = total * scale[:, here]
        potential[:, here] = total
        sums[:, here] = jnp.sum(total * weight, axis=0, keepdims=True)
    sums[:, points:] = jnp.broadcast_to(jnp.sum(weight), (1, sums.shape[1] - points))


def mean_kernel(mine, other, mean):
    points = mean.shape[1]
    total = mine[...] + other[...]
    mean[...] = total[:, :points] / total[:, points : points + 1]


def swapped(block, axis, partner):
    size = lax.axis_size(axis)
    return lax.ppermute(block, axis, [(partner(i), i) for i in range(size)])


def swapped_odd(block):
    boxes, cores = lax.axis_size("space"), lax.axis_size("sig")
    pairs = []
    for box in range(boxes):
        other = box + ACROSS if box // ACROSS % 2 else box - ACROSS
        for core in range(cores):
            source = other * cores + core if 0 <= other < boxes else box * cores + (core ^ 1)
            pairs.append((source, box * cores + core))
    return lax.ppermute(block, ("space", "sig"), pairs)


def per_device(positions, density, leaf_count, sigma_weights):
    fields, points = density.shape
    pts = points // 8
    depth = lax.axis_size("space") // ACROSS
    vmem, hbm = pl.BlockSpec(memory_space=pltpu.VMEM), pl.BlockSpec(memory_space=pltpu.HBM)

    def call(kernel, name, in_specs, outs, scratch, *args):
        return pl.pallas_call(
            kernel,
            in_specs=in_specs,
            out_specs=[vmem] * len(outs),
            out_shape=[jax.ShapeDtypeStruct(shape, dtype) for shape, dtype in outs],
            scratch_shapes=scratch,
            compiler_params=pltpu.CompilerParams(vmem_limit_bytes=24 * MEGA),
            name=name,
        )(*(pltpu.with_memory_space_constraint(a, pltpu.HBM) if s is hbm else a for s, a in zip(in_specs, args)))

    half, full = jnp.bfloat16, jnp.float32
    shift = shift_table()
    side_shape = ((ROWS, 4 * pts + LEAVES), half)
    given_shape = ((ROWS, 4 * pts + LEAVES + 2 * SLOT), half)
    faces_shape = ((ROWS, points + LEAVES), half)
    even_shape = ((ROWS, points + LEAVES + SLOT * ACROSS), half)
    rows_shape = ((ROWS, SLOT * ACROSS), half)
    both_shape = ((ROWS, 2 * SLOT * ACROSS), half)
    near_shape, sums_shape = ((ROWS, points), full), ((ROWS, LEAVES), full)
    side_scratch = [pltpu.VMEM((4 * pts, FEATURES), half)] * 2
    rows_scratch = pltpu.VMEM((8 * pts, FEATURES), half)
    own, mono, moments, totals, *given = call(
        pack_kernel,
        "pack",
        [hbm] * 5,
        [
            ((ROWS, points), half),
            ((SLOT, 8, pts), full),
            ((ROWS, LEAVES), half),
            ((ROWS, 2 * SLOT), half),
            given_shape,
            given_shape,
        ],
        [
            pltpu.SMEM((8,), jnp.int32),
            pltpu.VMEM((3, points), full),
            pltpu.VMEM((fields, points), half),
            pltpu.VMEM((LEAVES, SLOT), half),
            pltpu.VMEM((SLOT, SLOT), half),
            pltpu.SemaphoreType.DMA((5,)),
        ],
        leaf_count,
        positions,
        density,
        jnp.asarray(shift, half),
        jnp.asarray(heavy_table(), half),
    )
    from_2 = swapped(totals, "space", lambda i: i ^ 2)
    from_1 = swapped(given[0], "space", lambda i: i ^ 1)
    from_3 = swapped(given[1], "space", lambda i: i ^ 3)
    near, source, target, scale, column, far, spread, nodes = call(
        own_kernel,
        "near_own",
        [hbm] * 2 + [vmem] + [hbm] * 3,
        [
            ((ROWS, EARLY * points // 4), full),
            ((points, FEATURES), half),
            ((FEATURES, points), half),
            ((1, points), full),
            ((ROWS, 128), full),
            ((len(STEPS) * LEAVES, LEAVES), half),
            ((SLOT, LEAVES), half),
            ((3, SLOT, SLOT), full),
        ],
        [
            pltpu.SMEM((8,), jnp.int32),
            pltpu.SMEM((fields,), full),
            pltpu.SemaphoreType.DMA((5,)),
        ],
        leaf_count,
        sigma_weights,
        own,
        jnp.asarray(far_table(), half),
        jnp.asarray(shift.T.copy(), half),
        jnp.asarray(box_nodes()),
    )
    left, right, faces_even, rows = call(
        row_kernel,
        "row",
        [vmem] * 7,
        [side_shape, side_shape, even_shape, rows_shape],
        [],
        own,
        moments,
        totals,
        from_1,
        from_2,
        from_3,
        far,
    )
    faces_even = swapped(faces_even, "space", lambda i: i ^ ACROSS)
    near, faces_odd, same, columns, basis = call(
        functools.partial(middle_kernel, depth),
        "near_middle",
        [vmem] * 10,
        [
            near_shape,
            faces_shape,
            sums_shape,
            ((ACROSS * depth * SLOT, SLOT), half),
            ((2 * SLOT, points), half),
        ],
        side_scratch,
        own,
        left,
        right,
        moments,
        far,
        near,
        source,
        target,
        nodes,
        mono,
    )
    faces_odd = swapped_odd(faces_odd)
    near, = call(
        side_kernel,
        "near_side",
        [vmem] * 3,
        [near_shape],
        side_scratch[:1],
        right,
        near,
        target,
    )
    if depth == 4:
        both, = call(both_kernel, "row_pairs", [vmem] * 2, [both_shape], [], rows, faces_even)
        held = [rows, swapped(both, "space", lambda i: i ^ (2 * ACROSS))]
    else:
        groups = [[z * ACROSS + x for z in range(depth)] for x in range(ACROSS)]
        held = [lax.all_gather(rows, "space", axis_index_groups=groups)]
    near, = call(even_kernel, "near_even", [vmem] * 3, [near_shape], [rows_scratch], near, target, faces_even)
    near, = call(
        functools.partial(odd_kernel, depth),
        "near_odd",
        [vmem] * 3,
        [near_shape],
        [rows_scratch],
        near,
        target,
        faces_odd,
    )
    potential, sums = call(
        functools.partial(last_kernel, depth),
        "evaluate",
        [vmem] * (9 + len(held)),
        [((fields, points), full), ((1, points + 128), full)],
        [],
        near,
        faces_even,
        faces_odd,
        basis,
        scale,
        column,
        columns,
        spread,
        same,
        *held,
    )
    if lax.axis_size("sig") == 2:
        other = swapped(sums, "sig", lambda i: i ^ 1)
    else:
        other = lax.psum(sums, "sig") - sums
    mean, = call(mean_kernel, "mean", [vmem] * 2, [((1, points), full)], [], sums, other)
    return potential, mean.reshape(points)


def solution(mesh):
    in_specs = (P(None, "space"), P("sig", "space"), P("space"), P("sig"))
    out_specs = (P("sig", "space"), P("space"))
    return jax.shard_map(per_device, mesh=mesh, in_specs=in_specs, out_specs=out_specs, check_vma=False)
```

```python
import functools
import math

import jax
import jax.numpy as jnp
import numpy as np
from jax import lax
from jax.experimental import pallas as pl
from jax.experimental.pallas import tpu as pltpu
from jax.sharding import PartitionSpec as P

ORDER = 5
SOFTENING = 0.1
ACROSS = 4
SLOT = 64
ROWS = 24
LEAVES = 8 * SLOT
MEGA = 1024 * 1024
FEATURES = 48
EARLY = 3


def exponent_table(order_max):
    entries_list = []
    for degree in range(order_max + 1):
        for first_power in range(degree, -1, -1):
            for second_power in range(degree - first_power, -1, -1):
                entries_list.append((first_power, second_power, degree - first_power - second_power))
    return entries_list


def node_table(count_nodes, offset_value):
    counter = np.arange(1, count_nodes + 1, dtype=np.float32)[:, None]
    stride_set = np.array([0.7548776662466927, 0.5698402909980532, 0.4142135623730951], dtype=np.float32)[None, :]
    unit_points = np.mod(counter * stride_set + np.float32(offset_value), np.float32(1.0))
    return (np.float32(2.0) * unit_points - np.float32(1.0)).astype(np.float32)


EXPONENTS = exponent_table(ORDER)
COEFFS = len(EXPONENTS)
CHECK = node_table(COEFFS, 0.5).astype(np.float64)
EQUIV = node_table(COEFFS, 0.0).astype(np.float64)
HEAVY = [EXPONENTS.index(e) for e in ((0, 0, 0), (2, 0, 0), (0, 2, 0), (0, 0, 2), (4, 0, 0), (0, 4, 0), (0, 0, 4), (2, 0, 2))]
STEPS = [(sx, sz) for sz in (-1, 0, 1) for sx in (-1, 0, 1) if sx != 0 or sz != 0]


def bits(octant):
    return octant % 2, octant // 2 % 2, octant // 4


def leaf_slot(octant):
    bit_x, bit_y, bit_z = bits(octant)
    return (bit_x + 2 * bit_z) * 2 + bit_y


@functools.lru_cache(None)
def far_table():
    shape = (len(STEPS), 8, SLOT, 8, SLOT)
    table = np.zeros(shape)
    gap_nodes = 0.5 * (CHECK[None, :, :] - EQUIV[:, None, :])
    for index, (step_x, step_z) in enumerate(STEPS):
        for source in range(8):
            for target in range(8):
                s, t = bits(source), bits(target)
                gap = np.array([2 * step_x + s[0] - t[0], s[1] - t[1], 2 * step_z + s[2] - t[2]], np.float64)
                if max(abs(gap[0]), abs(gap[2])) >= 2:
                    shifted = gap_nodes - gap
                    value = 1.0 / np.sqrt(np.sum(shifted * shifted, -1) + SOFTENING * SOFTENING) / COEFFS
                    table[index, source, :COEFFS, target, :COEFFS] = value
    return table.reshape(len(STEPS) * LEAVES, LEAVES)


@functools.lru_cache(None)
def shift_table():
    table = np.zeros((8, SLOT, SLOT))
    for leaf in range(8):
        offset = [bit - 0.5 for bit in bits(leaf)]
        for k, target in enumerate(EXPONENTS):
            for i, source in enumerate(EXPONENTS):
                if all(b <= a for a, b in zip(target, source)):
                    value = 1.0
                    for a, b, h in zip(target, source, offset):
                        value *= math.comb(a, b) * 0.5**b * h ** (a - b)
                    table[leaf, i, k] = value
    return table.reshape(8 * SLOT, SLOT)


@functools.lru_cache(None)
def box_nodes():
    gaps = np.zeros((3, SLOT, SLOT))
    gaps[:, :COEFFS, :COEFFS] = np.moveaxis(CHECK[None, :, :] - EQUIV[:, None, :], -1, 0)
    gaps[:, COEFFS:] = gaps[:, HEAVY]
    gaps[1] = gaps[1] ** 2 + SOFTENING * SOFTENING
    return gaps.astype(np.float32)


def dot(left, right):
    return jnp.dot(left, right, preferred_element_type=jnp.float32)


def dot_nt(left, right):
    return lax.dot_general(left, right, (((1,), (1,)), ((), ())), preferred_element_type=jnp.float32)


def low_bits(value):
    return value.astype(jnp.bfloat16)


def heavy_table():
    table = np.zeros((SLOT, SLOT), np.float32)
    table[HEAVY, np.arange(COEFFS, SLOT)] = 1.0
    return table


def power_table():
    table = np.zeros((3, SLOT, 16), np.float32)
    for axis in range(3):
        for k, powers in enumerate(EXPONENTS):
            table[axis, k, powers[axis]] = 1.0
            table[axis, k, 8 + powers[axis]] = 1.0
    return table.reshape(3 * SLOT, 16)


def high_low(value):
    high = low_bits(value)
    return high, low_bits(value - high.astype(jnp.float32))


def by_row(values, shape):
    row = lax.broadcasted_iota(jnp.int32, shape, 0)
    result = jnp.zeros(shape, jnp.float32)
    for index, value in enumerate(values):
        result = jnp.where(row == index, value, result)
    return result


def box_place():
    label = lax.axis_index("space")
    return lax.rem(label, ACROSS), lax.div(label, ACROSS)


def lanes(start, size):
    return pl.ds(start if isinstance(start, int) else pl.multiple_of(start, 128), size)


def fetch(pairs, sems):
    copies = [pltpu.make_async_copy(src, dst, sems.at[i]) for i, (src, dst) in enumerate(pairs)]
    for copy in copies:
        copy.start()
    return copies


def pack_kernel(count_in, positions_in, density_in, shift_in, heavy_in, powers_in, own, basis, moments, totals, *rest):
    payloads, (count, positions, density, shift, heavy, powers, sems) = rest[:2], rest[2:]
    copies = fetch(
        [
            (count_in, count),
            (positions_in, positions),
            (density_in, density),
            (shift_in, shift),
            (heavy_in, heavy),
            (powers_in, powers),
        ],
        sems,
    )
    fields, points = density.shape
    pts = points // 8
    box_x, box_z = box_place()
    for copy in copies:
        copy.wait()
    local = []
    for leaf in range(8):
        bit_x, bit_y, bit_z = bits(leaf)
        centre = by_row(
            [2.0 * box_x.astype(jnp.float32) + (bit_x + 0.5), bit_y + 0.5, 2.0 * box_z.astype(jnp.float32) + (bit_z + 0.5)],
            (3, 1),
        )
        here = slice(leaf * pts, (leaf + 1) * pts)
        offset = positions[:, here] - centre
        local.append(offset)
        high = low_bits(offset).astype(jnp.float32)
        middle = low_bits(offset - high).astype(jnp.float32)
        raw = density[:, here].astype(jnp.float32)
        mass = jnp.where(lax.broadcasted_iota(jnp.int32, raw.shape, 1) < count[leaf], raw, 0.0)
        spare = jnp.zeros((ROWS - fields - 6, pts), jnp.float32)
        own[:, here] = low_bits(jnp.concatenate([mass, high, middle, spare], axis=0))

    scaled = 2.0 * jnp.concatenate(local, axis=1)
    row = lax.broadcasted_iota(jnp.int32, (8, points), 0)
    value = None
    for axis in range(3):
        base = jnp.broadcast_to(scaled[axis : axis + 1], (8, points))
        power = jnp.ones((8, points), jnp.float32)
        for degree in range(1, ORDER + 1):
            power = power * jnp.where(row >= degree, base, 1.0)
        pieces = jnp.concatenate(high_low(power), axis=0)
        picked = dot(powers[axis * SLOT : (axis + 1) * SLOT, :], pieces)
        value = picked if value is None else value * picked
    high, low = high_low(value)
    basis[0:SLOT, :] = high
    basis[SLOT:, :] = low
    parts = []
    for leaf in range(8):
        here = slice(leaf * pts, (leaf + 1) * pts)
        parts.append(dot_nt(own[:, here], high[:, here]))
    moment, rest = high_low(jnp.concatenate(parts, axis=1))
    moments[...] = moment
    total = dot(moment, shift[...]) + dot(rest, shift[...])
    total_high, total_low = high_low(total)
    total = low_bits(total_high.astype(jnp.float32) + dot(total_low, heavy[...]))
    total = jnp.concatenate([total, jnp.zeros_like(total)], axis=1)
    totals[...] = total
    for distance, payload in zip((1, 3), payloads):
        bit = jnp.where((box_x ^ distance) > box_x, 1, 0)
        for place in range(4):
            payload[:, lanes(place * pts, pts)] = own[:, lanes((bit + 2 * place) * pts, pts)]
        payload[:, lanes(4 * pts, LEAVES)] = moment
        payload[:, lanes(4 * pts + LEAVES, 2 * SLOT)] = total


def features(held, start, size, centre, target):
    value = held[16:ROWS, lanes(start, size)].astype(jnp.float32)
    x = value[1:4] + value[4:7] + by_row(centre, (3, 1))
    norm = jnp.sum(x * x, axis=0, keepdims=True)
    if target:
        norm = norm + SOFTENING * SOFTENING
    parts, norms = [], []
    for source, out in ((x, parts), (norm, norms)):
        left = source
        for _ in range(3):
            high = low_bits(left).astype(jnp.float32)
            out.append(high)
            left = left - high
    one = jnp.ones_like(norm)
    zero = jnp.zeros_like(norm)
    blank = jnp.zeros((3, norm.shape[1]), jnp.float32)
    blocks = []
    order = (0, 1, 0, 2, 0, 1) if target else (0, 0, 1, 0, 2, 1)
    for index, which in enumerate(order):
        coords = -2.0 * parts[which] if target else parts[which]
        if index < 3:
            pair = [one, norms[index]] if target else [norms[index], one]
        else:
            pair = [zero, zero]
        blocks += [coords, *pair, blank]
    return jnp.concatenate(blocks, axis=0)


def source_features(held, start, size, centre):
    return low_bits(jnp.transpose(features(held, start, size, centre, False)))


def pulled(near, jobs, target, size, first=None):
    width = target.shape[1] // 8
    tiles = []
    for group, source, masses, starts in jobs:
        for piece in range(2):
            here = lanes((2 * group + piece) * width, width)
            for turn, start in enumerate(starts):
                tiles.append((here, source, masses, lanes(start, size), turn == 0, turn + 1 == len(starts)))

    def squares(tile):
        return dot(tile[1][tile[3], :], target[:, tile[0]])

    ahead, kernel, total = squares(tiles[0]), None, None
    for turn in range(len(tiles) + 1):
        square = ahead
        if turn + 1 < len(tiles):
            ahead = squares(tiles[turn + 1])
        if turn > 0:
            here, _, masses, place, opens, closes = tiles[turn - 1]
            if opens:
                total = jnp.zeros((ROWS, width), jnp.float32) if first is None else first[:, here]
            total = total + dot(masses[:, place], kernel)
            if closes:
                near[:, here] = total
        if turn < len(tiles):
            kernel = low_bits(lax.rsqrt(square))


def own_groups(near, first, last, target, source, own):
    pts = source.shape[0] // 8
    starts = [2 * p * pts for p in range(4)]
    pulled(near, [(group, source, own, starts) for group in range(first, last)], target, 2 * pts)


def box_columns(depth, box_x, box_z, nodes):
    blocks = []
    for turn, distance in [(turn, distance) for turn in range(depth) for distance in range(ACROSS)]:
        gap_x = 2 * (box_x - (box_x ^ distance))
        gap_z = 2 * (box_z - ((box_z ^ turn) if depth == 4 else turn))
        across_x = nodes[0] + gap_x.astype(jnp.float32)
        across_z = nodes[2] + gap_z.astype(jnp.float32)
        apart = jnp.maximum(jnp.abs(gap_x), jnp.abs(gap_z)) >= 4
        value = lax.rsqrt(across_x * across_x + across_z * across_z + nodes[1])
        blocks.append(low_bits(value * jnp.where(apart, 1.0 / COEFFS, 0.0)))
    return jnp.concatenate(blocks, axis=0)


def own_kernel(depth, count_in, weights_in, own, *rest):
    tables, outs, (nodes, count, weights, sems) = rest[:3], rest[3:11], rest[11:]
    near, source, target, scale, column, columns, far, spread = outs
    copies = fetch([*zip(tables, (far, spread, nodes)), (count_in, count), (weights_in, weights)], sems)
    points = own.shape[1]
    pts = points // 8
    for leaf in range(8):
        centre = [bit - 0.5 for bit in bits(leaf)]
        source[lanes(leaf * pts, pts), :] = source_features(own, leaf * pts, pts, centre)
        target[:, lanes(leaf_slot(leaf) * pts, pts)] = low_bits(features(own, leaf * pts, pts, centre, True))
    own_groups(near, 0, EARLY, target, source, own)
    for copy in copies:
        copy.wait()
    columns[...] = box_columns(depth, *box_place(), nodes)
    column[...] = by_row([weights[field] for field in range(weights.shape[0])], column.shape)
    lane_index = lax.broadcasted_iota(jnp.int32, (1, pts), 1)
    for leaf in range(8):
        scale[:, leaf * pts : (leaf + 1) * pts] = jnp.where(lane_index < count[leaf], 1.0 / (128.0 * pts), 0.0)


def spread_first(value, node):
    starts = [leaf * SLOT + node for leaf in range(8)]
    return jnp.concatenate([jnp.broadcast_to(value[:, s : s + 1], (ROWS, SLOT)) for s in starts], axis=1)


def decoded(coded):
    value = coded.astype(jnp.float32)
    node = lax.broadcasted_iota(jnp.int32, value.shape, 1) % SLOT
    return jnp.where(node == 0, 0.0, value) + spread_first(value, 0) + spread_first(value, COEFFS)


def faces_of(faces, bit, given, own, left, right, rows=None):
    points = own.shape[1]
    pts = points // 8
    for y in range(2):
        for x in range(4):
            place = lanes((2 * x + y) * pts, pts)
            if x in (0, 3):
                side = left if x == 0 else right
                faces[:, place] = side[:, lanes((y + 2 * bit) * pts, pts)]
            else:
                faces[:, place] = own[:, lanes((x - 1 + 2 * y + 4 * bit) * pts, pts)]
    node = lax.broadcasted_iota(jnp.int32, given.shape, 1) % SLOT
    base = spread_first(given, 0)
    base_high = low_bits(base).astype(jnp.float32)
    coded = jnp.where(node == 0, base_high, jnp.where(node == COEFFS, base - base_high, given - base))
    faces[:, lanes(points, LEAVES)] = low_bits(coded)
    if rows is not None:
        faces[:, lanes(points + LEAVES, rows.shape[1])] = rows


def sums_for(above, left, moments, right, far):
    base = left.shape[1] - LEAVES
    around = jnp.concatenate([left[:, lanes(base, LEAVES)], moments[...], right[:, lanes(base, LEAVES)]], axis=1)
    return dot(around, far[lanes(jnp.where(above == 1, 0, 5 * LEAVES), 3 * LEAVES), :])


def row_kernel(own, moments, totals, from_1, from_2, from_3, far, left, right, faces_even, rows):
    box_x, box_z = box_place()
    for side, step in ((left, -1), (right, 1)):
        side[...] = jnp.zeros(side.shape, side.dtype)
        for distance, held in ((1, from_1), (3, from_3)):

            @pl.when((box_x ^ distance) - box_x == step)
            def _(side=side, held=held):
                side[...] = held[:, lanes(0, side.shape[1])]

    ends = lanes(left.shape[1], 2 * SLOT)
    row = [totals[...], from_1[:, ends], from_2[...], from_3[:, ends]]
    row = jnp.concatenate([box[:, :SLOT] for box in row], axis=1)
    rows[...] = row
    above = 1 - lax.rem(box_z, 2)
    faces_of(faces_even, above, sums_for(above, left, moments, right, far), own, left, right, row)


def side_pulls(near, faces, early, target, scratch):
    pts = early.shape[1] // 8
    jobs = []
    for (step, side), held in zip(faces, scratch):
        for place in range(4):
            centre = (1.5 if step else -1.5, place % 2 - 0.5, place // 2 - 0.5)
            held[lanes(place * pts, pts), :] = source_features(side, place * pts, pts, centre)
        jobs += [(step, held, side, [0, 2 * pts]), (step + 2, held, side, [0, 2 * pts])]
    pulled(near, jobs, target, 2 * pts, early)


def middle_kernel(own, left, right, moments, far, early, source, target, near, faces_odd, same, *sides):
    points = own.shape[1]
    _, box_z = box_place()
    above = lax.rem(box_z, 2)
    faces_of(faces_odd, above, sums_for(above, left, moments, right, far), own, left, right)
    base = left.shape[1] - LEAVES
    beside = jnp.concatenate([left[:, lanes(base, LEAVES)], right[:, lanes(base, LEAVES)]], axis=1)
    same[...] = dot(beside, far[lanes(3 * LEAVES, 2 * LEAVES), :])
    near[:, lanes(0, EARLY * points // 4)] = early[...]
    own_groups(near, EARLY, 4, target, source, own)

    @pl.when(above == 1)
    def _():
        side_pulls(near, [(0, left), (1, right)], near, target, sides)

    @pl.when(above == 0)
    def _():
        side_pulls(near, [(0, left)], near, target, sides)


def side_kernel(right, early, target, near, held):
    _, box_z = box_place()
    odd = lax.rem(box_z, 2) == 1

    @pl.when(odd)
    def _():
        near[...] = early[...]

    @pl.when(jnp.logical_not(odd))
    def _():
        pts = early.shape[1] // 8
        for group in (0, 2):
            here = lanes(2 * group * pts, 2 * pts)
            near[:, here] = early[:, here]
        side_pulls(near, [(1, right)], early, target, [held])


def both_kernel(rows, faces, both):
    width = rows.shape[1]
    both[:, lanes(0, width)] = rows[...]
    both[:, lanes(width, width)] = faces[:, lanes(faces.shape[1] - width, width)]


def layer_pulls(near, early, step, inside, target, faces, sides):
    points = early.shape[1]
    pts = points // 8

    @pl.when(inside)
    def _():
        for place in range(8):
            height = jnp.where(step == 1, 1.5, -1.5)
            centre = (place // 2 - 1.5, place % 2 - 0.5, height)
            sides[lanes(place * pts, pts), :] = source_features(faces, place * pts, pts, centre)

        jobs = [(i + 2 * step, sides, faces, [2 * (x + i) * pts for x in range(3)]) for i in range(2)]
        pulled(near, jobs, target, 2 * pts, early)

    @pl.when(jnp.logical_not(inside))
    def _():
        here = lanes(step * (points // 2), points // 2)
        near[:, here] = early[:, here]


def even_kernel(early, target, faces, near, sides):
    _, box_z = box_place()
    points = early.shape[1]
    step = 1 - lax.rem(box_z, 2)
    other = lanes((1 - step) * (points // 2), points // 2)
    near[:, other] = early[:, other]
    layer_pulls(near, early, step, box_z >= 0, target, faces, sides)


def odd_inside(depth):
    _, box_z = box_place()
    step = lax.rem(box_z, 2)
    return step, (box_z + 2 * step - 1 >= 0) & (box_z + 2 * step - 1 < depth)


def odd_kernel(depth, early, target, faces, near, sides):
    points = early.shape[1]
    step, inside = odd_inside(depth)
    other = lanes((1 - step) * (points // 2), points // 2)
    near[:, other] = early[:, other]
    layer_pulls(near, early, step, inside, target, faces, sides)


def last_kernel(depth, near, faces_even, faces_odd, basis, scale, column, columns, spread, same, *rest):
    held, (potential, sums) = rest[:-2], rest[-2:]
    fields, points = potential.shape
    pts = points // 8
    _, inside = odd_inside(depth)
    if depth == 4:
        rows, distant = held
        width = rows.shape[1]
        near_rows = faces_even[:, lanes(faces_even.shape[1] - width, width)]
        layers = [rows[...], near_rows, distant[:, lanes(0, width)], distant[:, lanes(width, width)]]
    else:
        layers = [held[0][layer] for layer in range(depth)]
    coarse_high, coarse_low = high_low(dot(jnp.concatenate(layers, axis=1), columns[...]))
    value = same[...] + dot(coarse_high, spread[...]) + dot(coarse_low, spread[...])
    value = value + decoded(faces_even[:, lanes(points, LEAVES)])
    value = value + jnp.where(inside, decoded(faces_odd[:, lanes(points, LEAVES)]), 0.0)
    local_high, local_low = high_low(value)
    weight = column[0:fields, 0:1]
    for leaf in range(8):
        here = slice(leaf * pts, (leaf + 1) * pts)
        slot = slice(leaf * SLOT, (leaf + 1) * SLOT)
        doubled = jnp.concatenate([local_high[:, slot], local_high[:, slot]], axis=1)
        far_part = dot(doubled, basis[:, here]) + dot(local_low[:, slot], basis[0:SLOT, here])
        total = near[0:fields, lanes(leaf_slot(leaf) * pts, pts)] + far_part[:fields]
        total = total * scale[:, here]
        potential[:, here] = total
        sums[:, here] = jnp.sum(total * weight, axis=0, keepdims=True)
    sums[:, points:] = jnp.broadcast_to(jnp.sum(weight), (1, sums.shape[1] - points))


def mean_kernel(mine, other, mean):
    points = mean.shape[1]
    total = mine[...] + other[...]
    mean[...] = total[:, :points] / total[:, points : points + 1]


def swapped(block, axis, partner):
    size = lax.axis_size(axis)
    return lax.ppermute(block, axis, [(partner(i), i) for i in range(size)])


def swapped_odd(block):
    boxes, cores = lax.axis_size("space"), lax.axis_size("sig")
    pairs = []
    for box in range(boxes):
        other = box + ACROSS if box // ACROSS % 2 else box - ACROSS
        for core in range(cores):
            source = other * cores + core if 0 <= other < boxes else box * cores + (core ^ 1)
            pairs.append((source, box * cores + core))
    return lax.ppermute(block, ("space", "sig"), pairs)


def per_device(positions, density, leaf_count, sigma_weights):
    fields, points = density.shape
    pts = points // 8
    depth = lax.axis_size("space") // ACROSS
    vmem, hbm = pl.BlockSpec(memory_space=pltpu.VMEM), pl.BlockSpec(memory_space=pltpu.HBM)

    def call(kernel, name, in_specs, outs, scratch, *args):
        return pl.pallas_call(
            kernel,
            in_specs=in_specs,
            out_specs=[vmem] * len(outs),
            out_shape=[jax.ShapeDtypeStruct(shape, dtype) for shape, dtype in outs],
            scratch_shapes=scratch,
            compiler_params=pltpu.CompilerParams(vmem_limit_bytes=24 * MEGA),
            name=name,
        )(*(pltpu.with_memory_space_constraint(a, pltpu.HBM) if s is hbm else a for s, a in zip(in_specs, args)))

    half, full = jnp.bfloat16, jnp.float32
    shift = shift_table()
    side_shape = ((ROWS, 4 * pts + LEAVES), half)
    given_shape = ((ROWS, 4 * pts + LEAVES + 2 * SLOT), half)
    faces_shape = ((ROWS, points + LEAVES), half)
    even_shape = ((ROWS, points + LEAVES + SLOT * ACROSS), half)
    rows_shape = ((ROWS, SLOT * ACROSS), half)
    both_shape = ((ROWS, 2 * SLOT * ACROSS), half)
    near_shape, sums_shape = ((ROWS, points), full), ((ROWS, LEAVES), full)
    side_scratch = [pltpu.VMEM((4 * pts, FEATURES), half)] * 2
    rows_scratch = pltpu.VMEM((8 * pts, FEATURES), half)
    own, basis, moments, totals, *given = call(
        pack_kernel,
        "pack",
        [hbm] * 6,
        [
            ((ROWS, points), half),
            ((2 * SLOT, points), half),
            ((ROWS, LEAVES), half),
            ((ROWS, 2 * SLOT), half),
            given_shape,
            given_shape,
        ],
        [
            pltpu.SMEM((8,), jnp.int32),
            pltpu.VMEM((3, points), full),
            pltpu.VMEM((fields, points), half),
            pltpu.VMEM((LEAVES, SLOT), half),
            pltpu.VMEM((SLOT, SLOT), half),
            pltpu.VMEM((3 * SLOT, 16), half),
            pltpu.SemaphoreType.DMA((6,)),
        ],
        leaf_count,
        positions,
        density,
        jnp.asarray(shift, half),
        jnp.asarray(heavy_table(), half),
        jnp.asarray(power_table(), half),
    )
    from_2 = swapped(totals, "space", lambda i: i ^ 2)
    from_1 = swapped(given[0], "space", lambda i: i ^ 1)
    from_3 = swapped(given[1], "space", lambda i: i ^ 3)
    near, source, target, scale, column, columns, far, spread = call(
        functools.partial(own_kernel, depth),
        "near_own",
        [hbm] * 2 + [vmem] + [hbm] * 3,
        [
            ((ROWS, EARLY * points // 4), full),
            ((points, FEATURES), half),
            ((FEATURES, points), half),
            ((1, points), full),
            ((ROWS, 128), full),
            ((ACROSS * depth * SLOT, SLOT), half),
            ((len(STEPS) * LEAVES, LEAVES), half),
            ((SLOT, LEAVES), half),
        ],
        [
            pltpu.VMEM((3, SLOT, SLOT), full),
            pltpu.SMEM((8,), jnp.int32),
            pltpu.SMEM((fields,), full),
            pltpu.SemaphoreType.DMA((5,)),
        ],
        leaf_count,
        sigma_weights,
        own,
        jnp.asarray(far_table(), half),
        jnp.asarray(shift.T.copy(), half),
        jnp.asarray(box_nodes()),
    )
    left, right, faces_even, rows = call(
        row_kernel,
        "row",
        [vmem] * 7,
        [side_shape, side_shape, even_shape, rows_shape],
        [],
        own,
        moments,
        totals,
        from_1,
        from_2,
        from_3,
        far,
    )
    faces_even = swapped(faces_even, "space", lambda i: i ^ ACROSS)
    near, faces_odd, same = call(
        middle_kernel,
        "near_middle",
        [vmem] * 8,
        [near_shape, faces_shape, sums_shape],
        side_scratch,
        own,
        left,
        right,
        moments,
        far,
        near,
        source,
        target,
    )
    faces_odd = swapped_odd(faces_odd)
    near, = call(
        side_kernel,
        "near_side",
        [vmem] * 3,
        [near_shape],
        side_scratch[:1],
        right,
        near,
        target,
    )
    if depth == 4:
        both, = call(both_kernel, "row_pairs", [vmem] * 2, [both_shape], [], rows, faces_even)
        held = [rows, swapped(both, "space", lambda i: i ^ (2 * ACROSS))]
    else:
        groups = [[z * ACROSS + x for z in range(depth)] for x in range(ACROSS)]
        held = [lax.all_gather(rows, "space", axis_index_groups=groups)]
    near, = call(even_kernel, "near_even", [vmem] * 3, [near_shape], [rows_scratch], near, target, faces_even)
    near, = call(
        functools.partial(odd_kernel, depth),
        "near_odd",
        [vmem] * 3,
        [near_shape],
        [rows_scratch],
        near,
        target,
        faces_odd,
    )
    potential, sums = call(
        functools.partial(last_kernel, depth),
        "evaluate",
        [vmem] * (9 + len(held)),
        [((fields, points), full), ((1, points + 128), full)],
        [],
        near,
        faces_even,
        faces_odd,
        basis,
        scale,
        column,
        columns,
        spread,
        same,
        *held,
    )
    if lax.axis_size("sig") == 2:
        other = swapped(sums, "sig", lambda i: i ^ 1)
    else:
        other = lax.psum(sums, "sig") - sums
    mean, = call(mean_kernel, "mean", [vmem] * 2, [((1, points), full)], [], sums, other)
    return potential, mean.reshape(points)


def solution(mesh):
    in_specs = (P(None, "space"), P("sig", "space"), P("space"), P("sig"))
    out_specs = (P("sig", "space"), P("space"))
    return jax.shard_map(per_device, mesh=mesh, in_specs=in_specs, out_specs=out_specs, check_vma=False)
```

```python
import functools
import math

import jax
import jax.numpy as jnp
import numpy as np
from jax import lax
from jax.experimental import pallas as pl
from jax.experimental.pallas import tpu as pltpu
from jax.sharding import PartitionSpec as P

ORDER = 5
SOFTENING = 0.1
ACROSS = 4
SLOT = 64
ROWS = 24
LEAVES = 8 * SLOT
MEGA = 1024 * 1024
FEATURES = 32
EARLY = 3


def exponent_table(order_max):
    entries_list = []
    for degree in range(order_max + 1):
        for first_power in range(degree, -1, -1):
            for second_power in range(degree - first_power, -1, -1):
                entries_list.append((first_power, second_power, degree - first_power - second_power))
    return entries_list


def node_table(count_nodes, offset_value):
    counter = np.arange(1, count_nodes + 1, dtype=np.float32)[:, None]
    stride_set = np.array([0.7548776662466927, 0.5698402909980532, 0.4142135623730951], dtype=np.float32)[None, :]
    unit_points = np.mod(counter * stride_set + np.float32(offset_value), np.float32(1.0))
    return (np.float32(2.0) * unit_points - np.float32(1.0)).astype(np.float32)


EXPONENTS = exponent_table(ORDER)
COEFFS = len(EXPONENTS)
CHECK = node_table(COEFFS, 0.5).astype(np.float64)
EQUIV = node_table(COEFFS, 0.0).astype(np.float64)
HEAVY = [EXPONENTS.index(e) for e in ((0, 0, 0), (2, 0, 0), (0, 2, 0), (0, 0, 2), (4, 0, 0), (0, 4, 0), (0, 0, 4), (2, 0, 2))]
STEPS = [(sx, sz) for sz in (-1, 0, 1) for sx in (-1, 0, 1) if sx != 0 or sz != 0]


def bits(octant):
    return octant % 2, octant // 2 % 2, octant // 4


def leaf_slot(octant):
    bit_x, bit_y, bit_z = bits(octant)
    return (bit_x + 2 * bit_z) * 2 + bit_y


@functools.lru_cache(None)
def far_table():
    shape = (len(STEPS), 8, SLOT, 8, SLOT)
    table = np.zeros(shape)
    gap_nodes = 0.5 * (CHECK[None, :, :] - EQUIV[:, None, :])
    for index, (step_x, step_z) in enumerate(STEPS):
        for source in range(8):
            for target in range(8):
                s, t = bits(source), bits(target)
                gap = np.array([2 * step_x + s[0] - t[0], s[1] - t[1], 2 * step_z + s[2] - t[2]], np.float64)
                if max(abs(gap[0]), abs(gap[2])) >= 2:
                    shifted = gap_nodes - gap
                    value = 1.0 / np.sqrt(np.sum(shifted * shifted, -1) + SOFTENING * SOFTENING) / COEFFS
                    table[index, source, :COEFFS, target, :COEFFS] = value
    return table.reshape(len(STEPS) * LEAVES, LEAVES)


@functools.lru_cache(None)
def shift_table():
    table = np.zeros((8, SLOT, SLOT))
    for leaf in range(8):
        offset = [bit - 0.5 for bit in bits(leaf)]
        for k, target in enumerate(EXPONENTS):
            for i, source in enumerate(EXPONENTS):
                if all(b <= a for a, b in zip(target, source)):
                    value = 1.0
                    for a, b, h in zip(target, source, offset):
                        value *= math.comb(a, b) * 0.5**b * h ** (a - b)
                    table[leaf, i, k] = value
    return table.reshape(8 * SLOT, SLOT)


@functools.lru_cache(None)
def box_nodes():
    gaps = np.zeros((3, SLOT, SLOT))
    gaps[:, :COEFFS, :COEFFS] = np.moveaxis(CHECK[None, :, :] - EQUIV[:, None, :], -1, 0)
    gaps[:, COEFFS:] = gaps[:, HEAVY]
    gaps[1] = gaps[1] ** 2 + SOFTENING * SOFTENING
    return gaps.astype(np.float32)


def dot(left, right):
    return jnp.dot(left, right, preferred_element_type=jnp.float32)


def dot_nt(left, right):
    return lax.dot_general(left, right, (((1,), (1,)), ((), ())), preferred_element_type=jnp.float32)


def low_bits(value):
    return value.astype(jnp.bfloat16)


def heavy_table():
    table = np.zeros((SLOT, SLOT), np.float32)
    table[HEAVY, np.arange(COEFFS, SLOT)] = 1.0
    return table


def power_table():
    table = np.zeros((3, SLOT, 16), np.float32)
    for axis in range(3):
        for k, powers in enumerate(EXPONENTS):
            table[axis, k, powers[axis]] = 1.0
            table[axis, k, 8 + powers[axis]] = 1.0
    return table.reshape(3 * SLOT, 16)


def pick_tables():
    source = np.zeros((FEATURES, 32), np.float32)
    target = np.zeros((FEATURES, 32), np.float32)
    row = 0
    for left, right in ((0, 0), (0, 8), (8, 0), (0, 16), (16, 0), (8, 8)):
        for axis in range(3):
            source[row, left + axis] = 1.0
            target[row, right + axis] = -2.0
            row += 1
    for piece in range(3):
        source[row, 24 + piece] = target[row, 27] = 1.0
        source[row + 1, 27] = target[row + 1, 24 + piece] = 1.0
        row += 2
    join = np.zeros((FEATURES, 32), np.float32)
    for axis in range(3):
        join[axis, 1 + axis] = join[axis, 4 + axis] = 1.0
    return np.concatenate([source, target, join], 0)


def high_low(value):
    high = low_bits(value)
    return high, low_bits(value - high.astype(jnp.float32))


def by_row(values, shape):
    row = lax.broadcasted_iota(jnp.int32, shape, 0)
    result = jnp.zeros(shape, jnp.float32)
    for index, value in enumerate(values):
        result = jnp.where(row == index, value, result)
    return result


def box_place():
    label = lax.axis_index("space")
    return lax.rem(label, ACROSS), lax.div(label, ACROSS)


def lanes(start, size):
    return pl.ds(start if isinstance(start, int) else pl.multiple_of(start, 128), size)


def fetch(pairs, sems):
    copies = [pltpu.make_async_copy(src, dst, sems.at[i]) for i, (src, dst) in enumerate(pairs)]
    for copy in copies:
        copy.start()
    return copies


def pack_kernel(count_in, positions_in, density_in, shift_in, heavy_in, powers_in, picks_in, own, picks, basis, moments, totals, *rest):
    payloads, (count, positions, density, shift, heavy, powers, sems) = rest[:2], rest[2:]
    copies = fetch(
        [
            (count_in, count),
            (positions_in, positions),
            (density_in, density),
            (shift_in, shift),
            (heavy_in, heavy),
            (powers_in, powers),
            (picks_in, picks),
        ],
        sems,
    )
    fields, points = density.shape
    pts = points // 8
    box_x, box_z = box_place()
    for copy in copies:
        copy.wait()
    local = []
    for leaf in range(8):
        bit_x, bit_y, bit_z = bits(leaf)
        centre = by_row(
            [2.0 * box_x.astype(jnp.float32) + (bit_x + 0.5), bit_y + 0.5, 2.0 * box_z.astype(jnp.float32) + (bit_z + 0.5)],
            (3, 1),
        )
        here = slice(leaf * pts, (leaf + 1) * pts)
        offset = positions[:, here] - centre
        local.append(offset)
        high = low_bits(offset).astype(jnp.float32)
        middle = low_bits(offset - high).astype(jnp.float32)
        raw = density[:, here].astype(jnp.float32)
        mass = jnp.where(lax.broadcasted_iota(jnp.int32, raw.shape, 1) < count[leaf], raw, 0.0)
        spare = jnp.zeros((ROWS - fields - 6, pts), jnp.float32)
        own[:, here] = low_bits(jnp.concatenate([mass, high, middle, spare], axis=0))

    scaled = 2.0 * jnp.concatenate(local, axis=1)
    row = lax.broadcasted_iota(jnp.int32, (8, points), 0)
    value = None
    for axis in range(3):
        base = jnp.broadcast_to(scaled[axis : axis + 1], (8, points))
        power = jnp.ones((8, points), jnp.float32)
        for degree in range(1, ORDER + 1):
            power = power * jnp.where(row >= degree, base, 1.0)
        pieces = jnp.concatenate(high_low(power), axis=0)
        picked = dot(powers[axis * SLOT : (axis + 1) * SLOT, :], pieces)
        value = picked if value is None else value * picked
    high, low = high_low(value)
    basis[0:SLOT, :] = high
    basis[SLOT:, :] = low
    parts = []
    for leaf in range(8):
        here = slice(leaf * pts, (leaf + 1) * pts)
        parts.append(dot_nt(own[:, here], high[:, here]))
    moment, rest = high_low(jnp.concatenate(parts, axis=1))
    moments[...] = moment
    total = dot(moment, shift[...]) + dot(rest, shift[...])
    total_high, total_low = high_low(total)
    total = low_bits(total_high.astype(jnp.float32) + dot(total_low, heavy[...]))
    total = jnp.concatenate([total, jnp.zeros_like(total)], axis=1)
    totals[...] = total
    for distance, payload in zip((1, 3), payloads):
        bit = jnp.where((box_x ^ distance) > box_x, 1, 0)
        for place in range(4):
            payload[:, lanes(place * pts, pts)] = own[:, lanes((bit + 2 * place) * pts, pts)]
        payload[:, lanes(4 * pts, LEAVES)] = moment
        payload[:, lanes(4 * pts + LEAVES, 2 * SLOT)] = total


def pieces_of(held, start, size, centre, target, picks):
    join = picks[2 * FEATURES : 2 * FEATURES + 8, 0:8]
    x = dot(join, held[16:ROWS, lanes(start, size)]) + by_row(centre, (8, 1))
    norm = jnp.sum(x * x, axis=0, keepdims=True)
    if target:
        norm = norm + SOFTENING * SOFTENING
    blocks = []
    left = x
    for _ in range(3):
        high = low_bits(left).astype(jnp.float32)
        blocks.append(high)
        left = left - high
    row = lax.broadcasted_iota(jnp.int32, x.shape, 0)
    norms = jnp.where(row == 3, 1.0, 0.0)
    left = norm
    for piece in range(3):
        high = low_bits(left).astype(jnp.float32)
        norms = jnp.where(row == piece, high, norms)
        left = left - high
    return low_bits(jnp.concatenate([*blocks, norms], axis=0))


def target_features(held, start, size, centre, picks):
    pieces = pieces_of(held, start, size, centre, True, picks)
    return low_bits(dot(picks[FEATURES : 2 * FEATURES, :], pieces))


def source_features(held, start, size, centre, picks):
    pieces = pieces_of(held, start, size, centre, False, picks)
    contract = (((0,), (1,)), ((), ()))
    picked = lax.dot_general(pieces, picks[0:FEATURES, :], contract, preferred_element_type=jnp.float32)
    return low_bits(picked)


def pulled(near, jobs, target, size, first=None):
    width = target.shape[1] // 8
    tiles = []
    for group, source, masses, starts in jobs:
        for piece in range(2):
            here = lanes((2 * group + piece) * width, width)
            for turn, start in enumerate(starts):
                tiles.append((here, source, masses, lanes(start, size), turn == 0, turn + 1 == len(starts)))

    def squares(tile):
        return dot(tile[1][tile[3], :], target[:, tile[0]])

    ahead, kernel, total = squares(tiles[0]), None, None
    for turn in range(len(tiles) + 1):
        square = ahead
        if turn + 1 < len(tiles):
            ahead = squares(tiles[turn + 1])
        if turn > 0:
            here, _, masses, place, opens, closes = tiles[turn - 1]
            if opens:
                total = jnp.zeros((ROWS, width), jnp.float32) if first is None else first[:, here]
            total = total + dot(masses[:, place], kernel)
            if closes:
                near[:, here] = total
        if turn < len(tiles):
            kernel = low_bits(lax.rsqrt(square))


def own_groups(near, first, last, target, source, own):
    pts = source.shape[0] // 8
    starts = [2 * p * pts for p in range(4)]
    pulled(near, [(group, source, own, starts) for group in range(first, last)], target, 2 * pts)


def box_columns(depth, box_x, box_z, nodes):
    blocks = []
    for turn, distance in [(turn, distance) for turn in range(depth) for distance in range(ACROSS)]:
        gap_x = 2 * (box_x - (box_x ^ distance))
        gap_z = 2 * (box_z - ((box_z ^ turn) if depth == 4 else turn))
        across_x = nodes[0] + gap_x.astype(jnp.float32)
        across_z = nodes[2] + gap_z.astype(jnp.float32)
        apart = jnp.maximum(jnp.abs(gap_x), jnp.abs(gap_z)) >= 4
        value = lax.rsqrt(across_x * across_x + across_z * across_z + nodes[1])
        blocks.append(low_bits(value * jnp.where(apart, 1.0 / COEFFS, 0.0)))
    return jnp.concatenate(blocks, axis=0)


def own_kernel(depth, count_in, weights_in, own, picks, *rest):
    tables, outs, (nodes, count, weights, sems) = rest[:3], rest[3:11], rest[11:]
    near, source, target, scale, column, columns, far, spread = outs
    copies = fetch([*zip(tables, (far, spread, nodes)), (count_in, count), (weights_in, weights)], sems)
    points = own.shape[1]
    pts = points // 8
    for leaf in range(8):
        centre = [bit - 0.5 for bit in bits(leaf)]
        source[lanes(leaf * pts, pts), :] = source_features(own, leaf * pts, pts, centre, picks)
        target[:, lanes(leaf_slot(leaf) * pts, pts)] = target_features(own, leaf * pts, pts, centre, picks)
    own_groups(near, 0, EARLY, target, source, own)
    for copy in copies:
        copy.wait()
    columns[...] = box_columns(depth, *box_place(), nodes)
    column[...] = by_row([weights[field] for field in range(weights.shape[0])], column.shape)
    lane_index = lax.broadcasted_iota(jnp.int32, (1, pts), 1)
    for leaf in range(8):
        scale[:, leaf * pts : (leaf + 1) * pts] = jnp.where(lane_index < count[leaf], 1.0 / (128.0 * pts), 0.0)


def spread_first(value, node):
    starts = [leaf * SLOT + node for leaf in range(8)]
    return jnp.concatenate([jnp.broadcast_to(value[:, s : s + 1], (ROWS, SLOT)) for s in starts], axis=1)


def decoded(coded):
    value = coded.astype(jnp.float32)
    node = lax.broadcasted_iota(jnp.int32, value.shape, 1) % SLOT
    return jnp.where(node == 0, 0.0, value) + spread_first(value, 0) + spread_first(value, COEFFS)


def faces_of(faces, bit, given, own, left, right, rows=None):
    points = own.shape[1]
    pts = points // 8
    for y in range(2):
        for x in range(4):
            place = lanes((2 * x + y) * pts, pts)
            if x in (0, 3):
                side = left if x == 0 else right
                faces[:, place] = side[:, lanes((y + 2 * bit) * pts, pts)]
            else:
                faces[:, place] = own[:, lanes((x - 1 + 2 * y + 4 * bit) * pts, pts)]
    node = lax.broadcasted_iota(jnp.int32, given.shape, 1) % SLOT
    base = spread_first(given, 0)
    base_high = low_bits(base).astype(jnp.float32)
    coded = jnp.where(node == 0, base_high, jnp.where(node == COEFFS, base - base_high, given - base))
    faces[:, lanes(points, LEAVES)] = low_bits(coded)
    if rows is not None:
        faces[:, lanes(points + LEAVES, rows.shape[1])] = rows


def sums_for(above, left, moments, right, far):
    base = left.shape[1] - LEAVES
    around = jnp.concatenate([left[:, lanes(base, LEAVES)], moments[...], right[:, lanes(base, LEAVES)]], axis=1)
    return dot(around, far[lanes(jnp.where(above == 1, 0, 5 * LEAVES), 3 * LEAVES), :])


def row_kernel(own, moments, totals, from_1, from_2, from_3, far, left, right, faces_even, rows):
    box_x, box_z = box_place()
    for side, step in ((left, -1), (right, 1)):
        side[...] = jnp.zeros(side.shape, side.dtype)
        for distance, held in ((1, from_1), (3, from_3)):

            @pl.when((box_x ^ distance) - box_x == step)
            def _(side=side, held=held):
                side[...] = held[:, lanes(0, side.shape[1])]

    ends = lanes(left.shape[1], 2 * SLOT)
    row = [totals[...], from_1[:, ends], from_2[...], from_3[:, ends]]
    row = jnp.concatenate([box[:, :SLOT] for box in row], axis=1)
    rows[...] = row
    above = 1 - lax.rem(box_z, 2)
    faces_of(faces_even, above, sums_for(above, left, moments, right, far), own, left, right, row)


def side_pulls(near, faces, early, target, picks, scratch):
    pts = early.shape[1] // 8
    jobs = []
    for (step, side), held in zip(faces, scratch):
        for place in range(4):
            centre = (1.5 if step else -1.5, place % 2 - 0.5, place // 2 - 0.5)
            held[lanes(place * pts, pts), :] = source_features(side, place * pts, pts, centre, picks)
        jobs += [(step, held, side, [0, 2 * pts]), (step + 2, held, side, [0, 2 * pts])]
    pulled(near, jobs, target, 2 * pts, early)


def middle_kernel(own, left, right, moments, far, early, source, target, picks, near, faces_odd, same, *sides):
    points = own.shape[1]
    _, box_z = box_place()
    above = lax.rem(box_z, 2)
    faces_of(faces_odd, above, sums_for(above, left, moments, right, far), own, left, right)
    base = left.shape[1] - LEAVES
    beside = jnp.concatenate([left[:, lanes(base, LEAVES)], right[:, lanes(base, LEAVES)]], axis=1)
    same[...] = dot(beside, far[lanes(3 * LEAVES, 2 * LEAVES), :])
    near[:, lanes(0, EARLY * points // 4)] = early[...]
    own_groups(near, EARLY, 4, target, source, own)

    @pl.when(above == 1)
    def _():
        side_pulls(near, [(0, left), (1, right)], near, target, picks, sides)


def side_kernel(left, right, early, target, picks, near, *sides):
    _, box_z = box_place()
    odd = lax.rem(box_z, 2) == 1

    @pl.when(odd)
    def _():
        near[...] = early[...]

    @pl.when(jnp.logical_not(odd))
    def _():
        side_pulls(near, [(0, left), (1, right)], early, target, picks, sides)


def both_kernel(rows, faces, near, both):
    width = rows.shape[1]
    both[:, lanes(0, width)] = rows[...]
    both[:, lanes(width, width)] = faces[:, lanes(faces.shape[1] - width, width)]


def layer_pulls(near, early, step, inside, target, picks, faces, sides):
    points = early.shape[1]
    pts = points // 8

    @pl.when(inside)
    def _():
        for place in range(8):
            height = jnp.where(step == 1, 1.5, -1.5)
            centre = (place // 2 - 1.5, place % 2 - 0.5, height)
            sides[lanes(place * pts, pts), :] = source_features(faces, place * pts, pts, centre, picks)

        jobs = [(i + 2 * step, sides, faces, [2 * (x + i) * pts for x in range(3)]) for i in range(2)]
        pulled(near, jobs, target, 2 * pts, early)

    @pl.when(jnp.logical_not(inside))
    def _():
        here = lanes(step * (points // 2), points // 2)
        near[:, here] = early[:, here]


def even_kernel(early, target, picks, faces, near, sides):
    _, box_z = box_place()
    points = early.shape[1]
    step = 1 - lax.rem(box_z, 2)
    other = lanes((1 - step) * (points // 2), points // 2)
    near[:, other] = early[:, other]
    layer_pulls(near, early, step, box_z >= 0, target, picks, faces, sides)


def odd_inside(depth):
    _, box_z = box_place()
    step = lax.rem(box_z, 2)
    return step, (box_z + 2 * step - 1 >= 0) & (box_z + 2 * step - 1 < depth)


def odd_kernel(depth, early, target, picks, faces, near, sides):
    points = early.shape[1]
    step, inside = odd_inside(depth)
    other = lanes((1 - step) * (points // 2), points // 2)
    near[:, other] = early[:, other]
    layer_pulls(near, early, step, inside, target, picks, faces, sides)


def last_kernel(depth, near, faces_even, faces_odd, basis, scale, column, columns, spread, same, *rest):
    held, (potential, sums) = rest[:-2], rest[-2:]
    fields, points = potential.shape
    pts = points // 8
    _, inside = odd_inside(depth)
    if depth == 4:
        rows, distant = held
        width = rows.shape[1]
        near_rows = faces_even[:, lanes(faces_even.shape[1] - width, width)]
        layers = [rows[...], near_rows, distant[:, lanes(0, width)], distant[:, lanes(width, width)]]
    else:
        layers = [held[0][layer] for layer in range(depth)]
    coarse_high, coarse_low = high_low(dot(jnp.concatenate(layers, axis=1), columns[...]))
    value = same[...] + dot(coarse_high, spread[...]) + dot(coarse_low, spread[...])
    value = value + decoded(faces_even[:, lanes(points, LEAVES)])
    value = value + jnp.where(inside, decoded(faces_odd[:, lanes(points, LEAVES)]), 0.0)
    local_high, local_low = high_low(value)
    weight = column[0:fields, 0:1]
    for leaf in range(8):
        here = slice(leaf * pts, (leaf + 1) * pts)
        slot = slice(leaf * SLOT, (leaf + 1) * SLOT)
        doubled = jnp.concatenate([local_high[:, slot], local_high[:, slot]], axis=1)
        far_part = dot(doubled, basis[:, here]) + dot(local_low[:, slot], basis[0:SLOT, here])
        total = near[0:fields, lanes(leaf_slot(leaf) * pts, pts)] + far_part[:fields]
        total = total * scale[:, here]
        potential[:, here] = total
        sums[:, here] = jnp.sum(total * weight, axis=0, keepdims=True)
    sums[:, points:] = jnp.broadcast_to(jnp.sum(weight), (1, sums.shape[1] - points))


def mean_kernel(mine, other, mean):
    points = mean.shape[1]
    total = mine[...] + other[...]
    mean[...] = total[:, :points] / total[:, points : points + 1]


def swapped(block, axis, partner):
    size = lax.axis_size(axis)
    return lax.ppermute(block, axis, [(partner(i), i) for i in range(size)])


def swapped_odd(block):
    boxes, cores = lax.axis_size("space"), lax.axis_size("sig")
    pairs = []
    for box in range(boxes):
        other = box + ACROSS if box // ACROSS % 2 else box - ACROSS
        for core in range(cores):
            source = other * cores + core if 0 <= other < boxes else box * cores + (core ^ 1)
            pairs.append((source, box * cores + core))
    return lax.ppermute(block, ("space", "sig"), pairs)


def per_device(positions, density, leaf_count, sigma_weights):
    fields, points = density.shape
    pts = points // 8
    depth = lax.axis_size("space") // ACROSS
    vmem, hbm = pl.BlockSpec(memory_space=pltpu.VMEM), pl.BlockSpec(memory_space=pltpu.HBM)

    def call(kernel, name, in_specs, outs, scratch, *args):
        return pl.pallas_call(
            kernel,
            in_specs=in_specs,
            out_specs=[vmem] * len(outs),
            out_shape=[jax.ShapeDtypeStruct(shape, dtype) for shape, dtype in outs],
            scratch_shapes=scratch,
            compiler_params=pltpu.CompilerParams(vmem_limit_bytes=24 * MEGA),
            name=name,
        )(*(pltpu.with_memory_space_constraint(a, pltpu.HBM) if s is hbm else a for s, a in zip(in_specs, args)))

    half, full = jnp.bfloat16, jnp.float32
    shift = shift_table()
    side_shape = ((ROWS, 4 * pts + LEAVES), half)
    given_shape = ((ROWS, 4 * pts + LEAVES + 2 * SLOT), half)
    faces_shape = ((ROWS, points + LEAVES), half)
    even_shape = ((ROWS, points + LEAVES + SLOT * ACROSS), half)
    rows_shape = ((ROWS, SLOT * ACROSS), half)
    both_shape = ((ROWS, 2 * SLOT * ACROSS), half)
    near_shape, sums_shape = ((ROWS, points), full), ((ROWS, LEAVES), full)
    side_scratch = [pltpu.VMEM((4 * pts, FEATURES), half)] * 2
    rows_scratch = pltpu.VMEM((8 * pts, FEATURES), half)
    own, picks, basis, moments, totals, *given = call(
        pack_kernel,
        "pack",
        [hbm] * 7,
        [
            ((ROWS, points), half),
            ((3 * FEATURES, 32), half),
            ((2 * SLOT, points), half),
            ((ROWS, LEAVES), half),
            ((ROWS, 2 * SLOT), half),
            given_shape,
            given_shape,
        ],
        [
            pltpu.SMEM((8,), jnp.int32),
            pltpu.VMEM((3, points), full),
            pltpu.VMEM((fields, points), half),
            pltpu.VMEM((LEAVES, SLOT), half),
            pltpu.VMEM((SLOT, SLOT), half),
            pltpu.VMEM((3 * SLOT, 16), half),
            pltpu.SemaphoreType.DMA((7,)),
        ],
        leaf_count,
        positions,
        density,
        jnp.asarray(shift, half),
        jnp.asarray(heavy_table(), half),
        jnp.asarray(power_table(), half),
        jnp.asarray(pick_tables(), half),
    )
    from_2 = swapped(totals, "space", lambda i: i ^ 2)
    from_1 = swapped(given[0], "space", lambda i: i ^ 1)
    from_3 = swapped(given[1], "space", lambda i: i ^ 3)
    near, source, target, scale, column, columns, far, spread = call(
        functools.partial(own_kernel, depth),
        "near_own",
        [hbm] * 2 + [vmem] * 2 + [hbm] * 3,
        [
            ((ROWS, EARLY * points // 4), full),
            ((points, FEATURES), half),
            ((FEATURES, points), half),
            ((1, points), full),
            ((ROWS, 128), full),
            ((ACROSS * depth * SLOT, SLOT), half),
            ((len(STEPS) * LEAVES, LEAVES), half),
            ((SLOT, LEAVES), half),
        ],
        [
            pltpu.VMEM((3, SLOT, SLOT), full),
            pltpu.SMEM((8,), jnp.int32),
            pltpu.SMEM((fields,), full),
            pltpu.SemaphoreType.DMA((5,)),
        ],
        leaf_count,
        sigma_weights,
        own,
        picks,
        jnp.asarray(far_table(), half),
        jnp.asarray(shift.T.copy(), half),
        jnp.asarray(box_nodes()),
    )
    left, right, faces_even, rows = call(
        row_kernel,
        "row",
        [vmem] * 7,
        [side_shape, side_shape, even_shape, rows_shape],
        [],
        own,
        moments,
        totals,
        from_1,
        from_2,
        from_3,
        far,
    )
    faces_even = swapped(faces_even, "space", lambda i: i ^ ACROSS)
    near, faces_odd, same = call(
        middle_kernel,
        "near_middle",
        [vmem] * 9,
        [near_shape, faces_shape, sums_shape],
        side_scratch,
        own,
        left,
        right,
        moments,
        far,
        near,
        source,
        target,
        picks,
    )
    faces_odd = swapped_odd(faces_odd)
    near, = call(
        side_kernel,
        "near_side",
        [vmem] * 5,
        [near_shape],
        side_scratch,
        left,
        right,
        near,
        target,
        picks,
    )
    if depth == 4:
        both, = call(both_kernel, "row_pairs", [vmem] * 3, [both_shape], [], rows, faces_even, near)
        held = [rows, swapped(both, "space", lambda i: i ^ (2 * ACROSS))]
    else:
        groups = [[z * ACROSS + x for z in range(depth)] for x in range(ACROSS)]
        held = [lax.all_gather(rows, "space", axis_index_groups=groups)]
    near, = call(even_kernel, "near_even", [vmem] * 4, [near_shape], [rows_scratch], near, target, picks, faces_even)
    near, = call(
        functools.partial(odd_kernel, depth),
        "near_odd",
        [vmem] * 4,
        [near_shape],
        [rows_scratch],
        near,
        target,
        picks,
        faces_odd,
    )
    potential, sums = call(
        functools.partial(last_kernel, depth),
        "evaluate",
        [vmem] * (9 + len(held)),
        [((fields, points), full), ((1, points + 128), full)],
        [],
        near,
        faces_even,
        faces_odd,
        basis,
        scale,
        column,
        columns,
        spread,
        same,
        *held,
    )
    if lax.axis_size("sig") == 2:
        other = swapped(sums, "sig", lambda i: i ^ 1)
    else:
        other = lax.psum(sums, "sig") - sums
    mean, = call(mean_kernel, "mean", [vmem] * 2, [((1, points), full)], [], sums, other)
    return potential, mean.reshape(points)


def solution(mesh):
    in_specs = (P(None, "space"), P("sig", "space"), P("space"), P("sig"))
    out_specs = (P("sig", "space"), P("space"))
    return jax.shard_map(per_device, mesh=mesh, in_specs=in_specs, out_specs=out_specs, check_vma=False)
```

```python
import functools
import math

import jax
import jax.numpy as jnp
import numpy as np
from jax import lax
from jax.experimental import pallas as pl
from jax.experimental.pallas import tpu as pltpu
from jax.sharding import PartitionSpec as P

ORDER = 5
SOFTENING = 0.1
ACROSS = 4
SLOT = 64
ROWS = 24
LEAVES = 8 * SLOT
MEGA = 1024 * 1024
FEATURES = 48
EARLY = 3


def exponent_table(order_max):
    entries_list = []
    for degree in range(order_max + 1):
        for first_power in range(degree, -1, -1):
            for second_power in range(degree - first_power, -1, -1):
                entries_list.append((first_power, second_power, degree - first_power - second_power))
    return entries_list


def node_table(count_nodes, offset_value):
    counter = np.arange(1, count_nodes + 1, dtype=np.float32)[:, None]
    stride_set = np.array([0.7548776662466927, 0.5698402909980532, 0.4142135623730951], dtype=np.float32)[None, :]
    unit_points = np.mod(counter * stride_set + np.float32(offset_value), np.float32(1.0))
    return (np.float32(2.0) * unit_points - np.float32(1.0)).astype(np.float32)


EXPONENTS = exponent_table(ORDER)
COEFFS = len(EXPONENTS)
CHECK = node_table(COEFFS, 0.5).astype(np.float64)
EQUIV = node_table(COEFFS, 0.0).astype(np.float64)
HEAVY = [EXPONENTS.index(e) for e in ((0, 0, 0), (2, 0, 0), (0, 2, 0), (0, 0, 2), (4, 0, 0), (0, 4, 0), (0, 0, 4), (2, 0, 2))]
STEPS = [(sx, sz) for sz in (-1, 0, 1) for sx in (-1, 0, 1) if sx != 0 or sz != 0]


def bits(octant):
    return octant % 2, octant // 2 % 2, octant // 4


def leaf_slot(octant):
    bit_x, bit_y, bit_z = bits(octant)
    return (bit_x + 2 * bit_z) * 2 + bit_y


@functools.lru_cache(None)
def far_table():
    shape = (len(STEPS), 8, SLOT, 8, SLOT)
    table = np.zeros(shape)
    gap_nodes = 0.5 * (CHECK[None, :, :] - EQUIV[:, None, :])
    for index, (step_x, step_z) in enumerate(STEPS):
        for source in range(8):
            for target in range(8):
                s, t = bits(source), bits(target)
                gap = np.array([2 * step_x + s[0] - t[0], s[1] - t[1], 2 * step_z + s[2] - t[2]], np.float64)
                if max(abs(gap[0]), abs(gap[2])) >= 2:
                    shifted = gap_nodes - gap
                    value = 1.0 / np.sqrt(np.sum(shifted * shifted, -1) + SOFTENING * SOFTENING) / COEFFS
                    table[index, source, :COEFFS, target, :COEFFS] = value
    return table.reshape(len(STEPS) * LEAVES, LEAVES)


@functools.lru_cache(None)
def shift_table():
    table = np.zeros((8, SLOT, SLOT))
    for leaf in range(8):
        offset = [bit - 0.5 for bit in bits(leaf)]
        for k, target in enumerate(EXPONENTS):
            for i, source in enumerate(EXPONENTS):
                if all(b <= a for a, b in zip(target, source)):
                    value = 1.0
                    for a, b, h in zip(target, source, offset):
                        value *= math.comb(a, b) * 0.5**b * h ** (a - b)
                    table[leaf, i, k] = value
    return table.reshape(8 * SLOT, SLOT)


@functools.lru_cache(None)
def box_nodes():
    gaps = np.zeros((3, SLOT, SLOT))
    gaps[:, :COEFFS, :COEFFS] = np.moveaxis(CHECK[None, :, :] - EQUIV[:, None, :], -1, 0)
    gaps[:, COEFFS:] = gaps[:, HEAVY]
    gaps[1] = gaps[1] ** 2 + SOFTENING * SOFTENING
    return gaps.astype(np.float32)


def dot(left, right):
    return jnp.dot(left, right, preferred_element_type=jnp.float32)


def dot_nt(left, right):
    return lax.dot_general(left, right, (((1,), (1,)), ((), ())), preferred_element_type=jnp.float32)


def low_bits(value):
    return value.astype(jnp.bfloat16)


def heavy_table():
    table = np.zeros((SLOT, SLOT), np.float32)
    table[HEAVY, np.arange(COEFFS, SLOT)] = 1.0
    return table


def power_table():
    table = np.zeros((3, SLOT, 16), np.float32)
    for axis in range(3):
        for k, powers in enumerate(EXPONENTS):
            table[axis, k, powers[axis]] = 1.0
            table[axis, k, 8 + powers[axis]] = 1.0
    return table.reshape(3 * SLOT, 16)


def high_low(value):
    high = low_bits(value)
    return high, low_bits(value - high.astype(jnp.float32))


def by_row(values, shape):
    row = lax.broadcasted_iota(jnp.int32, shape, 0)
    result = jnp.zeros(shape, jnp.float32)
    for index, value in enumerate(values):
        result = jnp.where(row == index, value, result)
    return result


def box_place():
    label = lax.axis_index("space")
    return lax.rem(label, ACROSS), lax.div(label, ACROSS)


def lanes(start, size):
    return pl.ds(start if isinstance(start, int) else pl.multiple_of(start, 128), size)


def fetch(pairs, sems):
    copies = [pltpu.make_async_copy(src, dst, sems.at[i]) for i, (src, dst) in enumerate(pairs)]
    for copy in copies:
        copy.start()
    return copies


def pack_kernel(count_in, positions_in, density_in, shift_in, heavy_in, powers_in, own, basis, moments, totals, *rest):
    payloads, (count, positions, density, shift, heavy, powers, sems) = rest[:2], rest[2:]
    copies = fetch(
        [
            (count_in, count),
            (positions_in, positions),
            (density_in, density),
            (shift_in, shift),
            (heavy_in, heavy),
            (powers_in, powers),
        ],
        sems,
    )
    fields, points = density.shape
    pts = points // 8
    box_x, box_z = box_place()
    for copy in copies:
        copy.wait()
    local = []
    for leaf in range(8):
        bit_x, bit_y, bit_z = bits(leaf)
        centre = by_row(
            [2.0 * box_x.astype(jnp.float32) + (bit_x + 0.5), bit_y + 0.5, 2.0 * box_z.astype(jnp.float32) + (bit_z + 0.5)],
            (3, 1),
        )
        here = slice(leaf * pts, (leaf + 1) * pts)
        offset = positions[:, here] - centre
        local.append(offset)
        high = low_bits(offset).astype(jnp.float32)
        middle = low_bits(offset - high).astype(jnp.float32)
        raw = density[:, here].astype(jnp.float32)
        mass = jnp.where(lax.broadcasted_iota(jnp.int32, raw.shape, 1) < count[leaf], raw, 0.0)
        spare = jnp.zeros((ROWS - fields - 6, pts), jnp.float32)
        own[:, here] = low_bits(jnp.concatenate([mass, high, middle, spare], axis=0))

    scaled = 2.0 * jnp.concatenate(local, axis=1)
    row = lax.broadcasted_iota(jnp.int32, (8, points), 0)
    value = None
    for axis in range(3):
        base = jnp.broadcast_to(scaled[axis : axis + 1], (8, points))
        power = jnp.ones((8, points), jnp.float32)
        for degree in range(1, ORDER + 1):
            power = power * jnp.where(row >= degree, base, 1.0)
        pieces = jnp.concatenate(high_low(power), axis=0)
        picked = dot(powers[axis * SLOT : (axis + 1) * SLOT, :], pieces)
        value = picked if value is None else value * picked
    high, low = high_low(value)
    basis[0:SLOT, :] = high
    basis[SLOT:, :] = low
    parts = []
    for leaf in range(8):
        here = slice(leaf * pts, (leaf + 1) * pts)
        parts.append(dot_nt(own[:, here], high[:, here]))
    moment, rest = high_low(jnp.concatenate(parts, axis=1))
    moments[...] = moment
    total = dot(moment, shift[...]) + dot(rest, shift[...])
    total_high, total_low = high_low(total)
    total = low_bits(total_high.astype(jnp.float32) + dot(total_low, heavy[...]))
    total = jnp.concatenate([total, jnp.zeros_like(total)], axis=1)
    totals[...] = total
    for distance, payload in zip((1, 3), payloads):
        bit = jnp.where((box_x ^ distance) > box_x, 1, 0)
        for place in range(4):
            payload[:, lanes(place * pts, pts)] = own[:, lanes((bit + 2 * place) * pts, pts)]
        payload[:, lanes(4 * pts, LEAVES)] = moment
        payload[:, lanes(4 * pts + LEAVES, 2 * SLOT)] = total


def features(held, start, size, centre, target):
    value = held[16:ROWS, lanes(start, size)].astype(jnp.float32)
    x = value[1:4] + value[4:7] + by_row(centre, (3, 1))
    norm = jnp.sum(x * x, axis=0, keepdims=True)
    if target:
        norm = norm + SOFTENING * SOFTENING
    parts, norms = [], []
    for source, out in ((x, parts), (norm, norms)):
        left = source
        for _ in range(3):
            high = low_bits(left).astype(jnp.float32)
            out.append(high)
            left = left - high
    one = jnp.ones_like(norm)
    zero = jnp.zeros_like(norm)
    blank = jnp.zeros((3, norm.shape[1]), jnp.float32)
    blocks = []
    order = (0, 1, 0, 2, 0, 1) if target else (0, 0, 1, 0, 2, 1)
    for index, which in enumerate(order):
        coords = -2.0 * parts[which] if target else parts[which]
        if index < 3:
            pair = [one, norms[index]] if target else [norms[index], one]
        else:
            pair = [zero, zero]
        blocks += [coords, *pair, blank]
    return jnp.concatenate(blocks, axis=0)


def source_features(held, start, size, centre):
    return low_bits(jnp.transpose(features(held, start, size, centre, False)))


def pulled(near, jobs, target, size, first=None):
    width = target.shape[1] // 8
    tiles = []
    for group, source, masses, starts in jobs:
        for piece in range(2):
            here = lanes((2 * group + piece) * width, width)
            for turn, start in enumerate(starts):
                tiles.append((here, source, masses, lanes(start, size), turn == 0, turn + 1 == len(starts)))

    def squares(tile):
        return dot(tile[1][tile[3], :], target[:, tile[0]])

    ahead, kernel, total = squares(tiles[0]), None, None
    for turn in range(len(tiles) + 1):
        square = ahead
        if turn + 1 < len(tiles):
            ahead = squares(tiles[turn + 1])
        if turn > 0:
            here, _, masses, place, opens, closes = tiles[turn - 1]
            if opens:
                total = jnp.zeros((ROWS, width), jnp.float32) if first is None else first[:, here]
            total = total + dot(masses[:, place], kernel)
            if closes:
                near[:, here] = total
        if turn < len(tiles):
            kernel = low_bits(lax.rsqrt(square))


def own_groups(near, first, last, target, source, own):
    pts = source.shape[0] // 8
    starts = [2 * p * pts for p in range(4)]
    pulled(near, [(group, source, own, starts) for group in range(first, last)], target, 2 * pts)


def box_columns(depth, box_x, box_z, nodes):
    blocks = []
    for turn, distance in [(turn, distance) for turn in range(depth) for distance in range(ACROSS)]:
        gap_x = 2 * (box_x - (box_x ^ distance))
        gap_z = 2 * (box_z - ((box_z ^ turn) if depth == 4 else turn))
        across_x = nodes[0] + gap_x.astype(jnp.float32)
        across_z = nodes[2] + gap_z.astype(jnp.float32)
        apart = jnp.maximum(jnp.abs(gap_x), jnp.abs(gap_z)) >= 4
        value = lax.rsqrt(across_x * across_x + across_z * across_z + nodes[1])
        blocks.append(low_bits(value * jnp.where(apart, 1.0 / COEFFS, 0.0)))
    return jnp.concatenate(blocks, axis=0)


def own_kernel(depth, count_in, weights_in, own, *rest):
    tables, outs, (nodes, count, weights, sems) = rest[:3], rest[3:11], rest[11:]
    near, source, target, scale, column, columns, far, spread = outs
    copies = fetch([*zip(tables, (far, spread, nodes)), (count_in, count), (weights_in, weights)], sems)
    points = own.shape[1]
    pts = points // 8
    for leaf in range(8):
        centre = [bit - 0.5 for bit in bits(leaf)]
        source[lanes(leaf * pts, pts), :] = source_features(own, leaf * pts, pts, centre)
        target[:, lanes(leaf_slot(leaf) * pts, pts)] = low_bits(features(own, leaf * pts, pts, centre, True))
    own_groups(near, 0, EARLY, target, source, own)
    for copy in copies:
        copy.wait()
    columns[...] = box_columns(depth, *box_place(), nodes)
    column[...] = by_row([weights[field] for field in range(weights.shape[0])], column.shape)
    lane_index = lax.broadcasted_iota(jnp.int32, (1, pts), 1)
    for leaf in range(8):
        scale[:, leaf * pts : (leaf + 1) * pts] = jnp.where(lane_index < count[leaf], 1.0 / (128.0 * pts), 0.0)


def spread_first(value, node):
    starts = [leaf * SLOT + node for leaf in range(8)]
    return jnp.concatenate([jnp.broadcast_to(value[:, s : s + 1], (ROWS, SLOT)) for s in starts], axis=1)


def decoded(coded):
    value = coded.astype(jnp.float32)
    node = lax.broadcasted_iota(jnp.int32, value.shape, 1) % SLOT
    return jnp.where(node == 0, 0.0, value) + spread_first(value, 0) + spread_first(value, COEFFS)


def faces_of(faces, bit, given, own, left, right, rows=None):
    points = own.shape[1]
    pts = points // 8
    for y in range(2):
        for x in range(4):
            place = lanes((2 * x + y) * pts, pts)
            if x in (0, 3):
                side = left if x == 0 else right
                faces[:, place] = side[:, lanes((y + 2 * bit) * pts, pts)]
            else:
                faces[:, place] = own[:, lanes((x - 1 + 2 * y + 4 * bit) * pts, pts)]
    node = lax.broadcasted_iota(jnp.int32, given.shape, 1) % SLOT
    base = spread_first(given, 0)
    base_high = low_bits(base).astype(jnp.float32)
    coded = jnp.where(node == 0, base_high, jnp.where(node == COEFFS, base - base_high, given - base))
    faces[:, lanes(points, LEAVES)] = low_bits(coded)
    if rows is not None:
        faces[:, lanes(points + LEAVES, rows.shape[1])] = rows


def sums_for(above, left, moments, right, far):
    base = left.shape[1] - LEAVES
    around = jnp.concatenate([left[:, lanes(base, LEAVES)], moments[...], right[:, lanes(base, LEAVES)]], axis=1)
    return dot(around, far[lanes(jnp.where(above == 1, 0, 5 * LEAVES), 3 * LEAVES), :])


def row_kernel(own, moments, totals, from_1, from_2, from_3, far, left, right, faces_even, rows):
    box_x, box_z = box_place()
    for side, step in ((left, -1), (right, 1)):
        side[...] = jnp.zeros(side.shape, side.dtype)
        for distance, held in ((1, from_1), (3, from_3)):

            @pl.when((box_x ^ distance) - box_x == step)
            def _(side=side, held=held):
                side[...] = held[:, lanes(0, side.shape[1])]

    ends = lanes(left.shape[1], 2 * SLOT)
    row = [totals[...], from_1[:, ends], from_2[...], from_3[:, ends]]
    row = jnp.concatenate([box[:, :SLOT] for box in row], axis=1)
    rows[...] = row
    above = 1 - lax.rem(box_z, 2)
    faces_of(faces_even, above, sums_for(above, left, moments, right, far), own, left, right, row)


def side_pulls(near, faces, early, target, scratch):
    pts = early.shape[1] // 8
    jobs = []
    for (step, side), held in zip(faces, scratch):
        for place in range(4):
            centre = (1.5 if step else -1.5, place % 2 - 0.5, place // 2 - 0.5)
            held[lanes(place * pts, pts), :] = source_features(side, place * pts, pts, centre)
        jobs += [(step, held, side, [0, 2 * pts]), (step + 2, held, side, [0, 2 * pts])]
    pulled(near, jobs, target, 2 * pts, early)


def middle_kernel(own, left, right, moments, far, early, source, target, near, faces_odd, same, *sides):
    points = own.shape[1]
    _, box_z = box_place()
    above = lax.rem(box_z, 2)
    faces_of(faces_odd, above, sums_for(above, left, moments, right, far), own, left, right)
    base = left.shape[1] - LEAVES
    beside = jnp.concatenate([left[:, lanes(base, LEAVES)], right[:, lanes(base, LEAVES)]], axis=1)
    same[...] = dot(beside, far[lanes(3 * LEAVES, 2 * LEAVES), :])
    near[:, lanes(0, EARLY * points // 4)] = early[...]
    own_groups(near, EARLY, 4, target, source, own)

    @pl.when(above == 1)
    def _():
        side_pulls(near, [(0, left), (1, right)], near, target, sides)


def side_kernel(left, right, early, target, near, *sides):
    _, box_z = box_place()
    odd = lax.rem(box_z, 2) == 1

    @pl.when(odd)
    def _():
        near[...] = early[...]

    @pl.when(jnp.logical_not(odd))
    def _():
        side_pulls(near, [(0, left), (1, right)], early, target, sides)


def both_kernel(rows, faces, near, both):
    width = rows.shape[1]
    both[:, lanes(0, width)] = rows[...]
    both[:, lanes(width, width)] = faces[:, lanes(faces.shape[1] - width, width)]


def layer_pulls(near, early, step, inside, target, faces, sides):
    points = early.shape[1]
    pts = points // 8

    @pl.when(inside)
    def _():
        for place in range(8):
            height = jnp.where(step == 1, 1.5, -1.5)
            centre = (place // 2 - 1.5, place % 2 - 0.5, height)
            sides[lanes(place * pts, pts), :] = source_features(faces, place * pts, pts, centre)

        jobs = [(i + 2 * step, sides, faces, [2 * (x + i) * pts for x in range(3)]) for i in range(2)]
        pulled(near, jobs, target, 2 * pts, early)

    @pl.when(jnp.logical_not(inside))
    def _():
        here = lanes(step * (points // 2), points // 2)
        near[:, here] = early[:, here]


def even_kernel(early, target, faces, near, sides):
    _, box_z = box_place()
    points = early.shape[1]
    step = 1 - lax.rem(box_z, 2)
    other = lanes((1 - step) * (points // 2), points // 2)
    near[:, other] = early[:, other]
    layer_pulls(near, early, step, box_z >= 0, target, faces, sides)


def odd_inside(depth):
    _, box_z = box_place()
    step = lax.rem(box_z, 2)
    return step, (box_z + 2 * step - 1 >= 0) & (box_z + 2 * step - 1 < depth)


def odd_kernel(depth, early, target, faces, near, sides):
    points = early.shape[1]
    step, inside = odd_inside(depth)
    other = lanes((1 - step) * (points // 2), points // 2)
    near[:, other] = early[:, other]
    layer_pulls(near, early, step, inside, target, faces, sides)


def last_kernel(depth, near, faces_even, faces_odd, basis, scale, column, columns, spread, same, *rest):
    held, (potential, sums) = rest[:-2], rest[-2:]
    fields, points = potential.shape
    pts = points // 8
    _, inside = odd_inside(depth)
    if depth == 4:
        rows, distant = held
        width = rows.shape[1]
        near_rows = faces_even[:, lanes(faces_even.shape[1] - width, width)]
        layers = [rows[...], near_rows, distant[:, lanes(0, width)], distant[:, lanes(width, width)]]
    else:
        layers = [held[0][layer] for layer in range(depth)]
    coarse_high, coarse_low = high_low(dot(jnp.concatenate(layers, axis=1), columns[...]))
    value = same[...] + dot(coarse_high, spread[...]) + dot(coarse_low, spread[...])
    value = value + decoded(faces_even[:, lanes(points, LEAVES)])
    value = value + jnp.where(inside, decoded(faces_odd[:, lanes(points, LEAVES)]), 0.0)
    local_high, local_low = high_low(value)
    weight = column[0:fields, 0:1]
    for leaf in range(8):
        here = slice(leaf * pts, (leaf + 1) * pts)
        slot = slice(leaf * SLOT, (leaf + 1) * SLOT)
        doubled = jnp.concatenate([local_high[:, slot], local_high[:, slot]], axis=1)
        far_part = dot(doubled, basis[:, here]) + dot(local_low[:, slot], basis[0:SLOT, here])
        total = near[0:fields, lanes(leaf_slot(leaf) * pts, pts)] + far_part[:fields]
        total = total * scale[:, here]
        potential[:, here] = total
        sums[:, here] = jnp.sum(total * weight, axis=0, keepdims=True)
    sums[:, points:] = jnp.broadcast_to(jnp.sum(weight), (1, sums.shape[1] - points))


def mean_kernel(mine, other, mean):
    points = mean.shape[1]
    total = mine[...] + other[...]
    mean[...] = total[:, :points] / total[:, points : points + 1]


def swapped(block, axis, partner):
    size = lax.axis_size(axis)
    return lax.ppermute(block, axis, [(partner(i), i) for i in range(size)])


def swapped_odd(block):
    boxes, cores = lax.axis_size("space"), lax.axis_size("sig")
    pairs = []
    for box in range(boxes):
        other = box + ACROSS if box // ACROSS % 2 else box - ACROSS
        for core in range(cores):
            source = other * cores + core if 0 <= other < boxes else box * cores + (core ^ 1)
            pairs.append((source, box * cores + core))
    return lax.ppermute(block, ("space", "sig"), pairs)


def per_device(positions, density, leaf_count, sigma_weights):
    fields, points = density.shape
    pts = points // 8
    depth = lax.axis_size("space") // ACROSS
    vmem, hbm = pl.BlockSpec(memory_space=pltpu.VMEM), pl.BlockSpec(memory_space=pltpu.HBM)

    def call(kernel, name, in_specs, outs, scratch, *args):
        return pl.pallas_call(
            kernel,
            in_specs=in_specs,
            out_specs=[vmem] * len(outs),
            out_shape=[jax.ShapeDtypeStruct(shape, dtype) for shape, dtype in outs],
            scratch_shapes=scratch,
            compiler_params=pltpu.CompilerParams(vmem_limit_bytes=24 * MEGA),
            name=name,
        )(*(pltpu.with_memory_space_constraint(a, pltpu.HBM) if s is hbm else a for s, a in zip(in_specs, args)))

    half, full = jnp.bfloat16, jnp.float32
    shift = shift_table()
    side_shape = ((ROWS, 4 * pts + LEAVES), half)
    given_shape = ((ROWS, 4 * pts + LEAVES + 2 * SLOT), half)
    faces_shape = ((ROWS, points + LEAVES), half)
    even_shape = ((ROWS, points + LEAVES + SLOT * ACROSS), half)
    rows_shape = ((ROWS, SLOT * ACROSS), half)
    both_shape = ((ROWS, 2 * SLOT * ACROSS), half)
    near_shape, sums_shape = ((ROWS, points), full), ((ROWS, LEAVES), full)
    side_scratch = [pltpu.VMEM((4 * pts, FEATURES), half)] * 2
    rows_scratch = pltpu.VMEM((8 * pts, FEATURES), half)
    own, basis, moments, totals, *given = call(
        pack_kernel,
        "pack",
        [hbm] * 6,
        [
            ((ROWS, points), half),
            ((2 * SLOT, points), half),
            ((ROWS, LEAVES), half),
            ((ROWS, 2 * SLOT), half),
            given_shape,
            given_shape,
        ],
        [
            pltpu.SMEM((8,), jnp.int32),
            pltpu.VMEM((3, points), full),
            pltpu.VMEM((fields, points), half),
            pltpu.VMEM((LEAVES, SLOT), half),
            pltpu.VMEM((SLOT, SLOT), half),
            pltpu.VMEM((3 * SLOT, 16), half),
            pltpu.SemaphoreType.DMA((6,)),
        ],
        leaf_count,
        positions,
        density,
        jnp.asarray(shift, half),
        jnp.asarray(heavy_table(), half),
        jnp.asarray(power_table(), half),
    )
    from_2 = swapped(totals, "space", lambda i: i ^ 2)
    from_1 = swapped(given[0], "space", lambda i: i ^ 1)
    from_3 = swapped(given[1], "space", lambda i: i ^ 3)
    near, source, target, scale, column, columns, far, spread = call(
        functools.partial(own_kernel, depth),
        "near_own",
        [hbm] * 2 + [vmem] + [hbm] * 3,
        [
            ((ROWS, EARLY * points // 4), full),
            ((points, FEATURES), half),
            ((FEATURES, points), half),
            ((1, points), full),
            ((ROWS, 128), full),
            ((ACROSS * depth * SLOT, SLOT), half),
            ((len(STEPS) * LEAVES, LEAVES), half),
            ((SLOT, LEAVES), half),
        ],
        [
            pltpu.VMEM((3, SLOT, SLOT), full),
            pltpu.SMEM((8,), jnp.int32),
            pltpu.SMEM((fields,), full),
            pltpu.SemaphoreType.DMA((5,)),
        ],
        leaf_count,
        sigma_weights,
        own,
        jnp.asarray(far_table(), half),
        jnp.asarray(shift.T.copy(), half),
        jnp.asarray(box_nodes()),
    )
    left, right, faces_even, rows = call(
        row_kernel,
        "row",
        [vmem] * 7,
        [side_shape, side_shape, even_shape, rows_shape],
        [],
        own,
        moments,
        totals,
        from_1,
        from_2,
        from_3,
        far,
    )
    faces_even = swapped(faces_even, "space", lambda i: i ^ ACROSS)
    near, faces_odd, same = call(
        middle_kernel,
        "near_middle",
        [vmem] * 8,
        [near_shape, faces_shape, sums_shape],
        side_scratch,
        own,
        left,
        right,
        moments,
        far,
        near,
        source,
        target,
    )
    faces_odd = swapped_odd(faces_odd)
    near, = call(
        side_kernel,
        "near_side",
        [vmem] * 4,
        [near_shape],
        side_scratch,
        left,
        right,
        near,
        target,
    )
    if depth == 4:
        both, = call(both_kernel, "row_pairs", [vmem] * 3, [both_shape], [], rows, faces_even, near)
        held = [rows, swapped(both, "space", lambda i: i ^ (2 * ACROSS))]
    else:
        groups = [[z * ACROSS + x for z in range(depth)] for x in range(ACROSS)]
        held = [lax.all_gather(rows, "space", axis_index_groups=groups)]
    near, = call(even_kernel, "near_even", [vmem] * 3, [near_shape], [rows_scratch], near, target, faces_even)
    near, = call(
        functools.partial(odd_kernel, depth),
        "near_odd",
        [vmem] * 3,
        [near_shape],
        [rows_scratch],
        near,
        target,
        faces_odd,
    )
    potential, sums = call(
        functools.partial(last_kernel, depth),
        "evaluate",
        [vmem] * (9 + len(held)),
        [((fields, points), full), ((1, points + 128), full)],
        [],
        near,
        faces_even,
        faces_odd,
        basis,
        scale,
        column,
        columns,
        spread,
        same,
        *held,
    )
    if lax.axis_size("sig") == 2:
        other = swapped(sums, "sig", lambda i: i ^ 1)
    else:
        other = lax.psum(sums, "sig") - sums
    mean, = call(mean_kernel, "mean", [vmem] * 2, [((1, points), full)], [], sums, other)
    return potential, mean.reshape(points)


def solution(mesh):
    in_specs = (P(None, "space"), P("sig", "space"), P("space"), P("sig"))
    out_specs = (P("sig", "space"), P("space"))
    return jax.shard_map(per_device, mesh=mesh, in_specs=in_specs, out_specs=out_specs, check_vma=False)
```

```python
import functools
import math

import jax
import jax.numpy as jnp
import numpy as np
from jax import lax
from jax.experimental import pallas as pl
from jax.experimental.pallas import tpu as pltpu
from jax.sharding import PartitionSpec as P

ORDER = 5
SOFTENING = 0.1
ACROSS = 4
SLOT = 64
ROWS = 24
LEAVES = 8 * SLOT
MEGA = 1024 * 1024
FEATURES = 48
EARLY = 3


def exponent_table(order_max):
    entries_list = []
    for degree in range(order_max + 1):
        for first_power in range(degree, -1, -1):
            for second_power in range(degree - first_power, -1, -1):
                entries_list.append((first_power, second_power, degree - first_power - second_power))
    return entries_list


def node_table(count_nodes, offset_value):
    counter = np.arange(1, count_nodes + 1, dtype=np.float32)[:, None]
    stride_set = np.array([0.7548776662466927, 0.5698402909980532, 0.4142135623730951], dtype=np.float32)[None, :]
    unit_points = np.mod(counter * stride_set + np.float32(offset_value), np.float32(1.0))
    return (np.float32(2.0) * unit_points - np.float32(1.0)).astype(np.float32)


EXPONENTS = exponent_table(ORDER)
COEFFS = len(EXPONENTS)
CHECK = node_table(COEFFS, 0.5).astype(np.float64)
EQUIV = node_table(COEFFS, 0.0).astype(np.float64)
HEAVY = [EXPONENTS.index(e) for e in ((0, 0, 0), (2, 0, 0), (0, 2, 0), (0, 0, 2), (4, 0, 0), (0, 4, 0), (0, 0, 4), (2, 0, 2))]
STEPS = [(sx, sz) for sz in (-1, 0, 1) for sx in (-1, 0, 1) if sx != 0 or sz != 0]


def bits(octant):
    return octant % 2, octant // 2 % 2, octant // 4


def leaf_slot(octant):
    bit_x, bit_y, bit_z = bits(octant)
    return (bit_x + 2 * bit_z) * 2 + bit_y


@functools.lru_cache(None)
def far_table():
    shape = (len(STEPS), 8, SLOT, 8, SLOT)
    table = np.zeros(shape)
    gap_nodes = 0.5 * (CHECK[None, :, :] - EQUIV[:, None, :])
    for index, (step_x, step_z) in enumerate(STEPS):
        for source in range(8):
            for target in range(8):
                s, t = bits(source), bits(target)
                gap = np.array([2 * step_x + s[0] - t[0], s[1] - t[1], 2 * step_z + s[2] - t[2]], np.float64)
                if max(abs(gap[0]), abs(gap[2])) >= 2:
                    shifted = gap_nodes - gap
                    value = 1.0 / np.sqrt(np.sum(shifted * shifted, -1) + SOFTENING * SOFTENING) / COEFFS
                    table[index, source, :COEFFS, target, :COEFFS] = value
    return table.reshape(len(STEPS) * LEAVES, LEAVES)


@functools.lru_cache(None)
def shift_table():
    table = np.zeros((8, SLOT, SLOT))
    for leaf in range(8):
        offset = [bit - 0.5 for bit in bits(leaf)]
        for k, target in enumerate(EXPONENTS):
            for i, source in enumerate(EXPONENTS):
                if all(b <= a for a, b in zip(target, source)):
                    value = 1.0
                    for a, b, h in zip(target, source, offset):
                        value *= math.comb(a, b) * 0.5**b * h ** (a - b)
                    table[leaf, i, k] = value
    return table.reshape(8 * SLOT, SLOT)


@functools.lru_cache(None)
def box_nodes():
    gaps = np.zeros((3, SLOT, SLOT))
    gaps[:, :COEFFS, :COEFFS] = np.moveaxis(CHECK[None, :, :] - EQUIV[:, None, :], -1, 0)
    gaps[:, COEFFS:] = gaps[:, HEAVY]
    gaps[1] = gaps[1] ** 2 + SOFTENING * SOFTENING
    return gaps.astype(np.float32)


def dot(left, right):
    return jnp.dot(left, right, preferred_element_type=jnp.float32)


def dot_nt(left, right):
    return lax.dot_general(left, right, (((1,), (1,)), ((), ())), preferred_element_type=jnp.float32)


def low_bits(value):
    return value.astype(jnp.bfloat16)


def heavy_table():
    table = np.zeros((SLOT, SLOT), np.float32)
    table[HEAVY, np.arange(COEFFS, SLOT)] = 1.0
    return table


def power_table():
    table = np.zeros((3, SLOT, 16), np.float32)
    for axis in range(3):
        for k, powers in enumerate(EXPONENTS):
            table[axis, k, powers[axis]] = 1.0
            table[axis, k, 8 + powers[axis]] = 1.0
    return table.reshape(3 * SLOT, 16)


def high_low(value):
    high = low_bits(value)
    return high, low_bits(value - high.astype(jnp.float32))


def by_row(values, shape):
    row = lax.broadcasted_iota(jnp.int32, shape, 0)
    result = jnp.zeros(shape, jnp.float32)
    for index, value in enumerate(values):
        result = jnp.where(row == index, value, result)
    return result


def box_place():
    label = lax.axis_index("space")
    return lax.rem(label, ACROSS), lax.div(label, ACROSS)


def lanes(start, size):
    return pl.ds(start if isinstance(start, int) else pl.multiple_of(start, 128), size)


def fetch(pairs, sems):
    copies = [pltpu.make_async_copy(src, dst, sems.at[i]) for i, (src, dst) in enumerate(pairs)]
    for copy in copies:
        copy.start()
    return copies


def pack_kernel(count_in, positions_in, density_in, shift_in, heavy_in, powers_in, own, basis, moments, totals, *rest):
    payloads, (count, positions, density, shift, heavy, powers, sems) = rest[:2], rest[2:]
    copies = fetch(
        [
            (count_in, count),
            (positions_in, positions),
            (density_in, density),
            (shift_in, shift),
            (heavy_in, heavy),
            (powers_in, powers),
        ],
        sems,
    )
    fields, points = density.shape
    pts = points // 8
    box_x, box_z = box_place()
    for copy in copies:
        copy.wait()
    local = []
    for leaf in range(8):
        bit_x, bit_y, bit_z = bits(leaf)
        centre = by_row(
            [2.0 * box_x.astype(jnp.float32) + (bit_x + 0.5), bit_y + 0.5, 2.0 * box_z.astype(jnp.float32) + (bit_z + 0.5)],
            (3, 1),
        )
        here = slice(leaf * pts, (leaf + 1) * pts)
        offset = positions[:, here] - centre
        local.append(offset)
        high = low_bits(offset).astype(jnp.float32)
        middle = low_bits(offset - high).astype(jnp.float32)
        raw = density[:, here].astype(jnp.float32)
        mass = jnp.where(lax.broadcasted_iota(jnp.int32, raw.shape, 1) < count[leaf], raw, 0.0)
        spare = jnp.zeros((ROWS - fields - 6, pts), jnp.float32)
        own[:, here] = low_bits(jnp.concatenate([mass, high, middle, spare], axis=0))

    scaled = 2.0 * jnp.concatenate(local, axis=1)
    row = lax.broadcasted_iota(jnp.int32, (8, points), 0)
    value = None
    for axis in range(3):
        base = jnp.broadcast_to(scaled[axis : axis + 1], (8, points))
        power = jnp.ones((8, points), jnp.float32)
        for degree in range(1, ORDER + 1):
            power = power * jnp.where(row >= degree, base, 1.0)
        pieces = jnp.concatenate(high_low(power), axis=0)
        picked = dot(powers[axis * SLOT : (axis + 1) * SLOT, :], pieces)
        value = picked if value is None else value * picked
    high, low = high_low(value)
    basis[0:SLOT, :] = high
    basis[SLOT:, :] = low
    parts = []
    for leaf in range(8):
        here = slice(leaf * pts, (leaf + 1) * pts)
        parts.append(dot_nt(own[:, here], high[:, here]))
    moment, rest = high_low(jnp.concatenate(parts, axis=1))
    moments[...] = moment
    total = dot(moment, shift[...]) + dot(rest, shift[...])
    total_high, total_low = high_low(total)
    total = low_bits(total_high.astype(jnp.float32) + dot(total_low, heavy[...]))
    total = jnp.concatenate([total, jnp.zeros_like(total)], axis=1)
    totals[...] = total
    for distance, payload in zip((1, 3), payloads):
        bit = jnp.where((box_x ^ distance) > box_x, 1, 0)
        for place in range(4):
            payload[:, lanes(place * pts, pts)] = own[:, lanes((bit + 2 * place) * pts, pts)]
        payload[:, lanes(4 * pts, LEAVES)] = moment
        payload[:, lanes(4 * pts + LEAVES, 2 * SLOT)] = total


def features(held, start, size, centre, target):
    value = held[16:ROWS, lanes(start, size)].astype(jnp.float32)
    x = value[1:4] + value[4:7] + by_row(centre, (3, 1))
    norm = jnp.sum(x * x, axis=0, keepdims=True)
    if target:
        norm = norm + SOFTENING * SOFTENING
    parts, norms = [], []
    for source, out in ((x, parts), (norm, norms)):
        left = source
        for _ in range(3):
            high = low_bits(left).astype(jnp.float32)
            out.append(high)
            left = left - high
    one = jnp.ones_like(norm)
    zero = jnp.zeros_like(norm)
    blank = jnp.zeros((3, norm.shape[1]), jnp.float32)
    blocks = []
    order = (0, 1, 0, 2, 0, 1) if target else (0, 0, 1, 0, 2, 1)
    for index, which in enumerate(order):
        coords = -2.0 * parts[which] if target else parts[which]
        if index < 3:
            pair = [one, norms[index]] if target else [norms[index], one]
        else:
            pair = [zero, zero]
        blocks += [coords, *pair, blank]
    return jnp.concatenate(blocks, axis=0)


def source_features(held, start, size, centre):
    return low_bits(jnp.transpose(features(held, start, size, centre, False)))


def pulled(near, jobs, target, size, first=None):
    width = target.shape[1] // 8
    tiles = []
    for group, source, masses, starts in jobs:
        for piece in range(2):
            here = lanes((2 * group + piece) * width, width)
            for turn, start in enumerate(starts):
                tiles.append((here, source, masses, lanes(start, size), turn == 0, turn + 1 == len(starts)))

    def squares(tile):
        return dot(tile[1][tile[3], :], target[:, tile[0]])

    ahead, kernel, total = squares(tiles[0]), None, None
    for turn in range(len(tiles) + 1):
        square = ahead
        if turn + 1 < len(tiles):
            ahead = squares(tiles[turn + 1])
        if turn > 0:
            here, _, masses, place, opens, closes = tiles[turn - 1]
            if opens:
                total = jnp.zeros((ROWS, width), jnp.float32) if first is None else first[:, here]
            total = total + dot(masses[:, place], kernel)
            if closes:
                near[:, here] = total
        if turn < len(tiles):
            kernel = low_bits(lax.rsqrt(square))


def own_groups(near, first, last, target, source, own):
    pts = source.shape[0] // 8
    starts = [2 * p * pts for p in range(4)]
    pulled(near, [(group, source, own, starts) for group in range(first, last)], target, 2 * pts)


def box_columns(depth, box_x, box_z, nodes):
    blocks = []
    for turn, distance in [(turn, distance) for turn in range(depth) for distance in range(ACROSS)]:
        gap_x = 2 * (box_x - (box_x ^ distance))
        gap_z = 2 * (box_z - ((box_z ^ turn) if depth == 4 else turn))
        across_x = nodes[0] + gap_x.astype(jnp.float32)
        across_z = nodes[2] + gap_z.astype(jnp.float32)
        apart = jnp.maximum(jnp.abs(gap_x), jnp.abs(gap_z)) >= 4
        value = lax.rsqrt(across_x * across_x + across_z * across_z + nodes[1])
        blocks.append(low_bits(value * jnp.where(apart, 1.0 / COEFFS, 0.0)))
    return jnp.concatenate(blocks, axis=0)


def own_kernel(depth, count_in, weights_in, own, *rest):
    tables, outs, (nodes, count, weights, sems) = rest[:3], rest[3:11], rest[11:]
    near, source, target, scale, column, columns, far, spread = outs
    copies = fetch([*zip(tables, (far, spread, nodes)), (count_in, count), (weights_in, weights)], sems)
    points = own.shape[1]
    pts = points // 8
    for leaf in range(8):
        centre = [bit - 0.5 for bit in bits(leaf)]
        source[lanes(leaf * pts, pts), :] = source_features(own, leaf * pts, pts, centre)
        target[:, lanes(leaf_slot(leaf) * pts, pts)] = low_bits(features(own, leaf * pts, pts, centre, True))
    own_groups(near, 0, EARLY, target, source, own)
    for copy in copies:
        copy.wait()
    columns[...] = box_columns(depth, *box_place(), nodes)
    column[...] = by_row([weights[field] for field in range(weights.shape[0])], column.shape)
    lane_index = lax.broadcasted_iota(jnp.int32, (1, pts), 1)
    for leaf in range(8):
        scale[:, leaf * pts : (leaf + 1) * pts] = jnp.where(lane_index < count[leaf], 1.0 / (128.0 * pts), 0.0)


def spread_first(value, node):
    starts = [leaf * SLOT + node for leaf in range(8)]
    return jnp.concatenate([jnp.broadcast_to(value[:, s : s + 1], (ROWS, SLOT)) for s in starts], axis=1)


def decoded(coded):
    value = coded.astype(jnp.float32)
    node = lax.broadcasted_iota(jnp.int32, value.shape, 1) % SLOT
    return jnp.where(node == 0, 0.0, value) + spread_first(value, 0) + spread_first(value, COEFFS)


def faces_of(faces, bit, given, own, left, right, rows=None):
    points = own.shape[1]
    pts = points // 8
    for y in range(2):
        for x in range(4):
            place = lanes((2 * x + y) * pts, pts)
            if x in (0, 3):
                side = left if x == 0 else right
                faces[:, place] = side[:, lanes((y + 2 * bit) * pts, pts)]
            else:
                faces[:, place] = own[:, lanes((x - 1 + 2 * y + 4 * bit) * pts, pts)]
    node = lax.broadcasted_iota(jnp.int32, given.shape, 1) % SLOT
    base = spread_first(given, 0)
    base_high = low_bits(base).astype(jnp.float32)
    coded = jnp.where(node == 0, base_high, jnp.where(node == COEFFS, base - base_high, given - base))
    faces[:, lanes(points, LEAVES)] = low_bits(coded)
    if rows is not None:
        faces[:, lanes(points + LEAVES, rows.shape[1])] = rows


def sums_for(above, left, moments, right, far):
    base = left.shape[1] - LEAVES
    around = jnp.concatenate([left[:, lanes(base, LEAVES)], moments[...], right[:, lanes(base, LEAVES)]], axis=1)
    return dot(around, far[lanes(jnp.where(above == 1, 0, 5 * LEAVES), 3 * LEAVES), :])


def row_kernel(own, moments, totals, from_1, from_2, from_3, far, left, right, faces_even, rows):
    box_x, box_z = box_place()
    for side, step in ((left, -1), (right, 1)):
        side[...] = jnp.zeros(side.shape, side.dtype)
        for distance, held in ((1, from_1), (3, from_3)):

            @pl.when((box_x ^ distance) - box_x == step)
            def _(side=side, held=held):
                side[...] = held[:, lanes(0, side.shape[1])]

    ends = lanes(left.shape[1], 2 * SLOT)
    row = [totals[...], from_1[:, ends], from_2[...], from_3[:, ends]]
    row = jnp.concatenate([box[:, :SLOT] for box in row], axis=1)
    rows[...] = row
    above = 1 - lax.rem(box_z, 2)
    faces_of(faces_even, above, sums_for(above, left, moments, right, far), own, left, right, row)


def side_pulls(near, faces, early, target, scratch):
    pts = early.shape[1] // 8
    jobs = []
    for (step, side), held in zip(faces, scratch):
        for place in range(4):
            centre = (1.5 if step else -1.5, place % 2 - 0.5, place // 2 - 0.5)
            held[lanes(place * pts, pts), :] = source_features(side, place * pts, pts, centre)
        jobs += [(step, held, side, [0, 2 * pts]), (step + 2, held, side, [0, 2 * pts])]
    pulled(near, jobs, target, 2 * pts, early)


def middle_kernel(own, left, right, moments, far, early, source, target, near, faces_odd, same, *sides):
    points = own.shape[1]
    _, box_z = box_place()
    above = lax.rem(box_z, 2)
    faces_of(faces_odd, above, sums_for(above, left, moments, right, far), own, left, right)
    base = left.shape[1] - LEAVES
    beside = jnp.concatenate([left[:, lanes(base, LEAVES)], right[:, lanes(base, LEAVES)]], axis=1)
    same[...] = dot(beside, far[lanes(3 * LEAVES, 2 * LEAVES), :])
    near[:, lanes(0, EARLY * points // 4)] = early[...]
    own_groups(near, EARLY, 4, target, source, own)

    @pl.when(above == 1)
    def _():
        side_pulls(near, [(0, left)], near, target, sides)


def one_side(near, step, side, early, target, held):
    pts = early.shape[1] // 8
    for group in (1 - step, 3 - step):
        here = lanes(2 * group * pts, 2 * pts)
        near[:, here] = early[:, here]
    side_pulls(near, [(step, side)], early, target, [held])


def side_kernel(left, right, early, target, near, held):
    _, box_z = box_place()
    odd = lax.rem(box_z, 2) == 1

    @pl.when(odd)
    def _():
        one_side(near, 1, right, early, target, held)

    @pl.when(jnp.logical_not(odd))
    def _():
        one_side(near, 0, left, early, target, held)


def both_kernel(rows, faces, near, both):
    width = rows.shape[1]
    both[:, lanes(0, width)] = rows[...]
    both[:, lanes(width, width)] = faces[:, lanes(faces.shape[1] - width, width)]


def layer_pulls(near, early, step, inside, target, faces, sides):
    points = early.shape[1]
    pts = points // 8

    @pl.when(inside)
    def _():
        for place in range(8):
            height = jnp.where(step == 1, 1.5, -1.5)
            centre = (place // 2 - 1.5, place % 2 - 0.5, height)
            sides[lanes(place * pts, pts), :] = source_features(faces, place * pts, pts, centre)

        jobs = [(i + 2 * step, sides, faces, [2 * (x + i) * pts for x in range(3)]) for i in range(2)]
        pulled(near, jobs, target, 2 * pts, early)

    @pl.when(jnp.logical_not(inside))
    def _():
        here = lanes(step * (points // 2), points // 2)
        near[:, here] = early[:, here]


def even_kernel(early, target, right, faces, near, sides, held):
    _, box_z = box_place()
    step = 1 - lax.rem(box_z, 2)

    @pl.when(step == 0)
    def _():
        near[...] = early[...]

    @pl.when(step == 1)
    def _():
        one_side(near, 1, right, early, target, held)

    layer_pulls(near, near, step, box_z >= 0, target, faces, sides)


def odd_inside(depth):
    _, box_z = box_place()
    step = lax.rem(box_z, 2)
    return step, (box_z + 2 * step - 1 >= 0) & (box_z + 2 * step - 1 < depth)


def odd_kernel(depth, early, target, faces, near, sides):
    points = early.shape[1]
    step, inside = odd_inside(depth)
    other = lanes((1 - step) * (points // 2), points // 2)
    near[:, other] = early[:, other]
    layer_pulls(near, early, step, inside, target, faces, sides)


def last_kernel(depth, near, faces_even, faces_odd, basis, scale, column, columns, spread, same, *rest):
    held, (potential, sums) = rest[:-2], rest[-2:]
    fields, points = potential.shape
    pts = points // 8
    _, inside = odd_inside(depth)
    if depth == 4:
        rows, distant = held
        width = rows.shape[1]
        near_rows = faces_even[:, lanes(faces_even.shape[1] - width, width)]
        layers = [rows[...], near_rows, distant[:, lanes(0, width)], distant[:, lanes(width, width)]]
    else:
        layers = [held[0][layer] for layer in range(depth)]
    coarse_high, coarse_low = high_low(dot(jnp.concatenate(layers, axis=1), columns[...]))
    value = same[...] + dot(coarse_high, spread[...]) + dot(coarse_low, spread[...])
    value = value + decoded(faces_even[:, lanes(points, LEAVES)])
    value = value + jnp.where(inside, decoded(faces_odd[:, lanes(points, LEAVES)]), 0.0)
    local_high, local_low = high_low(value)
    weight = column[0:fields, 0:1]
    for leaf in range(8):
        here = slice(leaf * pts, (leaf + 1) * pts)
        slot = slice(leaf * SLOT, (leaf + 1) * SLOT)
        doubled = jnp.concatenate([local_high[:, slot], local_high[:, slot]], axis=1)
        far_part = dot(doubled, basis[:, here]) + dot(local_low[:, slot], basis[0:SLOT, here])
        total = near[0:fields, lanes(leaf_slot(leaf) * pts, pts)] + far_part[:fields]
        total = total * scale[:, here]
        potential[:, here] = total
        sums[:, here] = jnp.sum(total * weight, axis=0, keepdims=True)
    sums[:, points:] = jnp.broadcast_to(jnp.sum(weight), (1, sums.shape[1] - points))


def mean_kernel(mine, other, mean):
    points = mean.shape[1]
    total = mine[...] + other[...]
    mean[...] = total[:, :points] / total[:, points : points + 1]


def swapped(block, axis, partner):
    size = lax.axis_size(axis)
    return lax.ppermute(block, axis, [(partner(i), i) for i in range(size)])


def swapped_odd(block):
    boxes, cores = lax.axis_size("space"), lax.axis_size("sig")
    pairs = []
    for box in range(boxes):
        other = box + ACROSS if box // ACROSS % 2 else box - ACROSS
        for core in range(cores):
            source = other * cores + core if 0 <= other < boxes else box * cores + (core ^ 1)
            pairs.append((source, box * cores + core))
    return lax.ppermute(block, ("space", "sig"), pairs)


def per_device(positions, density, leaf_count, sigma_weights):
    fields, points = density.shape
    pts = points // 8
    depth = lax.axis_size("space") // ACROSS
    vmem, hbm = pl.BlockSpec(memory_space=pltpu.VMEM), pl.BlockSpec(memory_space=pltpu.HBM)

    def call(kernel, name, in_specs, outs, scratch, *args):
        return pl.pallas_call(
            kernel,
            in_specs=in_specs,
            out_specs=[vmem] * len(outs),
            out_shape=[jax.ShapeDtypeStruct(shape, dtype) for shape, dtype in outs],
            scratch_shapes=scratch,
            compiler_params=pltpu.CompilerParams(vmem_limit_bytes=24 * MEGA),
            name=name,
        )(*(pltpu.with_memory_space_constraint(a, pltpu.HBM) if s is hbm else a for s, a in zip(in_specs, args)))

    half, full = jnp.bfloat16, jnp.float32
    shift = shift_table()
    side_shape = ((ROWS, 4 * pts + LEAVES), half)
    given_shape = ((ROWS, 4 * pts + LEAVES + 2 * SLOT), half)
    faces_shape = ((ROWS, points + LEAVES), half)
    even_shape = ((ROWS, points + LEAVES + SLOT * ACROSS), half)
    rows_shape = ((ROWS, SLOT * ACROSS), half)
    both_shape = ((ROWS, 2 * SLOT * ACROSS), half)
    near_shape, sums_shape = ((ROWS, points), full), ((ROWS, LEAVES), full)
    side_scratch = pltpu.VMEM((4 * pts, FEATURES), half)
    rows_scratch = pltpu.VMEM((8 * pts, FEATURES), half)
    own, basis, moments, totals, *given = call(
        pack_kernel,
        "pack",
        [hbm] * 6,
        [
            ((ROWS, points), half),
            ((2 * SLOT, points), half),
            ((ROWS, LEAVES), half),
            ((ROWS, 2 * SLOT), half),
            given_shape,
            given_shape,
        ],
        [
            pltpu.SMEM((8,), jnp.int32),
            pltpu.VMEM((3, points), full),
            pltpu.VMEM((fields, points), half),
            pltpu.VMEM((LEAVES, SLOT), half),
            pltpu.VMEM((SLOT, SLOT), half),
            pltpu.VMEM((3 * SLOT, 16), half),
            pltpu.SemaphoreType.DMA((6,)),
        ],
        leaf_count,
        positions,
        density,
        jnp.asarray(shift, half),
        jnp.asarray(heavy_table(), half),
        jnp.asarray(power_table(), half),
    )
    from_2 = swapped(totals, "space", lambda i: i ^ 2)
    from_1 = swapped(given[0], "space", lambda i: i ^ 1)
    from_3 = swapped(given[1], "space", lambda i: i ^ 3)
    near, source, target, scale, column, columns, far, spread = call(
        functools.partial(own_kernel, depth),
        "near_own",
        [hbm] * 2 + [vmem] + [hbm] * 3,
        [
            ((ROWS, EARLY * points // 4), full),
            ((points, FEATURES), half),
            ((FEATURES, points), half),
            ((1, points), full),
            ((ROWS, 128), full),
            ((ACROSS * depth * SLOT, SLOT), half),
            ((len(STEPS) * LEAVES, LEAVES), half),
            ((SLOT, LEAVES), half),
        ],
        [
            pltpu.VMEM((3, SLOT, SLOT), full),
            pltpu.SMEM((8,), jnp.int32),
            pltpu.SMEM((fields,), full),
            pltpu.SemaphoreType.DMA((5,)),
        ],
        leaf_count,
        sigma_weights,
        own,
        jnp.asarray(far_table(), half),
        jnp.asarray(shift.T.copy(), half),
        jnp.asarray(box_nodes()),
    )
    left, right, faces_even, rows = call(
        row_kernel,
        "row",
        [vmem] * 7,
        [side_shape, side_shape, even_shape, rows_shape],
        [],
        own,
        moments,
        totals,
        from_1,
        from_2,
        from_3,
        far,
    )
    faces_even = swapped(faces_even, "space", lambda i: i ^ ACROSS)
    near, faces_odd, same = call(
        middle_kernel,
        "near_middle",
        [vmem] * 8,
        [near_shape, faces_shape, sums_shape],
        [side_scratch],
        own,
        left,
        right,
        moments,
        far,
        near,
        source,
        target,
    )
    faces_odd = swapped_odd(faces_odd)
    near, = call(
        side_kernel,
        "near_side",
        [vmem] * 4,
        [near_shape],
        [side_scratch],
        left,
        right,
        near,
        target,
    )
    if depth == 4:
        both, = call(both_kernel, "row_pairs", [vmem] * 3, [both_shape], [], rows, faces_even, near)
        held = [rows, swapped(both, "space", lambda i: i ^ (2 * ACROSS))]
    else:
        groups = [[z * ACROSS + x for z in range(depth)] for x in range(ACROSS)]
        held = [lax.all_gather(rows, "space", axis_index_groups=groups)]
    near, = call(
        even_kernel,
        "near_even",
        [vmem] * 4,
        [near_shape],
        [rows_scratch, side_scratch],
        near,
        target,
        right,
        faces_even,
    )
    near, = call(
        functools.partial(odd_kernel, depth),
        "near_odd",
        [vmem] * 3,
        [near_shape],
        [rows_scratch],
        near,
        target,
        faces_odd,
    )
    potential, sums = call(
        functools.partial(last_kernel, depth),
        "evaluate",
        [vmem] * (9 + len(held)),
        [((fields, points), full), ((1, points + 128), full)],
        [],
        near,
        faces_even,
        faces_odd,
        basis,
        scale,
        column,
        columns,
        spread,
        same,
        *held,
    )
    if lax.axis_size("sig") == 2:
        other = swapped(sums, "sig", lambda i: i ^ 1)
    else:
        other = lax.psum(sums, "sig") - sums
    mean, = call(mean_kernel, "mean", [vmem] * 2, [((1, points), full)], [], sums, other)
    return potential, mean.reshape(points)


def solution(mesh):
    in_specs = (P(None, "space"), P("sig", "space"), P("space"), P("sig"))
    out_specs = (P("sig", "space"), P("space"))
    return jax.shard_map(per_device, mesh=mesh, in_specs=in_specs, out_specs=out_specs, check_vma=False)
```

```python
import functools
import math

import jax
import jax.numpy as jnp
import numpy as np
from jax import lax
from jax.experimental import pallas as pl
from jax.experimental.pallas import tpu as pltpu
from jax.sharding import PartitionSpec as P

ORDER = 5
SOFTENING = 0.1
ACROSS = 4
SLOT = 64
ROWS = 24
LEAVES = 8 * SLOT
MEGA = 1024 * 1024
FEATURES = 48
EARLY = 2


def exponent_table(order_max):
    entries_list = []
    for degree in range(order_max + 1):
        for first_power in range(degree, -1, -1):
            for second_power in range(degree - first_power, -1, -1):
                entries_list.append((first_power, second_power, degree - first_power - second_power))
    return entries_list


def node_table(count_nodes, offset_value):
    counter = np.arange(1, count_nodes + 1, dtype=np.float32)[:, None]
    stride_set = np.array([0.7548776662466927, 0.5698402909980532, 0.4142135623730951], dtype=np.float32)[None, :]
    unit_points = np.mod(counter * stride_set + np.float32(offset_value), np.float32(1.0))
    return (np.float32(2.0) * unit_points - np.float32(1.0)).astype(np.float32)


EXPONENTS = exponent_table(ORDER)
COEFFS = len(EXPONENTS)
CHECK = node_table(COEFFS, 0.5).astype(np.float64)
EQUIV = node_table(COEFFS, 0.0).astype(np.float64)
HEAVY = [EXPONENTS.index(e) for e in ((0, 0, 0), (2, 0, 0), (0, 2, 0), (0, 0, 2), (4, 0, 0), (0, 4, 0), (0, 0, 4), (2, 0, 2))]
STEPS = [(sx, sz) for sz in (-1, 0, 1) for sx in (-1, 0, 1) if sx != 0 or sz != 0]


def bits(octant):
    return octant % 2, octant // 2 % 2, octant // 4


def leaf_slot(octant):
    bit_x, bit_y, bit_z = bits(octant)
    return (bit_x + 2 * bit_z) * 2 + bit_y


@functools.lru_cache(None)
def far_table():
    shape = (len(STEPS), 8, SLOT, 8, SLOT)
    table = np.zeros(shape)
    gap_nodes = 0.5 * (CHECK[None, :, :] - EQUIV[:, None, :])
    for index, (step_x, step_z) in enumerate(STEPS):
        for source in range(8):
            for target in range(8):
                s, t = bits(source), bits(target)
                gap = np.array([2 * step_x + s[0] - t[0], s[1] - t[1], 2 * step_z + s[2] - t[2]], np.float64)
                if max(abs(gap[0]), abs(gap[2])) >= 2:
                    shifted = gap_nodes - gap
                    value = 1.0 / np.sqrt(np.sum(shifted * shifted, -1) + SOFTENING * SOFTENING) / COEFFS
                    table[index, source, :COEFFS, target, :COEFFS] = value
    return table.reshape(len(STEPS) * LEAVES, LEAVES)


@functools.lru_cache(None)
def shift_table():
    table = np.zeros((8, SLOT, SLOT))
    for leaf in range(8):
        offset = [bit - 0.5 for bit in bits(leaf)]
        for k, target in enumerate(EXPONENTS):
            for i, source in enumerate(EXPONENTS):
                if all(b <= a for a, b in zip(target, source)):
                    value = 1.0
                    for a, b, h in zip(target, source, offset):
                        value *= math.comb(a, b) * 0.5**b * h ** (a - b)
                    table[leaf, i, k] = value
    return table.reshape(8 * SLOT, SLOT)


@functools.lru_cache(None)
def box_nodes():
    gaps = np.zeros((3, SLOT, SLOT))
    gaps[:, :COEFFS, :COEFFS] = np.moveaxis(CHECK[None, :, :] - EQUIV[:, None, :], -1, 0)
    gaps[:, COEFFS:] = gaps[:, HEAVY]
    gaps[1] = gaps[1] ** 2 + SOFTENING * SOFTENING
    return gaps.astype(np.float32)


def dot(left, right):
    return jnp.dot(left, right, preferred_element_type=jnp.float32)


def dot_nt(left, right):
    return lax.dot_general(left, right, (((1,), (1,)), ((), ())), preferred_element_type=jnp.float32)


def low_bits(value):
    return value.astype(jnp.bfloat16)


def heavy_table():
    table = np.zeros((SLOT, SLOT), np.float32)
    table[HEAVY, np.arange(COEFFS, SLOT)] = 1.0
    return table


def power_table():
    table = np.zeros((3, SLOT, 16), np.float32)
    for axis in range(3):
        for k, powers in enumerate(EXPONENTS):
            table[axis, k, powers[axis]] = 1.0
            table[axis, k, 8 + powers[axis]] = 1.0
    return table.reshape(3 * SLOT, 16)


def high_low(value):
    high = low_bits(value)
    return high, low_bits(value - high.astype(jnp.float32))


def by_row(values, shape):
    row = lax.broadcasted_iota(jnp.int32, shape, 0)
    result = jnp.zeros(shape, jnp.float32)
    for index, value in enumerate(values):
        result = jnp.where(row == index, value, result)
    return result


def box_place():
    label = lax.axis_index("space")
    return lax.rem(label, ACROSS), lax.div(label, ACROSS)


def lanes(start, size):
    return pl.ds(start if isinstance(start, int) else pl.multiple_of(start, 128), size)


def fetch(pairs, sems):
    copies = [pltpu.make_async_copy(src, dst, sems.at[i]) for i, (src, dst) in enumerate(pairs)]
    for copy in copies:
        copy.start()
    return copies


def pack_kernel(count_in, positions_in, density_in, shift_in, heavy_in, powers_in, own, basis, moments, totals, *rest):
    payloads, (count, positions, density, shift, heavy, powers, sems) = rest[:2], rest[2:]
    copies = fetch(
        [
            (count_in, count),
            (positions_in, positions),
            (density_in, density),
            (shift_in, shift),
            (heavy_in, heavy),
            (powers_in, powers),
        ],
        sems,
    )
    fields, points = density.shape
    pts = points // 8
    box_x, box_z = box_place()
    for copy in copies:
        copy.wait()
    local = []
    for leaf in range(8):
        bit_x, bit_y, bit_z = bits(leaf)
        centre = by_row(
            [2.0 * box_x.astype(jnp.float32) + (bit_x + 0.5), bit_y + 0.5, 2.0 * box_z.astype(jnp.float32) + (bit_z + 0.5)],
            (3, 1),
        )
        here = slice(leaf * pts, (leaf + 1) * pts)
        offset = positions[:, here] - centre
        local.append(offset)
        high = low_bits(offset).astype(jnp.float32)
        middle = low_bits(offset - high).astype(jnp.float32)
        raw = density[:, here].astype(jnp.float32)
        mass = jnp.where(lax.broadcasted_iota(jnp.int32, raw.shape, 1) < count[leaf], raw, 0.0)
        spare = jnp.zeros((ROWS - fields - 6, pts), jnp.float32)
        own[:, here] = low_bits(jnp.concatenate([mass, high, middle, spare], axis=0))

    scaled = 2.0 * jnp.concatenate(local, axis=1)
    row = lax.broadcasted_iota(jnp.int32, (8, points), 0)
    value = None
    for axis in range(3):
        base = jnp.broadcast_to(scaled[axis : axis + 1], (8, points))
        power = jnp.ones((8, points), jnp.float32)
        for degree in range(1, ORDER + 1):
            power = power * jnp.where(row >= degree, base, 1.0)
        pieces = jnp.concatenate(high_low(power), axis=0)
        picked = dot(powers[axis * SLOT : (axis + 1) * SLOT, :], pieces)
        value = picked if value is None else value * picked
    high, low = high_low(value)
    basis[0:SLOT, :] = high
    basis[SLOT:, :] = low
    parts = []
    for leaf in range(8):
        here = slice(leaf * pts, (leaf + 1) * pts)
        parts.append(dot_nt(own[:, here], high[:, here]))
    moment, rest = high_low(jnp.concatenate(parts, axis=1))
    moments[...] = moment
    total = dot(moment, shift[...]) + dot(rest, shift[...])
    total_high, total_low = high_low(total)
    total = low_bits(total_high.astype(jnp.float32) + dot(total_low, heavy[...]))
    total = jnp.concatenate([total, jnp.zeros_like(total)], axis=1)
    totals[...] = total
    for distance, payload in zip((1, 3), payloads):
        bit = jnp.where((box_x ^ distance) > box_x, 1, 0)
        for place in range(4):
            payload[:, lanes(place * pts, pts)] = own[:, lanes((bit + 2 * place) * pts, pts)]
        payload[:, lanes(4 * pts, LEAVES)] = moment
        payload[:, lanes(4 * pts + LEAVES, 2 * SLOT)] = total


def features(held, start, size, centre, target):
    value = held[16:ROWS, lanes(start, size)].astype(jnp.float32)
    x = value[1:4] + value[4:7] + by_row(centre, (3, 1))
    norm = jnp.sum(x * x, axis=0, keepdims=True)
    if target:
        norm = norm + SOFTENING * SOFTENING
    parts, norms = [], []
    for source, out in ((x, parts), (norm, norms)):
        left = source
        for _ in range(3):
            high = low_bits(left).astype(jnp.float32)
            out.append(high)
            left = left - high
    one = jnp.ones_like(norm)
    zero = jnp.zeros_like(norm)
    blank = jnp.zeros((3, norm.shape[1]), jnp.float32)
    blocks = []
    order = (0, 1, 0, 2, 0, 1) if target else (0, 0, 1, 0, 2, 1)
    for index, which in enumerate(order):
        coords = -2.0 * parts[which] if target else parts[which]
        if index < 3:
            pair = [one, norms[index]] if target else [norms[index], one]
        else:
            pair = [zero, zero]
        blocks += [coords, *pair, blank]
    return jnp.concatenate(blocks, axis=0)


def source_features(held, start, size, centre):
    return low_bits(jnp.transpose(features(held, start, size, centre, False)))


def pulled(near, jobs, target, size, first=None):
    width = target.shape[1] // 8
    tiles = []
    for group, source, masses, starts in jobs:
        for piece in range(2):
            here = lanes((2 * group + piece) * width, width)
            for turn, start in enumerate(starts):
                tiles.append((here, source, masses, lanes(start, size), turn == 0, turn + 1 == len(starts)))

    def squares(tile):
        return dot(tile[1][tile[3], :], target[:, tile[0]])

    ahead, kernel, total = squares(tiles[0]), None, None
    for turn in range(len(tiles) + 1):
        square = ahead
        if turn + 1 < len(tiles):
            ahead = squares(tiles[turn + 1])
        if turn > 0:
            here, _, masses, place, opens, closes = tiles[turn - 1]
            if opens:
                total = jnp.zeros((ROWS, width), jnp.float32) if first is None else first[:, here]
            total = total + dot(masses[:, place], kernel)
            if closes:
                near[:, here] = total
        if turn < len(tiles):
            kernel = low_bits(lax.rsqrt(square))


def own_groups(near, first, last, target, source, own):
    pts = source.shape[0] // 8
    starts = [2 * p * pts for p in range(4)]
    pulled(near, [(group, source, own, starts) for group in range(first, last)], target, 2 * pts)


def box_columns(depth, box_x, box_z, nodes):
    blocks = []
    for turn, distance in [(turn, distance) for turn in range(depth) for distance in range(ACROSS)]:
        gap_x = 2 * (box_x - (box_x ^ distance))
        gap_z = 2 * (box_z - ((box_z ^ turn) if depth == 4 else turn))
        across_x = nodes[0] + gap_x.astype(jnp.float32)
        across_z = nodes[2] + gap_z.astype(jnp.float32)
        apart = jnp.maximum(jnp.abs(gap_x), jnp.abs(gap_z)) >= 4
        value = lax.rsqrt(across_x * across_x + across_z * across_z + nodes[1])
        blocks.append(low_bits(value * jnp.where(apart, 1.0 / COEFFS, 0.0)))
    return jnp.concatenate(blocks, axis=0)


def own_kernel(depth, count_in, weights_in, own, *rest):
    tables, outs, (nodes, count, weights, sems) = rest[:3], rest[3:11], rest[11:]
    near, source, target, scale, column, columns, far, spread = outs
    copies = fetch([*zip(tables, (far, spread, nodes)), (count_in, count), (weights_in, weights)], sems)
    points = own.shape[1]
    pts = points // 8
    for leaf in range(8):
        centre = [bit - 0.5 for bit in bits(leaf)]
        source[lanes(leaf * pts, pts), :] = source_features(own, leaf * pts, pts, centre)
        target[:, lanes(leaf_slot(leaf) * pts, pts)] = low_bits(features(own, leaf * pts, pts, centre, True))
    own_groups(near, 0, EARLY, target, source, own)
    for copy in copies:
        copy.wait()
    columns[...] = box_columns(depth, *box_place(), nodes)
    column[...] = by_row([weights[field] for field in range(weights.shape[0])], column.shape)
    lane_index = lax.broadcasted_iota(jnp.int32, (1, pts), 1)
    for leaf in range(8):
        scale[:, leaf * pts : (leaf + 1) * pts] = jnp.where(lane_index < count[leaf], 1.0 / (128.0 * pts), 0.0)


def spread_first(value, node):
    starts = [leaf * SLOT + node for leaf in range(8)]
    return jnp.concatenate([jnp.broadcast_to(value[:, s : s + 1], (ROWS, SLOT)) for s in starts], axis=1)


def decoded(coded):
    value = coded.astype(jnp.float32)
    node = lax.broadcasted_iota(jnp.int32, value.shape, 1) % SLOT
    return jnp.where(node == 0, 0.0, value) + spread_first(value, 0) + spread_first(value, COEFFS)


def faces_of(faces, bit, given, own, left, right, rows=None):
    points = own.shape[1]
    pts = points // 8
    for y in range(2):
        for x in range(4):
            place = lanes((2 * x + y) * pts, pts)
            if x in (0, 3):
                side = left if x == 0 else right
                faces[:, place] = side[:, lanes((y + 2 * bit) * pts, pts)]
            else:
                faces[:, place] = own[:, lanes((x - 1 + 2 * y + 4 * bit) * pts, pts)]
    node = lax.broadcasted_iota(jnp.int32, given.shape, 1) % SLOT
    base = spread_first(given, 0)
    base_high = low_bits(base).astype(jnp.float32)
    coded = jnp.where(node == 0, base_high, jnp.where(node == COEFFS, base - base_high, given - base))
    faces[:, lanes(points, LEAVES)] = low_bits(coded)
    if rows is not None:
        faces[:, lanes(points + LEAVES, rows.shape[1])] = rows


def sums_for(above, left, moments, right, far):
    base = left.shape[1] - LEAVES
    around = jnp.concatenate([left[:, lanes(base, LEAVES)], moments[...], right[:, lanes(base, LEAVES)]], axis=1)
    return dot(around, far[lanes(jnp.where(above == 1, 0, 5 * LEAVES), 3 * LEAVES), :])


def row_kernel(own, moments, totals, from_1, from_2, from_3, far, left, right, faces_even, rows):
    box_x, box_z = box_place()
    for side, step in ((left, -1), (right, 1)):
        side[...] = jnp.zeros(side.shape, side.dtype)
        for distance, held in ((1, from_1), (3, from_3)):

            @pl.when((box_x ^ distance) - box_x == step)
            def _(side=side, held=held):
                side[...] = held[:, lanes(0, side.shape[1])]

    ends = lanes(left.shape[1], 2 * SLOT)
    row = [totals[...], from_1[:, ends], from_2[...], from_3[:, ends]]
    row = jnp.concatenate([box[:, :SLOT] for box in row], axis=1)
    rows[...] = row
    above = 1 - lax.rem(box_z, 2)
    faces_of(faces_even, above, sums_for(above, left, moments, right, far), own, left, right, row)


def side_pulls(near, faces, early, target, scratch):
    pts = early.shape[1] // 8
    jobs = []
    for (step, side), held in zip(faces, scratch):
        for place in range(4):
            centre = (1.5 if step else -1.5, place % 2 - 0.5, place // 2 - 0.5)
            held[lanes(place * pts, pts), :] = source_features(side, place * pts, pts, centre)
        jobs += [(step, held, side, [0, 2 * pts]), (step + 2, held, side, [0, 2 * pts])]
    pulled(near, jobs, target, 2 * pts, early)


def middle_kernel(own, left, right, moments, far, early, source, target, near, faces_odd, same, *sides):
    points = own.shape[1]
    _, box_z = box_place()
    above = lax.rem(box_z, 2)
    faces_of(faces_odd, above, sums_for(above, left, moments, right, far), own, left, right)
    base = left.shape[1] - LEAVES
    beside = jnp.concatenate([left[:, lanes(base, LEAVES)], right[:, lanes(base, LEAVES)]], axis=1)
    same[...] = dot(beside, far[lanes(3 * LEAVES, 2 * LEAVES), :])
    near[:, lanes(0, EARLY * points // 4)] = early[...]
    own_groups(near, EARLY, 4, target, source, own)

    @pl.when(above == 1)
    def _():
        side_pulls(near, [(0, left)], near, target, sides)


def one_side(near, step, side, early, target, held):
    pts = early.shape[1] // 8
    for group in (1 - step, 3 - step):
        here = lanes(2 * group * pts, 2 * pts)
        near[:, here] = early[:, here]
    side_pulls(near, [(step, side)], early, target, [held])


def side_kernel(left, right, early, target, near, held):
    _, box_z = box_place()
    odd = lax.rem(box_z, 2) == 1

    @pl.when(odd)
    def _():
        one_side(near, 1, right, early, target, held)

    @pl.when(jnp.logical_not(odd))
    def _():
        one_side(near, 0, left, early, target, held)


def both_kernel(rows, faces, near, both):
    width = rows.shape[1]
    both[:, lanes(0, width)] = rows[...]
    both[:, lanes(width, width)] = faces[:, lanes(faces.shape[1] - width, width)]


def layer_pulls(near, early, step, inside, target, faces, sides):
    points = early.shape[1]
    pts = points // 8

    @pl.when(inside)
    def _():
        for place in range(8):
            height = jnp.where(step == 1, 1.5, -1.5)
            centre = (place // 2 - 1.5, place % 2 - 0.5, height)
            sides[lanes(place * pts, pts), :] = source_features(faces, place * pts, pts, centre)

        jobs = [(i + 2 * step, sides, faces, [2 * (x + i) * pts for x in range(3)]) for i in range(2)]
        pulled(near, jobs, target, 2 * pts, early)

    @pl.when(jnp.logical_not(inside))
    def _():
        here = lanes(step * (points // 2), points // 2)
        near[:, here] = early[:, here]


def even_kernel(early, target, right, faces, near, sides, held):
    _, box_z = box_place()
    step = 1 - lax.rem(box_z, 2)

    @pl.when(step == 0)
    def _():
        near[...] = early[...]

    @pl.when(step == 1)
    def _():
        one_side(near, 1, right, early, target, held)

    layer_pulls(near, near, step, box_z >= 0, target, faces, sides)


def odd_inside(depth):
    _, box_z = box_place()
    step = lax.rem(box_z, 2)
    return step, (box_z + 2 * step - 1 >= 0) & (box_z + 2 * step - 1 < depth)


def odd_kernel(depth, early, target, faces, near, sides):
    points = early.shape[1]
    step, inside = odd_inside(depth)
    other = lanes((1 - step) * (points // 2), points // 2)
    near[:, other] = early[:, other]
    layer_pulls(near, early, step, inside, target, faces, sides)


def last_kernel(depth, near, faces_even, faces_odd, basis, scale, column, columns, spread, same, *rest):
    held, (potential, sums) = rest[:-2], rest[-2:]
    fields, points = potential.shape
    pts = points // 8
    _, inside = odd_inside(depth)
    if depth == 4:
        rows, distant = held
        width = rows.shape[1]
        near_rows = faces_even[:, lanes(faces_even.shape[1] - width, width)]
        layers = [rows[...], near_rows, distant[:, lanes(0, width)], distant[:, lanes(width, width)]]
    else:
        layers = [held[0][layer] for layer in range(depth)]
    coarse_high, coarse_low = high_low(dot(jnp.concatenate(layers, axis=1), columns[...]))
    value = same[...] + dot(coarse_high, spread[...]) + dot(coarse_low, spread[...])
    value = value + decoded(faces_even[:, lanes(points, LEAVES)])
    value = value + jnp.where(inside, decoded(faces_odd[:, lanes(points, LEAVES)]), 0.0)
    local_high, local_low = high_low(value)
    weight = column[0:fields, 0:1]
    for leaf in range(8):
        here = slice(leaf * pts, (leaf + 1) * pts)
        slot = slice(leaf * SLOT, (leaf + 1) * SLOT)
        doubled = jnp.concatenate([local_high[:, slot], local_high[:, slot]], axis=1)
        far_part = dot(doubled, basis[:, here]) + dot(local_low[:, slot], basis[0:SLOT, here])
        total = near[0:fields, lanes(leaf_slot(leaf) * pts, pts)] + far_part[:fields]
        total = total * scale[:, here]
        potential[:, here] = total
        sums[:, here] = jnp.sum(total * weight, axis=0, keepdims=True)
    sums[:, points:] = jnp.broadcast_to(jnp.sum(weight), (1, sums.shape[1] - points))


def mean_kernel(mine, other, mean):
    points = mean.shape[1]
    total = mine[...] + other[...]
    mean[...] = total[:, :points] / total[:, points : points + 1]


def swapped(block, axis, partner):
    size = lax.axis_size(axis)
    return lax.ppermute(block, axis, [(partner(i), i) for i in range(size)])


def swapped_odd(block):
    boxes, cores = lax.axis_size("space"), lax.axis_size("sig")
    pairs = []
    for box in range(boxes):
        other = box + ACROSS if box // ACROSS % 2 else box - ACROSS
        for core in range(cores):
            source = other * cores + core if 0 <= other < boxes else box * cores + (core ^ 1)
            pairs.append((source, box * cores + core))
    return lax.ppermute(block, ("space", "sig"), pairs)


def per_device(positions, density, leaf_count, sigma_weights):
    fields, points = density.shape
    pts = points // 8
    depth = lax.axis_size("space") // ACROSS
    vmem, hbm = pl.BlockSpec(memory_space=pltpu.VMEM), pl.BlockSpec(memory_space=pltpu.HBM)

    def call(kernel, name, in_specs, outs, scratch, *args):
        return pl.pallas_call(
            kernel,
            in_specs=in_specs,
            out_specs=[vmem] * len(outs),
            out_shape=[jax.ShapeDtypeStruct(shape, dtype) for shape, dtype in outs],
            scratch_shapes=scratch,
            compiler_params=pltpu.CompilerParams(vmem_limit_bytes=24 * MEGA),
            name=name,
        )(*(pltpu.with_memory_space_constraint(a, pltpu.HBM) if s is hbm else a for s, a in zip(in_specs, args)))

    half, full = jnp.bfloat16, jnp.float32
    shift = shift_table()
    side_shape = ((ROWS, 4 * pts + LEAVES), half)
    given_shape = ((ROWS, 4 * pts + LEAVES + 2 * SLOT), half)
    faces_shape = ((ROWS, points + LEAVES), half)
    even_shape = ((ROWS, points + LEAVES + SLOT * ACROSS), half)
    rows_shape = ((ROWS, SLOT * ACROSS), half)
    both_shape = ((ROWS, 2 * SLOT * ACROSS), half)
    near_shape, sums_shape = ((ROWS, points), full), ((ROWS, LEAVES), full)
    side_scratch = pltpu.VMEM((4 * pts, FEATURES), half)
    rows_scratch = pltpu.VMEM((8 * pts, FEATURES), half)
    own, basis, moments, totals, *given = call(
        pack_kernel,
        "pack",
        [hbm] * 6,
        [
            ((ROWS, points), half),
            ((2 * SLOT, points), half),
            ((ROWS, LEAVES), half),
            ((ROWS, 2 * SLOT), half),
            given_shape,
            given_shape,
        ],
        [
            pltpu.SMEM((8,), jnp.int32),
            pltpu.VMEM((3, points), full),
            pltpu.VMEM((fields, points), half),
            pltpu.VMEM((LEAVES, SLOT), half),
            pltpu.VMEM((SLOT, SLOT), half),
            pltpu.VMEM((3 * SLOT, 16), half),
            pltpu.SemaphoreType.DMA((6,)),
        ],
        leaf_count,
        positions,
        density,
        jnp.asarray(shift, half),
        jnp.asarray(heavy_table(), half),
        jnp.asarray(power_table(), half),
    )
    from_2 = swapped(totals, "space", lambda i: i ^ 2)
    from_1 = swapped(given[0], "space", lambda i: i ^ 1)
    from_3 = swapped(given[1], "space", lambda i: i ^ 3)
    near, source, target, scale, column, columns, far, spread = call(
        functools.partial(own_kernel, depth),
        "near_own",
        [hbm] * 2 + [vmem] + [hbm] * 3,
        [
            ((ROWS, EARLY * points // 4), full),
            ((points, FEATURES), half),
            ((FEATURES, points), half),
            ((1, points), full),
            ((ROWS, 128), full),
            ((ACROSS * depth * SLOT, SLOT), half),
            ((len(STEPS) * LEAVES, LEAVES), half),
            ((SLOT, LEAVES), half),
        ],
        [
            pltpu.VMEM((3, SLOT, SLOT), full),
            pltpu.SMEM((8,), jnp.int32),
            pltpu.SMEM((fields,), full),
            pltpu.SemaphoreType.DMA((5,)),
        ],
        leaf_count,
        sigma_weights,
        own,
        jnp.asarray(far_table(), half),
        jnp.asarray(shift.T.copy(), half),
        jnp.asarray(box_nodes()),
    )
    left, right, faces_even, rows = call(
        row_kernel,
        "row",
        [vmem] * 7,
        [side_shape, side_shape, even_shape, rows_shape],
        [],
        own,
        moments,
        totals,
        from_1,
        from_2,
        from_3,
        far,
    )
    faces_even = swapped(faces_even, "space", lambda i: i ^ ACROSS)
    near, faces_odd, same = call(
        middle_kernel,
        "near_middle",
        [vmem] * 8,
        [near_shape, faces_shape, sums_shape],
        [side_scratch],
        own,
        left,
        right,
        moments,
        far,
        near,
        source,
        target,
    )
    faces_odd = swapped_odd(faces_odd)
    near, = call(
        side_kernel,
        "near_side",
        [vmem] * 4,
        [near_shape],
        [side_scratch],
        left,
        right,
        near,
        target,
    )
    if depth == 4:
        both, = call(both_kernel, "row_pairs", [vmem] * 3, [both_shape], [], rows, faces_even, near)
        held = [rows, swapped(both, "space", lambda i: i ^ (2 * ACROSS))]
    else:
        groups = [[z * ACROSS + x for z in range(depth)] for x in range(ACROSS)]
        held = [lax.all_gather(rows, "space", axis_index_groups=groups)]
    near, = call(
        even_kernel,
        "near_even",
        [vmem] * 4,
        [near_shape],
        [rows_scratch, side_scratch],
        near,
        target,
        right,
        faces_even,
    )
    near, = call(
        functools.partial(odd_kernel, depth),
        "near_odd",
        [vmem] * 3,
        [near_shape],
        [rows_scratch],
        near,
        target,
        faces_odd,
    )
    potential, sums = call(
        functools.partial(last_kernel, depth),
        "evaluate",
        [vmem] * (9 + len(held)),
        [((fields, points), full), ((1, points + 128), full)],
        [],
        near,
        faces_even,
        faces_odd,
        basis,
        scale,
        column,
        columns,
        spread,
        same,
        *held,
    )
    if lax.axis_size("sig") == 2:
        other = swapped(sums, "sig", lambda i: i ^ 1)
    else:
        other = lax.psum(sums, "sig") - sums
    mean, = call(mean_kernel, "mean", [vmem] * 2, [((1, points), full)], [], sums, other)
    return potential, mean.reshape(points)


def solution(mesh):
    in_specs = (P(None, "space"), P("sig", "space"), P("space"), P("sig"))
    out_specs = (P("sig", "space"), P("space"))
    return jax.shard_map(per_device, mesh=mesh, in_specs=in_specs, out_specs=out_specs, check_vma=False)
```

```python
import functools
import math

import jax
import jax.numpy as jnp
import numpy as np
from jax import lax
from jax.experimental import pallas as pl
from jax.experimental.pallas import tpu as pltpu
from jax.sharding import PartitionSpec as P

ORDER = 5
SOFTENING = 0.1
ACROSS = 4
SLOT = 64
ROWS = 24
LEAVES = 8 * SLOT
MEGA = 1024 * 1024
FEATURES = 48
EARLY = 3


def exponent_table(order_max):
    entries_list = []
    for degree in range(order_max + 1):
        for first_power in range(degree, -1, -1):
            for second_power in range(degree - first_power, -1, -1):
                entries_list.append((first_power, second_power, degree - first_power - second_power))
    return entries_list


def node_table(count_nodes, offset_value):
    counter = np.arange(1, count_nodes + 1, dtype=np.float32)[:, None]
    stride_set = np.array([0.7548776662466927, 0.5698402909980532, 0.4142135623730951], dtype=np.float32)[None, :]
    unit_points = np.mod(counter * stride_set + np.float32(offset_value), np.float32(1.0))
    return (np.float32(2.0) * unit_points - np.float32(1.0)).astype(np.float32)


EXPONENTS = exponent_table(ORDER)
COEFFS = len(EXPONENTS)
CHECK = node_table(COEFFS, 0.5).astype(np.float64)
EQUIV = node_table(COEFFS, 0.0).astype(np.float64)
HEAVY = [EXPONENTS.index(e) for e in ((0, 0, 0), (2, 0, 0), (0, 2, 0), (0, 0, 2), (4, 0, 0), (0, 4, 0), (0, 0, 4), (2, 0, 2))]
STEPS = [(sx, sz) for sz in (-1, 0, 1) for sx in (-1, 0, 1) if sx != 0 or sz != 0]


def bits(octant):
    return octant % 2, octant // 2 % 2, octant // 4


def leaf_slot(octant):
    bit_x, bit_y, bit_z = bits(octant)
    return (bit_x + 2 * bit_z) * 2 + bit_y


@functools.lru_cache(None)
def far_table():
    shape = (len(STEPS), 8, SLOT, 8, SLOT)
    table = np.zeros(shape)
    gap_nodes = 0.5 * (CHECK[None, :, :] - EQUIV[:, None, :])
    for index, (step_x, step_z) in enumerate(STEPS):
        for source in range(8):
            for target in range(8):
                s, t = bits(source), bits(target)
                gap = np.array([2 * step_x + s[0] - t[0], s[1] - t[1], 2 * step_z + s[2] - t[2]], np.float64)
                if max(abs(gap[0]), abs(gap[2])) >= 2:
                    shifted = gap_nodes - gap
                    value = 1.0 / np.sqrt(np.sum(shifted * shifted, -1) + SOFTENING * SOFTENING) / COEFFS
                    table[index, source, :COEFFS, target, :COEFFS] = value
    return table.reshape(len(STEPS) * LEAVES, LEAVES)


@functools.lru_cache(None)
def shift_table():
    table = np.zeros((8, SLOT, SLOT))
    for leaf in range(8):
        offset = [bit - 0.5 for bit in bits(leaf)]
        for k, target in enumerate(EXPONENTS):
            for i, source in enumerate(EXPONENTS):
                if all(b <= a for a, b in zip(target, source)):
                    value = 1.0
                    for a, b, h in zip(target, source, offset):
                        value *= math.comb(a, b) * 0.5**b * h ** (a - b)
                    table[leaf, i, k] = value
    return table.reshape(8 * SLOT, SLOT)


@functools.lru_cache(None)
def box_nodes():
    gaps = np.zeros((3, SLOT, SLOT))
    gaps[:, :COEFFS, :COEFFS] = np.moveaxis(CHECK[None, :, :] - EQUIV[:, None, :], -1, 0)
    gaps[:, COEFFS:] = gaps[:, HEAVY]
    gaps[1] = gaps[1] ** 2 + SOFTENING * SOFTENING
    return gaps.astype(np.float32)


def dot(left, right):
    return jnp.dot(left, right, preferred_element_type=jnp.float32)


def dot_nt(left, right):
    return lax.dot_general(left, right, (((1,), (1,)), ((), ())), preferred_element_type=jnp.float32)


def low_bits(value):
    return value.astype(jnp.bfloat16)


def heavy_table():
    table = np.zeros((SLOT, SLOT), np.float32)
    table[HEAVY, np.arange(COEFFS, SLOT)] = 1.0
    return table


def power_table():
    table = np.zeros((3, SLOT, 16), np.float32)
    for axis in range(3):
        for k, powers in enumerate(EXPONENTS):
            table[axis, k, powers[axis]] = 1.0
            table[axis, k, 8 + powers[axis]] = 1.0
    return table.reshape(3 * SLOT, 16)


def high_low(value):
    high = low_bits(value)
    return high, low_bits(value - high.astype(jnp.float32))


def by_row(values, shape):
    row = lax.broadcasted_iota(jnp.int32, shape, 0)
    result = jnp.zeros(shape, jnp.float32)
    for index, value in enumerate(values):
        result = jnp.where(row == index, value, result)
    return result


def box_place():
    label = lax.axis_index("space")
    return lax.rem(label, ACROSS), lax.div(label, ACROSS)


def lanes(start, size):
    return pl.ds(start if isinstance(start, int) else pl.multiple_of(start, 128), size)


def fetch(pairs, sems):
    copies = [pltpu.make_async_copy(src, dst, sems.at[i]) for i, (src, dst) in enumerate(pairs)]
    for copy in copies:
        copy.start()
    return copies


def pack_kernel(count_in, positions_in, density_in, shift_in, heavy_in, powers_in, own, basis, moments, totals, *rest):
    payloads, (count, positions, density, shift, heavy, powers, sems) = rest[:2], rest[2:]
    copies = fetch(
        [
            (count_in, count),
            (positions_in, positions),
            (density_in, density),
            (shift_in, shift),
            (heavy_in, heavy),
            (powers_in, powers),
        ],
        sems,
    )
    fields, points = density.shape
    pts = points // 8
    box_x, box_z = box_place()
    for copy in copies:
        copy.wait()
    local = []
    for leaf in range(8):
        bit_x, bit_y, bit_z = bits(leaf)
        centre = by_row(
            [2.0 * box_x.astype(jnp.float32) + (bit_x + 0.5), bit_y + 0.5, 2.0 * box_z.astype(jnp.float32) + (bit_z + 0.5)],
            (3, 1),
        )
        here = slice(leaf * pts, (leaf + 1) * pts)
        offset = positions[:, here] - centre
        local.append(offset)
        high = low_bits(offset).astype(jnp.float32)
        middle = low_bits(offset - high).astype(jnp.float32)
        raw = density[:, here].astype(jnp.float32)
        mass = jnp.where(lax.broadcasted_iota(jnp.int32, raw.shape, 1) < count[leaf], raw, 0.0)
        spare = jnp.zeros((ROWS - fields - 6, pts), jnp.float32)
        own[:, here] = low_bits(jnp.concatenate([mass, high, middle, spare], axis=0))

    scaled = 2.0 * jnp.concatenate(local, axis=1)
    row = lax.broadcasted_iota(jnp.int32, (8, points), 0)
    value = None
    for axis in range(3):
        base = jnp.broadcast_to(scaled[axis : axis + 1], (8, points))
        power = jnp.ones((8, points), jnp.float32)
        for degree in range(1, ORDER + 1):
            power = power * jnp.where(row >= degree, base, 1.0)
        pieces = jnp.concatenate(high_low(power), axis=0)
        picked = dot(powers[axis * SLOT : (axis + 1) * SLOT, :], pieces)
        value = picked if value is None else value * picked
    high, low = high_low(value)
    basis[0:SLOT, :] = high
    basis[SLOT:, :] = low
    parts = []
    for leaf in range(8):
        here = slice(leaf * pts, (leaf + 1) * pts)
        parts.append(dot_nt(own[:, here], high[:, here]))
    moment, rest = high_low(jnp.concatenate(parts, axis=1))
    moments[...] = moment
    total = dot(moment, shift[...]) + dot(rest, shift[...])
    total_high, total_low = high_low(total)
    total = low_bits(total_high.astype(jnp.float32) + dot(total_low, heavy[...]))
    total = jnp.concatenate([total, jnp.zeros_like(total)], axis=1)
    totals[...] = total
    for distance, payload in zip((1, 3), payloads):
        bit = jnp.where((box_x ^ distance) > box_x, 1, 0)
        for place in range(4):
            payload[:, lanes(place * pts, pts)] = own[:, lanes((bit + 2 * place) * pts, pts)]
        payload[:, lanes(4 * pts, LEAVES)] = moment
        payload[:, lanes(4 * pts + LEAVES, 2 * SLOT)] = total


def features(held, start, size, centre, target):
    value = held[16:ROWS, lanes(start, size)].astype(jnp.float32)
    x = value[1:4] + value[4:7] + by_row(centre, (3, 1))
    norm = jnp.sum(x * x, axis=0, keepdims=True)
    if target:
        norm = norm + SOFTENING * SOFTENING
    parts, norms = [], []
    for source, out in ((x, parts), (norm, norms)):
        left = source
        for _ in range(3):
            high = low_bits(left).astype(jnp.float32)
            out.append(high)
            left = left - high
    one = jnp.ones_like(norm)
    zero = jnp.zeros_like(norm)
    blank = jnp.zeros((3, norm.shape[1]), jnp.float32)
    blocks = []
    order = (0, 1, 0, 2, 0, 1) if target else (0, 0, 1, 0, 2, 1)
    for index, which in enumerate(order):
        coords = -2.0 * parts[which] if target else parts[which]
        if index < 3:
            pair = [one, norms[index]] if target else [norms[index], one]
        else:
            pair = [zero, zero]
        blocks += [coords, *pair, blank]
    return jnp.concatenate(blocks, axis=0)


def source_features(held, start, size, centre):
    return low_bits(jnp.transpose(features(held, start, size, centre, False)))


def pulled(near, jobs, target, size, first=None):
    width = target.shape[1] // 8
    tiles = []
    for group, source, masses, starts in jobs:
        for piece in range(2):
            here = lanes((2 * group + piece) * width, width)
            parts = [start + step for start in starts for step in (0, size // 2)]
            for turn, start in enumerate(parts):
                tiles.append((here, source, masses, lanes(start, size // 2), turn == 0, turn + 1 == len(parts)))

    def squares(tile):
        return dot(tile[1][tile[3], :], target[:, tile[0]])

    ahead, kernel, total = squares(tiles[0]), None, None
    for turn in range(len(tiles) + 1):
        square = ahead
        if turn + 1 < len(tiles):
            ahead = squares(tiles[turn + 1])
        if turn > 0:
            here, _, masses, place, opens, closes = tiles[turn - 1]
            if opens:
                total = jnp.zeros((ROWS, width), jnp.float32) if first is None else first[:, here]
            total = total + dot(masses[:, place], kernel)
            if closes:
                near[:, here] = total
        if turn < len(tiles):
            kernel = low_bits(lax.rsqrt(square))


def own_groups(near, first, last, target, source, own):
    pts = source.shape[0] // 8
    starts = [2 * p * pts for p in range(4)]
    pulled(near, [(group, source, own, starts) for group in range(first, last)], target, 2 * pts)


def box_columns(depth, box_x, box_z, nodes):
    blocks = []
    for turn, distance in [(turn, distance) for turn in range(depth) for distance in range(ACROSS)]:
        gap_x = 2 * (box_x - (box_x ^ distance))
        gap_z = 2 * (box_z - ((box_z ^ turn) if depth == 4 else turn))
        across_x = nodes[0] + gap_x.astype(jnp.float32)
        across_z = nodes[2] + gap_z.astype(jnp.float32)
        apart = jnp.maximum(jnp.abs(gap_x), jnp.abs(gap_z)) >= 4
        value = lax.rsqrt(across_x * across_x + across_z * across_z + nodes[1])
        blocks.append(low_bits(value * jnp.where(apart, 1.0 / COEFFS, 0.0)))
    return jnp.concatenate(blocks, axis=0)


def own_kernel(depth, count_in, weights_in, own, *rest):
    tables, outs, (nodes, count, weights, sems) = rest[:3], rest[3:11], rest[11:]
    near, source, target, scale, column, columns, far, spread = outs
    copies = fetch([*zip(tables, (far, spread, nodes)), (count_in, count), (weights_in, weights)], sems)
    points = own.shape[1]
    pts = points // 8
    for leaf in range(8):
        centre = [bit - 0.5 for bit in bits(leaf)]
        source[lanes(leaf * pts, pts), :] = source_features(own, leaf * pts, pts, centre)
        target[:, lanes(leaf_slot(leaf) * pts, pts)] = low_bits(features(own, leaf * pts, pts, centre, True))
    own_groups(near, 0, EARLY, target, source, own)
    for copy in copies:
        copy.wait()
    columns[...] = box_columns(depth, *box_place(), nodes)
    column[...] = by_row([weights[field] for field in range(weights.shape[0])], column.shape)
    lane_index = lax.broadcasted_iota(jnp.int32, (1, pts), 1)
    for leaf in range(8):
        scale[:, leaf * pts : (leaf + 1) * pts] = jnp.where(lane_index < count[leaf], 1.0 / (128.0 * pts), 0.0)


def spread_first(value, node):
    starts = [leaf * SLOT + node for leaf in range(8)]
    return jnp.concatenate([jnp.broadcast_to(value[:, s : s + 1], (ROWS, SLOT)) for s in starts], axis=1)


def decoded(coded):
    value = coded.astype(jnp.float32)
    node = lax.broadcasted_iota(jnp.int32, value.shape, 1) % SLOT
    return jnp.where(node == 0, 0.0, value) + spread_first(value, 0) + spread_first(value, COEFFS)


def faces_of(faces, bit, given, own, left, right, rows=None):
    points = own.shape[1]
    pts = points // 8
    for y in range(2):
        for x in range(4):
            place = lanes((2 * x + y) * pts, pts)
            if x in (0, 3):
                side = left if x == 0 else right
                faces[:, place] = side[:, lanes((y + 2 * bit) * pts, pts)]
            else:
                faces[:, place] = own[:, lanes((x - 1 + 2 * y + 4 * bit) * pts, pts)]
    node = lax.broadcasted_iota(jnp.int32, given.shape, 1) % SLOT
    base = spread_first(given, 0)
    base_high = low_bits(base).astype(jnp.float32)
    coded = jnp.where(node == 0, base_high, jnp.where(node == COEFFS, base - base_high, given - base))
    faces[:, lanes(points, LEAVES)] = low_bits(coded)
    if rows is not None:
        faces[:, lanes(points + LEAVES, rows.shape[1])] = rows


def sums_for(above, left, moments, right, far):
    base = left.shape[1] - LEAVES
    around = jnp.concatenate([left[:, lanes(base, LEAVES)], moments[...], right[:, lanes(base, LEAVES)]], axis=1)
    return dot(around, far[lanes(jnp.where(above == 1, 0, 5 * LEAVES), 3 * LEAVES), :])


def row_kernel(own, moments, totals, from_1, from_2, from_3, far, left, right, faces_even, rows):
    box_x, box_z = box_place()
    for side, step in ((left, -1), (right, 1)):
        side[...] = jnp.zeros(side.shape, side.dtype)
        for distance, held in ((1, from_1), (3, from_3)):

            @pl.when((box_x ^ distance) - box_x == step)
            def _(side=side, held=held):
                side[...] = held[:, lanes(0, side.shape[1])]

    ends = lanes(left.shape[1], 2 * SLOT)
    row = [totals[...], from_1[:, ends], from_2[...], from_3[:, ends]]
    row = jnp.concatenate([box[:, :SLOT] for box in row], axis=1)
    rows[...] = row
    above = 1 - lax.rem(box_z, 2)
    faces_of(faces_even, above, sums_for(above, left, moments, right, far), own, left, right, row)


def side_pulls(near, faces, early, target, scratch):
    pts = early.shape[1] // 8
    jobs = []
    for (step, side), held in zip(faces, scratch):
        for place in range(4):
            centre = (1.5 if step else -1.5, place % 2 - 0.5, place // 2 - 0.5)
            held[lanes(place * pts, pts), :] = source_features(side, place * pts, pts, centre)
        jobs += [(step, held, side, [0, 2 * pts]), (step + 2, held, side, [0, 2 * pts])]
    pulled(near, jobs, target, 2 * pts, early)


def middle_kernel(own, left, right, moments, far, early, source, target, near, faces_odd, same, *sides):
    points = own.shape[1]
    _, box_z = box_place()
    above = lax.rem(box_z, 2)
    faces_of(faces_odd, above, sums_for(above, left, moments, right, far), own, left, right)
    base = left.shape[1] - LEAVES
    beside = jnp.concatenate([left[:, lanes(base, LEAVES)], right[:, lanes(base, LEAVES)]], axis=1)
    same[...] = dot(beside, far[lanes(3 * LEAVES, 2 * LEAVES), :])
    near[:, lanes(0, EARLY * points // 4)] = early[...]
    own_groups(near, EARLY, 4, target, source, own)

    @pl.when(above == 1)
    def _():
        side_pulls(near, [(0, left)], near, target, sides)


def one_side(near, step, side, early, target, held):
    pts = early.shape[1] // 8
    for group in (1 - step, 3 - step):
        here = lanes(2 * group * pts, 2 * pts)
        near[:, here] = early[:, here]
    side_pulls(near, [(step, side)], early, target, [held])


def side_kernel(left, right, early, target, near, held):
    _, box_z = box_place()
    odd = lax.rem(box_z, 2) == 1

    @pl.when(odd)
    def _():
        one_side(near, 1, right, early, target, held)

    @pl.when(jnp.logical_not(odd))
    def _():
        one_side(near, 0, left, early, target, held)


def both_kernel(rows, faces, near, both):
    width = rows.shape[1]
    both[:, lanes(0, width)] = rows[...]
    both[:, lanes(width, width)] = faces[:, lanes(faces.shape[1] - width, width)]


def layer_pulls(near, early, step, inside, target, faces, sides):
    points = early.shape[1]
    pts = points // 8

    @pl.when(inside)
    def _():
        for place in range(8):
            height = jnp.where(step == 1, 1.5, -1.5)
            centre = (place // 2 - 1.5, place % 2 - 0.5, height)
            sides[lanes(place * pts, pts), :] = source_features(faces, place * pts, pts, centre)

        jobs = [(i + 2 * step, sides, faces, [2 * (x + i) * pts for x in range(3)]) for i in range(2)]
        pulled(near, jobs, target, 2 * pts, early)

    @pl.when(jnp.logical_not(inside))
    def _():
        here = lanes(step * (points // 2), points // 2)
        near[:, here] = early[:, here]


def even_kernel(early, target, right, faces, near, sides, held):
    _, box_z = box_place()
    step = 1 - lax.rem(box_z, 2)

    @pl.when(step == 0)
    def _():
        near[...] = early[...]

    @pl.when(step == 1)
    def _():
        one_side(near, 1, right, early, target, held)

    layer_pulls(near, near, step, box_z >= 0, target, faces, sides)


def odd_inside(depth):
    _, box_z = box_place()
    step = lax.rem(box_z, 2)
    return step, (box_z + 2 * step - 1 >= 0) & (box_z + 2 * step - 1 < depth)


def odd_kernel(depth, early, target, faces, near, sides):
    points = early.shape[1]
    step, inside = odd_inside(depth)
    other = lanes((1 - step) * (points // 2), points // 2)
    near[:, other] = early[:, other]
    layer_pulls(near, early, step, inside, target, faces, sides)


def last_kernel(depth, near, faces_even, faces_odd, basis, scale, column, columns, spread, same, *rest):
    held, (potential, sums) = rest[:-2], rest[-2:]
    fields, points = potential.shape
    pts = points // 8
    _, inside = odd_inside(depth)
    if depth == 4:
        rows, distant = held
        width = rows.shape[1]
        near_rows = faces_even[:, lanes(faces_even.shape[1] - width, width)]
        layers = [rows[...], near_rows, distant[:, lanes(0, width)], distant[:, lanes(width, width)]]
    else:
        layers = [held[0][layer] for layer in range(depth)]
    coarse_high, coarse_low = high_low(dot(jnp.concatenate(layers, axis=1), columns[...]))
    value = same[...] + dot(coarse_high, spread[...]) + dot(coarse_low, spread[...])
    value = value + decoded(faces_even[:, lanes(points, LEAVES)])
    value = value + jnp.where(inside, decoded(faces_odd[:, lanes(points, LEAVES)]), 0.0)
    local_high, local_low = high_low(value)
    weight = column[0:fields, 0:1]
    for leaf in range(8):
        here = slice(leaf * pts, (leaf + 1) * pts)
        slot = slice(leaf * SLOT, (leaf + 1) * SLOT)
        doubled = jnp.concatenate([local_high[:, slot], local_high[:, slot]], axis=1)
        far_part = dot(doubled, basis[:, here]) + dot(local_low[:, slot], basis[0:SLOT, here])
        total = near[0:fields, lanes(leaf_slot(leaf) * pts, pts)] + far_part[:fields]
        total = total * scale[:, here]
        potential[:, here] = total
        sums[:, here] = jnp.sum(total * weight, axis=0, keepdims=True)
    sums[:, points:] = jnp.broadcast_to(jnp.sum(weight), (1, sums.shape[1] - points))


def mean_kernel(mine, other, mean):
    points = mean.shape[1]
    total = mine[...] + other[...]
    mean[...] = total[:, :points] / total[:, points : points + 1]


def swapped(block, axis, partner):
    size = lax.axis_size(axis)
    return lax.ppermute(block, axis, [(partner(i), i) for i in range(size)])


def swapped_odd(block):
    boxes, cores = lax.axis_size("space"), lax.axis_size("sig")
    pairs = []
    for box in range(boxes):
        other = box + ACROSS if box // ACROSS % 2 else box - ACROSS
        for core in range(cores):
            source = other * cores + core if 0 <= other < boxes else box * cores + (core ^ 1)
            pairs.append((source, box * cores + core))
    return lax.ppermute(block, ("space", "sig"), pairs)


def per_device(positions, density, leaf_count, sigma_weights):
    fields, points = density.shape
    pts = points // 8
    depth = lax.axis_size("space") // ACROSS
    vmem, hbm = pl.BlockSpec(memory_space=pltpu.VMEM), pl.BlockSpec(memory_space=pltpu.HBM)

    def call(kernel, name, in_specs, outs, scratch, *args):
        return pl.pallas_call(
            kernel,
            in_specs=in_specs,
            out_specs=[vmem] * len(outs),
            out_shape=[jax.ShapeDtypeStruct(shape, dtype) for shape, dtype in outs],
            scratch_shapes=scratch,
            compiler_params=pltpu.CompilerParams(vmem_limit_bytes=24 * MEGA),
            name=name,
        )(*(pltpu.with_memory_space_constraint(a, pltpu.HBM) if s is hbm else a for s, a in zip(in_specs, args)))

    half, full = jnp.bfloat16, jnp.float32
    shift = shift_table()
    side_shape = ((ROWS, 4 * pts + LEAVES), half)
    given_shape = ((ROWS, 4 * pts + LEAVES + 2 * SLOT), half)
    faces_shape = ((ROWS, points + LEAVES), half)
    even_shape = ((ROWS, points + LEAVES + SLOT * ACROSS), half)
    rows_shape = ((ROWS, SLOT * ACROSS), half)
    both_shape = ((ROWS, 2 * SLOT * ACROSS), half)
    near_shape, sums_shape = ((ROWS, points), full), ((ROWS, LEAVES), full)
    side_scratch = pltpu.VMEM((4 * pts, FEATURES), half)
    rows_scratch = pltpu.VMEM((8 * pts, FEATURES), half)
    own, basis, moments, totals, *given = call(
        pack_kernel,
        "pack",
        [hbm] * 6,
        [
            ((ROWS, points), half),
            ((2 * SLOT, points), half),
            ((ROWS, LEAVES), half),
            ((ROWS, 2 * SLOT), half),
            given_shape,
            given_shape,
        ],
        [
            pltpu.SMEM((8,), jnp.int32),
            pltpu.VMEM((3, points), full),
            pltpu.VMEM((fields, points), half),
            pltpu.VMEM((LEAVES, SLOT), half),
            pltpu.VMEM((SLOT, SLOT), half),
            pltpu.VMEM((3 * SLOT, 16), half),
            pltpu.SemaphoreType.DMA((6,)),
        ],
        leaf_count,
        positions,
        density,
        jnp.asarray(shift, half),
        jnp.asarray(heavy_table(), half),
        jnp.asarray(power_table(), half),
    )
    from_2 = swapped(totals, "space", lambda i: i ^ 2)
    from_1 = swapped(given[0], "space", lambda i: i ^ 1)
    from_3 = swapped(given[1], "space", lambda i: i ^ 3)
    near, source, target, scale, column, columns, far, spread = call(
        functools.partial(own_kernel, depth),
        "near_own",
        [hbm] * 2 + [vmem] + [hbm] * 3,
        [
            ((ROWS, EARLY * points // 4), full),
            ((points, FEATURES), half),
            ((FEATURES, points), half),
            ((1, points), full),
            ((ROWS, 128), full),
            ((ACROSS * depth * SLOT, SLOT), half),
            ((len(STEPS) * LEAVES, LEAVES), half),
            ((SLOT, LEAVES), half),
        ],
        [
            pltpu.VMEM((3, SLOT, SLOT), full),
            pltpu.SMEM((8,), jnp.int32),
            pltpu.SMEM((fields,), full),
            pltpu.SemaphoreType.DMA((5,)),
        ],
        leaf_count,
        sigma_weights,
        own,
        jnp.asarray(far_table(), half),
        jnp.asarray(shift.T.copy(), half),
        jnp.asarray(box_nodes()),
    )
    left, right, faces_even, rows = call(
        row_kernel,
        "row",
        [vmem] * 7,
        [side_shape, side_shape, even_shape, rows_shape],
        [],
        own,
        moments,
        totals,
        from_1,
        from_2,
        from_3,
        far,
    )
    faces_even = swapped(faces_even, "space", lambda i: i ^ ACROSS)
    near, faces_odd, same = call(
        middle_kernel,
        "near_middle",
        [vmem] * 8,
        [near_shape, faces_shape, sums_shape],
        [side_scratch],
        own,
        left,
        right,
        moments,
        far,
        near,
        source,
        target,
    )
    faces_odd = swapped_odd(faces_odd)
    near, = call(
        side_kernel,
        "near_side",
        [vmem] * 4,
        [near_shape],
        [side_scratch],
        left,
        right,
        near,
        target,
    )
    if depth == 4:
        both, = call(both_kernel, "row_pairs", [vmem] * 3, [both_shape], [], rows, faces_even, near)
        held = [rows, swapped(both, "space", lambda i: i ^ (2 * ACROSS))]
    else:
        groups = [[z * ACROSS + x for z in range(depth)] for x in range(ACROSS)]
        held = [lax.all_gather(rows, "space", axis_index_groups=groups)]
    near, = call(
        even_kernel,
        "near_even",
        [vmem] * 4,
        [near_shape],
        [rows_scratch, side_scratch],
        near,
        target,
        right,
        faces_even,
    )
    near, = call(
        functools.partial(odd_kernel, depth),
        "near_odd",
        [vmem] * 3,
        [near_shape],
        [rows_scratch],
        near,
        target,
        faces_odd,
    )
    potential, sums = call(
        functools.partial(last_kernel, depth),
        "evaluate",
        [vmem] * (9 + len(held)),
        [((fields, points), full), ((1, points + 128), full)],
        [],
        near,
        faces_even,
        faces_odd,
        basis,
        scale,
        column,
        columns,
        spread,
        same,
        *held,
    )
    if lax.axis_size("sig") == 2:
        other = swapped(sums, "sig", lambda i: i ^ 1)
    else:
        other = lax.psum(sums, "sig") - sums
    mean, = call(mean_kernel, "mean", [vmem] * 2, [((1, points), full)], [], sums, other)
    return potential, mean.reshape(points)


def solution(mesh):
    in_specs = (P(None, "space"), P("sig", "space"), P("space"), P("sig"))
    out_specs = (P("sig", "space"), P("space"))
    return jax.shard_map(per_device, mesh=mesh, in_specs=in_specs, out_specs=out_specs, check_vma=False)
```

```python
import functools
import math

import jax
import jax.numpy as jnp
import numpy as np
from jax import lax
from jax.experimental import pallas as pl
from jax.experimental.pallas import tpu as pltpu
from jax.sharding import PartitionSpec as P

ORDER = 5
SOFTENING = 0.1
ACROSS = 4
SLOT = 64
ROWS = 24
LEAVES = 8 * SLOT
MEGA = 1024 * 1024
FEATURES = 48
EARLY = 3


def exponent_table(order_max):
    entries_list = []
    for degree in range(order_max + 1):
        for first_power in range(degree, -1, -1):
            for second_power in range(degree - first_power, -1, -1):
                entries_list.append((first_power, second_power, degree - first_power - second_power))
    return entries_list


def node_table(count_nodes, offset_value):
    counter = np.arange(1, count_nodes + 1, dtype=np.float32)[:, None]
    stride_set = np.array([0.7548776662466927, 0.5698402909980532, 0.4142135623730951], dtype=np.float32)[None, :]
    unit_points = np.mod(counter * stride_set + np.float32(offset_value), np.float32(1.0))
    return (np.float32(2.0) * unit_points - np.float32(1.0)).astype(np.float32)


EXPONENTS = exponent_table(ORDER)
COEFFS = len(EXPONENTS)
CHECK = node_table(COEFFS, 0.5).astype(np.float64)
EQUIV = node_table(COEFFS, 0.0).astype(np.float64)
HEAVY = [EXPONENTS.index(e) for e in ((0, 0, 0), (2, 0, 0), (0, 2, 0), (0, 0, 2), (4, 0, 0), (0, 4, 0), (0, 0, 4), (2, 0, 2))]
STEPS = [(sx, sz) for sz in (-1, 0, 1) for sx in (-1, 0, 1) if sx != 0 or sz != 0]


def bits(octant):
    return octant % 2, octant // 2 % 2, octant // 4


def leaf_slot(octant):
    bit_x, bit_y, bit_z = bits(octant)
    return (bit_x + 2 * bit_z) * 2 + bit_y


@functools.lru_cache(None)
def far_table():
    shape = (len(STEPS), 8, SLOT, 8, SLOT)
    table = np.zeros(shape)
    gap_nodes = 0.5 * (CHECK[None, :, :] - EQUIV[:, None, :])
    for index, (step_x, step_z) in enumerate(STEPS):
        for source in range(8):
            for target in range(8):
                s, t = bits(source), bits(target)
                gap = np.array([2 * step_x + s[0] - t[0], s[1] - t[1], 2 * step_z + s[2] - t[2]], np.float64)
                if max(abs(gap[0]), abs(gap[2])) >= 2:
                    shifted = gap_nodes - gap
                    value = 1.0 / np.sqrt(np.sum(shifted * shifted, -1) + SOFTENING * SOFTENING) / COEFFS
                    table[index, source, :COEFFS, target, :COEFFS] = value
    return table.reshape(len(STEPS) * LEAVES, LEAVES)


@functools.lru_cache(None)
def shift_table():
    table = np.zeros((8, SLOT, SLOT))
    for leaf in range(8):
        offset = [bit - 0.5 for bit in bits(leaf)]
        for k, target in enumerate(EXPONENTS):
            for i, source in enumerate(EXPONENTS):
                if all(b <= a for a, b in zip(target, source)):
                    value = 1.0
                    for a, b, h in zip(target, source, offset):
                        value *= math.comb(a, b) * 0.5**b * h ** (a - b)
                    table[leaf, i, k] = value
    return table.reshape(8 * SLOT, SLOT)


@functools.lru_cache(None)
def box_nodes():
    gaps = np.zeros((3, SLOT, SLOT))
    gaps[:, :COEFFS, :COEFFS] = np.moveaxis(CHECK[None, :, :] - EQUIV[:, None, :], -1, 0)
    gaps[:, COEFFS:] = gaps[:, HEAVY]
    gaps[1] = gaps[1] ** 2 + SOFTENING * SOFTENING
    return gaps.astype(np.float32)


def dot(left, right):
    return jnp.dot(left, right, preferred_element_type=jnp.float32)


def dot_nt(left, right):
    return lax.dot_general(left, right, (((1,), (1,)), ((), ())), preferred_element_type=jnp.float32)


def low_bits(value):
    return value.astype(jnp.bfloat16)


def heavy_table():
    table = np.zeros((SLOT, SLOT), np.float32)
    table[HEAVY, np.arange(COEFFS, SLOT)] = 1.0
    return table


def power_table():
    table = np.zeros((3, SLOT, 16), np.float32)
    for axis in range(3):
        for k, powers in enumerate(EXPONENTS):
            table[axis, k, powers[axis]] = 1.0
            table[axis, k, 8 + powers[axis]] = 1.0
    return table.reshape(3 * SLOT, 16)


def high_low(value):
    high = low_bits(value)
    return high, low_bits(value - high.astype(jnp.float32))


def by_row(values, shape):
    row = lax.broadcasted_iota(jnp.int32, shape, 0)
    result = jnp.zeros(shape, jnp.float32)
    for index, value in enumerate(values):
        result = jnp.where(row == index, value, result)
    return result


def box_place():
    label = lax.axis_index("space")
    return lax.rem(label, ACROSS), lax.div(label, ACROSS)


def lanes(start, size):
    return pl.ds(start if isinstance(start, int) else pl.multiple_of(start, 128), size)


def fetch(pairs, sems):
    copies = [pltpu.make_async_copy(src, dst, sems.at[i]) for i, (src, dst) in enumerate(pairs)]
    for copy in copies:
        copy.start()
    return copies


def pack_kernel(count_in, positions_in, density_in, shift_in, heavy_in, powers_in, own, basis, moments, totals, *rest):
    payloads, (count, positions, density, shift, heavy, powers, sems) = rest[:2], rest[2:]
    copies = fetch(
        [
            (count_in, count),
            (positions_in, positions),
            (density_in, density),
            (shift_in, shift),
            (heavy_in, heavy),
            (powers_in, powers),
        ],
        sems,
    )
    fields, points = density.shape
    pts = points // 8
    box_x, box_z = box_place()
    for copy in copies:
        copy.wait()
    local = []
    for leaf in range(8):
        bit_x, bit_y, bit_z = bits(leaf)
        centre = by_row(
            [2.0 * box_x.astype(jnp.float32) + (bit_x + 0.5), bit_y + 0.5, 2.0 * box_z.astype(jnp.float32) + (bit_z + 0.5)],
            (3, 1),
        )
        here = slice(leaf * pts, (leaf + 1) * pts)
        offset = positions[:, here] - centre
        local.append(offset)
        high = low_bits(offset).astype(jnp.float32)
        middle = low_bits(offset - high).astype(jnp.float32)
        raw = density[:, here].astype(jnp.float32)
        mass = jnp.where(lax.broadcasted_iota(jnp.int32, raw.shape, 1) < count[leaf], raw, 0.0)
        spare = jnp.zeros((ROWS - fields - 6, pts), jnp.float32)
        own[:, here] = low_bits(jnp.concatenate([mass, high, middle, spare], axis=0))

    scaled = 2.0 * jnp.concatenate(local, axis=1)
    row = lax.broadcasted_iota(jnp.int32, (8, points), 0)
    value = None
    for axis in range(3):
        base = jnp.broadcast_to(scaled[axis : axis + 1], (8, points))
        power = jnp.ones((8, points), jnp.float32)
        for degree in range(1, ORDER + 1):
            power = power * jnp.where(row >= degree, base, 1.0)
        pieces = jnp.concatenate(high_low(power), axis=0)
        picked = dot(powers[axis * SLOT : (axis + 1) * SLOT, :], pieces)
        value = picked if value is None else value * picked
    high, low = high_low(value)
    basis[0:SLOT, :] = high
    basis[SLOT:, :] = low
    parts = []
    for leaf in range(8):
        here = slice(leaf * pts, (leaf + 1) * pts)
        parts.append(dot_nt(own[:, here], high[:, here]))
    moment, rest = high_low(jnp.concatenate(parts, axis=1))
    moments[...] = moment
    total = dot(moment, shift[...]) + dot(rest, shift[...])
    total_high, total_low = high_low(total)
    total = low_bits(total_high.astype(jnp.float32) + dot(total_low, heavy[...]))
    total = jnp.concatenate([total, jnp.zeros_like(total)], axis=1)
    totals[...] = total
    for distance, payload in zip((1, 3), payloads):
        bit = jnp.where((box_x ^ distance) > box_x, 1, 0)
        for place in range(4):
            payload[:, lanes(place * pts, pts)] = own[:, lanes((bit + 2 * place) * pts, pts)]
        payload[:, lanes(4 * pts, LEAVES)] = moment
        payload[:, lanes(4 * pts + LEAVES, 2 * SLOT)] = total


def features(held, start, size, centre, target):
    value = held[16:ROWS, lanes(start, size)].astype(jnp.float32)
    x = value[1:4] + value[4:7] + by_row(centre, (3, 1))
    norm = jnp.sum(x * x, axis=0, keepdims=True)
    if target:
        norm = norm + SOFTENING * SOFTENING
    parts, norms = [], []
    for source, out in ((x, parts), (norm, norms)):
        left = source
        for _ in range(3):
            high = low_bits(left).astype(jnp.float32)
            out.append(high)
            left = left - high
    one = jnp.ones_like(norm)
    zero = jnp.zeros_like(norm)
    blank = jnp.zeros((3, norm.shape[1]), jnp.float32)
    blocks = []
    order = (0, 1, 0, 2, 0, 1) if target else (0, 0, 1, 0, 2, 1)
    for index, which in enumerate(order):
        coords = -2.0 * parts[which] if target else parts[which]
        if index < 3:
            pair = [one, norms[index]] if target else [norms[index], one]
        else:
            pair = [zero, zero]
        blocks += [coords, *pair, blank]
    return jnp.concatenate(blocks, axis=0)


def source_features(held, start, size, centre):
    return low_bits(jnp.transpose(features(held, start, size, centre, False)))


def pulled(near, jobs, target, size, first=None):
    width = target.shape[1] // 8
    tiles = []
    for group, source, masses, starts in jobs:
        for piece in range(2):
            here = lanes((2 * group + piece) * width, width)
            for turn, start in enumerate(starts):
                tiles.append((here, source, masses, lanes(start, size), turn == 0, turn + 1 == len(starts)))

    def squares(tile):
        return dot(tile[1][tile[3], :], target[:, tile[0]])

    ahead, kernel, total = squares(tiles[0]), None, None
    for turn in range(len(tiles) + 1):
        square = ahead
        if turn + 1 < len(tiles):
            ahead = squares(tiles[turn + 1])
        if turn > 0:
            here, _, masses, place, opens, closes = tiles[turn - 1]
            if opens:
                total = jnp.zeros((ROWS, width), jnp.float32) if first is None else first[:, here]
            total = total + dot(masses[:, place], kernel)
            if closes:
                near[:, here] = total
        if turn < len(tiles):
            kernel = low_bits(lax.rsqrt(square))


def own_groups(near, first, last, target, source, own):
    pts = source.shape[0] // 8
    starts = [0, 4 * pts]
    pulled(near, [(group, source, own, starts) for group in range(first, last)], target, 4 * pts)


def box_columns(depth, box_x, box_z, nodes):
    blocks = []
    for turn, distance in [(turn, distance) for turn in range(depth) for distance in range(ACROSS)]:
        gap_x = 2 * (box_x - (box_x ^ distance))
        gap_z = 2 * (box_z - ((box_z ^ turn) if depth == 4 else turn))
        across_x = nodes[0] + gap_x.astype(jnp.float32)
        across_z = nodes[2] + gap_z.astype(jnp.float32)
        apart = jnp.maximum(jnp.abs(gap_x), jnp.abs(gap_z)) >= 4
        value = lax.rsqrt(across_x * across_x + across_z * across_z + nodes[1])
        blocks.append(low_bits(value * jnp.where(apart, 1.0 / COEFFS, 0.0)))
    return jnp.concatenate(blocks, axis=0)


def own_kernel(depth, count_in, weights_in, own, *rest):
    tables, outs, (nodes, count, weights, sems) = rest[:3], rest[3:11], rest[11:]
    near, source, target, scale, column, columns, far, spread = outs
    copies = fetch([*zip(tables, (far, spread, nodes)), (count_in, count), (weights_in, weights)], sems)
    points = own.shape[1]
    pts = points // 8
    for leaf in range(8):
        centre = [bit - 0.5 for bit in bits(leaf)]
        source[lanes(leaf * pts, pts), :] = source_features(own, leaf * pts, pts, centre)
        target[:, lanes(leaf_slot(leaf) * pts, pts)] = low_bits(features(own, leaf * pts, pts, centre, True))
    own_groups(near, 0, EARLY, target, source, own)
    for copy in copies:
        copy.wait()
    columns[...] = box_columns(depth, *box_place(), nodes)
    column[...] = by_row([weights[field] for field in range(weights.shape[0])], column.shape)
    lane_index = lax.broadcasted_iota(jnp.int32, (1, pts), 1)
    for leaf in range(8):
        scale[:, leaf * pts : (leaf + 1) * pts] = jnp.where(lane_index < count[leaf], 1.0 / (128.0 * pts), 0.0)


def spread_first(value, node):
    starts = [leaf * SLOT + node for leaf in range(8)]
    return jnp.concatenate([jnp.broadcast_to(value[:, s : s + 1], (ROWS, SLOT)) for s in starts], axis=1)


def decoded(coded):
    value = coded.astype(jnp.float32)
    node = lax.broadcasted_iota(jnp.int32, value.shape, 1) % SLOT
    return jnp.where(node == 0, 0.0, value) + spread_first(value, 0) + spread_first(value, COEFFS)


def faces_of(faces, bit, given, own, left, right, rows=None):
    points = own.shape[1]
    pts = points // 8
    for y in range(2):
        for x in range(4):
            place = lanes((2 * x + y) * pts, pts)
            if x in (0, 3):
                side = left if x == 0 else right
                faces[:, place] = side[:, lanes((y + 2 * bit) * pts, pts)]
            else:
                faces[:, place] = own[:, lanes((x - 1 + 2 * y + 4 * bit) * pts, pts)]
    node = lax.broadcasted_iota(jnp.int32, given.shape, 1) % SLOT
    base = spread_first(given, 0)
    base_high = low_bits(base).astype(jnp.float32)
    coded = jnp.where(node == 0, base_high, jnp.where(node == COEFFS, base - base_high, given - base))
    faces[:, lanes(points, LEAVES)] = low_bits(coded)
    if rows is not None:
        faces[:, lanes(points + LEAVES, rows.shape[1])] = rows


def sums_for(above, left, moments, right, far):
    base = left.shape[1] - LEAVES
    around = jnp.concatenate([left[:, lanes(base, LEAVES)], moments[...], right[:, lanes(base, LEAVES)]], axis=1)
    return dot(around, far[lanes(jnp.where(above == 1, 0, 5 * LEAVES), 3 * LEAVES), :])


def row_kernel(own, moments, totals, from_1, from_2, from_3, far, left, right, faces_even, rows):
    box_x, box_z = box_place()
    for side, step in ((left, -1), (right, 1)):
        side[...] = jnp.zeros(side.shape, side.dtype)
        for distance, held in ((1, from_1), (3, from_3)):

            @pl.when((box_x ^ distance) - box_x == step)
            def _(side=side, held=held):
                side[...] = held[:, lanes(0, side.shape[1])]

    ends = lanes(left.shape[1], 2 * SLOT)
    row = [totals[...], from_1[:, ends], from_2[...], from_3[:, ends]]
    row = jnp.concatenate([box[:, :SLOT] for box in row], axis=1)
    rows[...] = row
    above = 1 - lax.rem(box_z, 2)
    faces_of(faces_even, above, sums_for(above, left, moments, right, far), own, left, right, row)


def side_pulls(near, faces, early, target, scratch):
    pts = early.shape[1] // 8
    jobs = []
    for (step, side), held in zip(faces, scratch):
        for place in range(4):
            centre = (1.5 if step else -1.5, place % 2 - 0.5, place // 2 - 0.5)
            held[lanes(place * pts, pts), :] = source_features(side, place * pts, pts, centre)
        jobs += [(step, held, side, [0]), (step + 2, held, side, [0])]
    pulled(near, jobs, target, 4 * pts, early)


def middle_kernel(own, left, right, moments, far, early, source, target, near, faces_odd, same, *sides):
    points = own.shape[1]
    _, box_z = box_place()
    above = lax.rem(box_z, 2)
    faces_of(faces_odd, above, sums_for(above, left, moments, right, far), own, left, right)
    base = left.shape[1] - LEAVES
    beside = jnp.concatenate([left[:, lanes(base, LEAVES)], right[:, lanes(base, LEAVES)]], axis=1)
    same[...] = dot(beside, far[lanes(3 * LEAVES, 2 * LEAVES), :])
    near[:, lanes(0, EARLY * points // 4)] = early[...]
    own_groups(near, EARLY, 4, target, source, own)

    @pl.when(above == 1)
    def _():
        side_pulls(near, [(0, left)], near, target, sides)


def one_side(near, step, side, early, target, held):
    pts = early.shape[1] // 8
    for group in (1 - step, 3 - step):
        here = lanes(2 * group * pts, 2 * pts)
        near[:, here] = early[:, here]
    side_pulls(near, [(step, side)], early, target, [held])


def side_kernel(left, right, early, target, near, held):
    _, box_z = box_place()
    odd = lax.rem(box_z, 2) == 1

    @pl.when(odd)
    def _():
        one_side(near, 1, right, early, target, held)

    @pl.when(jnp.logical_not(odd))
    def _():
        one_side(near, 0, left, early, target, held)


def both_kernel(rows, faces, near, both):
    width = rows.shape[1]
    both[:, lanes(0, width)] = rows[...]
    both[:, lanes(width, width)] = faces[:, lanes(faces.shape[1] - width, width)]


def layer_pulls(near, early, step, inside, target, faces, sides):
    points = early.shape[1]
    pts = points // 8

    @pl.when(inside)
    def _():
        for place in range(8):
            height = jnp.where(step == 1, 1.5, -1.5)
            centre = (place // 2 - 1.5, place % 2 - 0.5, height)
            sides[lanes(place * pts, pts), :] = source_features(faces, place * pts, pts, centre)

        jobs = [(i + 2 * step, sides, faces, [(2 * i + 3 * turn) * pts for turn in range(2)]) for i in range(2)]
        pulled(near, jobs, target, 3 * pts, early)

    @pl.when(jnp.logical_not(inside))
    def _():
        here = lanes(step * (points // 2), points // 2)
        near[:, here] = early[:, here]


def even_kernel(early, target, right, faces, near, sides, held):
    _, box_z = box_place()
    step = 1 - lax.rem(box_z, 2)

    @pl.when(step == 0)
    def _():
        near[...] = early[...]

    @pl.when(step == 1)
    def _():
        one_side(near, 1, right, early, target, held)

    layer_pulls(near, near, step, box_z >= 0, target, faces, sides)


def odd_inside(depth):
    _, box_z = box_place()
    step = lax.rem(box_z, 2)
    return step, (box_z + 2 * step - 1 >= 0) & (box_z + 2 * step - 1 < depth)


def odd_kernel(depth, early, target, faces, near, sides):
    points = early.shape[1]
    step, inside = odd_inside(depth)
    other = lanes((1 - step) * (points // 2), points // 2)
    near[:, other] = early[:, other]
    layer_pulls(near, early, step, inside, target, faces, sides)


def last_kernel(depth, near, faces_even, faces_odd, basis, scale, column, columns, spread, same, *rest):
    held, (potential, sums) = rest[:-2], rest[-2:]
    fields, points = potential.shape
    pts = points // 8
    _, inside = odd_inside(depth)
    if depth == 4:
        rows, distant = held
        width = rows.shape[1]
        near_rows = faces_even[:, lanes(faces_even.shape[1] - width, width)]
        layers = [rows[...], near_rows, distant[:, lanes(0, width)], distant[:, lanes(width, width)]]
    else:
        layers = [held[0][layer] for layer in range(depth)]
    coarse_high, coarse_low = high_low(dot(jnp.concatenate(layers, axis=1), columns[...]))
    value = same[...] + dot(coarse_high, spread[...]) + dot(coarse_low, spread[...])
    value = value + decoded(faces_even[:, lanes(points, LEAVES)])
    value = value + jnp.where(inside, decoded(faces_odd[:, lanes(points, LEAVES)]), 0.0)
    local_high, local_low = high_low(value)
    weight = column[0:fields, 0:1]
    for leaf in range(8):
        here = slice(leaf * pts, (leaf + 1) * pts)
        slot = slice(leaf * SLOT, (leaf + 1) * SLOT)
        doubled = jnp.concatenate([local_high[:, slot], local_high[:, slot]], axis=1)
        far_part = dot(doubled, basis[:, here]) + dot(local_low[:, slot], basis[0:SLOT, here])
        total = near[0:fields, lanes(leaf_slot(leaf) * pts, pts)] + far_part[:fields]
        total = total * scale[:, here]
        potential[:, here] = total
        sums[:, here] = jnp.sum(total * weight, axis=0, keepdims=True)
    sums[:, points:] = jnp.broadcast_to(jnp.sum(weight), (1, sums.shape[1] - points))


def mean_kernel(mine, other, mean):
    points = mean.shape[1]
    total = mine[...] + other[...]
    mean[...] = total[:, :points] / total[:, points : points + 1]


def swapped(block, axis, partner):
    size = lax.axis_size(axis)
    return lax.ppermute(block, axis, [(partner(i), i) for i in range(size)])


def swapped_odd(block):
    boxes, cores = lax.axis_size("space"), lax.axis_size("sig")
    pairs = []
    for box in range(boxes):
        other = box + ACROSS if box // ACROSS % 2 else box - ACROSS
        for core in range(cores):
            source = other * cores + core if 0 <= other < boxes else box * cores + (core ^ 1)
            pairs.append((source, box * cores + core))
    return lax.ppermute(block, ("space", "sig"), pairs)


def per_device(positions, density, leaf_count, sigma_weights):
    fields, points = density.shape
    pts = points // 8
    depth = lax.axis_size("space") // ACROSS
    vmem, hbm = pl.BlockSpec(memory_space=pltpu.VMEM), pl.BlockSpec(memory_space=pltpu.HBM)

    def call(kernel, name, in_specs, outs, scratch, *args):
        return pl.pallas_call(
            kernel,
            in_specs=in_specs,
            out_specs=[vmem] * len(outs),
            out_shape=[jax.ShapeDtypeStruct(shape, dtype) for shape, dtype in outs],
            scratch_shapes=scratch,
            compiler_params=pltpu.CompilerParams(vmem_limit_bytes=24 * MEGA),
            name=name,
        )(*(pltpu.with_memory_space_constraint(a, pltpu.HBM) if s is hbm else a for s, a in zip(in_specs, args)))

    half, full = jnp.bfloat16, jnp.float32
    shift = shift_table()
    side_shape = ((ROWS, 4 * pts + LEAVES), half)
    given_shape = ((ROWS, 4 * pts + LEAVES + 2 * SLOT), half)
    faces_shape = ((ROWS, points + LEAVES), half)
    even_shape = ((ROWS, points + LEAVES + SLOT * ACROSS), half)
    rows_shape = ((ROWS, SLOT * ACROSS), half)
    both_shape = ((ROWS, 2 * SLOT * ACROSS), half)
    near_shape, sums_shape = ((ROWS, points), full), ((ROWS, LEAVES), full)
    side_scratch = pltpu.VMEM((4 * pts, FEATURES), half)
    rows_scratch = pltpu.VMEM((8 * pts, FEATURES), half)
    own, basis, moments, totals, *given = call(
        pack_kernel,
        "pack",
        [hbm] * 6,
        [
            ((ROWS, points), half),
            ((2 * SLOT, points), half),
            ((ROWS, LEAVES), half),
            ((ROWS, 2 * SLOT), half),
            given_shape,
            given_shape,
        ],
        [
            pltpu.SMEM((8,), jnp.int32),
            pltpu.VMEM((3, points), full),
            pltpu.VMEM((fields, points), half),
            pltpu.VMEM((LEAVES, SLOT), half),
            pltpu.VMEM((SLOT, SLOT), half),
            pltpu.VMEM((3 * SLOT, 16), half),
            pltpu.SemaphoreType.DMA((6,)),
        ],
        leaf_count,
        positions,
        density,
        jnp.asarray(shift, half),
        jnp.asarray(heavy_table(), half),
        jnp.asarray(power_table(), half),
    )
    from_2 = swapped(totals, "space", lambda i: i ^ 2)
    from_1 = swapped(given[0], "space", lambda i: i ^ 1)
    from_3 = swapped(given[1], "space", lambda i: i ^ 3)
    near, source, target, scale, column, columns, far, spread = call(
        functools.partial(own_kernel, depth),
        "near_own",
        [hbm] * 2 + [vmem] + [hbm] * 3,
        [
            ((ROWS, EARLY * points // 4), full),
            ((points, FEATURES), half),
            ((FEATURES, points), half),
            ((1, points), full),
            ((ROWS, 128), full),
            ((ACROSS * depth * SLOT, SLOT), half),
            ((len(STEPS) * LEAVES, LEAVES), half),
            ((SLOT, LEAVES), half),
        ],
        [
            pltpu.VMEM((3, SLOT, SLOT), full),
            pltpu.SMEM((8,), jnp.int32),
            pltpu.SMEM((fields,), full),
            pltpu.SemaphoreType.DMA((5,)),
        ],
        leaf_count,
        sigma_weights,
        own,
        jnp.asarray(far_table(), half),
        jnp.asarray(shift.T.copy(), half),
        jnp.asarray(box_nodes()),
    )
    left, right, faces_even, rows = call(
        row_kernel,
        "row",
        [vmem] * 7,
        [side_shape, side_shape, even_shape, rows_shape],
        [],
        own,
        moments,
        totals,
        from_1,
        from_2,
        from_3,
        far,
    )
    faces_even = swapped(faces_even, "space", lambda i: i ^ ACROSS)
    near, faces_odd, same = call(
        middle_kernel,
        "near_middle",
        [vmem] * 8,
        [near_shape, faces_shape, sums_shape],
        [side_scratch],
        own,
        left,
        right,
        moments,
        far,
        near,
        source,
        target,
    )
    faces_odd = swapped_odd(faces_odd)
    near, = call(
        side_kernel,
        "near_side",
        [vmem] * 4,
        [near_shape],
        [side_scratch],
        left,
        right,
        near,
        target,
    )
    if depth == 4:
        both, = call(both_kernel, "row_pairs", [vmem] * 3, [both_shape], [], rows, faces_even, near)
        held = [rows, swapped(both, "space", lambda i: i ^ (2 * ACROSS))]
    else:
        groups = [[z * ACROSS + x for z in range(depth)] for x in range(ACROSS)]
        held = [lax.all_gather(rows, "space", axis_index_groups=groups)]
    near, = call(
        even_kernel,
        "near_even",
        [vmem] * 4,
        [near_shape],
        [rows_scratch, side_scratch],
        near,
        target,
        right,
        faces_even,
    )
    near, = call(
        functools.partial(odd_kernel, depth),
        "near_odd",
        [vmem] * 3,
        [near_shape],
        [rows_scratch],
        near,
        target,
        faces_odd,
    )
    potential, sums = call(
        functools.partial(last_kernel, depth),
        "evaluate",
        [vmem] * (9 + len(held)),
        [((fields, points), full), ((1, points + 128), full)],
        [],
        near,
        faces_even,
        faces_odd,
        basis,
        scale,
        column,
        columns,
        spread,
        same,
        *held,
    )
    if lax.axis_size("sig") == 2:
        other = swapped(sums, "sig", lambda i: i ^ 1)
    else:
        other = lax.psum(sums, "sig") - sums
    mean, = call(mean_kernel, "mean", [vmem] * 2, [((1, points), full)], [], sums, other)
    return potential, mean.reshape(points)


def solution(mesh):
    in_specs = (P(None, "space"), P("sig", "space"), P("space"), P("sig"))
    out_specs = (P("sig", "space"), P("space"))
    return jax.shard_map(per_device, mesh=mesh, in_specs=in_specs, out_specs=out_specs, check_vma=False)
```

```python
import functools
import math

import jax
import jax.numpy as jnp
import numpy as np
from jax import lax
from jax.experimental import pallas as pl
from jax.experimental.pallas import tpu as pltpu
from jax.sharding import PartitionSpec as P

ORDER = 5
SOFTENING = 0.1
ACROSS = 4
SLOT = 64
ROWS = 24
LEAVES = 8 * SLOT
MEGA = 1024 * 1024
FEATURES = 48
EARLY = 3


def exponent_table(order_max):
    entries_list = []
    for degree in range(order_max + 1):
        for first_power in range(degree, -1, -1):
            for second_power in range(degree - first_power, -1, -1):
                entries_list.append((first_power, second_power, degree - first_power - second_power))
    return entries_list


def node_table(count_nodes, offset_value):
    counter = np.arange(1, count_nodes + 1, dtype=np.float32)[:, None]
    stride_set = np.array([0.7548776662466927, 0.5698402909980532, 0.4142135623730951], dtype=np.float32)[None, :]
    unit_points = np.mod(counter * stride_set + np.float32(offset_value), np.float32(1.0))
    return (np.float32(2.0) * unit_points - np.float32(1.0)).astype(np.float32)


EXPONENTS = exponent_table(ORDER)
COEFFS = len(EXPONENTS)
CHECK = node_table(COEFFS, 0.5).astype(np.float64)
EQUIV = node_table(COEFFS, 0.0).astype(np.float64)
HEAVY = [EXPONENTS.index(e) for e in ((0, 0, 0), (2, 0, 0), (0, 2, 0), (0, 0, 2), (4, 0, 0), (0, 4, 0), (0, 0, 4), (2, 0, 2))]
STEPS = [(sx, sz) for sz in (-1, 0, 1) for sx in (-1, 0, 1) if sx != 0 or sz != 0]


def bits(octant):
    return octant % 2, octant // 2 % 2, octant // 4


def leaf_slot(octant):
    bit_x, bit_y, bit_z = bits(octant)
    return (bit_x + 2 * bit_z) * 2 + bit_y


@functools.lru_cache(None)
def far_table():
    shape = (len(STEPS), 8, SLOT, 8, SLOT)
    table = np.zeros(shape)
    gap_nodes = 0.5 * (CHECK[None, :, :] - EQUIV[:, None, :])
    for index, (step_x, step_z) in enumerate(STEPS):
        for source in range(8):
            for target in range(8):
                s, t = bits(source), bits(target)
                gap = np.array([2 * step_x + s[0] - t[0], s[1] - t[1], 2 * step_z + s[2] - t[2]], np.float64)
                if max(abs(gap[0]), abs(gap[2])) >= 2:
                    shifted = gap_nodes - gap
                    value = 1.0 / np.sqrt(np.sum(shifted * shifted, -1) + SOFTENING * SOFTENING) / COEFFS
                    table[index, source, :COEFFS, target, :COEFFS] = value
    return table.reshape(len(STEPS) * LEAVES, LEAVES)


@functools.lru_cache(None)
def shift_table():
    table = np.zeros((8, SLOT, SLOT))
    for leaf in range(8):
        offset = [bit - 0.5 for bit in bits(leaf)]
        for k, target in enumerate(EXPONENTS):
            for i, source in enumerate(EXPONENTS):
                if all(b <= a for a, b in zip(target, source)):
                    value = 1.0
                    for a, b, h in zip(target, source, offset):
                        value *= math.comb(a, b) * 0.5**b * h ** (a - b)
                    table[leaf, i, k] = value
    return table.reshape(8 * SLOT, SLOT)


@functools.lru_cache(None)
def box_nodes():
    gaps = np.zeros((3, SLOT, SLOT))
    gaps[:, :COEFFS, :COEFFS] = np.moveaxis(CHECK[None, :, :] - EQUIV[:, None, :], -1, 0)
    gaps[:, COEFFS:] = gaps[:, HEAVY]
    gaps[1] = gaps[1] ** 2 + SOFTENING * SOFTENING
    return gaps.astype(np.float32)


def dot(left, right):
    return jnp.dot(left, right, preferred_element_type=jnp.float32)


def dot_nt(left, right):
    return lax.dot_general(left, right, (((1,), (1,)), ((), ())), preferred_element_type=jnp.float32)


def low_bits(value):
    return value.astype(jnp.bfloat16)


def heavy_table():
    table = np.zeros((SLOT, SLOT), np.float32)
    table[HEAVY, np.arange(COEFFS, SLOT)] = 1.0
    return table


def power_table():
    table = np.zeros((3, SLOT, 16), np.float32)
    for axis in range(3):
        for k, powers in enumerate(EXPONENTS):
            table[axis, k, powers[axis]] = 1.0
            table[axis, k, 8 + powers[axis]] = 1.0
    return table.reshape(3 * SLOT, 16)


def high_low(value):
    high = low_bits(value)
    return high, low_bits(value - high.astype(jnp.float32))


def by_row(values, shape):
    row = lax.broadcasted_iota(jnp.int32, shape, 0)
    result = jnp.zeros(shape, jnp.float32)
    for index, value in enumerate(values):
        result = jnp.where(row == index, value, result)
    return result


def box_place():
    label = lax.axis_index("space")
    return lax.rem(label, ACROSS), lax.div(label, ACROSS)


def lanes(start, size):
    return pl.ds(start if isinstance(start, int) else pl.multiple_of(start, 128), size)


def fetch(pairs, sems):
    copies = [pltpu.make_async_copy(src, dst, sems.at[i]) for i, (src, dst) in enumerate(pairs)]
    for copy in copies:
        copy.start()
    return copies


def pack_kernel(count_in, positions_in, density_in, shift_in, heavy_in, powers_in, own, basis, moments, totals, *rest):
    payloads, (count, positions, density, shift, heavy, powers, sems) = rest[:2], rest[2:]
    copies = fetch(
        [
            (count_in, count),
            (positions_in, positions),
            (density_in, density),
            (shift_in, shift),
            (heavy_in, heavy),
            (powers_in, powers),
        ],
        sems,
    )
    fields, points = density.shape
    pts = points // 8
    box_x, box_z = box_place()
    for copy in copies:
        copy.wait()
    local = []
    for leaf in range(8):
        bit_x, bit_y, bit_z = bits(leaf)
        centre = by_row(
            [2.0 * box_x.astype(jnp.float32) + (bit_x + 0.5), bit_y + 0.5, 2.0 * box_z.astype(jnp.float32) + (bit_z + 0.5)],
            (3, 1),
        )
        here = slice(leaf * pts, (leaf + 1) * pts)
        offset = positions[:, here] - centre
        local.append(offset)
        high = low_bits(offset).astype(jnp.float32)
        middle = low_bits(offset - high).astype(jnp.float32)
        raw = density[:, here].astype(jnp.float32)
        mass = jnp.where(lax.broadcasted_iota(jnp.int32, raw.shape, 1) < count[leaf], raw, 0.0)
        spare = jnp.zeros((ROWS - fields - 6, pts), jnp.float32)
        own[:, here] = low_bits(jnp.concatenate([mass, high, middle, spare], axis=0))

    scaled = 2.0 * jnp.concatenate(local, axis=1)
    row = lax.broadcasted_iota(jnp.int32, (8, points), 0)
    value = None
    for axis in range(3):
        base = jnp.broadcast_to(scaled[axis : axis + 1], (8, points))
        power = jnp.ones((8, points), jnp.float32)
        for degree in range(1, ORDER + 1):
            power = power * jnp.where(row >= degree, base, 1.0)
        pieces = jnp.concatenate(high_low(power), axis=0)
        picked = dot(powers[axis * SLOT : (axis + 1) * SLOT, :], pieces)
        value = picked if value is None else value * picked
    high, low = high_low(value)
    basis[0:SLOT, :] = high
    basis[SLOT:, :] = low
    parts = []
    for leaf in range(8):
        here = slice(leaf * pts, (leaf + 1) * pts)
        parts.append(dot_nt(own[:, here], high[:, here]))
    moment, rest = high_low(jnp.concatenate(parts, axis=1))
    moments[...] = moment
    total = dot(moment, shift[...]) + dot(rest, shift[...])
    total_high, total_low = high_low(total)
    total = low_bits(total_high.astype(jnp.float32) + dot(total_low, heavy[...]))
    total = jnp.concatenate([total, jnp.zeros_like(total)], axis=1)
    totals[...] = total
    for distance, payload in zip((1, 3), payloads):
        bit = jnp.where((box_x ^ distance) > box_x, 1, 0)
        for place in range(4):
            payload[:, lanes(place * pts, pts)] = own[:, lanes((bit + 2 * place) * pts, pts)]
        payload[:, lanes(4 * pts, LEAVES)] = moment
        payload[:, lanes(4 * pts + LEAVES, 2 * SLOT)] = total


def features(held, start, size, centre, target):
    value = held[16:ROWS, lanes(start, size)].astype(jnp.float32)
    x = value[1:4] + value[4:7] + by_row(centre, (3, 1))
    norm = jnp.sum(x * x, axis=0, keepdims=True)
    if target:
        norm = norm + SOFTENING * SOFTENING
    parts, norms = [], []
    for source, out in ((x, parts), (norm, norms)):
        left = source
        for _ in range(3):
            high = low_bits(left).astype(jnp.float32)
            out.append(high)
            left = left - high
    one = jnp.ones_like(norm)
    zero = jnp.zeros_like(norm)
    blank = jnp.zeros((3, norm.shape[1]), jnp.float32)
    blocks = []
    order = (0, 1, 0, 2, 0, 1) if target else (0, 0, 1, 0, 2, 1)
    for index, which in enumerate(order):
        coords = -2.0 * parts[which] if target else parts[which]
        if index < 3:
            pair = [one, norms[index]] if target else [norms[index], one]
        else:
            pair = [zero, zero]
        blocks += [coords, *pair, blank]
    return jnp.concatenate(blocks, axis=0)


def source_features(held, start, size, centre):
    return low_bits(jnp.transpose(features(held, start, size, centre, False)))


def pulled(near, jobs, target, size, first=None):
    width = target.shape[1] // 8
    tiles = []
    for group, source, masses, starts in jobs:
        for piece in range(2):
            here = lanes((2 * group + piece) * width, width)
            for turn, start in enumerate(starts):
                tiles.append((here, source, masses, lanes(start, size), turn == 0, turn + 1 == len(starts)))

    def squares(tile):
        return dot(tile[1][tile[3], :], target[:, tile[0]])

    ahead, kernel, total = squares(tiles[0]), None, None
    for turn in range(len(tiles) + 1):
        square = ahead
        if turn + 1 < len(tiles):
            ahead = squares(tiles[turn + 1])
        if turn > 0:
            here, _, masses, place, opens, closes = tiles[turn - 1]
            if opens:
                total = jnp.zeros((ROWS, width), jnp.float32) if first is None else first[:, here]
            total = total + dot(masses[:, place], kernel)
            if closes:
                near[:, here] = total
        if turn < len(tiles):
            kernel = low_bits(lax.rsqrt(square))


def own_groups(near, first, last, target, source, own):
    pts = source.shape[0] // 8
    pulled(near, [(group, source, own, [0]) for group in range(first, last)], target, 8 * pts)


def box_columns(depth, box_x, box_z, nodes):
    blocks = []
    for turn, distance in [(turn, distance) for turn in range(depth) for distance in range(ACROSS)]:
        gap_x = 2 * (box_x - (box_x ^ distance))
        gap_z = 2 * (box_z - ((box_z ^ turn) if depth == 4 else turn))
        across_x = nodes[0] + gap_x.astype(jnp.float32)
        across_z = nodes[2] + gap_z.astype(jnp.float32)
        apart = jnp.maximum(jnp.abs(gap_x), jnp.abs(gap_z)) >= 4
        value = lax.rsqrt(across_x * across_x + across_z * across_z + nodes[1])
        blocks.append(low_bits(value * jnp.where(apart, 1.0 / COEFFS, 0.0)))
    return jnp.concatenate(blocks, axis=0)


def own_kernel(depth, count_in, weights_in, own, *rest):
    tables, outs, (nodes, count, weights, sems) = rest[:3], rest[3:11], rest[11:]
    near, source, target, scale, column, columns, far, spread = outs
    copies = fetch([*zip(tables, (far, spread, nodes)), (count_in, count), (weights_in, weights)], sems)
    points = own.shape[1]
    pts = points // 8
    for leaf in range(8):
        centre = [bit - 0.5 for bit in bits(leaf)]
        source[lanes(leaf * pts, pts), :] = source_features(own, leaf * pts, pts, centre)
        target[:, lanes(leaf_slot(leaf) * pts, pts)] = low_bits(features(own, leaf * pts, pts, centre, True))
    own_groups(near, 0, EARLY, target, source, own)
    for copy in copies:
        copy.wait()
    columns[...] = box_columns(depth, *box_place(), nodes)
    column[...] = by_row([weights[field] for field in range(weights.shape[0])], column.shape)
    lane_index = lax.broadcasted_iota(jnp.int32, (1, pts), 1)
    for leaf in range(8):
        scale[:, leaf * pts : (leaf + 1) * pts] = jnp.where(lane_index < count[leaf], 1.0 / (128.0 * pts), 0.0)


def spread_first(value, node):
    starts = [leaf * SLOT + node for leaf in range(8)]
    return jnp.concatenate([jnp.broadcast_to(value[:, s : s + 1], (ROWS, SLOT)) for s in starts], axis=1)


def decoded(coded):
    value = coded.astype(jnp.float32)
    node = lax.broadcasted_iota(jnp.int32, value.shape, 1) % SLOT
    return jnp.where(node == 0, 0.0, value) + spread_first(value, 0) + spread_first(value, COEFFS)


def faces_of(faces, bit, given, own, left, right, rows=None):
    points = own.shape[1]
    pts = points // 8
    for y in range(2):
        for x in range(4):
            place = lanes((2 * x + y) * pts, pts)
            if x in (0, 3):
                side = left if x == 0 else right
                faces[:, place] = side[:, lanes((y + 2 * bit) * pts, pts)]
            else:
                faces[:, place] = own[:, lanes((x - 1 + 2 * y + 4 * bit) * pts, pts)]
    node = lax.broadcasted_iota(jnp.int32, given.shape, 1) % SLOT
    base = spread_first(given, 0)
    base_high = low_bits(base).astype(jnp.float32)
    coded = jnp.where(node == 0, base_high, jnp.where(node == COEFFS, base - base_high, given - base))
    faces[:, lanes(points, LEAVES)] = low_bits(coded)
    if rows is not None:
        faces[:, lanes(points + LEAVES, rows.shape[1])] = rows


def sums_for(above, left, moments, right, far):
    base = left.shape[1] - LEAVES
    around = jnp.concatenate([left[:, lanes(base, LEAVES)], moments[...], right[:, lanes(base, LEAVES)]], axis=1)
    return dot(around, far[lanes(jnp.where(above == 1, 0, 5 * LEAVES), 3 * LEAVES), :])


def row_kernel(own, moments, totals, from_1, from_2, from_3, far, left, right, faces_even, rows):
    box_x, box_z = box_place()
    for side, step in ((left, -1), (right, 1)):
        side[...] = jnp.zeros(side.shape, side.dtype)
        for distance, held in ((1, from_1), (3, from_3)):

            @pl.when((box_x ^ distance) - box_x == step)
            def _(side=side, held=held):
                side[...] = held[:, lanes(0, side.shape[1])]

    ends = lanes(left.shape[1], 2 * SLOT)
    row = [totals[...], from_1[:, ends], from_2[...], from_3[:, ends]]
    row = jnp.concatenate([box[:, :SLOT] for box in row], axis=1)
    rows[...] = row
    above = 1 - lax.rem(box_z, 2)
    faces_of(faces_even, above, sums_for(above, left, moments, right, far), own, left, right, row)


def side_pulls(near, faces, early, target, scratch):
    pts = early.shape[1] // 8
    jobs = []
    for (step, side), held in zip(faces, scratch):
        for place in range(4):
            centre = (1.5 if step else -1.5, place % 2 - 0.5, place // 2 - 0.5)
            held[lanes(place * pts, pts), :] = source_features(side, place * pts, pts, centre)
        jobs += [(step, held, side, [0]), (step + 2, held, side, [0])]
    pulled(near, jobs, target, 4 * pts, early)


def middle_kernel(own, left, right, moments, far, early, source, target, near, faces_odd, same, *sides):
    points = own.shape[1]
    _, box_z = box_place()
    above = lax.rem(box_z, 2)
    faces_of(faces_odd, above, sums_for(above, left, moments, right, far), own, left, right)
    base = left.shape[1] - LEAVES
    beside = jnp.concatenate([left[:, lanes(base, LEAVES)], right[:, lanes(base, LEAVES)]], axis=1)
    same[...] = dot(beside, far[lanes(3 * LEAVES, 2 * LEAVES), :])
    near[:, lanes(0, EARLY * points // 4)] = early[...]
    own_groups(near, EARLY, 4, target, source, own)

    @pl.when(above == 1)
    def _():
        side_pulls(near, [(0, left)], near, target, sides)


def one_side(near, step, side, early, target, held):
    pts = early.shape[1] // 8
    for group in (1 - step, 3 - step):
        here = lanes(2 * group * pts, 2 * pts)
        near[:, here] = early[:, here]
    side_pulls(near, [(step, side)], early, target, [held])


def side_kernel(left, right, early, target, near, held):
    _, box_z = box_place()
    odd = lax.rem(box_z, 2) == 1

    @pl.when(odd)
    def _():
        one_side(near, 1, right, early, target, held)

    @pl.when(jnp.logical_not(odd))
    def _():
        one_side(near, 0, left, early, target, held)


def both_kernel(rows, faces, near, both):
    width = rows.shape[1]
    both[:, lanes(0, width)] = rows[...]
    both[:, lanes(width, width)] = faces[:, lanes(faces.shape[1] - width, width)]


def layer_pulls(near, early, step, inside, target, faces, sides):
    points = early.shape[1]
    pts = points // 8

    @pl.when(inside)
    def _():
        for place in range(8):
            height = jnp.where(step == 1, 1.5, -1.5)
            centre = (place // 2 - 1.5, place % 2 - 0.5, height)
            sides[lanes(place * pts, pts), :] = source_features(faces, place * pts, pts, centre)

        jobs = [(i + 2 * step, sides, faces, [2 * i * pts]) for i in range(2)]
        pulled(near, jobs, target, 6 * pts, early)

    @pl.when(jnp.logical_not(inside))
    def _():
        here = lanes(step * (points // 2), points // 2)
        near[:, here] = early[:, here]


def even_kernel(early, target, right, faces, near, sides, held):
    _, box_z = box_place()
    step = 1 - lax.rem(box_z, 2)

    @pl.when(step == 0)
    def _():
        near[...] = early[...]

    @pl.when(step == 1)
    def _():
        one_side(near, 1, right, early, target, held)

    layer_pulls(near, near, step, box_z >= 0, target, faces, sides)


def odd_inside(depth):
    _, box_z = box_place()
    step = lax.rem(box_z, 2)
    return step, (box_z + 2 * step - 1 >= 0) & (box_z + 2 * step - 1 < depth)


def odd_kernel(depth, early, target, faces, near, sides):
    points = early.shape[1]
    step, inside = odd_inside(depth)
    other = lanes((1 - step) * (points // 2), points // 2)
    near[:, other] = early[:, other]
    layer_pulls(near, early, step, inside, target, faces, sides)


def last_kernel(depth, near, faces_even, faces_odd, basis, scale, column, columns, spread, same, *rest):
    held, (potential, sums) = rest[:-2], rest[-2:]
    fields, points = potential.shape
    pts = points // 8
    _, inside = odd_inside(depth)
    if depth == 4:
        rows, distant = held
        width = rows.shape[1]
        near_rows = faces_even[:, lanes(faces_even.shape[1] - width, width)]
        layers = [rows[...], near_rows, distant[:, lanes(0, width)], distant[:, lanes(width, width)]]
    else:
        layers = [held[0][layer] for layer in range(depth)]
    coarse_high, coarse_low = high_low(dot(jnp.concatenate(layers, axis=1), columns[...]))
    value = same[...] + dot(coarse_high, spread[...]) + dot(coarse_low, spread[...])
    value = value + decoded(faces_even[:, lanes(points, LEAVES)])
    value = value + jnp.where(inside, decoded(faces_odd[:, lanes(points, LEAVES)]), 0.0)
    local_high, local_low = high_low(value)
    weight = column[0:fields, 0:1]
    for leaf in range(8):
        here = slice(leaf * pts, (leaf + 1) * pts)
        slot = slice(leaf * SLOT, (leaf + 1) * SLOT)
        doubled = jnp.concatenate([local_high[:, slot], local_high[:, slot]], axis=1)
        far_part = dot(doubled, basis[:, here]) + dot(local_low[:, slot], basis[0:SLOT, here])
        total = near[0:fields, lanes(leaf_slot(leaf) * pts, pts)] + far_part[:fields]
        total = total * scale[:, here]
        potential[:, here] = total
        sums[:, here] = jnp.sum(total * weight, axis=0, keepdims=True)
    sums[:, points:] = jnp.broadcast_to(jnp.sum(weight), (1, sums.shape[1] - points))


def mean_kernel(mine, other, mean):
    points = mean.shape[1]
    total = mine[...] + other[...]
    mean[...] = total[:, :points] / total[:, points : points + 1]


def swapped(block, axis, partner):
    size = lax.axis_size(axis)
    return lax.ppermute(block, axis, [(partner(i), i) for i in range(size)])


def swapped_odd(block):
    boxes, cores = lax.axis_size("space"), lax.axis_size("sig")
    pairs = []
    for box in range(boxes):
        other = box + ACROSS if box // ACROSS % 2 else box - ACROSS
        for core in range(cores):
            source = other * cores + core if 0 <= other < boxes else box * cores + (core ^ 1)
            pairs.append((source, box * cores + core))
    return lax.ppermute(block, ("space", "sig"), pairs)


def per_device(positions, density, leaf_count, sigma_weights):
    fields, points = density.shape
    pts = points // 8
    depth = lax.axis_size("space") // ACROSS
    vmem, hbm = pl.BlockSpec(memory_space=pltpu.VMEM), pl.BlockSpec(memory_space=pltpu.HBM)

    def call(kernel, name, in_specs, outs, scratch, *args):
        return pl.pallas_call(
            kernel,
            in_specs=in_specs,
            out_specs=[vmem] * len(outs),
            out_shape=[jax.ShapeDtypeStruct(shape, dtype) for shape, dtype in outs],
            scratch_shapes=scratch,
            compiler_params=pltpu.CompilerParams(vmem_limit_bytes=24 * MEGA),
            name=name,
        )(*(pltpu.with_memory_space_constraint(a, pltpu.HBM) if s is hbm else a for s, a in zip(in_specs, args)))

    half, full = jnp.bfloat16, jnp.float32
    shift = shift_table()
    side_shape = ((ROWS, 4 * pts + LEAVES), half)
    given_shape = ((ROWS, 4 * pts + LEAVES + 2 * SLOT), half)
    faces_shape = ((ROWS, points + LEAVES), half)
    even_shape = ((ROWS, points + LEAVES + SLOT * ACROSS), half)
    rows_shape = ((ROWS, SLOT * ACROSS), half)
    both_shape = ((ROWS, 2 * SLOT * ACROSS), half)
    near_shape, sums_shape = ((ROWS, points), full), ((ROWS, LEAVES), full)
    side_scratch = pltpu.VMEM((4 * pts, FEATURES), half)
    rows_scratch = pltpu.VMEM((8 * pts, FEATURES), half)
    own, basis, moments, totals, *given = call(
        pack_kernel,
        "pack",
        [hbm] * 6,
        [
            ((ROWS, points), half),
            ((2 * SLOT, points), half),
            ((ROWS, LEAVES), half),
            ((ROWS, 2 * SLOT), half),
            given_shape,
            given_shape,
        ],
        [
            pltpu.SMEM((8,), jnp.int32),
            pltpu.VMEM((3, points), full),
            pltpu.VMEM((fields, points), half),
            pltpu.VMEM((LEAVES, SLOT), half),
            pltpu.VMEM((SLOT, SLOT), half),
            pltpu.VMEM((3 * SLOT, 16), half),
            pltpu.SemaphoreType.DMA((6,)),
        ],
        leaf_count,
        positions,
        density,
        jnp.asarray(shift, half),
        jnp.asarray(heavy_table(), half),
        jnp.asarray(power_table(), half),
    )
    from_2 = swapped(totals, "space", lambda i: i ^ 2)
    from_1 = swapped(given[0], "space", lambda i: i ^ 1)
    from_3 = swapped(given[1], "space", lambda i: i ^ 3)
    near, source, target, scale, column, columns, far, spread = call(
        functools.partial(own_kernel, depth),
        "near_own",
        [hbm] * 2 + [vmem] + [hbm] * 3,
        [
            ((ROWS, EARLY * points // 4), full),
            ((points, FEATURES), half),
            ((FEATURES, points), half),
            ((1, points), full),
            ((ROWS, 128), full),
            ((ACROSS * depth * SLOT, SLOT), half),
            ((len(STEPS) * LEAVES, LEAVES), half),
            ((SLOT, LEAVES), half),
        ],
        [
            pltpu.VMEM((3, SLOT, SLOT), full),
            pltpu.SMEM((8,), jnp.int32),
            pltpu.SMEM((fields,), full),
            pltpu.SemaphoreType.DMA((5,)),
        ],
        leaf_count,
        sigma_weights,
        own,
        jnp.asarray(far_table(), half),
        jnp.asarray(shift.T.copy(), half),
        jnp.asarray(box_nodes()),
    )
    left, right, faces_even, rows = call(
        row_kernel,
        "row",
        [vmem] * 7,
        [side_shape, side_shape, even_shape, rows_shape],
        [],
        own,
        moments,
        totals,
        from_1,
        from_2,
        from_3,
        far,
    )
    faces_even = swapped(faces_even, "space", lambda i: i ^ ACROSS)
    near, faces_odd, same = call(
        middle_kernel,
        "near_middle",
        [vmem] * 8,
        [near_shape, faces_shape, sums_shape],
        [side_scratch],
        own,
        left,
        right,
        moments,
        far,
        near,
        source,
        target,
    )
    faces_odd = swapped_odd(faces_odd)
    near, = call(
        side_kernel,
        "near_side",
        [vmem] * 4,
        [near_shape],
        [side_scratch],
        left,
        right,
        near,
        target,
    )
    if depth == 4:
        both, = call(both_kernel, "row_pairs", [vmem] * 3, [both_shape], [], rows, faces_even, near)
        held = [rows, swapped(both, "space", lambda i: i ^ (2 * ACROSS))]
    else:
        groups = [[z * ACROSS + x for z in range(depth)] for x in range(ACROSS)]
        held = [lax.all_gather(rows, "space", axis_index_groups=groups)]
    near, = call(
        even_kernel,
        "near_even",
        [vmem] * 4,
        [near_shape],
        [rows_scratch, side_scratch],
        near,
        target,
        right,
        faces_even,
    )
    near, = call(
        functools.partial(odd_kernel, depth),
        "near_odd",
        [vmem] * 3,
        [near_shape],
        [rows_scratch],
        near,
        target,
        faces_odd,
    )
    potential, sums = call(
        functools.partial(last_kernel, depth),
        "evaluate",
        [vmem] * (9 + len(held)),
        [((fields, points), full), ((1, points + 128), full)],
        [],
        near,
        faces_even,
        faces_odd,
        basis,
        scale,
        column,
        columns,
        spread,
        same,
        *held,
    )
    if lax.axis_size("sig") == 2:
        other = swapped(sums, "sig", lambda i: i ^ 1)
    else:
        other = lax.psum(sums, "sig") - sums
    mean, = call(mean_kernel, "mean", [vmem] * 2, [((1, points), full)], [], sums, other)
    return potential, mean.reshape(points)


def solution(mesh):
    in_specs = (P(None, "space"), P("sig", "space"), P("space"), P("sig"))
    out_specs = (P("sig", "space"), P("space"))
    return jax.shard_map(per_device, mesh=mesh, in_specs=in_specs, out_specs=out_specs, check_vma=False)
```
